32 devices in a mesh: dp: 16 (over z, y, core), ctx: 2 (over x).
Axes of the slice: x: 2, y: 2, z: 4, core: 2. Of those that a mesh axis runs over, the one named last changes fastest.
Arguments:
- inputs: bfloat16 [16, 256, 1280], P(None, ('dp', 'ctx')), may hold values from -6 to 6
- cotangent: bfloat16 [16, 256, 1280], P(None, ('dp', 'ctx')), may hold values from -6 to 6
- w_query: float32 [1280, 1280], P(('dp', 'ctx')), may hold values from -0.15625 to 0.15625
- w_key: float32 [1280, 1280], P(('dp', 'ctx')), may hold values from -0.15625 to 0.15625
- w_value: float32 [1280, 1280], P(('dp', 'ctx')), may hold values from -0.15625 to 0.15625
- w_output: float32 [1280, 1280], P(('dp', 'ctx')), may hold values from -1.25 to 1.25
- w_up: float32 [1280, 1280], P(('dp', 'ctx')), may hold values from -0.15625 to 0.15625
- w_down: float32 [1280, 1280], P(('dp', 'ctx')), may hold values from -0.15625 to 0.15625
- attn_gain: float32 [1280], P(('dp', 'ctx')), may hold values from 0.1 to 1.9
- mlp_gain: float32 [1280], P(('dp', 'ctx')), may hold values from 0.1 to 1.9
- query_scale: float32 [1280], P(('dp', 'ctx')), may hold values from -1 to 1
- deal: int32 [16], replicated, may hold values from 0 to 15, each once
- lengths: int32 [16], replicated, may hold values from 64 to 256, as said below
Outputs:
- outputs: bfloat16 [16, 256, 1280], P(None, ('dp', 'ctx'))
- grad_inputs: bfloat16 [16, 256, 1280], P(None, ('dp', 'ctx'))
- grad_w_query: float32 [1280, 1280], P(('dp', 'ctx'))
- grad_w_key: float32 [1280, 1280], P(('dp', 'ctx'))
- grad_w_value: float32 [1280, 1280], P(('dp', 'ctx'))
- grad_w_output: float32 [1280, 1280], P(('dp', 'ctx'))
- grad_w_up: float32 [1280, 1280], P(('dp', 'ctx'))
- grad_w_down: float32 [1280, 1280], P(('dp', 'ctx'))
- grad_attn_gain: float32 [1280], P(('dp', 'ctx'))
- grad_mlp_gain: float32 [1280], P(('dp', 'ctx'))
- grad_query_scale: float32 [1280], P(('dp', 'ctx'))
The draws below stay inside these ranges and needn't reach their ends.
Inputs may be any that keep to these rules, and one draw needn't show every extreme that they name: lengths[i] is the length of sequence deal[i]; one sequence has exactly 256.
All inputs are finite; a program needn't handle non-finite values.
Results may differ from the reference program's by a relative error of at most 0.028.
Values may be sent and summed in bfloat16 or wider, within the bound.
No kernel may reach another device: no remote copies, remote signals or barrier semaphores. Data moves between devices by JAX's collectives and lax.ppermute only.
A program may use at most 256 MiB of HBM per device.

```python
import math
import jax
import jax.numpy as jnp
from jax import lax

D = 1280
F = 1280
H = 16
HD = 80
SEQ_LEN = 256
SEQS = 16


def draw_lengths(key, part):
    key = jax.random.fold_in(key, 11)
    first_key, second_key = jax.random.split(key)
    drawn = jax.random.randint(first_key, (SEQS,), SEQ_LEN // 4, SEQ_LEN + 1)
    chosen = jax.random.randint(second_key, (), 0, SEQS)
    return jnp.where(jnp.arange(SEQS) == chosen, SEQ_LEN, drawn).astype(jnp.int32)


def block_levels(key, shape, cuts, least, high):
    level, own = 1.0, jax.random.fold_in(key, 6)
    for position, blocks in cuts:
        heights = jnp.exp(jax.random.uniform(jax.random.fold_in(own, position), (blocks,), jnp.float32, least / len(cuts), high / len(cuts)))
        level = level * jnp.repeat(heights, shape[position] // blocks).reshape([-1 if axis == position else 1 for axis in range(len(shape))])
    return level


def scatter_about(rng, extent, scale, limit, cuts=(), kind=jnp.bfloat16):
    array = jax.random.normal(rng, extent, jnp.float32) * scale
    if len(cuts) > 0:
        array = block_levels(rng, extent, cuts, -0.22, 0.18) * array
    return jnp.clip(array, min=-limit, max=limit).astype(kind)


def setup_inputs(seed: int = 0) -> dict:
    key_list = jax.random.split(jax.random.key(seed), 14)
    inputs = scatter_about(key_list[0], (SEQS, SEQ_LEN, D), 1.0, 6.0, ((1, 32),))
    cotangent = scatter_about(key_list[1], (SEQS, SEQ_LEN, D), 1.0, 6.0, ((1, 32),))
    w_query = scatter_about(key_list[2], (D, D), D ** -0.5, 0.15625, ((0, 32),), jnp.float32)
    w_key = scatter_about(key_list[3], (D, D), D ** -0.5, 0.15625, ((0, 32),), jnp.float32)
    w_value = scatter_about(key_list[4], (D, D), D ** -0.5, 0.15625, ((0, 32),), jnp.float32)
    w_output = scatter_about(key_list[5], (D, D), (max(1, 4 * D // SEQ_LEN)) ** -0.5, 1.25, ((0, 32),), jnp.float32)
    w_up = scatter_about(key_list[6], (D, F), D ** -0.5, 0.15625, ((0, 32),), jnp.float32)
    w_down = scatter_about(key_list[7], (F, D), F ** -0.5, 0.15625, ((0, 32),), jnp.float32)
    attn_gain = jnp.clip(1.0 + 0.18 * jax.random.normal(key_list[8], (D,), jnp.float32), 0.1, 1.9)
    mlp_gain = jnp.clip(1.0 + 0.18 * jax.random.normal(key_list[9], (D,), jnp.float32), 0.1, 1.9)
    query_scale = jnp.clip(jax.random.uniform(key_list[10], (D,), jnp.float32, -1.0, 1.0) * block_levels(key_list[10], (D,), ((0, 32),), -0.4, 0.0), -1.0, 1.0)
    deal = jax.random.permutation(key_list[11], SEQS).astype(jnp.int32)
    lengths = draw_lengths(jax.random.fold_in(key_list[13], 71), 0)
    return {"inputs": inputs, "cotangent": cotangent, "w_query": w_query, "w_key": w_key, "w_value": w_value, "w_output": w_output, "w_up": w_up, "w_down": w_down, "attn_gain": attn_gain, "mlp_gain": mlp_gain, "query_scale": query_scale, "deal": deal, "lengths": lengths}


@jax.custom_vjp
def low(v):
    return lax.optimization_barrier(v.astype(jnp.bfloat16)).astype(jnp.float32)

@jax.custom_vjp
def low_back(v):
    return v

def low_keep(v):
    return (low(v), None)

def low_pass(kept, grad):
    return (grad,)

def back_keep(v):
    return (v, None)

def back_low(kept, grad):
    return (low(grad),)
low.defvjp(low_keep, low_pass)
low_back.defvjp(back_keep, back_low)

def norm_rows(values, gain):
    return values * lax.rsqrt(lax.optimization_barrier(jnp.mean(values * values, axis=-1, keepdims=True)) + 1e-06) * gain

def mult(left, right):
    return jnp.dot(left, right, precision=lax.Precision.HIGHEST, preferred_element_type=jnp.float32)

def sequence_layer(seq_in, seq_length, params):
    query_w, key_w, value_w, output_w, up_w, down_w, gain_one, gain_two, scale_param = params
    total = seq_in.shape[0]
    hidden_one = low(norm_rows(seq_in, gain_one))
    factor = 1.442695041 / math.sqrt(HD) * jax.nn.softplus(scale_param)
    queries = low(low_back(mult(hidden_one, query_w)) * factor).reshape(total, H, HD)
    keys_all = low(low_back(mult(hidden_one, key_w))).reshape(total, H, HD)
    values_all = low(low_back(mult(hidden_one, value_w))).reshape(total, H, HD)
    positions = jnp.arange(total, dtype=jnp.int32)
    block_rows = min(512, total)

    def attend(first_row):
        query_block = lax.dynamic_slice_in_dim(queries, first_row, block_rows, 0)
        query_pos = first_row + jnp.arange(block_rows, dtype=jnp.int32)
        scores = low_back(jnp.einsum('rhd,khd->hrk', query_block, keys_all, precision=lax.Precision.HIGHEST))
        allowed = (positions[None, :] <= query_pos[:, None]) & (positions[None, :] < seq_length)
        scores = jnp.where(allowed[None], scores, -1e+30)
        probs = low(jax.nn.softmax(scores, axis=-1))
        return jnp.einsum('hrk,khd->rhd', probs, values_all, precision=lax.Precision.HIGHEST)
    starts = (jnp.arange(total // block_rows, dtype=jnp.int32) * block_rows).astype(jnp.int32)
    attended = lax.map(jax.checkpoint(attend), starts).reshape(total, H * HD)
    attended = low(low_back(attended))
    middle = seq_in + low_back(mult(attended, output_w))
    hidden_two = low(norm_rows(middle, gain_two))
    active = low(jax.nn.silu(low_back(mult(hidden_two, up_w))))
    return middle + low_back(mult(active, down_w))

def reference(inputs, cotangent, w_query, w_key, w_value, w_output, w_up, w_down, attn_gain, mlp_gain, query_scale, deal, lengths):
    seq_lengths = jnp.zeros_like(lengths).at[deal].set(lengths)
    layer_in = inputs.astype(jnp.float32)

    def layer(values_in, query_w, key_w, value_w, output_w, up_w, down_w, gain_one, gain_two, scale_param):
        rounded = [low(item) for item in (query_w, key_w, value_w, output_w, up_w, down_w, gain_one, gain_two, scale_param)]
        per_sequence = jax.checkpoint(lambda pair: sequence_layer(pair[0], pair[1], rounded))
        return lax.map(per_sequence, (values_in, seq_lengths))
    result, pull = jax.vjp(layer, layer_in, w_query, w_key, w_value, w_output, w_up, w_down, attn_gain, mlp_gain, query_scale)
    grads = pull(cotangent.astype(jnp.float32))
    return (result.astype(jnp.bfloat16), grads[0].astype(jnp.bfloat16), grads[1], grads[2], grads[3], grads[4], grads[5], grads[6], grads[7], grads[8], grads[9])
```

```python
import math

import jax
import jax.numpy as jnp
from jax import lax
from jax.experimental import pallas as pl
from jax.experimental.pallas import tpu as pltpu
from jax.sharding import Mesh, PartitionSpec as P

H = 16
HD = 80


def mult_trans(left, right):
    return lax.dot_general(
        left, right, (((1,), (1,)), ((), ())), preferred_element_type=jnp.float32
    )


def trans_mult(left, right):
    return lax.dot_general(
        left, right, (((0,), (0,)), ((), ())), preferred_element_type=jnp.float32
    )


def position_of(index, local_rows, piece_rows, groups):
    column = index // local_rows
    within = index % local_rows
    return (within // piece_rows * groups + column) * piece_rows + within % piece_rows


def norm_back(grad_hidden, normed, inverse, gain_value):
    grad_normed = grad_hidden * gain_value
    return inverse * (grad_normed - normed * jnp.mean(grad_normed * normed, axis=1, keepdims=True))


def per_device(
    inputs,
    cotangent,
    w_query,
    w_key,
    w_value,
    w_output,
    w_up,
    w_down,
    attn_gain,
    mlp_gain,
    query_scale,
    deal,
    lengths,
):
    groups = lax.axis_size("ctx")
    group_index = lax.axis_index("dp")
    ctx_index = lax.axis_index("ctx")
    head_count = H
    head_dim = HD
    piece_rows = inputs.shape[1]
    seq_numbers = jnp.arange(inputs.shape[0], dtype=jnp.int32)
    seq_lengths = jnp.sum(
        jnp.where(deal[None, :] == seq_numbers[:, None], lengths[None, :], 0), axis=1
    )
    local_in, local_cot = (
        lax.all_to_all(inputs, "dp", split_axis=0, concat_axis=1, tiled=True),
        lax.all_to_all(cotangent, "dp", split_axis=0, concat_axis=1, tiled=True),
    )
    seq_count, local_rows, model_width = local_in.shape
    padded = local_rows * groups
    token_count = seq_count * local_rows
    my_lengths = lax.dynamic_slice_in_dim(seq_lengths, group_index * seq_count, seq_count, 0)
    query_pos = position_of(
        ctx_index * local_rows + jnp.arange(local_rows, dtype=jnp.int32),
        local_rows,
        piece_rows,
        groups,
    )
    flat_in = local_in.reshape(token_count, model_width).astype(jnp.float32)
    flat_cot = local_cot.reshape(token_count, model_width)
    lowered = (
        w_query.astype(jnp.bfloat16),
        w_key.astype(jnp.bfloat16),
        w_value.astype(jnp.bfloat16),
        w_output.astype(jnp.bfloat16),
        w_up.astype(jnp.bfloat16),
        w_down.astype(jnp.bfloat16),
        attn_gain.astype(jnp.bfloat16),
        mlp_gain.astype(jnp.bfloat16),
        query_scale.astype(jnp.bfloat16),
    )
    gathered = (
        lax.all_gather(lowered[0], ("dp", "ctx"), axis=0, tiled=True),
        lax.all_gather(lowered[1], ("dp", "ctx"), axis=0, tiled=True),
        lax.all_gather(lowered[2], ("dp", "ctx"), axis=0, tiled=True),
        lax.all_gather(lowered[3], ("dp", "ctx"), axis=0, tiled=True),
        lax.all_gather(lowered[4], ("dp", "ctx"), axis=0, tiled=True),
        lax.all_gather(lowered[5], ("dp", "ctx"), axis=0, tiled=True),
        lax.all_gather(lowered[6], ("dp", "ctx"), axis=0, tiled=True),
        lax.all_gather(lowered[7], ("dp", "ctx"), axis=0, tiled=True),
        lax.all_gather(lowered[8], ("dp", "ctx"), axis=0, tiled=True),
    )
    (
        query_full,
        key_full,
        value_full,
        output_full,
        up_full,
        down_full,
        gain_one,
        gain_two,
        scale_raw,
    ) = gathered
    inv_one = lax.rsqrt(jnp.mean(flat_in * flat_in, axis=1, keepdims=True) + 1e-06)
    normed_one = flat_in * inv_one
    hidden_one = (normed_one * gain_one.astype(jnp.float32)).astype(jnp.bfloat16)
    scale_param = scale_raw.astype(jnp.float32)
    query_mult = 1.442695041 / math.sqrt(head_dim) * jax.nn.softplus(scale_param)
    query_pre = jnp.dot(hidden_one, query_full, preferred_element_type=jnp.float32)
    queries = (query_pre * query_mult).astype(jnp.bfloat16)
    keys_local = jnp.dot(hidden_one, key_full, preferred_element_type=jnp.float32).astype(
        jnp.bfloat16
    )
    values_local = jnp.dot(hidden_one, value_full, preferred_element_type=jnp.float32).astype(
        jnp.bfloat16
    )
    four_shape = (seq_count, local_rows, head_count, head_dim)
    query_four = queries.reshape(four_shape)
    keys_three = keys_local.reshape(seq_count, local_rows, model_width)
    values_three = values_local.reshape(seq_count, local_rows, model_width)

    def live_between(row_pos, key_pos):
        allowed = (key_pos[None, None, :] <= row_pos[None, :, None]) & (
            key_pos[None, None, :] < my_lengths[:, None, None]
        )
        return allowed[:, :, None, :]

    def live_mask(key_pos):
        return live_between(query_pos, key_pos)

    def attend_block(state_now, key_block, value_block, first_row):
        run_max, run_sum, run_acc = state_now
        block_len = key_block.shape[1]
        key_pos = position_of(
            first_row + jnp.arange(block_len, dtype=jnp.int32), local_rows, piece_rows, groups
        )
        key_four = key_block.reshape(seq_count, block_len, head_count, head_dim)
        value_four = value_block.reshape(seq_count, block_len, head_count, head_dim)
        scores = jnp.einsum(
            "srhd,skhd->srhk", query_four, key_four, preferred_element_type=jnp.float32
        )
        allowed = live_mask(key_pos)
        masked = jnp.where(allowed, scores, -1e30)
        new_max = jnp.maximum(run_max, jnp.max(masked, axis=3))
        weights_now = jnp.exp(jnp.where(allowed, masked - new_max[..., None], -1e30))
        factor = jnp.exp(run_max - new_max)
        new_sum = run_sum * factor + jnp.sum(weights_now, axis=3)
        added = jnp.einsum(
            "srhk,skhd->srhd",
            weights_now.astype(jnp.bfloat16),
            value_four,
            preferred_element_type=jnp.float32,
        )
        return (new_max, new_sum, run_acc * factor[..., None] + added)

    start_state = (
        jnp.full((seq_count, local_rows, head_count), -1e30, jnp.float32),
        jnp.zeros((seq_count, local_rows, head_count), jnp.float32),
        jnp.zeros(four_shape, jnp.float32),
    )
    key_piece = lax.all_gather(keys_three, "ctx", axis=1, tiled=True)
    value_piece = lax.all_gather(values_three, "ctx", axis=1, tiled=True)
    piece_len = key_piece.shape[1]
    fold_block_len = 512 if piece_len % 512 == 0 else piece_len

    def one_block(state_now, block_index):
        offset = block_index * fold_block_len
        key_block = lax.dynamic_slice_in_dim(key_piece, offset, fold_block_len, 1)
        value_block = lax.dynamic_slice_in_dim(value_piece, offset, fold_block_len, 1)
        return (attend_block(state_now, key_block, value_block, offset), None)

    result_state, unused = lax.scan(
        one_block, start_state, jnp.arange(piece_len // fold_block_len, dtype=jnp.int32)
    )
    run_max, run_sum, run_acc = result_state
    log_total = run_max + jnp.log(run_sum)
    attn_exact = run_acc / run_sum[..., None]
    attended = attn_exact.reshape(token_count, model_width).astype(jnp.bfloat16)
    middle = flat_in + jnp.dot(attended, output_full, preferred_element_type=jnp.float32)
    inv_two = lax.rsqrt(jnp.mean(middle * middle, axis=1, keepdims=True) + 1e-06)
    normed_two = middle * inv_two
    hidden_two = (normed_two * gain_two.astype(jnp.float32)).astype(jnp.bfloat16)
    up_pre = jnp.dot(hidden_two, up_full, preferred_element_type=jnp.float32)
    active = jax.nn.silu(up_pre).astype(jnp.bfloat16)
    result = (middle + jnp.dot(active, down_full, preferred_element_type=jnp.float32)).astype(
        jnp.bfloat16
    )
    back_weights = (
        lax.all_gather(lowered[0], ("dp", "ctx"), axis=0, tiled=True),
        lax.all_gather(lowered[1], ("dp", "ctx"), axis=0, tiled=True),
        lax.all_gather(lowered[2], ("dp", "ctx"), axis=0, tiled=True),
        lax.all_gather(lowered[3], ("dp", "ctx"), axis=0, tiled=True),
        lax.all_gather(lowered[4], ("dp", "ctx"), axis=0, tiled=True),
        lax.all_gather(lowered[5], ("dp", "ctx"), axis=0, tiled=True),
        lax.all_gather(lowered[6], ("dp", "ctx"), axis=0, tiled=True),
        lax.all_gather(lowered[7], ("dp", "ctx"), axis=0, tiled=True),
        lax.all_gather(lowered[8], ("dp", "ctx"), axis=0, tiled=True),
    )
    (
        query_back,
        key_back,
        value_back,
        output_back,
        up_back,
        down_back,
        gain_one_back,
        gain_two_back,
        scale_back,
    ) = back_weights
    cot_wide = flat_cot.astype(jnp.float32)
    grad_down = trans_mult(active, flat_cot)
    grad_active = mult_trans(flat_cot, down_back)
    sigma_up = jax.nn.sigmoid(up_pre)
    grad_up_pre = (grad_active * sigma_up * (1.0 + up_pre * (1.0 - sigma_up))).astype(jnp.bfloat16)
    grad_up = trans_mult(hidden_two, grad_up_pre)
    grad_hidden_two = mult_trans(grad_up_pre, up_back)
    grad_gain_two = jnp.sum(grad_hidden_two * normed_two, axis=0)
    grad_middle = cot_wide + norm_back(
        grad_hidden_two, normed_two, inv_two, gain_two_back.astype(jnp.float32)
    )
    grad_middle_low = grad_middle.astype(jnp.bfloat16)
    grad_output = trans_mult(attended, grad_middle_low)
    grad_attended = mult_trans(grad_middle_low, output_back).astype(jnp.bfloat16)
    grad_att_four = grad_attended.reshape(four_shape)
    delta_rows = jnp.sum(grad_att_four.astype(jnp.float32) * attn_exact, axis=3)
    key_all, value_all = (
        lax.all_gather(keys_three, "ctx", axis=1, tiled=True),
        lax.all_gather(values_three, "ctx", axis=1, tiled=True),
    )
    block_len = min(512, padded)

    def back_block(block_index, state_now):
        grad_query, grad_key_all, grad_value_all = state_now
        offset = block_index * block_len
        key_block = lax.dynamic_slice_in_dim(key_all, offset, block_len, 1).reshape(
            seq_count, block_len, head_count, head_dim
        )
        value_block = lax.dynamic_slice_in_dim(value_all, offset, block_len, 1).reshape(
            seq_count, block_len, head_count, head_dim
        )
        key_pos = position_of(
            offset + jnp.arange(block_len, dtype=jnp.int32), local_rows, piece_rows, groups
        )
        scores = jnp.einsum(
            "srhd,skhd->srhk", query_four, key_block, preferred_element_type=jnp.float32
        )
        probs = jnp.exp(jnp.where(live_mask(key_pos), scores - log_total[..., None], -1e30))
        grad_value_block = jnp.einsum(
            "srhk,srhd->skhd",
            probs.astype(jnp.bfloat16),
            grad_att_four,
            preferred_element_type=jnp.float32,
        )
        grad_probs = jnp.einsum(
            "srhd,skhd->srhk", grad_att_four, value_block, preferred_element_type=jnp.float32
        )
        grad_scores = (probs * (grad_probs - delta_rows[..., None])).astype(jnp.bfloat16)
        grad_query = grad_query + jnp.einsum(
            "srhk,skhd->srhd", grad_scores, key_block, preferred_element_type=jnp.float32
        )
        grad_key_block = jnp.einsum(
            "srhk,srhd->skhd", grad_scores, query_four, preferred_element_type=jnp.float32
        )
        grad_key_all = lax.dynamic_update_slice_in_dim(
            grad_key_all, grad_key_block.reshape(seq_count, block_len, model_width), offset, 1
        )
        grad_value_all = lax.dynamic_update_slice_in_dim(
            grad_value_all, grad_value_block.reshape(seq_count, block_len, model_width), offset, 1
        )
        return (grad_query, grad_key_all, grad_value_all)

    zero_all = jnp.zeros((seq_count, padded, model_width), jnp.float32)
    grad_query, grad_key_all, grad_value_all = lax.fori_loop(
        0, padded // block_len, back_block, (jnp.zeros(four_shape, jnp.float32), zero_all, zero_all)
    )
    grad_key_mine, grad_value_mine = (
        lax.psum_scatter(
            grad_key_all.astype(jnp.bfloat16), "ctx", scatter_dimension=1, tiled=True
        ).astype(jnp.float32),
        lax.psum_scatter(
            grad_value_all.astype(jnp.bfloat16), "ctx", scatter_dimension=1, tiled=True
        ).astype(jnp.float32),
    )
    grad_query_flat = grad_query.reshape(token_count, model_width)
    grad_query_pre = (grad_query_flat * query_mult).astype(jnp.bfloat16)
    grad_scale = (
        1.442695041
        / math.sqrt(head_dim)
        * jax.nn.sigmoid(scale_back.astype(jnp.float32))
        * jnp.sum(grad_query_flat * query_pre, axis=0)
    )
    grad_key_low = grad_key_mine.reshape(token_count, model_width).astype(jnp.bfloat16)
    grad_value_low = grad_value_mine.reshape(token_count, model_width).astype(jnp.bfloat16)
    grad_wq = trans_mult(hidden_one, grad_query_pre)
    grad_wk = trans_mult(hidden_one, grad_key_low)
    grad_wv = trans_mult(hidden_one, grad_value_low)
    grad_hidden_one = (
        mult_trans(grad_query_pre, query_back)
        + mult_trans(grad_key_low, key_back)
        + mult_trans(grad_value_low, value_back)
    )
    grad_gain_one = jnp.sum(grad_hidden_one * normed_one, axis=0)
    grad_in = grad_middle + norm_back(
        grad_hidden_one, normed_one, inv_one, gain_one_back.astype(jnp.float32)
    )
    matrix_stack = jnp.stack([grad_wq, grad_wk, grad_wv, grad_output, grad_up, grad_down], axis=0)
    vector_stack = jnp.stack([grad_gain_one, grad_gain_two, grad_scale], axis=0)
    matrix_sums, vector_sums = (
        lax.psum_scatter(matrix_stack, ("dp", "ctx"), scatter_dimension=1, tiled=True),
        lax.psum_scatter(vector_stack, ("dp", "ctx"), scatter_dimension=1, tiled=True),
    )
    out_local = result.reshape(seq_count, local_rows, model_width)
    grad_local = grad_in.astype(jnp.bfloat16).reshape(seq_count, local_rows, model_width)
    back_out, back_grad = (
        lax.all_to_all(out_local, "dp", split_axis=1, concat_axis=0, tiled=True),
        lax.all_to_all(grad_local, "dp", split_axis=1, concat_axis=0, tiled=True),
    )
    return (
        back_out,
        back_grad,
        matrix_sums[0],
        matrix_sums[1],
        matrix_sums[2],
        matrix_sums[3],
        matrix_sums[4],
        matrix_sums[5],
        vector_sums[0],
        vector_sums[1],
        vector_sums[2],
    )


LOG2E = 1.442695041
CODES = (0, 1, 4, 5)


def plane_shift(value, step):
    if step == 1:
        return lax.ppermute(value, "x", [(0, 1), (1, 0)])
    if step == 2:
        return lax.ppermute(value, "y", [(0, 1), (1, 0)])
    return lax.ppermute(value, ("y", "x"), [(0, 3), (1, 2), (2, 1), (3, 0)])


def core_swap(value):
    return lax.ppermute(value, "core", [(0, 1), (1, 0)])


def ring_shift(value, step):
    return lax.ppermute(value, "z", [(i, (i + step) % 4) for i in range(4)])


def pick(array, index):
    return lax.dynamic_index_in_dim(array, index, 0, keepdims=False)


def by_source(pieces, z_index):
    own, one, two, three = pieces
    line = jnp.stack([three, two, one, own, three, two, one])
    return lax.dynamic_slice_in_dim(line, 3 - z_index, 4, 0)


def pair(mine, other, index, axis):
    first = index == 0
    return jnp.stack([jnp.where(first, mine, other), jnp.where(first, other, mine)], axis=axis)


def row_positions(shape, dim, z_index, plane_index):
    row = lax.broadcasted_iota(jnp.int32, shape, dim)
    chip = (row // 32) % 4
    code = (chip % 2) + 4 * (chip // 2) + 2 * (row // 128)
    hop = (row % 32) // 8
    return 64 * ((z_index - hop) & 3) + 8 * (plane_index ^ code) + row % 8


def live_pairs(info_ref, seq):
    z_index, plane_index = info_ref[0], info_ref[1]
    shape = (256, 256)
    query_pos = row_positions(shape, 0, z_index, plane_index)
    key_pos = row_positions(shape, 1, z_index, plane_index)
    return (key_pos <= query_pos) & (key_pos < info_ref[2 + seq])


def block_rows(near_ref, far_ref):
    return jnp.concatenate([near_ref[...], far_ref[...]], axis=0).reshape(256, near_ref.shape[2])


def soft_probs(query, key, live):
    scores = mult_trans(query, key)
    scores = jnp.where(live, scores, -1e30)
    top = jnp.max(scores, axis=1, keepdims=True)
    weights = jnp.where(live, jnp.exp(scores - top), 0.0)
    return weights / jnp.sum(weights, axis=1, keepdims=True)


def attend_kernel(info_ref, near_ref, far_ref, gain_ref, mult_ref, w_ref, pre_ref, att_near, att_far):
    seq = pl.program_id(0)
    live = live_pairs(info_ref, seq)
    wide = block_rows(near_ref, far_ref).astype(jnp.float32)
    inverse = lax.rsqrt(jnp.mean(wide * wide, axis=1, keepdims=True) + 1e-06)
    hidden = (wide * inverse * gain_ref[...]).astype(jnp.bfloat16)
    pre = jnp.dot(hidden, w_ref[...], preferred_element_type=jnp.float32)
    pre_ref[...] = pre.reshape(2, 4, 32, 480)
    query = (pre[:, 0:160] * mult_ref[...]).astype(jnp.bfloat16)
    key = pre[:, 160:320].astype(jnp.bfloat16)
    value = pre[:, 320:480].astype(jnp.bfloat16)
    heads = []
    for head in range(2):
        part = slice(80 * head, 80 * head + 80)
        probs = soft_probs(query[:, part], key[:, part], live).astype(jnp.bfloat16)
        heads.append(jnp.dot(probs, value[:, part], preferred_element_type=jnp.float32))
    att = jnp.concatenate(heads, axis=1).astype(jnp.bfloat16).reshape(2, 4, 32, 160)
    att_near[...] = att[0]
    att_far[...] = att[1]


def attend_back_kernel(
    info_ref, near_ref, far_ref, gain_ref, mult_ref, w_ref, pre_ref, grad_near, grad_far,
    hid_near, hid_far, w_grad, gain_grad, scale_grad, w_acc, gain_acc, scale_acc,
):
    seq = pl.program_id(0)

    @pl.when(seq == 0)
    def _():
        w_acc[...] = jnp.zeros_like(w_acc)
        gain_acc[...] = jnp.zeros_like(gain_acc)
        scale_acc[...] = jnp.zeros_like(scale_acc)

    live = live_pairs(info_ref, seq)
    wide = block_rows(near_ref, far_ref).astype(jnp.float32)
    inverse = lax.rsqrt(jnp.mean(wide * wide, axis=1, keepdims=True) + 1e-06)
    normed = wide * inverse
    hidden = (normed * gain_ref[...]).astype(jnp.bfloat16)
    pre = pre_ref[...].reshape(256, 480)
    mult = mult_ref[...]
    query = (pre[:, 0:160] * mult).astype(jnp.bfloat16)
    key = pre[:, 160:320].astype(jnp.bfloat16)
    value = pre[:, 320:480].astype(jnp.bfloat16)
    grad_att = block_rows(grad_near, grad_far)
    grad_q, grad_k, grad_v = [], [], []
    for head in range(2):
        part = slice(80 * head, 80 * head + 80)
        probs = soft_probs(query[:, part], key[:, part], live)
        grad_probs = mult_trans(grad_att[:, part], value[:, part])
        delta = jnp.sum(probs * grad_probs, axis=1, keepdims=True)
        grad_scores = (probs * (grad_probs - delta)).astype(jnp.bfloat16)
        grad_v.append(trans_mult(probs.astype(jnp.bfloat16), grad_att[:, part]))
        grad_q.append(jnp.dot(grad_scores, key[:, part], preferred_element_type=jnp.float32))
        grad_k.append(trans_mult(grad_scores, query[:, part]))
    grad_query = jnp.concatenate(grad_q, axis=1)
    scale_acc[...] += jnp.sum(grad_query * pre[:, 0:160], axis=0, keepdims=True)
    joined = jnp.concatenate([grad_query * mult] + grad_k + grad_v, axis=1).astype(jnp.bfloat16)
    w_acc[...] += trans_mult(hidden, joined)
    grad_hidden = mult_trans(joined, w_ref[...])
    gain_acc[...] += jnp.sum(grad_hidden * normed, axis=0, keepdims=True)
    low = grad_hidden.astype(jnp.bfloat16).reshape(2, 4, 32, 1280)
    hid_near[...] = low[0]
    hid_far[...] = low[1]

    @pl.when(seq == 3)
    def _():
        w_grad[...] = w_acc[...].astype(jnp.bfloat16)
        gain_grad[...] = gain_acc[...]
        scale_grad[...] = scale_acc[...]


def feed_kernel(
    info_ref, x_ref, g_ref, att_0, att_1, att_2, att_3, gain_ref, wo_ref, up_ref, down_ref,
    out_ref, act_ref, hid_ref, dup_ref, dm_ref, dmid_ref, datt_0, datt_1, datt_2, datt_3, gain_grad,
):
    plane_index = info_ref[1]
    atts, datts = (att_0, att_1, att_2, att_3), (datt_0, datt_1, datt_2, datt_3)

    def rows_of(chip, core):
        source = plane_index ^ (CODES[chip] + 2 * core)
        return pl.ds(pl.multiple_of(source * 160, 160), 160)

    middle = x_ref[...].astype(jnp.float32)
    for chip in range(4):
        for core in range(2):
            middle += jnp.dot(
                atts[chip][core], wo_ref[rows_of(chip, core), :], preferred_element_type=jnp.float32
            )
    inverse = lax.rsqrt(jnp.mean(middle * middle, axis=1, keepdims=True) + 1e-06)
    normed = middle * inverse
    gain = gain_ref[...]
    hidden = (normed * gain).astype(jnp.bfloat16)
    hid_ref[...] = hidden
    up = jnp.dot(hidden, up_ref[...], preferred_element_type=jnp.float32)
    sigma = jax.nn.sigmoid(up)
    active = (up * sigma).astype(jnp.bfloat16)
    act_ref[...] = active
    down = jnp.dot(active, down_ref[...], preferred_element_type=jnp.float32)
    out_ref[...] = (middle + down).astype(jnp.bfloat16)
    cot = g_ref[...]
    grad_act = mult_trans(cot, down_ref[...])
    grad_up = (grad_act * sigma * (1.0 + up * (1.0 - sigma))).astype(jnp.bfloat16)
    dup_ref[...] = grad_up
    grad_hidden = mult_trans(grad_up, up_ref[...])
    gain_grad[...] = jnp.sum(grad_hidden * normed, axis=0, keepdims=True)
    grad_mid = cot.astype(jnp.float32) + norm_back(grad_hidden, normed, inverse, gain)
    dmid_ref[...] = grad_mid
    low = grad_mid.astype(jnp.bfloat16)
    dm_ref[...] = low
    for chip in range(4):
        for core in range(2):
            datts[chip][core] = mult_trans(low, wo_ref[rows_of(chip, core), :]).astype(jnp.bfloat16)


def whole(shape):
    return pl.BlockSpec(shape, lambda *_: (0,) * len(shape))


def seq_block(*lead, width):
    count = len(lead)
    return pl.BlockSpec((*lead, 32, width), lambda s, info: (*(0,) * count, s, 0))


def planes(
    inputs, cotangent, w_query, w_key, w_value, w_output, w_up, w_down,
    attn_gain, mlp_gain, query_scale, deal, lengths,
):
    f32, bf16 = jnp.float32, jnp.bfloat16
    z, y, c, x = (lax.axis_index(name) for name in ("z", "y", "core", "x"))
    plane = 4 * y + 2 * c + x
    width = 1280
    seqs = jnp.arange(16, dtype=jnp.int32)
    seq_lengths = jnp.sum(jnp.where(deal[None, :] == seqs[:, None], lengths[None, :], 0), axis=1)
    my_lengths = lax.dynamic_slice_in_dim(seq_lengths, 4 * z, 4, 0)
    info = jnp.concatenate([jnp.stack([z, plane]), my_lengths]).astype(jnp.int32)

    vec = jnp.concatenate([attn_gain, mlp_gain, query_scale]).astype(bf16)
    vec_block = jnp.zeros((1, 8, width), bf16).at[0, 0, :120].set(vec)
    in_four = inputs.reshape(4, 4, 8, width)
    cot_four = cotangent.reshape(4, 4, 8, width)
    sent = [jnp.concatenate([pick(in_four, (z + k) % 4), vec_block]) for k in range(4)]
    got = [sent[0]] + [ring_shift(sent[k], k) for k in (1, 2, 3)]
    x_rows = jnp.stack([item[:4] for item in got], axis=1).reshape(128, width)
    vec_rows = jnp.concatenate([item[4, :1] for item in got] + [jnp.zeros((4, width), bf16)])
    own = jnp.concatenate([x_rows, vec_rows])

    qkv = jnp.stack([w_query, w_key, w_value]).astype(bf16)
    qkv = qkv.reshape(3, 40, 8, 160).transpose(2, 1, 0, 3).reshape(8, 40, 480)
    qkv = lax.all_to_all(qkv, ("y", "core", "x"), split_axis=0, concat_axis=0, tiled=True)
    qkv = qkv.reshape(320, 480)
    w_qkv = by_source([qkv] + [ring_shift(qkv, k) for k in (1, 2, 3)], z).reshape(width, 480)

    near = jnp.stack([own] + [plane_shift(own, step) for step in (1, 2, 3)])
    far = core_swap(near)

    big = jnp.stack([w_output, w_up, w_down]).astype(bf16)
    big = lax.all_gather(big, "z", axis=0)
    part_a, part_b = big[:2], big[2:]
    part_a = pair(part_a, plane_shift(part_a, 1), x, 2)
    part_b = pair(part_b, plane_shift(part_b, 2), y, 2)
    part_a = pair(part_a, plane_shift(part_a, 2), y, 2)
    part_b = pair(part_b, plane_shift(part_b, 1), x, 3)
    big = jnp.concatenate([part_a, part_b])
    other = core_swap(big)
    w_out_full, w_up_full, w_down_full = (
        pair(big[:, i], other[:, i], c, 2).reshape(width, width) for i in range(3)
    )

    vecs = jnp.stack([near[:, 128:132, :120], far[:, 128:132, :120]])
    vecs = vecs.astype(f32).reshape(2, 2, 2, 4, 120)
    vecs = jnp.where(c == 0, vecs, vecs[::-1])
    vecs = jnp.where(y == 0, vecs, vecs[:, ::-1])
    vecs = jnp.where(x == 0, vecs, vecs[:, :, ::-1])
    fours = jnp.arange(4, dtype=jnp.int32)
    from_hop = (z - fours[:, None]) % 4 == fours[None, :]
    vecs = jnp.sum(jnp.where(from_hop[:, None, None, None, :, None], vecs[None], 0.0), axis=4)
    vecs = vecs.reshape(4, 2, 2, 2, 3, 40).transpose(4, 0, 2, 1, 3, 5).reshape(3, width)
    gain_one, gain_two = vecs[0:1], vecs[1:2]
    my_scale = lax.dynamic_slice_in_dim(vecs[2:3], 160 * plane, 160, 1)
    query_mult = LOG2E / math.sqrt(HD) * jax.nn.softplus(my_scale)

    limit = pltpu.CompilerParams(vmem_limit_bytes=50 * 1024 * 1024)
    pre, att_near, att_far = pl.pallas_call(
        attend_kernel,
        grid_spec=pltpu.PrefetchScalarGridSpec(
            num_scalar_prefetch=1,
            grid=(4,),
            in_specs=[
                seq_block(4, width=width), seq_block(4, width=width),
                whole((1, width)), whole((1, 160)), whole((width, 480)),
            ],
            out_specs=[seq_block(2, 4, width=480), seq_block(4, width=160), seq_block(4, width=160)],
        ),
        out_shape=[
            jax.ShapeDtypeStruct((2, 4, 128, 480), f32),
            jax.ShapeDtypeStruct((4, 128, 160), bf16),
            jax.ShapeDtypeStruct((4, 128, 160), bf16),
        ],
        compiler_params=limit,
        cost_estimate=pl.CostEstimate(flops=1_500_000_000, bytes_accessed=8_000_000, transcendentals=600_000),
        name="attend",
    )(info, near, far, gain_one, query_mult, w_qkv)

    att_pair = jnp.stack([att_near, core_swap(att_far)], axis=1)
    atts = [att_pair[0]] + [plane_shift(att_pair[step], step) for step in (1, 2, 3)]

    cot_sent = [pick(cot_four, (z + k) % 4) for k in range(4)]
    cot_got = [cot_sent[0]] + [ring_shift(cot_sent[k], k) for k in (1, 2, 3)]
    cot_rows = jnp.stack(cot_got, axis=1).reshape(128, width)

    low_rows = jax.ShapeDtypeStruct((128, width), bf16)
    datt_shape = jax.ShapeDtypeStruct((2, 128, 160), bf16)
    smem = pl.BlockSpec(memory_space=pltpu.SMEM)
    vmem = pl.BlockSpec(memory_space=pltpu.VMEM)
    out_rows, active, hidden_two, grad_up, dm, grad_mid, *datts, gain_two_grad = pl.pallas_call(
        feed_kernel,
        in_specs=[smem] + [vmem] * 10,
        out_specs=[vmem] * 11,
        out_shape=[low_rows] * 5
        + [jax.ShapeDtypeStruct((128, width), f32)]
        + [datt_shape] * 4
        + [jax.ShapeDtypeStruct((1, width), f32)],
        compiler_params=limit,
        cost_estimate=pl.CostEstimate(flops=2_600_000_000, bytes_accessed=13_000_000, transcendentals=200_000),
        name="feed",
    )(info, x_rows, cot_rows, *atts, gain_two, w_out_full, w_up_full, w_down_full)

    back = [datts[0]] + [plane_shift(datts[step], step) for step in (1, 2, 3)]
    grad_att_near = jnp.stack([item[0] for item in back])
    grad_att_far = core_swap(jnp.stack([item[1] for item in back]))

    att_all = jnp.stack(atts).reshape(2, 2, 2, 128, 160)
    att_all = jnp.where(y == 0, att_all, att_all[::-1])
    att_all = jnp.where(x == 0, att_all, att_all[:, ::-1])
    att_all = jnp.where(c == 0, att_all, att_all[:, :, ::-1])
    att_all = att_all.transpose(3, 0, 2, 1, 4).reshape(128, width)

    def weight_grad(left, right):
        made = lax.dot_general(left, right, (((0,), (0,)), ((), ())), preferred_element_type=bf16)
        return made.reshape(4, 2, 2, 2, 40, width)

    grads = jnp.stack(
        [weight_grad(att_all, dm), weight_grad(hidden_two, grad_up), weight_grad(active, cot_rows)], axis=1
    )

    def added(left, right):
        return (left.astype(f32) + right.astype(f32)).astype(bf16)

    def halves(array, index, axis):
        first, second = (lax.index_in_dim(array, i, axis, keepdims=False) for i in (0, 1))
        return jnp.where(index == 0, first, second), jnp.where(index == 0, second, first)

    kept, away = halves(grads, c, 3)
    kept = added(kept, core_swap(away))
    kept_a, away_a = halves(kept[:2], x, 3)
    kept_b, away_b = halves(kept[2:], y, 2)
    kept_a = added(kept_a, plane_shift(away_a, 1))
    kept_b = added(kept_b, plane_shift(away_b, 2))
    kept_a, away_a = halves(kept_a, y, 2)
    kept_b, away_b = halves(kept_b, x, 2)
    kept_a = added(kept_a, plane_shift(away_a, 2))
    kept_b = added(kept_b, plane_shift(away_b, 1))
    kept = jnp.concatenate([kept_a, kept_b])

    def ring_sum(array):
        total = pick(array, z).astype(f32)
        for k in (1, 2, 3):
            total += ring_shift(pick(array, (z + k) % 4), k).astype(f32)
        return total

    big_sums = ring_sum(kept)

    hid_near, hid_far, qkv_grad, gain_one_grad, scale_grad = pl.pallas_call(
        attend_back_kernel,
        grid_spec=pltpu.PrefetchScalarGridSpec(
            num_scalar_prefetch=1,
            grid=(4,),
            in_specs=[
                seq_block(4, width=width), seq_block(4, width=width),
                whole((1, width)), whole((1, 160)), whole((width, 480)),
                seq_block(2, 4, width=480), seq_block(4, width=160), seq_block(4, width=160),
            ],
            out_specs=[
                seq_block(4, width=width), seq_block(4, width=width),
                whole((width, 480)), whole((1, width)), whole((1, 160)),
            ],
            scratch_shapes=[
                pltpu.VMEM((width, 480), f32), pltpu.VMEM((1, width), f32), pltpu.VMEM((1, 160), f32),
            ],
        ),
        out_shape=[
            jax.ShapeDtypeStruct((4, 128, width), bf16),
            jax.ShapeDtypeStruct((4, 128, width), bf16),
            jax.ShapeDtypeStruct((width, 480), bf16),
            jax.ShapeDtypeStruct((1, width), f32),
            jax.ShapeDtypeStruct((1, 160), f32),
        ],
        compiler_params=limit,
        cost_estimate=pl.CostEstimate(flops=3_500_000_000, bytes_accessed=12_000_000, transcendentals=600_000),
        name="attend_back",
    )(info, near, far, gain_one, query_mult, w_qkv, pre, grad_att_near, grad_att_far)

    hid = added(hid_near, core_swap(hid_far))
    grad_hid = hid[0].astype(f32)
    for step in (1, 2, 3):
        grad_hid += plane_shift(hid[step], step).astype(f32)
    wide = x_rows.astype(f32)
    inverse = lax.rsqrt(jnp.mean(wide * wide, axis=1, keepdims=True) + 1e-06)
    grad_in = (grad_mid + norm_back(grad_hid, wide * inverse, inverse, gain_one)).astype(bf16)

    scale_line = lax.dynamic_update_slice(jnp.zeros((1, width), f32), scale_grad, (0, 160 * plane))
    lines = jnp.concatenate([gain_one_grad, gain_two_grad, scale_line])
    lines = lines.reshape(3, 4, 8, 40).transpose(1, 2, 0, 3).reshape(4, 8, 1, 120).astype(bf16)
    lines = jnp.pad(lines, ((0, 0), (0, 0), (0, 7), (0, 360)))
    send = jnp.concatenate([qkv_grad.reshape(4, 8, 40, 480), lines], axis=2)
    sums = ring_sum(send).astype(bf16)
    sums = lax.all_to_all(sums, ("y", "core", "x"), split_axis=0, concat_axis=0, tiled=True)
    qkv_sums = sums[:, :40].reshape(8, 40, 3, 160).transpose(2, 1, 0, 3).reshape(3, 40, width).astype(f32)
    line_sums = jnp.sum(sums[:, 40, :120].astype(f32), axis=0).reshape(3, 40)
    scale_low = query_scale.astype(bf16).astype(f32)
    scale_sum = LOG2E / math.sqrt(HD) * jax.nn.sigmoid(scale_low) * line_sums[2]

    def home(rows):
        rows = rows.reshape(4, 4, 8, width)
        parts = [rows[:, 0]] + [ring_shift(rows[:, k], -k) for k in (1, 2, 3)]
        line = jnp.stack(parts + parts[:3])
        return lax.dynamic_slice_in_dim(line, (4 - z) % 4, 4, 0).reshape(16, 8, width)

    return (
        home(out_rows), home(grad_in), qkv_sums[0], qkv_sums[1], qkv_sums[2],
        big_sums[0], big_sums[1], big_sums[2], line_sums[0], line_sums[1], scale_sum,
    )


def solution(mesh):
    names = ("dp", "ctx")
    body = per_device
    if dict(mesh.shape) == {"dp": 16, "ctx": 2}:
        mesh = Mesh(mesh.devices.reshape(4, 2, 2, 2), ("z", "y", "core", "x"))
        names = mesh.axis_names
        body = planes
    seq, mat, line = P(None, names, None), P(names, None), P(names)
    return jax.shard_map(
        body,
        mesh=mesh,
        in_specs=(seq,) * 2 + (mat,) * 6 + (line,) * 3 + (P(), P()),
        out_specs=(seq,) * 2 + (mat,) * 6 + (line,) * 3,
        check_vma=False,
    )
```

```python
import math

import jax
import jax.numpy as jnp
from jax import lax
from jax.experimental import pallas as pl
from jax.experimental.pallas import tpu as pltpu
from jax.sharding import Mesh, PartitionSpec as P

H = 16
HD = 80


def mult_trans(left, right):
    return lax.dot_general(
        left, right, (((1,), (1,)), ((), ())), preferred_element_type=jnp.float32
    )


def trans_mult(left, right):
    return lax.dot_general(
        left, right, (((0,), (0,)), ((), ())), preferred_element_type=jnp.float32
    )


def position_of(index, local_rows, piece_rows, groups):
    column = index // local_rows
    within = index % local_rows
    return (within // piece_rows * groups + column) * piece_rows + within % piece_rows


def norm_back(grad_hidden, normed, inverse, gain_value):
    grad_normed = grad_hidden * gain_value
    return inverse * (grad_normed - normed * jnp.mean(grad_normed * normed, axis=1, keepdims=True))


def per_device(
    inputs,
    cotangent,
    w_query,
    w_key,
    w_value,
    w_output,
    w_up,
    w_down,
    attn_gain,
    mlp_gain,
    query_scale,
    deal,
    lengths,
):
    groups = lax.axis_size("ctx")
    group_index = lax.axis_index("dp")
    ctx_index = lax.axis_index("ctx")
    head_count = H
    head_dim = HD
    piece_rows = inputs.shape[1]
    seq_numbers = jnp.arange(inputs.shape[0], dtype=jnp.int32)
    seq_lengths = jnp.sum(
        jnp.where(deal[None, :] == seq_numbers[:, None], lengths[None, :], 0), axis=1
    )
    local_in, local_cot = (
        lax.all_to_all(inputs, "dp", split_axis=0, concat_axis=1, tiled=True),
        lax.all_to_all(cotangent, "dp", split_axis=0, concat_axis=1, tiled=True),
    )
    seq_count, local_rows, model_width = local_in.shape
    padded = local_rows * groups
    token_count = seq_count * local_rows
    my_lengths = lax.dynamic_slice_in_dim(seq_lengths, group_index * seq_count, seq_count, 0)
    query_pos = position_of(
        ctx_index * local_rows + jnp.arange(local_rows, dtype=jnp.int32),
        local_rows,
        piece_rows,
        groups,
    )
    flat_in = local_in.reshape(token_count, model_width).astype(jnp.float32)
    flat_cot = local_cot.reshape(token_count, model_width)
    lowered = (
        w_query.astype(jnp.bfloat16),
        w_key.astype(jnp.bfloat16),
        w_value.astype(jnp.bfloat16),
        w_output.astype(jnp.bfloat16),
        w_up.astype(jnp.bfloat16),
        w_down.astype(jnp.bfloat16),
        attn_gain.astype(jnp.bfloat16),
        mlp_gain.astype(jnp.bfloat16),
        query_scale.astype(jnp.bfloat16),
    )
    gathered = (
        lax.all_gather(lowered[0], ("dp", "ctx"), axis=0, tiled=True),
        lax.all_gather(lowered[1], ("dp", "ctx"), axis=0, tiled=True),
        lax.all_gather(lowered[2], ("dp", "ctx"), axis=0, tiled=True),
        lax.all_gather(lowered[3], ("dp", "ctx"), axis=0, tiled=True),
        lax.all_gather(lowered[4], ("dp", "ctx"), axis=0, tiled=True),
        lax.all_gather(lowered[5], ("dp", "ctx"), axis=0, tiled=True),
        lax.all_gather(lowered[6], ("dp", "ctx"), axis=0, tiled=True),
        lax.all_gather(lowered[7], ("dp", "ctx"), axis=0, tiled=True),
        lax.all_gather(lowered[8], ("dp", "ctx"), axis=0, tiled=True),
    )
    (
        query_full,
        key_full,
        value_full,
        output_full,
        up_full,
        down_full,
        gain_one,
        gain_two,
        scale_raw,
    ) = gathered
    inv_one = lax.rsqrt(jnp.mean(flat_in * flat_in, axis=1, keepdims=True) + 1e-06)
    normed_one = flat_in * inv_one
    hidden_one = (normed_one * gain_one.astype(jnp.float32)).astype(jnp.bfloat16)
    scale_param = scale_raw.astype(jnp.float32)
    query_mult = 1.442695041 / math.sqrt(head_dim) * jax.nn.softplus(scale_param)
    query_pre = jnp.dot(hidden_one, query_full, preferred_element_type=jnp.float32)
    queries = (query_pre * query_mult).astype(jnp.bfloat16)
    keys_local = jnp.dot(hidden_one, key_full, preferred_element_type=jnp.float32).astype(
        jnp.bfloat16
    )
    values_local = jnp.dot(hidden_one, value_full, preferred_element_type=jnp.float32).astype(
        jnp.bfloat16
    )
    four_shape = (seq_count, local_rows, head_count, head_dim)
    query_four = queries.reshape(four_shape)
    keys_three = keys_local.reshape(seq_count, local_rows, model_width)
    values_three = values_local.reshape(seq_count, local_rows, model_width)

    def live_between(row_pos, key_pos):
        allowed = (key_pos[None, None, :] <= row_pos[None, :, None]) & (
            key_pos[None, None, :] < my_lengths[:, None, None]
        )
        return allowed[:, :, None, :]

    def live_mask(key_pos):
        return live_between(query_pos, key_pos)

    def attend_block(state_now, key_block, value_block, first_row):
        run_max, run_sum, run_acc = state_now
        block_len = key_block.shape[1]
        key_pos = position_of(
            first_row + jnp.arange(block_len, dtype=jnp.int32), local_rows, piece_rows, groups
        )
        key_four = key_block.reshape(seq_count, block_len, head_count, head_dim)
        value_four = value_block.reshape(seq_count, block_len, head_count, head_dim)
        scores = jnp.einsum(
            "srhd,skhd->srhk", query_four, key_four, preferred_element_type=jnp.float32
        )
        allowed = live_mask(key_pos)
        masked = jnp.where(allowed, scores, -1e30)
        new_max = jnp.maximum(run_max, jnp.max(masked, axis=3))
        weights_now = jnp.exp(jnp.where(allowed, masked - new_max[..., None], -1e30))
        factor = jnp.exp(run_max - new_max)
        new_sum = run_sum * factor + jnp.sum(weights_now, axis=3)
        added = jnp.einsum(
            "srhk,skhd->srhd",
            weights_now.astype(jnp.bfloat16),
            value_four,
            preferred_element_type=jnp.float32,
        )
        return (new_max, new_sum, run_acc * factor[..., None] + added)

    start_state = (
        jnp.full((seq_count, local_rows, head_count), -1e30, jnp.float32),
        jnp.zeros((seq_count, local_rows, head_count), jnp.float32),
        jnp.zeros(four_shape, jnp.float32),
    )
    key_piece = lax.all_gather(keys_three, "ctx", axis=1, tiled=True)
    value_piece = lax.all_gather(values_three, "ctx", axis=1, tiled=True)
    piece_len = key_piece.shape[1]
    fold_block_len = 512 if piece_len % 512 == 0 else piece_len

    def one_block(state_now, block_index):
        offset = block_index * fold_block_len
        key_block = lax.dynamic_slice_in_dim(key_piece, offset, fold_block_len, 1)
        value_block = lax.dynamic_slice_in_dim(value_piece, offset, fold_block_len, 1)
        return (attend_block(state_now, key_block, value_block, offset), None)

    result_state, unused = lax.scan(
        one_block, start_state, jnp.arange(piece_len // fold_block_len, dtype=jnp.int32)
    )
    run_max, run_sum, run_acc = result_state
    log_total = run_max + jnp.log(run_sum)
    attn_exact = run_acc / run_sum[..., None]
    attended = attn_exact.reshape(token_count, model_width).astype(jnp.bfloat16)
    middle = flat_in + jnp.dot(attended, output_full, preferred_element_type=jnp.float32)
    inv_two = lax.rsqrt(jnp.mean(middle * middle, axis=1, keepdims=True) + 1e-06)
    normed_two = middle * inv_two
    hidden_two = (normed_two * gain_two.astype(jnp.float32)).astype(jnp.bfloat16)
    up_pre = jnp.dot(hidden_two, up_full, preferred_element_type=jnp.float32)
    active = jax.nn.silu(up_pre).astype(jnp.bfloat16)
    result = (middle + jnp.dot(active, down_full, preferred_element_type=jnp.float32)).astype(
        jnp.bfloat16
    )
    back_weights = (
        lax.all_gather(lowered[0], ("dp", "ctx"), axis=0, tiled=True),
        lax.all_gather(lowered[1], ("dp", "ctx"), axis=0, tiled=True),
        lax.all_gather(lowered[2], ("dp", "ctx"), axis=0, tiled=True),
        lax.all_gather(lowered[3], ("dp", "ctx"), axis=0, tiled=True),
        lax.all_gather(lowered[4], ("dp", "ctx"), axis=0, tiled=True),
        lax.all_gather(lowered[5], ("dp", "ctx"), axis=0, tiled=True),
        lax.all_gather(lowered[6], ("dp", "ctx"), axis=0, tiled=True),
        lax.all_gather(lowered[7], ("dp", "ctx"), axis=0, tiled=True),
        lax.all_gather(lowered[8], ("dp", "ctx"), axis=0, tiled=True),
    )
    (
        query_back,
        key_back,
        value_back,
        output_back,
        up_back,
        down_back,
        gain_one_back,
        gain_two_back,
        scale_back,
    ) = back_weights
    cot_wide = flat_cot.astype(jnp.float32)
    grad_down = trans_mult(active, flat_cot)
    grad_active = mult_trans(flat_cot, down_back)
    sigma_up = jax.nn.sigmoid(up_pre)
    grad_up_pre = (grad_active * sigma_up * (1.0 + up_pre * (1.0 - sigma_up))).astype(jnp.bfloat16)
    grad_up = trans_mult(hidden_two, grad_up_pre)
    grad_hidden_two = mult_trans(grad_up_pre, up_back)
    grad_gain_two = jnp.sum(grad_hidden_two * normed_two, axis=0)
    grad_middle = cot_wide + norm_back(
        grad_hidden_two, normed_two, inv_two, gain_two_back.astype(jnp.float32)
    )
    grad_middle_low = grad_middle.astype(jnp.bfloat16)
    grad_output = trans_mult(attended, grad_middle_low)
    grad_attended = mult_trans(grad_middle_low, output_back).astype(jnp.bfloat16)
    grad_att_four = grad_attended.reshape(four_shape)
    delta_rows = jnp.sum(grad_att_four.astype(jnp.float32) * attn_exact, axis=3)
    key_all, value_all = (
        lax.all_gather(keys_three, "ctx", axis=1, tiled=True),
        lax.all_gather(values_three, "ctx", axis=1, tiled=True),
    )
    block_len = min(512, padded)

    def back_block(block_index, state_now):
        grad_query, grad_key_all, grad_value_all = state_now
        offset = block_index * block_len
        key_block = lax.dynamic_slice_in_dim(key_all, offset, block_len, 1).reshape(
            seq_count, block_len, head_count, head_dim
        )
        value_block = lax.dynamic_slice_in_dim(value_all, offset, block_len, 1).reshape(
            seq_count, block_len, head_count, head_dim
        )
        key_pos = position_of(
            offset + jnp.arange(block_len, dtype=jnp.int32), local_rows, piece_rows, groups
        )
        scores = jnp.einsum(
            "srhd,skhd->srhk", query_four, key_block, preferred_element_type=jnp.float32
        )
        probs = jnp.exp(jnp.where(live_mask(key_pos), scores - log_total[..., None], -1e30))
        grad_value_block = jnp.einsum(
            "srhk,srhd->skhd",
            probs.astype(jnp.bfloat16),
            grad_att_four,
            preferred_element_type=jnp.float32,
        )
        grad_probs = jnp.einsum(
            "srhd,skhd->srhk", grad_att_four, value_block, preferred_element_type=jnp.float32
        )
        grad_scores = (probs * (grad_probs - delta_rows[..., None])).astype(jnp.bfloat16)
        grad_query = grad_query + jnp.einsum(
            "srhk,skhd->srhd", grad_scores, key_block, preferred_element_type=jnp.float32
        )
        grad_key_block = jnp.einsum(
            "srhk,srhd->skhd", grad_scores, query_four, preferred_element_type=jnp.float32
        )
        grad_key_all = lax.dynamic_update_slice_in_dim(
            grad_key_all, grad_key_block.reshape(seq_count, block_len, model_width), offset, 1
        )
        grad_value_all = lax.dynamic_update_slice_in_dim(
            grad_value_all, grad_value_block.reshape(seq_count, block_len, model_width), offset, 1
        )
        return (grad_query, grad_key_all, grad_value_all)

    zero_all = jnp.zeros((seq_count, padded, model_width), jnp.float32)
    grad_query, grad_key_all, grad_value_all = lax.fori_loop(
        0, padded // block_len, back_block, (jnp.zeros(four_shape, jnp.float32), zero_all, zero_all)
    )
    grad_key_mine, grad_value_mine = (
        lax.psum_scatter(
            grad_key_all.astype(jnp.bfloat16), "ctx", scatter_dimension=1, tiled=True
        ).astype(jnp.float32),
        lax.psum_scatter(
            grad_value_all.astype(jnp.bfloat16), "ctx", scatter_dimension=1, tiled=True
        ).astype(jnp.float32),
    )
    grad_query_flat = grad_query.reshape(token_count, model_width)
    grad_query_pre = (grad_query_flat * query_mult).astype(jnp.bfloat16)
    grad_scale = (
        1.442695041
        / math.sqrt(head_dim)
        * jax.nn.sigmoid(scale_back.astype(jnp.float32))
        * jnp.sum(grad_query_flat * query_pre, axis=0)
    )
    grad_key_low = grad_key_mine.reshape(token_count, model_width).astype(jnp.bfloat16)
    grad_value_low = grad_value_mine.reshape(token_count, model_width).astype(jnp.bfloat16)
    grad_wq = trans_mult(hidden_one, grad_query_pre)
    grad_wk = trans_mult(hidden_one, grad_key_low)
    grad_wv = trans_mult(hidden_one, grad_value_low)
    grad_hidden_one = (
        mult_trans(grad_query_pre, query_back)
        + mult_trans(grad_key_low, key_back)
        + mult_trans(grad_value_low, value_back)
    )
    grad_gain_one = jnp.sum(grad_hidden_one * normed_one, axis=0)
    grad_in = grad_middle + norm_back(
        grad_hidden_one, normed_one, inv_one, gain_one_back.astype(jnp.float32)
    )
    matrix_stack = jnp.stack([grad_wq, grad_wk, grad_wv, grad_output, grad_up, grad_down], axis=0)
    vector_stack = jnp.stack([grad_gain_one, grad_gain_two, grad_scale], axis=0)
    matrix_sums, vector_sums = (
        lax.psum_scatter(matrix_stack, ("dp", "ctx"), scatter_dimension=1, tiled=True),
        lax.psum_scatter(vector_stack, ("dp", "ctx"), scatter_dimension=1, tiled=True),
    )
    out_local = result.reshape(seq_count, local_rows, model_width)
    grad_local = grad_in.astype(jnp.bfloat16).reshape(seq_count, local_rows, model_width)
    back_out, back_grad = (
        lax.all_to_all(out_local, "dp", split_axis=1, concat_axis=0, tiled=True),
        lax.all_to_all(grad_local, "dp", split_axis=1, concat_axis=0, tiled=True),
    )
    return (
        back_out,
        back_grad,
        matrix_sums[0],
        matrix_sums[1],
        matrix_sums[2],
        matrix_sums[3],
        matrix_sums[4],
        matrix_sums[5],
        vector_sums[0],
        vector_sums[1],
        vector_sums[2],
    )


LOG2E = 1.442695041
CODES = (0, 1, 4, 5)


def plane_shift(value, step):
    if step == 1:
        return lax.ppermute(value, "x", [(0, 1), (1, 0)])
    if step == 2:
        return lax.ppermute(value, "y", [(0, 1), (1, 0)])
    return lax.ppermute(value, ("y", "x"), [(0, 3), (1, 2), (2, 1), (3, 0)])


def core_swap(value):
    return lax.ppermute(value, "core", [(0, 1), (1, 0)])


def ring_shift(value, step):
    return lax.ppermute(value, "z", [(i, (i + step) % 4) for i in range(4)])


def pick(array, index):
    return lax.dynamic_index_in_dim(array, index, 0, keepdims=False)


def by_source(pieces, z_index):
    own, one, two, three = pieces
    line = jnp.stack([three, two, one, own, three, two, one])
    return lax.dynamic_slice_in_dim(line, 3 - z_index, 4, 0)


def pair(mine, other, index, axis):
    first = index == 0
    return jnp.stack([jnp.where(first, mine, other), jnp.where(first, other, mine)], axis=axis)


def row_positions(shape, dim, z_index, plane_index):
    row = lax.broadcasted_iota(jnp.int32, shape, dim)
    chip = (row // 32) % 4
    code = (chip % 2) + 4 * (chip // 2) + 2 * (row // 128)
    hop = (row % 32) // 8
    return 64 * ((z_index - hop) & 3) + 8 * (plane_index ^ code) + row % 8


def live_pairs(info_ref, seq):
    z_index, plane_index = info_ref[0], info_ref[1]
    shape = (256, 256)
    query_pos = row_positions(shape, 0, z_index, plane_index)
    key_pos = row_positions(shape, 1, z_index, plane_index)
    return (key_pos <= query_pos) & (key_pos < info_ref[2 + seq])


def block_rows(near_ref, far_ref):
    return jnp.concatenate([near_ref[...], far_ref[...]], axis=0).reshape(256, near_ref.shape[2])


def soft_probs(query, key, live):
    scores = mult_trans(query, key)
    scores = jnp.where(live, scores, -1e30)
    top = jnp.max(scores, axis=1, keepdims=True)
    weights = jnp.where(live, jnp.exp(scores - top), 0.0)
    return weights / jnp.sum(weights, axis=1, keepdims=True)


def attend_kernel(info_ref, near_ref, far_ref, gain_ref, mult_ref, w_ref, pre_ref, att_near, att_far):
    seq = pl.program_id(0)
    live = live_pairs(info_ref, seq)
    wide = block_rows(near_ref, far_ref).astype(jnp.float32)
    inverse = lax.rsqrt(jnp.mean(wide * wide, axis=1, keepdims=True) + 1e-06)
    hidden = (wide * inverse * gain_ref[...]).astype(jnp.bfloat16)
    pre = jnp.dot(hidden, w_ref[...], preferred_element_type=jnp.float32)
    pre_ref[...] = pre.reshape(2, 4, 32, 480)
    query = (pre[:, 0:160] * mult_ref[...]).astype(jnp.bfloat16)
    key = pre[:, 160:320].astype(jnp.bfloat16)
    value = pre[:, 320:480].astype(jnp.bfloat16)
    heads = []
    for head in range(2):
        part = slice(80 * head, 80 * head + 80)
        probs = soft_probs(query[:, part], key[:, part], live).astype(jnp.bfloat16)
        heads.append(jnp.dot(probs, value[:, part], preferred_element_type=jnp.float32))
    att = jnp.concatenate(heads, axis=1).astype(jnp.bfloat16).reshape(2, 4, 32, 160)
    att_near[...] = att[0]
    att_far[...] = att[1]


def attend_back_kernel(
    info_ref, near_ref, far_ref, gain_ref, mult_ref, w_ref, pre_ref, grad_near, grad_far,
    hid_near, hid_far, w_grad, gain_grad, scale_grad, w_acc, gain_acc, scale_acc,
):
    seq = pl.program_id(0)

    @pl.when(seq == 0)
    def _():
        w_acc[...] = jnp.zeros_like(w_acc)
        gain_acc[...] = jnp.zeros_like(gain_acc)
        scale_acc[...] = jnp.zeros_like(scale_acc)

    live = live_pairs(info_ref, seq)
    wide = block_rows(near_ref, far_ref).astype(jnp.float32)
    inverse = lax.rsqrt(jnp.mean(wide * wide, axis=1, keepdims=True) + 1e-06)
    normed = wide * inverse
    hidden = (normed * gain_ref[...]).astype(jnp.bfloat16)
    pre = pre_ref[...].reshape(256, 480)
    mult = mult_ref[...]
    query = (pre[:, 0:160] * mult).astype(jnp.bfloat16)
    key = pre[:, 160:320].astype(jnp.bfloat16)
    value = pre[:, 320:480].astype(jnp.bfloat16)
    grad_att = block_rows(grad_near, grad_far)
    grad_q, grad_k, grad_v = [], [], []
    for head in range(2):
        part = slice(80 * head, 80 * head + 80)
        probs = soft_probs(query[:, part], key[:, part], live)
        grad_probs = mult_trans(grad_att[:, part], value[:, part])
        delta = jnp.sum(probs * grad_probs, axis=1, keepdims=True)
        grad_scores = (probs * (grad_probs - delta)).astype(jnp.bfloat16)
        grad_v.append(trans_mult(probs.astype(jnp.bfloat16), grad_att[:, part]))
        grad_q.append(jnp.dot(grad_scores, key[:, part], preferred_element_type=jnp.float32))
        grad_k.append(trans_mult(grad_scores, query[:, part]))
    grad_query = jnp.concatenate(grad_q, axis=1)
    scale_acc[...] += jnp.sum(grad_query * pre[:, 0:160], axis=0, keepdims=True)
    joined = jnp.concatenate([grad_query * mult] + grad_k + grad_v, axis=1).astype(jnp.bfloat16)
    w_acc[...] += trans_mult(hidden, joined)
    grad_hidden = mult_trans(joined, w_ref[...])
    gain_acc[...] += jnp.sum(grad_hidden * normed, axis=0, keepdims=True)
    low = grad_hidden.astype(jnp.bfloat16).reshape(2, 4, 32, 1280)
    hid_near[...] = low[0]
    hid_far[...] = low[1]

    @pl.when(seq == 3)
    def _():
        w_grad[...] = w_acc[...].astype(jnp.bfloat16)
        gain_grad[...] = gain_acc[...]
        scale_grad[...] = scale_acc[...]


def block_index(z_index, y_index, core):
    return pl.ds(pl.multiple_of((4 * z_index + 2 * y_index + core) * 80, 80), 80)


def source_rows(info_ref, chip, core):
    source = info_ref[1] ^ (CODES[chip] + 2 * core)
    return pl.ds(pl.multiple_of(source * 160, 160), 160)


def feed_kernel(
    info_ref, x_ref, g_ref, att_0, att_1, att_2, att_3, gain_ref,
    near_a, across_a, all_b, far_near_a, far_across_a, far_b,
    out_ref, act_ref, hid_ref, dup_ref, dm_ref, dmid_ref, datt_0, datt_1, datt_2, datt_3, gain_grad,
    weights, sems,
):
    y_index, core_index = info_ref[1] // 4, (info_ref[1] // 2) % 2
    copies = []
    for w in range(3):
        moved = []
        for core, refs in ((core_index, (near_a, across_a, all_b)), (1 - core_index, (far_near_a, far_across_a, far_b))):
            for half in range(2):
                moved.append((refs[0].at[half, w], half, y_index, core))
                moved.append((refs[1].at[half, w], half, 1 - y_index, core))
                for row in range(2):
                    moved.append((refs[2].at[half, w, row], 2 + half, row, core))
        copies.append([
            pltpu.make_async_copy(src, weights.at[w, block_index(*place)], sems.at[w, i])
            for i, (src, *place) in enumerate(moved)
        ])
    for group in copies:
        for copy in group:
            copy.start()
    atts, datts = (att_0, att_1, att_2, att_3), (datt_0, datt_1, datt_2, datt_3)

    for copy in copies[0]:
        copy.wait()
    middle = x_ref[...].astype(jnp.float32)
    for chip in range(4):
        for core in range(2):
            middle += jnp.dot(
                atts[chip][core], weights[0, source_rows(info_ref, chip, core), :],
                preferred_element_type=jnp.float32,
            )
    inverse = lax.rsqrt(jnp.mean(middle * middle, axis=1, keepdims=True) + 1e-06)
    normed = middle * inverse
    gain = gain_ref[...]
    hidden = (normed * gain).astype(jnp.bfloat16)
    hid_ref[...] = hidden
    for copy in copies[1]:
        copy.wait()
    up = jnp.dot(hidden, weights[1], preferred_element_type=jnp.float32)
    sigma = jax.nn.sigmoid(up)
    active = (up * sigma).astype(jnp.bfloat16)
    act_ref[...] = active
    for copy in copies[2]:
        copy.wait()
    down = jnp.dot(active, weights[2], preferred_element_type=jnp.float32)
    out_ref[...] = (middle + down).astype(jnp.bfloat16)
    cot = g_ref[...]
    grad_act = mult_trans(cot, weights[2])
    grad_up = (grad_act * sigma * (1.0 + up * (1.0 - sigma))).astype(jnp.bfloat16)
    dup_ref[...] = grad_up
    grad_hidden = mult_trans(grad_up, weights[1])
    gain_grad[...] = jnp.sum(grad_hidden * normed, axis=0, keepdims=True)
    grad_mid = cot.astype(jnp.float32) + norm_back(grad_hidden, normed, inverse, gain)
    dmid_ref[...] = grad_mid
    low = grad_mid.astype(jnp.bfloat16)
    dm_ref[...] = low
    for chip in range(4):
        for core in range(2):
            datts[chip][core] = mult_trans(low, weights[0, source_rows(info_ref, chip, core), :]).astype(jnp.bfloat16)


def grads_kernel(
    info_ref, att_0, att_1, att_2, att_3, hid_ref, act_ref, dup_ref, dm_ref, g_ref,
    kept, away, stage, sems,
):
    core_index = (info_ref[1] // 2) % 2
    copies = []

    def leave(w):
        for z_index in range(4):
            for row in range(2):
                for which, (core, target) in enumerate(((core_index, kept), (1 - core_index, away))):
                    copy = pltpu.make_async_copy(
                        stage.at[w, block_index(z_index, row, core)],
                        target.at[z_index, w, row],
                        sems.at[w, 4 * z_index + 2 * row + which],
                    )
                    copy.start()
                    copies.append(copy)

    for w, left, right in ((2, act_ref, g_ref), (1, hid_ref, dup_ref)):
        for chunk in range(5):
            part = slice(256 * chunk, 256 * chunk + 256)
            stage[w, part, :] = trans_mult(left[:, part], right[...]).astype(jnp.bfloat16)
        leave(w)
    for chip, att in enumerate((att_0, att_1, att_2, att_3)):
        for core in range(2):
            stage[0, source_rows(info_ref, chip, core), :] = trans_mult(att[core], dm_ref[...]).astype(jnp.bfloat16)
    leave(0)
    for copy in copies:
        copy.wait()


def whole(shape):
    return pl.BlockSpec(shape, lambda *_: (0,) * len(shape))


def seq_block(*lead, width):
    count = len(lead)
    return pl.BlockSpec((*lead, 32, width), lambda s, info: (*(0,) * count, s, 0))


def planes(
    inputs, cotangent, w_query, w_key, w_value, w_output, w_up, w_down,
    attn_gain, mlp_gain, query_scale, deal, lengths,
):
    f32, bf16 = jnp.float32, jnp.bfloat16
    z, y, c, x = (lax.axis_index(name) for name in ("z", "y", "core", "x"))
    plane = 4 * y + 2 * c + x
    width = 1280
    seqs = jnp.arange(16, dtype=jnp.int32)
    seq_lengths = jnp.sum(jnp.where(deal[None, :] == seqs[:, None], lengths[None, :], 0), axis=1)
    my_lengths = lax.dynamic_slice_in_dim(seq_lengths, 4 * z, 4, 0)
    info = jnp.concatenate([jnp.stack([z, plane]), my_lengths]).astype(jnp.int32)

    vec = jnp.concatenate([attn_gain, mlp_gain, query_scale]).astype(bf16)
    vec_block = jnp.zeros((1, 8, width), bf16).at[0, 0, :120].set(vec)
    in_four = inputs.reshape(4, 4, 8, width)
    cot_four = cotangent.reshape(4, 4, 8, width)
    sent = [jnp.concatenate([pick(in_four, (z + k) % 4), vec_block]) for k in range(4)]
    got = [sent[0]] + [ring_shift(sent[k], k) for k in (1, 2, 3)]
    x_rows = jnp.stack([item[:4] for item in got], axis=1).reshape(128, width)
    vec_rows = jnp.concatenate([item[4, :1] for item in got] + [jnp.zeros((4, width), bf16)])
    own = jnp.concatenate([x_rows, vec_rows])

    qkv = jnp.stack([w_query, w_key, w_value]).astype(bf16)
    qkv = qkv.reshape(3, 40, 8, 160).transpose(2, 1, 0, 3).reshape(8, 40, 480)
    qkv = lax.all_to_all(qkv, ("y", "core", "x"), split_axis=0, concat_axis=0, tiled=True)
    qkv = qkv.reshape(320, 480)
    w_qkv = by_source([qkv] + [ring_shift(qkv, k) for k in (1, 2, 3)], z).reshape(width, 480)

    near = jnp.stack([own] + [plane_shift(own, step) for step in (1, 2, 3)])

    big = jnp.stack([w_output, w_up, w_down]).astype(bf16)
    big = lax.all_gather(big, "z", axis=0)
    big, near = lax.optimization_barrier((big, near))
    far = core_swap(near)
    part_a, part_b = big[:2], big[2:]
    near_a = pair(part_a, plane_shift(part_a, 1), x, 2).reshape(2, 3, 80, width)
    part_b = pair(part_b, plane_shift(part_b, 2), y, 2)
    near_a, part_b, w_qkv, cot_four = lax.optimization_barrier((near_a, part_b, w_qkv, cot_four))
    cot_sent = [pick(cot_four, (z + k) % 4) for k in range(4)]
    cot_got = [cot_sent[0]] + [ring_shift(cot_sent[k], k) for k in (1, 2, 3)]
    cot_rows = jnp.stack(cot_got, axis=1).reshape(128, width)

    across_a = plane_shift(near_a, 2)
    across_b = plane_shift(part_b, 1)

    vecs = jnp.stack([near[:, 128:132, :120], far[:, 128:132, :120]])
    vecs = vecs.astype(f32).reshape(2, 2, 2, 4, 120)
    vecs = jnp.where(c == 0, vecs, vecs[::-1])
    vecs = jnp.where(y == 0, vecs, vecs[:, ::-1])
    vecs = jnp.where(x == 0, vecs, vecs[:, :, ::-1])
    fours = jnp.arange(4, dtype=jnp.int32)
    from_hop = (z - fours[:, None]) % 4 == fours[None, :]
    vecs = jnp.sum(jnp.where(from_hop[:, None, None, None, :, None], vecs[None], 0.0), axis=4)
    vecs = vecs.reshape(4, 2, 2, 2, 3, 40).transpose(4, 0, 2, 1, 3, 5).reshape(3, width)
    gain_one, gain_two = vecs[0:1], vecs[1:2]
    my_scale = lax.dynamic_slice_in_dim(vecs[2:3], 160 * plane, 160, 1)
    query_mult = LOG2E / math.sqrt(HD) * jax.nn.softplus(my_scale)

    limit = pltpu.CompilerParams(vmem_limit_bytes=50 * 1024 * 1024)
    pre, att_near, att_far = pl.pallas_call(
        attend_kernel,
        grid_spec=pltpu.PrefetchScalarGridSpec(
            num_scalar_prefetch=1,
            grid=(4,),
            in_specs=[
                seq_block(4, width=width), seq_block(4, width=width),
                whole((1, width)), whole((1, 160)), whole((width, 480)),
            ],
            out_specs=[seq_block(2, 4, width=480), seq_block(4, width=160), seq_block(4, width=160)],
        ),
        out_shape=[
            jax.ShapeDtypeStruct((2, 4, 128, 480), f32),
            jax.ShapeDtypeStruct((4, 128, 160), bf16),
            jax.ShapeDtypeStruct((4, 128, 160), bf16),
        ],
        compiler_params=limit,
        cost_estimate=pl.CostEstimate(flops=9_000_000_000, bytes_accessed=8_000_000, transcendentals=600_000),
        name="attend",
    )(info, near, far, gain_one, query_mult, w_qkv)

    att_near, att_far, cot_rows, near_a = lax.optimization_barrier((att_near, att_far, cot_rows, near_a))
    far_near_a = core_swap(near_a)
    att_pair = jnp.stack([att_near, core_swap(att_far)], axis=1)
    atts = [att_pair[0]] + [plane_shift(att_pair[step], step) for step in (1, 2, 3)]
    *atts, far_near_a, across_a, across_b = lax.optimization_barrier((*atts, far_near_a, across_a, across_b))
    far_across_a = core_swap(across_a)
    all_b = pair(part_b, across_b, x, 3).reshape(2, 3, 2, 80, width)
    far_b = core_swap(all_b)

    low_rows = jax.ShapeDtypeStruct((128, width), bf16)
    datt_shape = jax.ShapeDtypeStruct((2, 128, 160), bf16)
    smem = pl.BlockSpec(memory_space=pltpu.SMEM)
    vmem = pl.BlockSpec(memory_space=pltpu.VMEM)
    hbm = pl.BlockSpec(memory_space=pl.ANY)
    out_rows, active, hidden_two, grad_up, dm, grad_mid, *datts, gain_two_grad = pl.pallas_call(
        feed_kernel,
        in_specs=[smem] + [vmem] * 7 + [hbm] * 6,
        out_specs=[vmem] * 11,
        out_shape=[low_rows] * 5
        + [jax.ShapeDtypeStruct((128, width), f32)]
        + [datt_shape] * 4
        + [jax.ShapeDtypeStruct((1, width), f32)],
        scratch_shapes=[pltpu.VMEM((3, width, width), bf16), pltpu.SemaphoreType.DMA((3, 16))],
        compiler_params=limit,
        cost_estimate=pl.CostEstimate(flops=12_000_000_000, bytes_accessed=13_000_000, transcendentals=200_000),
        name="feed",
    )(info, x_rows, cot_rows, *atts, gain_two, near_a, across_a, all_b, far_near_a, far_across_a, far_b)

    def home(rows):
        rows = rows.reshape(4, 4, 8, width)
        parts = [rows[:, 0]] + [ring_shift(rows[:, k], -k) for k in (1, 2, 3)]
        line = jnp.stack(parts + parts[:3])
        return lax.dynamic_slice_in_dim(line, (4 - z) % 4, 4, 0).reshape(16, 8, width)

    back = [datts[0]] + [plane_shift(datts[step], step) for step in (1, 2, 3)]
    *back, out_rows = lax.optimization_barrier((*back, out_rows))
    outputs = home(out_rows)
    grad_att_near = jnp.stack([item[0] for item in back])
    grad_att_far = core_swap(jnp.stack([item[1] for item in back]))

    block_shape = jax.ShapeDtypeStruct((4, 3, 2, 80, width), bf16)
    kept, away = pl.pallas_call(
        grads_kernel,
        in_specs=[smem] + [vmem] * 9,
        out_specs=[hbm] * 2,
        out_shape=[block_shape] * 2,
        scratch_shapes=[pltpu.VMEM((3, width, width), bf16), pltpu.SemaphoreType.DMA((3, 16))],
        compiler_params=limit,
        cost_estimate=pl.CostEstimate(flops=6_000_000_000, bytes_accessed=12_000_000, transcendentals=0),
        name="grads",
    )(info, *atts, hidden_two, active, grad_up, dm, cot_rows)

    def added(left, right):
        return (left.astype(f32) + right.astype(f32)).astype(bf16)

    def halves(array, index, axis):
        first, second = (lax.index_in_dim(array, i, axis, keepdims=False) for i in (0, 1))
        return jnp.where(index == 0, first, second), jnp.where(index == 0, second, first)

    kept = added(kept, core_swap(away))
    kept, grad_att_near, grad_att_far, outputs = lax.optimization_barrier(
        (kept, grad_att_near, grad_att_far, outputs)
    )
    kept = kept.reshape(4, 3, 2, 2, 40, width)
    kept_a, away_a = halves(kept[:2], x, 3)
    kept_b, away_b = halves(kept[2:], y, 2)
    kept_a = added(kept_a, plane_shift(away_a, 1))
    kept_b = added(kept_b, plane_shift(away_b, 2))
    def ring_sum(array):
        total = pick(array, z).astype(f32)
        for k in (1, 2, 3):
            total += ring_shift(pick(array, (z + k) % 4), k).astype(f32)
        return total


    hid_near, hid_far, qkv_grad, gain_one_grad, scale_grad = pl.pallas_call(
        attend_back_kernel,
        grid_spec=pltpu.PrefetchScalarGridSpec(
            num_scalar_prefetch=1,
            grid=(4,),
            in_specs=[
                seq_block(4, width=width), seq_block(4, width=width),
                whole((1, width)), whole((1, 160)), whole((width, 480)),
                seq_block(2, 4, width=480), seq_block(4, width=160), seq_block(4, width=160),
            ],
            out_specs=[
                seq_block(4, width=width), seq_block(4, width=width),
                whole((width, 480)), whole((1, width)), whole((1, 160)),
            ],
            scratch_shapes=[
                pltpu.VMEM((width, 480), f32), pltpu.VMEM((1, width), f32), pltpu.VMEM((1, 160), f32),
            ],
        ),
        out_shape=[
            jax.ShapeDtypeStruct((4, 128, width), bf16),
            jax.ShapeDtypeStruct((4, 128, width), bf16),
            jax.ShapeDtypeStruct((width, 480), bf16),
            jax.ShapeDtypeStruct((1, width), f32),
            jax.ShapeDtypeStruct((1, 160), f32),
        ],
        compiler_params=limit,
        cost_estimate=pl.CostEstimate(flops=15_000_000_000, bytes_accessed=12_000_000, transcendentals=600_000),
        name="attend_back",
    )(info, near, far, gain_one, query_mult, w_qkv, pre, grad_att_near, grad_att_far)

    kept_a, kept_b, hid_near, hid_far, qkv_grad = lax.optimization_barrier(
        (kept_a, kept_b, hid_near, hid_far, qkv_grad)
    )
    kept_a, away_a = halves(kept_a, y, 2)
    kept_b, away_b = halves(kept_b, x, 2)
    kept_a = added(kept_a, plane_shift(away_a, 2))
    kept_b = added(kept_b, plane_shift(away_b, 1))
    kept = jnp.concatenate([kept_a, kept_b])
    scale_line = lax.dynamic_update_slice(jnp.zeros((1, width), f32), scale_grad, (0, 160 * plane))
    lines = jnp.concatenate([gain_one_grad, gain_two_grad, scale_line])
    lines = lines.reshape(3, 4, 8, 40).transpose(1, 2, 0, 3).reshape(4, 8, 1, 120).astype(bf16)
    lines = jnp.pad(lines, ((0, 0), (0, 0), (0, 7), (0, 360)))
    send = jnp.concatenate([qkv_grad.reshape(4, 8, 40, 480), lines], axis=2)
    one, three = (ring_shift(pick(send, (z + k) % 4), k) for k in (1, 3))
    hid = added(hid_near, core_swap(hid_far))
    hid, send = lax.optimization_barrier((hid, send))
    two = ring_shift(pick(send, (z + 2) % 4), 2)
    grad_hid = hid[0].astype(f32)
    moved = [plane_shift(hid[step], step) for step in (1, 2, 3)]
    *moved, kept = lax.optimization_barrier((*moved, kept))
    for item in moved:
        grad_hid += item.astype(f32)
    wide = x_rows.astype(f32)
    inverse = lax.rsqrt(jnp.mean(wide * wide, axis=1, keepdims=True) + 1e-06)
    grad_in = (grad_mid + norm_back(grad_hid, wide * inverse, inverse, gain_one)).astype(bf16)

    sums = sum((item.astype(f32) for item in (one, two, three)), pick(send, z).astype(f32)).astype(bf16)
    sums = lax.all_to_all(sums, ("y", "core", "x"), split_axis=0, concat_axis=0, tiled=True)
    big_sums = ring_sum(kept)
    qkv_sums = sums[:, :40].reshape(8, 40, 3, 160).transpose(2, 1, 0, 3).reshape(3, 40, width).astype(f32)
    line_sums = jnp.sum(sums[:, 40, :120].astype(f32), axis=0).reshape(3, 40)
    scale_low = query_scale.astype(bf16).astype(f32)
    scale_sum = LOG2E / math.sqrt(HD) * jax.nn.sigmoid(scale_low) * line_sums[2]

    return (
        outputs, home(grad_in), qkv_sums[0], qkv_sums[1], qkv_sums[2],
        big_sums[0], big_sums[1], big_sums[2], line_sums[0], line_sums[1], scale_sum,
    )


def solution(mesh):
    names = ("dp", "ctx")
    body = per_device
    if dict(mesh.shape) == {"dp": 16, "ctx": 2}:
        mesh = Mesh(mesh.devices.reshape(4, 2, 2, 2), ("z", "y", "core", "x"))
        names = mesh.axis_names
        body = planes
    seq, mat, line = P(None, names, None), P(names, None), P(names)
    return jax.shard_map(
        body,
        mesh=mesh,
        in_specs=(seq,) * 2 + (mat,) * 6 + (line,) * 3 + (P(), P()),
        out_specs=(seq,) * 2 + (mat,) * 6 + (line,) * 3,
        check_vma=False,
    )
```

```python
import math

import jax
import jax.numpy as jnp
from jax import lax
from jax.experimental import pallas as pl
from jax.experimental.pallas import tpu as pltpu
from jax.sharding import Mesh, PartitionSpec as P

H = 16
HD = 80


def mult_trans(left, right):
    return lax.dot_general(
        left, right, (((1,), (1,)), ((), ())), preferred_element_type=jnp.float32
    )


def trans_mult(left, right):
    return lax.dot_general(
        left, right, (((0,), (0,)), ((), ())), preferred_element_type=jnp.float32
    )


def position_of(index, local_rows, piece_rows, groups):
    column = index // local_rows
    within = index % local_rows
    return (within // piece_rows * groups + column) * piece_rows + within % piece_rows


def norm_back(grad_hidden, normed, inverse, gain_value):
    grad_normed = grad_hidden * gain_value
    return inverse * (grad_normed - normed * jnp.mean(grad_normed * normed, axis=1, keepdims=True))


def per_device(
    inputs,
    cotangent,
    w_query,
    w_key,
    w_value,
    w_output,
    w_up,
    w_down,
    attn_gain,
    mlp_gain,
    query_scale,
    deal,
    lengths,
):
    groups = lax.axis_size("ctx")
    group_index = lax.axis_index("dp")
    ctx_index = lax.axis_index("ctx")
    head_count = H
    head_dim = HD
    piece_rows = inputs.shape[1]
    seq_numbers = jnp.arange(inputs.shape[0], dtype=jnp.int32)
    seq_lengths = jnp.sum(
        jnp.where(deal[None, :] == seq_numbers[:, None], lengths[None, :], 0), axis=1
    )
    local_in, local_cot = (
        lax.all_to_all(inputs, "dp", split_axis=0, concat_axis=1, tiled=True),
        lax.all_to_all(cotangent, "dp", split_axis=0, concat_axis=1, tiled=True),
    )
    seq_count, local_rows, model_width = local_in.shape
    padded = local_rows * groups
    token_count = seq_count * local_rows
    my_lengths = lax.dynamic_slice_in_dim(seq_lengths, group_index * seq_count, seq_count, 0)
    query_pos = position_of(
        ctx_index * local_rows + jnp.arange(local_rows, dtype=jnp.int32),
        local_rows,
        piece_rows,
        groups,
    )
    flat_in = local_in.reshape(token_count, model_width).astype(jnp.float32)
    flat_cot = local_cot.reshape(token_count, model_width)
    lowered = (
        w_query.astype(jnp.bfloat16),
        w_key.astype(jnp.bfloat16),
        w_value.astype(jnp.bfloat16),
        w_output.astype(jnp.bfloat16),
        w_up.astype(jnp.bfloat16),
        w_down.astype(jnp.bfloat16),
        attn_gain.astype(jnp.bfloat16),
        mlp_gain.astype(jnp.bfloat16),
        query_scale.astype(jnp.bfloat16),
    )
    gathered = (
        lax.all_gather(lowered[0], ("dp", "ctx"), axis=0, tiled=True),
        lax.all_gather(lowered[1], ("dp", "ctx"), axis=0, tiled=True),
        lax.all_gather(lowered[2], ("dp", "ctx"), axis=0, tiled=True),
        lax.all_gather(lowered[3], ("dp", "ctx"), axis=0, tiled=True),
        lax.all_gather(lowered[4], ("dp", "ctx"), axis=0, tiled=True),
        lax.all_gather(lowered[5], ("dp", "ctx"), axis=0, tiled=True),
        lax.all_gather(lowered[6], ("dp", "ctx"), axis=0, tiled=True),
        lax.all_gather(lowered[7], ("dp", "ctx"), axis=0, tiled=True),
        lax.all_gather(lowered[8], ("dp", "ctx"), axis=0, tiled=True),
    )
    (
        query_full,
        key_full,
        value_full,
        output_full,
        up_full,
        down_full,
        gain_one,
        gain_two,
        scale_raw,
    ) = gathered
    inv_one = lax.rsqrt(jnp.mean(flat_in * flat_in, axis=1, keepdims=True) + 1e-06)
    normed_one = flat_in * inv_one
    hidden_one = (normed_one * gain_one.astype(jnp.float32)).astype(jnp.bfloat16)
    scale_param = scale_raw.astype(jnp.float32)
    query_mult = 1.442695041 / math.sqrt(head_dim) * jax.nn.softplus(scale_param)
    query_pre = jnp.dot(hidden_one, query_full, preferred_element_type=jnp.float32)
    queries = (query_pre * query_mult).astype(jnp.bfloat16)
    keys_local = jnp.dot(hidden_one, key_full, preferred_element_type=jnp.float32).astype(
        jnp.bfloat16
    )
    values_local = jnp.dot(hidden_one, value_full, preferred_element_type=jnp.float32).astype(
        jnp.bfloat16
    )
    four_shape = (seq_count, local_rows, head_count, head_dim)
    query_four = queries.reshape(four_shape)
    keys_three = keys_local.reshape(seq_count, local_rows, model_width)
    values_three = values_local.reshape(seq_count, local_rows, model_width)

    def live_between(row_pos, key_pos):
        allowed = (key_pos[None, None, :] <= row_pos[None, :, None]) & (
            key_pos[None, None, :] < my_lengths[:, None, None]
        )
        return allowed[:, :, None, :]

    def live_mask(key_pos):
        return live_between(query_pos, key_pos)

    def attend_block(state_now, key_block, value_block, first_row):
        run_max, run_sum, run_acc = state_now
        block_len = key_block.shape[1]
        key_pos = position_of(
            first_row + jnp.arange(block_len, dtype=jnp.int32), local_rows, piece_rows, groups
        )
        key_four = key_block.reshape(seq_count, block_len, head_count, head_dim)
        value_four = value_block.reshape(seq_count, block_len, head_count, head_dim)
        scores = jnp.einsum(
            "srhd,skhd->srhk", query_four, key_four, preferred_element_type=jnp.float32
        )
        allowed = live_mask(key_pos)
        masked = jnp.where(allowed, scores, -1e30)
        new_max = jnp.maximum(run_max, jnp.max(masked, axis=3))
        weights_now = jnp.exp(jnp.where(allowed, masked - new_max[..., None], -1e30))
        factor = jnp.exp(run_max - new_max)
        new_sum = run_sum * factor + jnp.sum(weights_now, axis=3)
        added = jnp.einsum(
            "srhk,skhd->srhd",
            weights_now.astype(jnp.bfloat16),
            value_four,
            preferred_element_type=jnp.float32,
        )
        return (new_max, new_sum, run_acc * factor[..., None] + added)

    start_state = (
        jnp.full((seq_count, local_rows, head_count), -1e30, jnp.float32),
        jnp.zeros((seq_count, local_rows, head_count), jnp.float32),
        jnp.zeros(four_shape, jnp.float32),
    )
    key_piece = lax.all_gather(keys_three, "ctx", axis=1, tiled=True)
    value_piece = lax.all_gather(values_three, "ctx", axis=1, tiled=True)
    piece_len = key_piece.shape[1]
    fold_block_len = 512 if piece_len % 512 == 0 else piece_len

    def one_block(state_now, block_index):
        offset = block_index * fold_block_len
        key_block = lax.dynamic_slice_in_dim(key_piece, offset, fold_block_len, 1)
        value_block = lax.dynamic_slice_in_dim(value_piece, offset, fold_block_len, 1)
        return (attend_block(state_now, key_block, value_block, offset), None)

    result_state, unused = lax.scan(
        one_block, start_state, jnp.arange(piece_len // fold_block_len, dtype=jnp.int32)
    )
    run_max, run_sum, run_acc = result_state
    log_total = run_max + jnp.log(run_sum)
    attn_exact = run_acc / run_sum[..., None]
    attended = attn_exact.reshape(token_count, model_width).astype(jnp.bfloat16)
    middle = flat_in + jnp.dot(attended, output_full, preferred_element_type=jnp.float32)
    inv_two = lax.rsqrt(jnp.mean(middle * middle, axis=1, keepdims=True) + 1e-06)
    normed_two = middle * inv_two
    hidden_two = (normed_two * gain_two.astype(jnp.float32)).astype(jnp.bfloat16)
    up_pre = jnp.dot(hidden_two, up_full, preferred_element_type=jnp.float32)
    active = jax.nn.silu(up_pre).astype(jnp.bfloat16)
    result = (middle + jnp.dot(active, down_full, preferred_element_type=jnp.float32)).astype(
        jnp.bfloat16
    )
    back_weights = (
        lax.all_gather(lowered[0], ("dp", "ctx"), axis=0, tiled=True),
        lax.all_gather(lowered[1], ("dp", "ctx"), axis=0, tiled=True),
        lax.all_gather(lowered[2], ("dp", "ctx"), axis=0, tiled=True),
        lax.all_gather(lowered[3], ("dp", "ctx"), axis=0, tiled=True),
        lax.all_gather(lowered[4], ("dp", "ctx"), axis=0, tiled=True),
        lax.all_gather(lowered[5], ("dp", "ctx"), axis=0, tiled=True),
        lax.all_gather(lowered[6], ("dp", "ctx"), axis=0, tiled=True),
        lax.all_gather(lowered[7], ("dp", "ctx"), axis=0, tiled=True),
        lax.all_gather(lowered[8], ("dp", "ctx"), axis=0, tiled=True),
    )
    (
        query_back,
        key_back,
        value_back,
        output_back,
        up_back,
        down_back,
        gain_one_back,
        gain_two_back,
        scale_back,
    ) = back_weights
    cot_wide = flat_cot.astype(jnp.float32)
    grad_down = trans_mult(active, flat_cot)
    grad_active = mult_trans(flat_cot, down_back)
    sigma_up = jax.nn.sigmoid(up_pre)
    grad_up_pre = (grad_active * sigma_up * (1.0 + up_pre * (1.0 - sigma_up))).astype(jnp.bfloat16)
    grad_up = trans_mult(hidden_two, grad_up_pre)
    grad_hidden_two = mult_trans(grad_up_pre, up_back)
    grad_gain_two = jnp.sum(grad_hidden_two * normed_two, axis=0)
    grad_middle = cot_wide + norm_back(
        grad_hidden_two, normed_two, inv_two, gain_two_back.astype(jnp.float32)
    )
    grad_middle_low = grad_middle.astype(jnp.bfloat16)
    grad_output = trans_mult(attended, grad_middle_low)
    grad_attended = mult_trans(grad_middle_low, output_back).astype(jnp.bfloat16)
    grad_att_four = grad_attended.reshape(four_shape)
    delta_rows = jnp.sum(grad_att_four.astype(jnp.float32) * attn_exact, axis=3)
    key_all, value_all = (
        lax.all_gather(keys_three, "ctx", axis=1, tiled=True),
        lax.all_gather(values_three, "ctx", axis=1, tiled=True),
    )
    block_len = min(512, padded)

    def back_block(block_index, state_now):
        grad_query, grad_key_all, grad_value_all = state_now
        offset = block_index * block_len
        key_block = lax.dynamic_slice_in_dim(key_all, offset, block_len, 1).reshape(
            seq_count, block_len, head_count, head_dim
        )
        value_block = lax.dynamic_slice_in_dim(value_all, offset, block_len, 1).reshape(
            seq_count, block_len, head_count, head_dim
        )
        key_pos = position_of(
            offset + jnp.arange(block_len, dtype=jnp.int32), local_rows, piece_rows, groups
        )
        scores = jnp.einsum(
            "srhd,skhd->srhk", query_four, key_block, preferred_element_type=jnp.float32
        )
        probs = jnp.exp(jnp.where(live_mask(key_pos), scores - log_total[..., None], -1e30))
        grad_value_block = jnp.einsum(
            "srhk,srhd->skhd",
            probs.astype(jnp.bfloat16),
            grad_att_four,
            preferred_element_type=jnp.float32,
        )
        grad_probs = jnp.einsum(
            "srhd,skhd->srhk", grad_att_four, value_block, preferred_element_type=jnp.float32
        )
        grad_scores = (probs * (grad_probs - delta_rows[..., None])).astype(jnp.bfloat16)
        grad_query = grad_query + jnp.einsum(
            "srhk,skhd->srhd", grad_scores, key_block, preferred_element_type=jnp.float32
        )
        grad_key_block = jnp.einsum(
            "srhk,srhd->skhd", grad_scores, query_four, preferred_element_type=jnp.float32
        )
        grad_key_all = lax.dynamic_update_slice_in_dim(
            grad_key_all, grad_key_block.reshape(seq_count, block_len, model_width), offset, 1
        )
        grad_value_all = lax.dynamic_update_slice_in_dim(
            grad_value_all, grad_value_block.reshape(seq_count, block_len, model_width), offset, 1
        )
        return (grad_query, grad_key_all, grad_value_all)

    zero_all = jnp.zeros((seq_count, padded, model_width), jnp.float32)
    grad_query, grad_key_all, grad_value_all = lax.fori_loop(
        0, padded // block_len, back_block, (jnp.zeros(four_shape, jnp.float32), zero_all, zero_all)
    )
    grad_key_mine, grad_value_mine = (
        lax.psum_scatter(
            grad_key_all.astype(jnp.bfloat16), "ctx", scatter_dimension=1, tiled=True
        ).astype(jnp.float32),
        lax.psum_scatter(
            grad_value_all.astype(jnp.bfloat16), "ctx", scatter_dimension=1, tiled=True
        ).astype(jnp.float32),
    )
    grad_query_flat = grad_query.reshape(token_count, model_width)
    grad_query_pre = (grad_query_flat * query_mult).astype(jnp.bfloat16)
    grad_scale = (
        1.442695041
        / math.sqrt(head_dim)
        * jax.nn.sigmoid(scale_back.astype(jnp.float32))
        * jnp.sum(grad_query_flat * query_pre, axis=0)
    )
    grad_key_low = grad_key_mine.reshape(token_count, model_width).astype(jnp.bfloat16)
    grad_value_low = grad_value_mine.reshape(token_count, model_width).astype(jnp.bfloat16)
    grad_wq = trans_mult(hidden_one, grad_query_pre)
    grad_wk = trans_mult(hidden_one, grad_key_low)
    grad_wv = trans_mult(hidden_one, grad_value_low)
    grad_hidden_one = (
        mult_trans(grad_query_pre, query_back)
        + mult_trans(grad_key_low, key_back)
        + mult_trans(grad_value_low, value_back)
    )
    grad_gain_one = jnp.sum(grad_hidden_one * normed_one, axis=0)
    grad_in = grad_middle + norm_back(
        grad_hidden_one, normed_one, inv_one, gain_one_back.astype(jnp.float32)
    )
    matrix_stack = jnp.stack([grad_wq, grad_wk, grad_wv, grad_output, grad_up, grad_down], axis=0)
    vector_stack = jnp.stack([grad_gain_one, grad_gain_two, grad_scale], axis=0)
    matrix_sums, vector_sums = (
        lax.psum_scatter(matrix_stack, ("dp", "ctx"), scatter_dimension=1, tiled=True),
        lax.psum_scatter(vector_stack, ("dp", "ctx"), scatter_dimension=1, tiled=True),
    )
    out_local = result.reshape(seq_count, local_rows, model_width)
    grad_local = grad_in.astype(jnp.bfloat16).reshape(seq_count, local_rows, model_width)
    back_out, back_grad = (
        lax.all_to_all(out_local, "dp", split_axis=1, concat_axis=0, tiled=True),
        lax.all_to_all(grad_local, "dp", split_axis=1, concat_axis=0, tiled=True),
    )
    return (
        back_out,
        back_grad,
        matrix_sums[0],
        matrix_sums[1],
        matrix_sums[2],
        matrix_sums[3],
        matrix_sums[4],
        matrix_sums[5],
        vector_sums[0],
        vector_sums[1],
        vector_sums[2],
    )


LOG2E = 1.442695041
CODES = (0, 1, 4, 5)


def plane_shift(value, step):
    if step == 1:
        return lax.ppermute(value, "x", [(0, 1), (1, 0)])
    if step == 2:
        return lax.ppermute(value, "y", [(0, 1), (1, 0)])
    return lax.ppermute(value, ("y", "x"), [(0, 3), (1, 2), (2, 1), (3, 0)])


def core_swap(value):
    return lax.ppermute(value, "core", [(0, 1), (1, 0)])


def ring_shift(value, step):
    return lax.ppermute(value, "z", [(i, (i + step) % 4) for i in range(4)])


def pick(array, index):
    return lax.dynamic_index_in_dim(array, index, 0, keepdims=False)


def by_source(pieces, z_index):
    own, one, two, three = pieces
    line = jnp.stack([three, two, one, own, three, two, one])
    return lax.dynamic_slice_in_dim(line, 3 - z_index, 4, 0)


def pair(mine, other, index, axis):
    first = index == 0
    return jnp.stack([jnp.where(first, mine, other), jnp.where(first, other, mine)], axis=axis)


def row_positions(shape, dim, z_index, plane_index):
    row = lax.broadcasted_iota(jnp.int32, shape, dim)
    chip = (row // 32) % 4
    code = (chip % 2) + 4 * (chip // 2) + 2 * (row // 128)
    hop = (row % 32) // 8
    return 64 * ((z_index - hop) & 3) + 8 * (plane_index ^ code) + row % 8


def live_pairs(info_ref, seq):
    z_index, plane_index = info_ref[0], info_ref[1]
    shape = (256, 256)
    query_pos = row_positions(shape, 0, z_index, plane_index)
    key_pos = row_positions(shape, 1, z_index, plane_index)
    return (key_pos <= query_pos) & (key_pos < info_ref[2 + seq])


def block_rows(near_ref, far_ref):
    return jnp.concatenate([near_ref[...], far_ref[...]], axis=0).reshape(256, near_ref.shape[2])


def soft_probs(query, key, live):
    scores = mult_trans(query, key)
    scores = jnp.where(live, scores, -1e30)
    top = jnp.max(scores, axis=1, keepdims=True)
    weights = jnp.where(live, jnp.exp(scores - top), 0.0)
    return weights / jnp.sum(weights, axis=1, keepdims=True)


def attend_kernel(info_ref, near_ref, far_ref, gain_ref, mult_ref, w_ref, pre_ref, att_near, att_far):
    seq = pl.program_id(0)
    live = live_pairs(info_ref, seq)
    wide = block_rows(near_ref, far_ref).astype(jnp.float32)
    inverse = lax.rsqrt(jnp.mean(wide * wide, axis=1, keepdims=True) + 1e-06)
    hidden = (wide * inverse * gain_ref[...]).astype(jnp.bfloat16)
    pre = jnp.dot(hidden, w_ref[...], preferred_element_type=jnp.float32)
    pre_ref[...] = pre.reshape(2, 4, 32, 480)
    query = (pre[:, 0:160] * mult_ref[...]).astype(jnp.bfloat16)
    key = pre[:, 160:320].astype(jnp.bfloat16)
    value = pre[:, 320:480].astype(jnp.bfloat16)
    heads = []
    for head in range(2):
        part = slice(80 * head, 80 * head + 80)
        probs = soft_probs(query[:, part], key[:, part], live).astype(jnp.bfloat16)
        heads.append(jnp.dot(probs, value[:, part], preferred_element_type=jnp.float32))
    att = jnp.concatenate(heads, axis=1).astype(jnp.bfloat16).reshape(2, 4, 32, 160)
    att_near[...] = att[0]
    att_far[...] = att[1]


def attend_back_kernel(
    info_ref, near_ref, far_ref, gain_ref, mult_ref, w_ref, pre_ref, grad_near, grad_far,
    hid_near, hid_far, w_grad, gain_grad, scale_grad, w_acc, gain_acc, scale_acc,
):
    seq = pl.program_id(0)

    @pl.when(seq == 0)
    def _():
        w_acc[...] = jnp.zeros_like(w_acc)
        gain_acc[...] = jnp.zeros_like(gain_acc)
        scale_acc[...] = jnp.zeros_like(scale_acc)

    live = live_pairs(info_ref, seq)
    wide = block_rows(near_ref, far_ref).astype(jnp.float32)
    inverse = lax.rsqrt(jnp.mean(wide * wide, axis=1, keepdims=True) + 1e-06)
    normed = wide * inverse
    hidden = (normed * gain_ref[...]).astype(jnp.bfloat16)
    pre = pre_ref[...].reshape(256, 480)
    mult = mult_ref[...]
    query = (pre[:, 0:160] * mult).astype(jnp.bfloat16)
    key = pre[:, 160:320].astype(jnp.bfloat16)
    value = pre[:, 320:480].astype(jnp.bfloat16)
    grad_att = block_rows(grad_near, grad_far)
    grad_q, grad_k, grad_v = [], [], []
    for head in range(2):
        part = slice(80 * head, 80 * head + 80)
        probs = soft_probs(query[:, part], key[:, part], live)
        grad_probs = mult_trans(grad_att[:, part], value[:, part])
        delta = jnp.sum(probs * grad_probs, axis=1, keepdims=True)
        grad_scores = (probs * (grad_probs - delta)).astype(jnp.bfloat16)
        grad_v.append(trans_mult(probs.astype(jnp.bfloat16), grad_att[:, part]))
        grad_q.append(jnp.dot(grad_scores, key[:, part], preferred_element_type=jnp.float32))
        grad_k.append(trans_mult(grad_scores, query[:, part]))
    grad_query = jnp.concatenate(grad_q, axis=1)
    scale_acc[...] += jnp.sum(grad_query * pre[:, 0:160], axis=0, keepdims=True)
    joined = jnp.concatenate([grad_query * mult] + grad_k + grad_v, axis=1).astype(jnp.bfloat16)
    w_acc[...] += trans_mult(hidden, joined)
    grad_hidden = mult_trans(joined, w_ref[...])
    gain_acc[...] += jnp.sum(grad_hidden * normed, axis=0, keepdims=True)
    low = grad_hidden.astype(jnp.bfloat16).reshape(2, 4, 32, 1280)
    hid_near[...] = low[0]
    hid_far[...] = low[1]

    @pl.when(seq == 3)
    def _():
        w_grad[...] = w_acc[...].astype(jnp.bfloat16)
        gain_grad[...] = gain_acc[...]
        scale_grad[...] = scale_acc[...]


def block_index(z_index, y_index, core):
    return pl.ds(pl.multiple_of((4 * z_index + 2 * y_index + core) * 80, 80), 80)


def source_rows(info_ref, chip, core):
    source = info_ref[1] ^ (CODES[chip] + 2 * core)
    return pl.ds(pl.multiple_of(source * 160, 160), 160)


def feed_kernel(
    info_ref, x_ref, g_ref, att_0, att_1, att_2, att_3, gain_ref,
    near_a, across_a, all_b, far_near_a, far_across_a, far_b,
    out_ref, pack_ref, att_pack, dmid_ref, datt_0, datt_1, datt_2, datt_3, gain_grad,
    weights, sems,
):
    y_index, core_index = info_ref[1] // 4, (info_ref[1] // 2) % 2
    copies = []
    for w in range(3):
        moved = []
        for core, refs in ((core_index, (near_a, across_a, all_b)), (1 - core_index, (far_near_a, far_across_a, far_b))):
            for half in range(2):
                moved.append((refs[0].at[half, w], half, y_index, core))
                moved.append((refs[1].at[half, w], half, 1 - y_index, core))
                for row in range(2):
                    moved.append((refs[2].at[half, w, row], 2 + half, row, core))
        copies.append([
            pltpu.make_async_copy(src, weights.at[w, block_index(*place)], sems.at[w, i])
            for i, (src, *place) in enumerate(moved)
        ])
    for group in copies:
        for copy in group:
            copy.start()
    atts, datts = (att_0, att_1, att_2, att_3), (datt_0, datt_1, datt_2, datt_3)

    for copy in copies[0]:
        copy.wait()
    middle = x_ref[...].astype(jnp.float32)
    for chip in range(4):
        for core in range(2):
            middle += jnp.dot(
                atts[chip][core], weights[0, source_rows(info_ref, chip, core), :],
                preferred_element_type=jnp.float32,
            )
    inverse = lax.rsqrt(jnp.mean(middle * middle, axis=1, keepdims=True) + 1e-06)
    normed = middle * inverse
    gain = gain_ref[...]
    hidden = (normed * gain).astype(jnp.bfloat16)
    pack_ref[1] = hidden
    for copy in copies[1]:
        copy.wait()
    up = jnp.dot(hidden, weights[1], preferred_element_type=jnp.float32)
    sigma = jax.nn.sigmoid(up)
    active = (up * sigma).astype(jnp.bfloat16)
    pack_ref[0] = active
    for copy in copies[2]:
        copy.wait()
    down = jnp.dot(active, weights[2], preferred_element_type=jnp.float32)
    out_ref[...] = (middle + down).astype(jnp.bfloat16)
    cot = g_ref[...]
    grad_act = mult_trans(cot, weights[2])
    grad_up = (grad_act * sigma * (1.0 + up * (1.0 - sigma))).astype(jnp.bfloat16)
    pack_ref[2] = grad_up
    pack_ref[4] = cot
    grad_hidden = mult_trans(grad_up, weights[1])
    gain_grad[...] = jnp.sum(grad_hidden * normed, axis=0, keepdims=True)
    grad_mid = cot.astype(jnp.float32) + norm_back(grad_hidden, normed, inverse, gain)
    dmid_ref[...] = grad_mid
    low = grad_mid.astype(jnp.bfloat16)
    pack_ref[3] = low
    for chip in range(4):
        for core in range(2):
            att_pack[2 * chip + core] = atts[chip][core]
            datts[chip][core] = mult_trans(low, weights[0, source_rows(info_ref, chip, core), :]).astype(jnp.bfloat16)


def grads_kernel(info_ref, pack_ref, att_pack, far_pack, far_att, kept, stage, sems):
    core_index = (info_ref[1] // 2) % 2
    copies = []

    def leave(w):
        for z_index in range(4):
            for row in range(2):
                copy = pltpu.make_async_copy(
                    stage.at[w, block_index(z_index, row, core_index)],
                    kept.at[z_index, w, row],
                    sems.at[w, 2 * z_index + row],
                )
                copy.start()
                copies.append(copy)

    def both(index, part):
        return jnp.concatenate([pack_ref[index, :, part], far_pack[index, :, part]], axis=0)

    everything = slice(0, pack_ref.shape[2])
    for w, left, right in ((2, 0, 4), (1, 1, 2)):
        grads = both(right, everything)
        for chunk in range(5):
            part = slice(256 * chunk, 256 * chunk + 256)
            stage[w, part, :] = trans_mult(both(left, part), grads).astype(jnp.bfloat16)
        leave(w)
    grads = both(3, everything)
    for chip in range(4):
        for core in range(2):
            att = jnp.concatenate([att_pack[2 * chip + core], far_att[2 * chip + 1 - core]], axis=0)
            stage[0, source_rows(info_ref, chip, core), :] = trans_mult(att, grads).astype(jnp.bfloat16)
    leave(0)
    for copy in copies:
        copy.wait()


def whole(shape):
    return pl.BlockSpec(shape, lambda *_: (0,) * len(shape))


def seq_block(*lead, width):
    count = len(lead)
    return pl.BlockSpec((*lead, 32, width), lambda s, info: (*(0,) * count, s, 0))


def planes(
    inputs, cotangent, w_query, w_key, w_value, w_output, w_up, w_down,
    attn_gain, mlp_gain, query_scale, deal, lengths,
):
    f32, bf16 = jnp.float32, jnp.bfloat16
    z, y, c, x = (lax.axis_index(name) for name in ("z", "y", "core", "x"))
    plane = 4 * y + 2 * c + x
    width = 1280
    seqs = jnp.arange(16, dtype=jnp.int32)
    seq_lengths = jnp.sum(jnp.where(deal[None, :] == seqs[:, None], lengths[None, :], 0), axis=1)
    my_lengths = lax.dynamic_slice_in_dim(seq_lengths, 4 * z, 4, 0)
    info = jnp.concatenate([jnp.stack([z, plane]), my_lengths]).astype(jnp.int32)

    vec = jnp.concatenate([attn_gain, mlp_gain, query_scale]).astype(bf16)
    vec_block = jnp.zeros((1, 8, width), bf16).at[0, 0, :120].set(vec)
    in_four = inputs.reshape(4, 4, 8, width)
    sent = [jnp.concatenate([pick(in_four, (z + k) % 4), vec_block]) for k in range(4)]
    got = [sent[0]] + [ring_shift(sent[k], k) for k in (1, 2, 3)]
    x_rows = jnp.stack([item[:4] for item in got], axis=1).reshape(128, width)
    vec_rows = jnp.concatenate([item[4, :1] for item in got] + [jnp.zeros((4, width), bf16)])
    own = jnp.concatenate([x_rows, vec_rows])

    big = jnp.stack([w_output, w_up, w_down]).astype(bf16)
    big = lax.all_gather(big, "z", axis=0)

    qkv = jnp.stack([w_query, w_key, w_value]).astype(bf16)
    own, qkv = lax.optimization_barrier((own, qkv))
    near = jnp.stack([own] + [plane_shift(own, step) for step in (1, 2, 3)])
    qkv = qkv.reshape(3, 40, 8, 160).transpose(2, 1, 0, 3).reshape(8, 40, 480)
    qkv = lax.all_to_all(qkv, ("y", "core", "x"), split_axis=0, concat_axis=0, tiled=True)
    qkv = qkv.reshape(320, 480)

    late = qkv
    big, near, qkv = lax.optimization_barrier((big, near, qkv))
    one, three = ring_shift(qkv, 1), ring_shift(qkv, 3)
    far = core_swap(near)
    part_a, part_b = big[:2], big[2:]
    near_a = pair(part_a, plane_shift(part_a, 1), x, 2).reshape(2, 3, 80, width)
    part_b = pair(part_b, plane_shift(part_b, 2), y, 2)
    near_a, part_b, cotangent, late, one, three = lax.optimization_barrier(
        (near_a, part_b, cotangent, late, one, three)
    )
    w_qkv = by_source([qkv, one, ring_shift(late, 2), three], z).reshape(width, 480)
    across_a = plane_shift(near_a, 2)
    across_b = plane_shift(part_b, 1)
    cot_four = lax.all_to_all(cotangent.reshape(4, 4, 8, width), "z", split_axis=0, concat_axis=0, tiled=True)
    cot_rows = jnp.stack([pick(cot_four, (z - k) % 4) for k in range(4)], axis=1).reshape(128, width)

    vecs = jnp.stack([near[:, 128:132, :120], far[:, 128:132, :120]])
    vecs = vecs.astype(f32).reshape(2, 2, 2, 4, 120)
    vecs = jnp.where(c == 0, vecs, vecs[::-1])
    vecs = jnp.where(y == 0, vecs, vecs[:, ::-1])
    vecs = jnp.where(x == 0, vecs, vecs[:, :, ::-1])
    fours = jnp.arange(4, dtype=jnp.int32)
    from_hop = (z - fours[:, None]) % 4 == fours[None, :]
    vecs = jnp.sum(jnp.where(from_hop[:, None, None, None, :, None], vecs[None], 0.0), axis=4)
    vecs = vecs.reshape(4, 2, 2, 2, 3, 40).transpose(4, 0, 2, 1, 3, 5).reshape(3, width)
    gain_one, gain_two = vecs[0:1], vecs[1:2]
    my_scale = lax.dynamic_slice_in_dim(vecs[2:3], 160 * plane, 160, 1)
    query_mult = LOG2E / math.sqrt(HD) * jax.nn.softplus(my_scale)

    limit = pltpu.CompilerParams(vmem_limit_bytes=50 * 1024 * 1024)
    pre, att_near, att_far = pl.pallas_call(
        attend_kernel,
        grid_spec=pltpu.PrefetchScalarGridSpec(
            num_scalar_prefetch=1,
            grid=(4,),
            in_specs=[
                seq_block(4, width=width), seq_block(4, width=width),
                whole((1, width)), whole((1, 160)), whole((width, 480)),
            ],
            out_specs=[seq_block(2, 4, width=480), seq_block(4, width=160), seq_block(4, width=160)],
        ),
        out_shape=[
            jax.ShapeDtypeStruct((2, 4, 128, 480), f32),
            jax.ShapeDtypeStruct((4, 128, 160), bf16),
            jax.ShapeDtypeStruct((4, 128, 160), bf16),
        ],
        compiler_params=limit,
        cost_estimate=pl.CostEstimate(flops=9_000_000_000, bytes_accessed=8_000_000, transcendentals=600_000),
        name="attend",
    )(info, near, far, gain_one, query_mult, w_qkv)

    att_near, att_far, cot_rows, near_a = lax.optimization_barrier((att_near, att_far, cot_rows, near_a))
    far_near_a = core_swap(near_a)
    att_pair = jnp.stack([att_near, core_swap(att_far)], axis=1)
    atts = [att_pair[0]] + [plane_shift(att_pair[step], step) for step in (1, 2, 3)]
    *atts, far_near_a, across_a, across_b = lax.optimization_barrier((*atts, far_near_a, across_a, across_b))
    far_across_a = core_swap(across_a)
    all_b = pair(part_b, across_b, x, 3).reshape(2, 3, 2, 80, width)
    far_b = core_swap(all_b)

    low_rows = jax.ShapeDtypeStruct((128, width), bf16)
    datt_shape = jax.ShapeDtypeStruct((2, 128, 160), bf16)
    smem = pl.BlockSpec(memory_space=pltpu.SMEM)
    vmem = pl.BlockSpec(memory_space=pltpu.VMEM)
    hbm = pl.BlockSpec(memory_space=pl.ANY)
    out_rows, pack, att_pack, grad_mid, *datts, gain_two_grad = pl.pallas_call(
        feed_kernel,
        in_specs=[smem] + [vmem] * 7 + [hbm] * 6,
        out_specs=[vmem] * 9,
        out_shape=[
            low_rows,
            jax.ShapeDtypeStruct((5, 128, width), bf16),
            jax.ShapeDtypeStruct((8, 128, 160), bf16),
            jax.ShapeDtypeStruct((128, width), f32),
        ]
        + [datt_shape] * 4
        + [jax.ShapeDtypeStruct((1, width), f32)],
        scratch_shapes=[pltpu.VMEM((3, width, width), bf16), pltpu.SemaphoreType.DMA((3, 16))],
        compiler_params=limit,
        cost_estimate=pl.CostEstimate(flops=12_000_000_000, bytes_accessed=13_000_000, transcendentals=200_000),
        name="feed",
    )(info, x_rows, cot_rows, *atts, gain_two, near_a, across_a, all_b, far_near_a, far_across_a, far_b)

    def home(rows):
        rows = rows.reshape(4, 4, 8, width)
        parts = [rows[:, 0]] + [ring_shift(rows[:, k], -k) for k in (1, 2, 3)]
        line = jnp.stack(parts + parts[:3])
        return lax.dynamic_slice_in_dim(line, (4 - z) % 4, 4, 0).reshape(16, 8, width)

    back = [datts[0]] + [plane_shift(datts[step], step) for step in (1, 2, 3)]
    *back, out_rows = lax.optimization_barrier((*back, out_rows))
    outputs = home(out_rows)
    grad_att_near = jnp.stack([item[0] for item in back])
    grad_att_far = core_swap(jnp.stack([item[1] for item in back]))

    kept = pl.pallas_call(
        grads_kernel,
        in_specs=[smem] + [vmem] * 4,
        out_specs=hbm,
        out_shape=jax.ShapeDtypeStruct((4, 3, 2, 80, width), bf16),
        scratch_shapes=[pltpu.VMEM((3, width, width), bf16), pltpu.SemaphoreType.DMA((3, 8))],
        compiler_params=limit,
        cost_estimate=pl.CostEstimate(flops=6_000_000_000, bytes_accessed=8_000_000, transcendentals=0),
        name="grads",
    )(info, pack, att_pack, core_swap(pack), core_swap(att_pack))

    def added(left, right):
        return (left.astype(f32) + right.astype(f32)).astype(bf16)

    def halves(array, index, axis):
        first, second = (lax.index_in_dim(array, i, axis, keepdims=False) for i in (0, 1))
        return jnp.where(index == 0, first, second), jnp.where(index == 0, second, first)

    kept, grad_att_near, grad_att_far, outputs = lax.optimization_barrier(
        (kept, grad_att_near, grad_att_far, outputs)
    )
    kept = kept.reshape(4, 3, 2, 2, 40, width)
    kept_a, away_a = halves(kept[:2], x, 3)
    kept_b, away_b = halves(kept[2:], y, 2)
    kept_a = added(kept_a, plane_shift(away_a, 1))
    kept_b = added(kept_b, plane_shift(away_b, 2))
    def ring_sum(array):
        total = pick(array, z).astype(f32)
        for k in (1, 2, 3):
            total += ring_shift(pick(array, (z + k) % 4), k).astype(f32)
        return total


    hid_near, hid_far, qkv_grad, gain_one_grad, scale_grad = pl.pallas_call(
        attend_back_kernel,
        grid_spec=pltpu.PrefetchScalarGridSpec(
            num_scalar_prefetch=1,
            grid=(4,),
            in_specs=[
                seq_block(4, width=width), seq_block(4, width=width),
                whole((1, width)), whole((1, 160)), whole((width, 480)),
                seq_block(2, 4, width=480), seq_block(4, width=160), seq_block(4, width=160),
            ],
            out_specs=[
                seq_block(4, width=width), seq_block(4, width=width),
                whole((width, 480)), whole((1, width)), whole((1, 160)),
            ],
            scratch_shapes=[
                pltpu.VMEM((width, 480), f32), pltpu.VMEM((1, width), f32), pltpu.VMEM((1, 160), f32),
            ],
        ),
        out_shape=[
            jax.ShapeDtypeStruct((4, 128, width), bf16),
            jax.ShapeDtypeStruct((4, 128, width), bf16),
            jax.ShapeDtypeStruct((width, 480), bf16),
            jax.ShapeDtypeStruct((1, width), f32),
            jax.ShapeDtypeStruct((1, 160), f32),
        ],
        compiler_params=limit,
        cost_estimate=pl.CostEstimate(flops=15_000_000_000, bytes_accessed=12_000_000, transcendentals=600_000),
        name="attend_back",
    )(info, near, far, gain_one, query_mult, w_qkv, pre, grad_att_near, grad_att_far)

    scale_line = lax.dynamic_update_slice(jnp.zeros((1, width), f32), scale_grad, (0, 160 * plane))
    lines = jnp.concatenate([gain_one_grad, gain_two_grad, scale_line])
    lines = lines.reshape(3, 4, 8, 40).transpose(1, 2, 0, 3).reshape(4, 8, 1, 120).astype(bf16)
    lines = jnp.pad(lines, ((0, 0), (0, 0), (0, 7), (0, 360)))
    send = jnp.concatenate([qkv_grad.reshape(4, 8, 40, 480), lines], axis=2)
    one, three = (ring_shift(pick(send, (z + k) % 4), k) for k in (1, 3))
    hid = added(hid_near, core_swap(hid_far))
    later = send
    kept_a, kept_b, hid, one, three, later = lax.optimization_barrier((kept_a, kept_b, hid, one, three, later))
    kept_a, away_a = halves(kept_a, y, 2)
    kept_b, away_b = halves(kept_b, x, 2)
    kept_a = added(kept_a, plane_shift(away_a, 2))
    kept_b = added(kept_b, plane_shift(away_b, 1))
    kept = jnp.concatenate([kept_a, kept_b])
    two = ring_shift(pick(later, (z + 2) % 4), 2)
    grad_hid = hid[0].astype(f32)
    moved = [plane_shift(hid[step], step) for step in (1, 2, 3)]
    *moved, kept = lax.optimization_barrier((*moved, kept))
    for item in moved:
        grad_hid += item.astype(f32)
    wide = x_rows.astype(f32)
    inverse = lax.rsqrt(jnp.mean(wide * wide, axis=1, keepdims=True) + 1e-06)
    grad_in = (grad_mid + norm_back(grad_hid, wide * inverse, inverse, gain_one)).astype(bf16)

    sums = sum((item.astype(f32) for item in (one, two, three)), pick(send, z).astype(f32)).astype(bf16)
    sums = lax.all_to_all(sums, ("y", "core", "x"), split_axis=0, concat_axis=0, tiled=True)
    big_sums = ring_sum(kept)
    qkv_sums = sums[:, :40].reshape(8, 40, 3, 160).transpose(2, 1, 0, 3).reshape(3, 40, width).astype(f32)
    line_sums = jnp.sum(sums[:, 40, :120].astype(f32), axis=0).reshape(3, 40)
    scale_low = query_scale.astype(bf16).astype(f32)
    scale_sum = LOG2E / math.sqrt(HD) * jax.nn.sigmoid(scale_low) * line_sums[2]

    return (
        outputs, home(grad_in), qkv_sums[0], qkv_sums[1], qkv_sums[2],
        big_sums[0], big_sums[1], big_sums[2], line_sums[0], line_sums[1], scale_sum,
    )


def solution(mesh):
    names = ("dp", "ctx")
    body = per_device
    if dict(mesh.shape) == {"dp": 16, "ctx": 2}:
        mesh = Mesh(mesh.devices.reshape(4, 2, 2, 2), ("z", "y", "core", "x"))
        names = mesh.axis_names
        body = planes
    seq, mat, line = P(None, names, None), P(names, None), P(names)
    return jax.shard_map(
        body,
        mesh=mesh,
        in_specs=(seq,) * 2 + (mat,) * 6 + (line,) * 3 + (P(), P()),
        out_specs=(seq,) * 2 + (mat,) * 6 + (line,) * 3,
        check_vma=False,
    )
```

```python
import math

import jax
import jax.numpy as jnp
from jax import lax
from jax.experimental import pallas as pl
from jax.experimental.pallas import tpu as pltpu
from jax.sharding import Mesh, PartitionSpec as P

H = 16
HD = 80


def mult_trans(left, right):
    return lax.dot_general(
        left, right, (((1,), (1,)), ((), ())), preferred_element_type=jnp.float32
    )


def trans_mult(left, right):
    return lax.dot_general(
        left, right, (((0,), (0,)), ((), ())), preferred_element_type=jnp.float32
    )


def position_of(index, local_rows, piece_rows, groups):
    column = index // local_rows
    within = index % local_rows
    return (within // piece_rows * groups + column) * piece_rows + within % piece_rows


def norm_back(grad_hidden, normed, inverse, gain_value):
    grad_normed = grad_hidden * gain_value
    return inverse * (grad_normed - normed * jnp.mean(grad_normed * normed, axis=1, keepdims=True))


def per_device(
    inputs,
    cotangent,
    w_query,
    w_key,
    w_value,
    w_output,
    w_up,
    w_down,
    attn_gain,
    mlp_gain,
    query_scale,
    deal,
    lengths,
):
    groups = lax.axis_size("ctx")
    group_index = lax.axis_index("dp")
    ctx_index = lax.axis_index("ctx")
    head_count = H
    head_dim = HD
    piece_rows = inputs.shape[1]
    seq_numbers = jnp.arange(inputs.shape[0], dtype=jnp.int32)
    seq_lengths = jnp.sum(
        jnp.where(deal[None, :] == seq_numbers[:, None], lengths[None, :], 0), axis=1
    )
    local_in, local_cot = (
        lax.all_to_all(inputs, "dp", split_axis=0, concat_axis=1, tiled=True),
        lax.all_to_all(cotangent, "dp", split_axis=0, concat_axis=1, tiled=True),
    )
    seq_count, local_rows, model_width = local_in.shape
    padded = local_rows * groups
    token_count = seq_count * local_rows
    my_lengths = lax.dynamic_slice_in_dim(seq_lengths, group_index * seq_count, seq_count, 0)
    query_pos = position_of(
        ctx_index * local_rows + jnp.arange(local_rows, dtype=jnp.int32),
        local_rows,
        piece_rows,
        groups,
    )
    flat_in = local_in.reshape(token_count, model_width).astype(jnp.float32)
    flat_cot = local_cot.reshape(token_count, model_width)
    lowered = (
        w_query.astype(jnp.bfloat16),
        w_key.astype(jnp.bfloat16),
        w_value.astype(jnp.bfloat16),
        w_output.astype(jnp.bfloat16),
        w_up.astype(jnp.bfloat16),
        w_down.astype(jnp.bfloat16),
        attn_gain.astype(jnp.bfloat16),
        mlp_gain.astype(jnp.bfloat16),
        query_scale.astype(jnp.bfloat16),
    )
    gathered = (
        lax.all_gather(lowered[0], ("dp", "ctx"), axis=0, tiled=True),
        lax.all_gather(lowered[1], ("dp", "ctx"), axis=0, tiled=True),
        lax.all_gather(lowered[2], ("dp", "ctx"), axis=0, tiled=True),
        lax.all_gather(lowered[3], ("dp", "ctx"), axis=0, tiled=True),
        lax.all_gather(lowered[4], ("dp", "ctx"), axis=0, tiled=True),
        lax.all_gather(lowered[5], ("dp", "ctx"), axis=0, tiled=True),
        lax.all_gather(lowered[6], ("dp", "ctx"), axis=0, tiled=True),
        lax.all_gather(lowered[7], ("dp", "ctx"), axis=0, tiled=True),
        lax.all_gather(lowered[8], ("dp", "ctx"), axis=0, tiled=True),
    )
    (
        query_full,
        key_full,
        value_full,
        output_full,
        up_full,
        down_full,
        gain_one,
        gain_two,
        scale_raw,
    ) = gathered
    inv_one = lax.rsqrt(jnp.mean(flat_in * flat_in, axis=1, keepdims=True) + 1e-06)
    normed_one = flat_in * inv_one
    hidden_one = (normed_one * gain_one.astype(jnp.float32)).astype(jnp.bfloat16)
    scale_param = scale_raw.astype(jnp.float32)
    query_mult = 1.442695041 / math.sqrt(head_dim) * jax.nn.softplus(scale_param)
    query_pre = jnp.dot(hidden_one, query_full, preferred_element_type=jnp.float32)
    queries = (query_pre * query_mult).astype(jnp.bfloat16)
    keys_local = jnp.dot(hidden_one, key_full, preferred_element_type=jnp.float32).astype(
        jnp.bfloat16
    )
    values_local = jnp.dot(hidden_one, value_full, preferred_element_type=jnp.float32).astype(
        jnp.bfloat16
    )
    four_shape = (seq_count, local_rows, head_count, head_dim)
    query_four = queries.reshape(four_shape)
    keys_three = keys_local.reshape(seq_count, local_rows, model_width)
    values_three = values_local.reshape(seq_count, local_rows, model_width)

    def live_between(row_pos, key_pos):
        allowed = (key_pos[None, None, :] <= row_pos[None, :, None]) & (
            key_pos[None, None, :] < my_lengths[:, None, None]
        )
        return allowed[:, :, None, :]

    def live_mask(key_pos):
        return live_between(query_pos, key_pos)

    def attend_block(state_now, key_block, value_block, first_row):
        run_max, run_sum, run_acc = state_now
        block_len = key_block.shape[1]
        key_pos = position_of(
            first_row + jnp.arange(block_len, dtype=jnp.int32), local_rows, piece_rows, groups
        )
        key_four = key_block.reshape(seq_count, block_len, head_count, head_dim)
        value_four = value_block.reshape(seq_count, block_len, head_count, head_dim)
        scores = jnp.einsum(
            "srhd,skhd->srhk", query_four, key_four, preferred_element_type=jnp.float32
        )
        allowed = live_mask(key_pos)
        masked = jnp.where(allowed, scores, -1e30)
        new_max = jnp.maximum(run_max, jnp.max(masked, axis=3))
        weights_now = jnp.exp(jnp.where(allowed, masked - new_max[..., None], -1e30))
        factor = jnp.exp(run_max - new_max)
        new_sum = run_sum * factor + jnp.sum(weights_now, axis=3)
        added = jnp.einsum(
            "srhk,skhd->srhd",
            weights_now.astype(jnp.bfloat16),
            value_four,
            preferred_element_type=jnp.float32,
        )
        return (new_max, new_sum, run_acc * factor[..., None] + added)

    start_state = (
        jnp.full((seq_count, local_rows, head_count), -1e30, jnp.float32),
        jnp.zeros((seq_count, local_rows, head_count), jnp.float32),
        jnp.zeros(four_shape, jnp.float32),
    )
    key_piece = lax.all_gather(keys_three, "ctx", axis=1, tiled=True)
    value_piece = lax.all_gather(values_three, "ctx", axis=1, tiled=True)
    piece_len = key_piece.shape[1]
    fold_block_len = 512 if piece_len % 512 == 0 else piece_len

    def one_block(state_now, block_index):
        offset = block_index * fold_block_len
        key_block = lax.dynamic_slice_in_dim(key_piece, offset, fold_block_len, 1)
        value_block = lax.dynamic_slice_in_dim(value_piece, offset, fold_block_len, 1)
        return (attend_block(state_now, key_block, value_block, offset), None)

    result_state, unused = lax.scan(
        one_block, start_state, jnp.arange(piece_len // fold_block_len, dtype=jnp.int32)
    )
    run_max, run_sum, run_acc = result_state
    log_total = run_max + jnp.log(run_sum)
    attn_exact = run_acc / run_sum[..., None]
    attended = attn_exact.reshape(token_count, model_width).astype(jnp.bfloat16)
    middle = flat_in + jnp.dot(attended, output_full, preferred_element_type=jnp.float32)
    inv_two = lax.rsqrt(jnp.mean(middle * middle, axis=1, keepdims=True) + 1e-06)
    normed_two = middle * inv_two
    hidden_two = (normed_two * gain_two.astype(jnp.float32)).astype(jnp.bfloat16)
    up_pre = jnp.dot(hidden_two, up_full, preferred_element_type=jnp.float32)
    active = jax.nn.silu(up_pre).astype(jnp.bfloat16)
    result = (middle + jnp.dot(active, down_full, preferred_element_type=jnp.float32)).astype(
        jnp.bfloat16
    )
    back_weights = (
        lax.all_gather(lowered[0], ("dp", "ctx"), axis=0, tiled=True),
        lax.all_gather(lowered[1], ("dp", "ctx"), axis=0, tiled=True),
        lax.all_gather(lowered[2], ("dp", "ctx"), axis=0, tiled=True),
        lax.all_gather(lowered[3], ("dp", "ctx"), axis=0, tiled=True),
        lax.all_gather(lowered[4], ("dp", "ctx"), axis=0, tiled=True),
        lax.all_gather(lowered[5], ("dp", "ctx"), axis=0, tiled=True),
        lax.all_gather(lowered[6], ("dp", "ctx"), axis=0, tiled=True),
        lax.all_gather(lowered[7], ("dp", "ctx"), axis=0, tiled=True),
        lax.all_gather(lowered[8], ("dp", "ctx"), axis=0, tiled=True),
    )
    (
        query_back,
        key_back,
        value_back,
        output_back,
        up_back,
        down_back,
        gain_one_back,
        gain_two_back,
        scale_back,
    ) = back_weights
    cot_wide = flat_cot.astype(jnp.float32)
    grad_down = trans_mult(active, flat_cot)
    grad_active = mult_trans(flat_cot, down_back)
    sigma_up = jax.nn.sigmoid(up_pre)
    grad_up_pre = (grad_active * sigma_up * (1.0 + up_pre * (1.0 - sigma_up))).astype(jnp.bfloat16)
    grad_up = trans_mult(hidden_two, grad_up_pre)
    grad_hidden_two = mult_trans(grad_up_pre, up_back)
    grad_gain_two = jnp.sum(grad_hidden_two * normed_two, axis=0)
    grad_middle = cot_wide + norm_back(
        grad_hidden_two, normed_two, inv_two, gain_two_back.astype(jnp.float32)
    )
    grad_middle_low = grad_middle.astype(jnp.bfloat16)
    grad_output = trans_mult(attended, grad_middle_low)
    grad_attended = mult_trans(grad_middle_low, output_back).astype(jnp.bfloat16)
    grad_att_four = grad_attended.reshape(four_shape)
    delta_rows = jnp.sum(grad_att_four.astype(jnp.float32) * attn_exact, axis=3)
    key_all, value_all = (
        lax.all_gather(keys_three, "ctx", axis=1, tiled=True),
        lax.all_gather(values_three, "ctx", axis=1, tiled=True),
    )
    block_len = min(512, padded)

    def back_block(block_index, state_now):
        grad_query, grad_key_all, grad_value_all = state_now
        offset = block_index * block_len
        key_block = lax.dynamic_slice_in_dim(key_all, offset, block_len, 1).reshape(
            seq_count, block_len, head_count, head_dim
        )
        value_block = lax.dynamic_slice_in_dim(value_all, offset, block_len, 1).reshape(
            seq_count, block_len, head_count, head_dim
        )
        key_pos = position_of(
            offset + jnp.arange(block_len, dtype=jnp.int32), local_rows, piece_rows, groups
        )
        scores = jnp.einsum(
            "srhd,skhd->srhk", query_four, key_block, preferred_element_type=jnp.float32
        )
        probs = jnp.exp(jnp.where(live_mask(key_pos), scores - log_total[..., None], -1e30))
        grad_value_block = jnp.einsum(
            "srhk,srhd->skhd",
            probs.astype(jnp.bfloat16),
            grad_att_four,
            preferred_element_type=jnp.float32,
        )
        grad_probs = jnp.einsum(
            "srhd,skhd->srhk", grad_att_four, value_block, preferred_element_type=jnp.float32
        )
        grad_scores = (probs * (grad_probs - delta_rows[..., None])).astype(jnp.bfloat16)
        grad_query = grad_query + jnp.einsum(
            "srhk,skhd->srhd", grad_scores, key_block, preferred_element_type=jnp.float32
        )
        grad_key_block = jnp.einsum(
            "srhk,srhd->skhd", grad_scores, query_four, preferred_element_type=jnp.float32
        )
        grad_key_all = lax.dynamic_update_slice_in_dim(
            grad_key_all, grad_key_block.reshape(seq_count, block_len, model_width), offset, 1
        )
        grad_value_all = lax.dynamic_update_slice_in_dim(
            grad_value_all, grad_value_block.reshape(seq_count, block_len, model_width), offset, 1
        )
        return (grad_query, grad_key_all, grad_value_all)

    zero_all = jnp.zeros((seq_count, padded, model_width), jnp.float32)
    grad_query, grad_key_all, grad_value_all = lax.fori_loop(
        0, padded // block_len, back_block, (jnp.zeros(four_shape, jnp.float32), zero_all, zero_all)
    )
    grad_key_mine, grad_value_mine = (
        lax.psum_scatter(
            grad_key_all.astype(jnp.bfloat16), "ctx", scatter_dimension=1, tiled=True
        ).astype(jnp.float32),
        lax.psum_scatter(
            grad_value_all.astype(jnp.bfloat16), "ctx", scatter_dimension=1, tiled=True
        ).astype(jnp.float32),
    )
    grad_query_flat = grad_query.reshape(token_count, model_width)
    grad_query_pre = (grad_query_flat * query_mult).astype(jnp.bfloat16)
    grad_scale = (
        1.442695041
        / math.sqrt(head_dim)
        * jax.nn.sigmoid(scale_back.astype(jnp.float32))
        * jnp.sum(grad_query_flat * query_pre, axis=0)
    )
    grad_key_low = grad_key_mine.reshape(token_count, model_width).astype(jnp.bfloat16)
    grad_value_low = grad_value_mine.reshape(token_count, model_width).astype(jnp.bfloat16)
    grad_wq = trans_mult(hidden_one, grad_query_pre)
    grad_wk = trans_mult(hidden_one, grad_key_low)
    grad_wv = trans_mult(hidden_one, grad_value_low)
    grad_hidden_one = (
        mult_trans(grad_query_pre, query_back)
        + mult_trans(grad_key_low, key_back)
        + mult_trans(grad_value_low, value_back)
    )
    grad_gain_one = jnp.sum(grad_hidden_one * normed_one, axis=0)
    grad_in = grad_middle + norm_back(
        grad_hidden_one, normed_one, inv_one, gain_one_back.astype(jnp.float32)
    )
    matrix_stack = jnp.stack([grad_wq, grad_wk, grad_wv, grad_output, grad_up, grad_down], axis=0)
    vector_stack = jnp.stack([grad_gain_one, grad_gain_two, grad_scale], axis=0)
    matrix_sums, vector_sums = (
        lax.psum_scatter(matrix_stack, ("dp", "ctx"), scatter_dimension=1, tiled=True),
        lax.psum_scatter(vector_stack, ("dp", "ctx"), scatter_dimension=1, tiled=True),
    )
    out_local = result.reshape(seq_count, local_rows, model_width)
    grad_local = grad_in.astype(jnp.bfloat16).reshape(seq_count, local_rows, model_width)
    back_out, back_grad = (
        lax.all_to_all(out_local, "dp", split_axis=1, concat_axis=0, tiled=True),
        lax.all_to_all(grad_local, "dp", split_axis=1, concat_axis=0, tiled=True),
    )
    return (
        back_out,
        back_grad,
        matrix_sums[0],
        matrix_sums[1],
        matrix_sums[2],
        matrix_sums[3],
        matrix_sums[4],
        matrix_sums[5],
        vector_sums[0],
        vector_sums[1],
        vector_sums[2],
    )


LOG2E = 1.442695041
CODES = (0, 1, 4, 5)


def plane_shift(value, step):
    if step == 1:
        return lax.ppermute(value, "x", [(0, 1), (1, 0)])
    if step == 2:
        return lax.ppermute(value, "y", [(0, 1), (1, 0)])
    return lax.ppermute(value, ("y", "x"), [(0, 3), (1, 2), (2, 1), (3, 0)])


def core_swap(value):
    return lax.ppermute(value, "core", [(0, 1), (1, 0)])


def ring_shift(value, step):
    return lax.ppermute(value, "z", [(i, (i + step) % 4) for i in range(4)])


def pick(array, index):
    return lax.dynamic_index_in_dim(array, index, 0, keepdims=False)


def by_source(pieces, z_index, axis):
    pieces = [jnp.expand_dims(item, axis) for item in pieces]
    shape = [1] * pieces[0].ndim
    shape[axis] = 4
    hop = ((z_index - jnp.arange(4, dtype=jnp.int32)) % 4).reshape(shape)
    made = pieces[0]
    for k in (1, 2, 3):
        made = jnp.where(hop == k, pieces[k], made)
    return made


def pair(mine, other, index, axis):
    first = index == 0
    return jnp.stack([jnp.where(first, mine, other), jnp.where(first, other, mine)], axis=axis)


def row_positions(shape, dim, plane_index):
    row = lax.broadcasted_iota(jnp.int32, shape, dim)
    chip = (row // 32) % 4
    code = (chip % 2) + 4 * (chip // 2) + 2 * (row // 128)
    return 64 * ((row % 32) // 8) + 8 * (plane_index ^ code) + row % 8


def live_pairs(info_ref, seq):
    shape = (256, 256)
    query_pos = row_positions(shape, 0, info_ref[1])
    key_pos = row_positions(shape, 1, info_ref[1])
    return (key_pos <= query_pos) & (key_pos < info_ref[2 + seq])


def block_rows(near_ref, far_ref):
    return jnp.concatenate([near_ref[...], far_ref[...]], axis=0).reshape(256, near_ref.shape[2])


def soft_probs(query, key, live):
    scores = mult_trans(query, key)
    scores = jnp.where(live, scores, -1e30)
    top = jnp.max(scores, axis=1, keepdims=True)
    weights = jnp.where(live, jnp.exp(scores - top), 0.0)
    return weights / jnp.sum(weights, axis=1, keepdims=True)


def attend_kernel(
    info_ref, near_ref, far_ref, gain_ref, mult_ref, w_ref, pre_ref, att_near, att_far
):
    seq = pl.program_id(0)
    live = live_pairs(info_ref, seq)
    wide = block_rows(near_ref, far_ref).astype(jnp.float32)
    inverse = lax.rsqrt(jnp.mean(wide * wide, axis=1, keepdims=True) + 1e-06)
    hidden = (wide * inverse * gain_ref[...]).astype(jnp.bfloat16)
    pre = jnp.dot(hidden, w_ref[...], preferred_element_type=jnp.float32)
    pre_ref[...] = pre.reshape(2, 4, 32, 480)
    query = (pre[:, 0:160] * mult_ref[...]).astype(jnp.bfloat16)
    key = pre[:, 160:320].astype(jnp.bfloat16)
    value = pre[:, 320:480].astype(jnp.bfloat16)
    heads = []
    for head in range(2):
        part = slice(80 * head, 80 * head + 80)
        probs = soft_probs(query[:, part], key[:, part], live).astype(jnp.bfloat16)
        heads.append(jnp.dot(probs, value[:, part], preferred_element_type=jnp.float32))
    att = jnp.concatenate(heads, axis=1).astype(jnp.bfloat16).reshape(2, 4, 32, 160)
    att_near[...] = att[0]
    att_far[...] = att[1]


def attend_back_kernel(
    info_ref, near_ref, far_ref, gain_ref, mult_ref, w_ref, pre_ref, grad_near, grad_far,
    hid_near, hid_far, w_grad, gain_grad, scale_grad, w_acc, gain_acc, scale_acc,
):
    seq = pl.program_id(0)

    @pl.when(seq == 0)
    def _():
        w_acc[...] = jnp.zeros_like(w_acc)
        gain_acc[...] = jnp.zeros_like(gain_acc)
        scale_acc[...] = jnp.zeros_like(scale_acc)

    live = live_pairs(info_ref, seq)
    wide = block_rows(near_ref, far_ref).astype(jnp.float32)
    inverse = lax.rsqrt(jnp.mean(wide * wide, axis=1, keepdims=True) + 1e-06)
    normed = wide * inverse
    hidden = (normed * gain_ref[...]).astype(jnp.bfloat16)
    pre = pre_ref[...].reshape(256, 480)
    mult = mult_ref[...]
    query = (pre[:, 0:160] * mult).astype(jnp.bfloat16)
    key = pre[:, 160:320].astype(jnp.bfloat16)
    value = pre[:, 320:480].astype(jnp.bfloat16)
    grad_att = block_rows(grad_near, grad_far)
    grad_q, grad_k, grad_v = [], [], []
    for head in range(2):
        part = slice(80 * head, 80 * head + 80)
        probs = soft_probs(query[:, part], key[:, part], live)
        grad_probs = mult_trans(grad_att[:, part], value[:, part])
        delta = jnp.sum(probs * grad_probs, axis=1, keepdims=True)
        grad_scores = (probs * (grad_probs - delta)).astype(jnp.bfloat16)
        grad_v.append(trans_mult(probs.astype(jnp.bfloat16), grad_att[:, part]))
        grad_q.append(jnp.dot(grad_scores, key[:, part], preferred_element_type=jnp.float32))
        grad_k.append(trans_mult(grad_scores, query[:, part]))
    grad_query = jnp.concatenate(grad_q, axis=1)
    scale_acc[...] += jnp.sum(grad_query * pre[:, 0:160], axis=0, keepdims=True)
    joined = jnp.concatenate([grad_query * mult] + grad_k + grad_v, axis=1).astype(jnp.bfloat16)
    w_acc[...] += trans_mult(hidden, joined)
    grad_hidden = mult_trans(joined, w_ref[...])
    gain_acc[...] += jnp.sum(grad_hidden * normed, axis=0, keepdims=True)
    low = grad_hidden.astype(jnp.bfloat16).reshape(2, 4, 32, 1280)
    hid_near[...] = low[0]
    hid_far[...] = low[1]

    @pl.when(seq == 3)
    def _():
        w_grad[...] = w_acc[...].astype(jnp.bfloat16)
        gain_grad[...] = gain_acc[...]
        scale_grad[...] = scale_acc[...]


def block_index(z_index, y_index, core):
    return pl.ds(pl.multiple_of((4 * z_index + 2 * y_index + core) * 80, 80), 80)


def source_rows(info_ref, chip, core):
    source = info_ref[1] ^ (CODES[chip] + 2 * core)
    return pl.ds(pl.multiple_of(source * 160, 160), 160)


def feed_kernel(
    info_ref, x_ref, g_ref, att_0, att_1, att_2, att_3, gain_ref,
    near_a, across_a, all_b, far_near_a, far_across_a, far_b,
    out_ref, pack_ref, att_pack, dmid_ref, datt_0, datt_1, datt_2, datt_3, gain_grad,
    weights, sems,
):
    y_index, core_index = info_ref[1] // 4, (info_ref[1] // 2) % 2
    copies = []
    for w in range(3):
        moved = []
        for core, refs in ((core_index, (near_a, across_a, all_b)), (1 - core_index, (far_near_a, far_across_a, far_b))):
            for half in range(2):
                moved.append((refs[0].at[half, w], half, y_index, core))
                moved.append((refs[1].at[half, w], half, 1 - y_index, core))
                for row in range(2):
                    moved.append((refs[2].at[half, w, row], 2 + half, row, core))
        copies.append([
            pltpu.make_async_copy(src, weights.at[w, block_index(*place)], sems.at[w, i])
            for i, (src, *place) in enumerate(moved)
        ])
    for group in copies:
        for copy in group:
            copy.start()
    atts, datts = (att_0, att_1, att_2, att_3), (datt_0, datt_1, datt_2, datt_3)

    for copy in copies[0]:
        copy.wait()
    middle = x_ref[...].astype(jnp.float32)
    for chip in range(4):
        for core in range(2):
            middle += jnp.dot(
                atts[chip][core], weights[0, source_rows(info_ref, chip, core), :],
                preferred_element_type=jnp.float32,
            )
    inverse = lax.rsqrt(jnp.mean(middle * middle, axis=1, keepdims=True) + 1e-06)
    normed = middle * inverse
    gain = gain_ref[...]
    hidden = (normed * gain).astype(jnp.bfloat16)
    pack_ref[1] = hidden
    for copy in copies[1]:
        copy.wait()
    up = jnp.dot(hidden, weights[1], preferred_element_type=jnp.float32)
    sigma = jax.nn.sigmoid(up)
    active = (up * sigma).astype(jnp.bfloat16)
    pack_ref[0] = active
    for copy in copies[2]:
        copy.wait()
    down = jnp.dot(active, weights[2], preferred_element_type=jnp.float32)
    out_ref[...] = (middle + down).astype(jnp.bfloat16)
    cot = g_ref[...]
    grad_act = mult_trans(cot, weights[2])
    grad_up = (grad_act * sigma * (1.0 + up * (1.0 - sigma))).astype(jnp.bfloat16)
    pack_ref[2] = grad_up
    pack_ref[4] = cot
    grad_hidden = mult_trans(grad_up, weights[1])
    gain_grad[...] = jnp.sum(grad_hidden * normed, axis=0, keepdims=True)
    grad_mid = cot.astype(jnp.float32) + norm_back(grad_hidden, normed, inverse, gain)
    dmid_ref[...] = grad_mid
    low = grad_mid.astype(jnp.bfloat16)
    pack_ref[3] = low
    for chip in range(4):
        for core in range(2):
            att_pack[2 * chip + core] = atts[chip][core]
            datts[chip][core] = mult_trans(low, weights[0, source_rows(info_ref, chip, core), :]).astype(jnp.bfloat16)


def grads_kernel(info_ref, pack_ref, att_pack, far_pack, far_att, kept, stage, sems):
    core_index = (info_ref[1] // 2) % 2
    copies = []

    def leave(w):
        for z_index in range(4):
            for row in range(2):
                copy = pltpu.make_async_copy(
                    stage.at[w, block_index(z_index, row, core_index)],
                    kept.at[z_index, w, row],
                    sems.at[w, 2 * z_index + row],
                )
                copy.start()
                copies.append(copy)

    def both(index, part):
        return jnp.concatenate([pack_ref[index, :, part], far_pack[index, :, part]], axis=0)

    everything = slice(0, pack_ref.shape[2])
    for w, left, right in ((2, 0, 4), (1, 1, 2)):
        grads = both(right, everything)
        for chunk in range(5):
            part = slice(256 * chunk, 256 * chunk + 256)
            stage[w, part, :] = trans_mult(both(left, part), grads).astype(jnp.bfloat16)
        leave(w)
    grads = both(3, everything)
    for chip in range(4):
        for core in range(2):
            att = jnp.concatenate([att_pack[2 * chip + core], far_att[2 * chip + 1 - core]], axis=0)
            stage[0, source_rows(info_ref, chip, core), :] = trans_mult(att, grads).astype(jnp.bfloat16)
    leave(0)
    for copy in copies:
        copy.wait()


def whole(shape):
    return pl.BlockSpec(shape, lambda *_: (0,) * len(shape))


def seq_block(*lead, width):
    count = len(lead)
    return pl.BlockSpec((*lead, 32, width), lambda s, info: (*(0,) * count, s, 0))


def planes(
    inputs, cotangent, w_query, w_key, w_value, w_output, w_up, w_down,
    attn_gain, mlp_gain, query_scale, deal, lengths,
):
    f32, bf16 = jnp.float32, jnp.bfloat16
    z, y, c, x = (lax.axis_index(name) for name in ("z", "y", "core", "x"))
    plane = 4 * y + 2 * c + x
    width = 1280
    seqs = jnp.arange(16, dtype=jnp.int32)
    seq_lengths = jnp.sum(jnp.where(deal[None, :] == seqs[:, None], lengths[None, :], 0), axis=1)
    my_lengths = lax.dynamic_slice_in_dim(seq_lengths, 4 * z, 4, 0)
    info = jnp.concatenate([jnp.stack([z, plane]), my_lengths]).astype(jnp.int32)

    vec = jnp.concatenate([attn_gain, mlp_gain, query_scale]).astype(bf16)
    vec_block = jnp.zeros((1, 8, width), bf16).at[0, 0, :120].set(vec)
    in_four = inputs.reshape(4, 4, 8, width)
    sent = [jnp.concatenate([pick(in_four, (z + k) % 4), vec_block]) for k in range(4)]
    got = [sent[0]] + [ring_shift(sent[k], k) for k in (1, 2, 3)]
    x_rows = by_source([item[:4] for item in got], z, 1).reshape(128, width)
    vec_rows = by_source([item[4, 0] for item in got], z, 0)
    vec_rows = jnp.concatenate([vec_rows, jnp.zeros((4, width), bf16)])
    own = jnp.concatenate([x_rows, vec_rows])

    big = jnp.stack([w_output, w_up, w_down]).astype(bf16)
    big = lax.all_gather(big, "z", axis=0)

    qkv = jnp.stack([w_query, w_key, w_value]).astype(bf16)
    own, qkv = lax.optimization_barrier((own, qkv))
    near = jnp.stack([own] + [plane_shift(own, step) for step in (1, 2, 3)])
    qkv = qkv.reshape(3, 40, 8, 160).transpose(2, 1, 0, 3).reshape(8, 40, 480)
    qkv = lax.all_to_all(qkv, ("y", "core", "x"), split_axis=0, concat_axis=0, tiled=True)
    qkv = qkv.reshape(320, 480)

    big, near, qkv = lax.optimization_barrier((big, near, qkv))
    w_qkv = lax.all_gather(qkv, "z", axis=0, tiled=True)
    far = core_swap(near)
    part_a, part_b = big[:2], big[2:]
    near_a = pair(part_a, plane_shift(part_a, 1), x, 2).reshape(2, 3, 80, width)
    part_b = pair(part_b, plane_shift(part_b, 2), y, 2)
    near_a, part_b, far = lax.optimization_barrier((near_a, part_b, far))
    across_a = plane_shift(near_a, 2)
    across_b = plane_shift(part_b, 1)

    vecs = jnp.stack([near[:, 128:132, :120], far[:, 128:132, :120]])
    vecs = vecs.astype(f32).reshape(2, 2, 2, 4, 120)
    vecs = jnp.where(c == 0, vecs, vecs[::-1])
    vecs = jnp.where(y == 0, vecs, vecs[:, ::-1])
    vecs = jnp.where(x == 0, vecs, vecs[:, :, ::-1])
    vecs = vecs.reshape(2, 2, 2, 4, 3, 40).transpose(4, 3, 1, 0, 2, 5).reshape(3, width)
    gain_one, gain_two = vecs[0:1], vecs[1:2]
    my_scale = lax.dynamic_slice_in_dim(vecs[2:3], 160 * plane, 160, 1)
    query_mult = LOG2E / math.sqrt(HD) * jax.nn.softplus(my_scale)

    limit = pltpu.CompilerParams(vmem_limit_bytes=50 * 1024 * 1024)
    pre, att_near, att_far = pl.pallas_call(
        attend_kernel,
        grid_spec=pltpu.PrefetchScalarGridSpec(
            num_scalar_prefetch=1,
            grid=(4,),
            in_specs=[
                seq_block(4, width=width), seq_block(4, width=width),
                whole((1, width)), whole((1, 160)), whole((width, 480)),
            ],
            out_specs=[seq_block(2, 4, width=480), seq_block(4, width=160), seq_block(4, width=160)],
        ),
        out_shape=[
            jax.ShapeDtypeStruct((2, 4, 128, 480), f32),
            jax.ShapeDtypeStruct((4, 128, 160), bf16),
            jax.ShapeDtypeStruct((4, 128, 160), bf16),
        ],
        compiler_params=limit,
        cost_estimate=pl.CostEstimate(flops=9_000_000_000, bytes_accessed=8_000_000, transcendentals=600_000),
        name="attend",
    )(info, near, far, gain_one, query_mult, w_qkv)

    att_near, att_far, near_a = lax.optimization_barrier((att_near, att_far, near_a))
    far_near_a = core_swap(near_a)
    att_pair = jnp.stack([att_near, core_swap(att_far)], axis=1)
    att_pair, cotangent = lax.optimization_barrier((att_pair, cotangent))
    cot_rows = lax.all_to_all(cotangent.reshape(4, 4, 8, width), "z", split_axis=0, concat_axis=0, tiled=True)
    cot_rows = cot_rows.transpose(1, 0, 2, 3).reshape(128, width)
    atts = [att_pair[0]] + [plane_shift(att_pair[step], step) for step in (1, 2, 3)]
    *atts, far_near_a, across_a, across_b, cot_rows = lax.optimization_barrier(
        (*atts, far_near_a, across_a, across_b, cot_rows)
    )
    far_across_a = core_swap(across_a)
    all_b = pair(part_b, across_b, x, 3).reshape(2, 3, 2, 80, width)
    far_b = core_swap(all_b)

    low_rows = jax.ShapeDtypeStruct((128, width), bf16)
    datt_shape = jax.ShapeDtypeStruct((2, 128, 160), bf16)
    smem = pl.BlockSpec(memory_space=pltpu.SMEM)
    vmem = pl.BlockSpec(memory_space=pltpu.VMEM)
    hbm = pl.BlockSpec(memory_space=pl.ANY)
    out_rows, pack, att_pack, grad_mid, *datts, gain_two_grad = pl.pallas_call(
        feed_kernel,
        in_specs=[smem] + [vmem] * 7 + [hbm] * 6,
        out_specs=[vmem] * 9,
        out_shape=[
            low_rows,
            jax.ShapeDtypeStruct((5, 128, width), bf16),
            jax.ShapeDtypeStruct((8, 128, 160), bf16),
            jax.ShapeDtypeStruct((128, width), f32),
        ]
        + [datt_shape] * 4
        + [jax.ShapeDtypeStruct((1, width), f32)],
        scratch_shapes=[pltpu.VMEM((3, width, width), bf16), pltpu.SemaphoreType.DMA((3, 16))],
        compiler_params=limit,
        cost_estimate=pl.CostEstimate(flops=12_000_000_000, bytes_accessed=13_000_000, transcendentals=200_000),
        name="feed",
    )(info, x_rows, cot_rows, *atts, gain_two, near_a, across_a, all_b, far_near_a, far_across_a, far_b)

    def home(rows):
        rows = rows.reshape(4, 4, 8, width).transpose(1, 0, 2, 3)
        return lax.all_to_all(rows, "z", split_axis=0, concat_axis=0, tiled=True).reshape(16, 8, width)

    back = [datts[0]] + [plane_shift(datts[step], step) for step in (1, 2, 3)]
    outputs = home(out_rows)
    grad_att_near = jnp.stack([item[0] for item in back])
    grad_att_far = core_swap(jnp.stack([item[1] for item in back]))

    kept = pl.pallas_call(
        grads_kernel,
        in_specs=[smem] + [vmem] * 4,
        out_specs=hbm,
        out_shape=jax.ShapeDtypeStruct((4, 3, 2, 80, width), bf16),
        scratch_shapes=[pltpu.VMEM((3, width, width), bf16), pltpu.SemaphoreType.DMA((3, 8))],
        compiler_params=limit,
        cost_estimate=pl.CostEstimate(flops=6_000_000_000, bytes_accessed=8_000_000, transcendentals=0),
        name="grads",
    )(info, pack, att_pack, core_swap(pack), core_swap(att_pack))

    def added(left, right):
        return (left.astype(f32) + right.astype(f32)).astype(bf16)

    def halves(array, index, axis):
        first, second = (lax.index_in_dim(array, i, axis, keepdims=False) for i in (0, 1))
        return jnp.where(index == 0, first, second), jnp.where(index == 0, second, first)

    kept, grad_att_near, grad_att_far, outputs = lax.optimization_barrier(
        (kept, grad_att_near, grad_att_far, outputs)
    )
    kept = kept.reshape(4, 3, 2, 2, 40, width)
    kept_a, away_a = halves(kept[:2], x, 3)
    kept_b, away_b = halves(kept[2:], y, 2)
    kept_a = added(kept_a, plane_shift(away_a, 1))
    kept_b = added(kept_b, plane_shift(away_b, 2))
    hid_near, hid_far, qkv_grad, gain_one_grad, scale_grad = pl.pallas_call(
        attend_back_kernel,
        grid_spec=pltpu.PrefetchScalarGridSpec(
            num_scalar_prefetch=1,
            grid=(4,),
            in_specs=[
                seq_block(4, width=width), seq_block(4, width=width),
                whole((1, width)), whole((1, 160)), whole((width, 480)),
                seq_block(2, 4, width=480), seq_block(4, width=160), seq_block(4, width=160),
            ],
            out_specs=[
                seq_block(4, width=width), seq_block(4, width=width),
                whole((width, 480)), whole((1, width)), whole((1, 160)),
            ],
            scratch_shapes=[
                pltpu.VMEM((width, 480), f32), pltpu.VMEM((1, width), f32), pltpu.VMEM((1, 160), f32),
            ],
        ),
        out_shape=[
            jax.ShapeDtypeStruct((4, 128, width), bf16),
            jax.ShapeDtypeStruct((4, 128, width), bf16),
            jax.ShapeDtypeStruct((width, 480), bf16),
            jax.ShapeDtypeStruct((1, width), f32),
            jax.ShapeDtypeStruct((1, 160), f32),
        ],
        compiler_params=limit,
        cost_estimate=pl.CostEstimate(flops=15_000_000_000, bytes_accessed=12_000_000, transcendentals=600_000),
        name="attend_back",
    )(info, near, far, gain_one, query_mult, w_qkv, pre, grad_att_near, grad_att_far)

    scale_line = lax.dynamic_update_slice(jnp.zeros((1, width), f32), scale_grad, (0, 160 * plane))
    lines = jnp.concatenate([gain_one_grad, gain_two_grad, scale_line])
    lines = lines.reshape(3, 4, 8, 40).transpose(1, 2, 0, 3).reshape(4, 2, 480).astype(bf16)
    lines = jnp.pad(lines, ((0, 0), (0, 6), (0, 0)))
    send = jnp.concatenate([qkv_grad.reshape(4, 320, 480), lines], axis=1)
    one = ring_shift(pick(send, (z + 1) % 4), 1)
    hid = added(hid_near, core_swap(hid_far))
    kept_a, kept_b, hid_sum, one, later = lax.optimization_barrier((kept_a, kept_b, hid, one, send))
    three = ring_shift(pick(later, (z + 3) % 4), 3)
    two = ring_shift(pick(later, (z + 2) % 4), 2)
    kept_a, away_a = halves(kept_a, y, 2)
    kept_b, away_b = halves(kept_b, x, 2)
    kept_a = added(kept_a, plane_shift(away_a, 2))
    kept_b = added(kept_b, plane_shift(away_b, 1))
    kept = jnp.concatenate([kept_a, kept_b])
    hid, kept = lax.optimization_barrier((hid, kept))
    grad_hid = hid[0].astype(f32)
    moved = [plane_shift(hid[step], step) for step in (1, 2, 3)]
    *moved, three, two = lax.optimization_barrier((*moved, three, two))
    sums = sum((item.astype(f32) for item in (one, two, three)), pick(send, z).astype(f32)).astype(bf16)
    lines = jnp.pad(sums[320:322].reshape(8, 1, 120), ((0, 0), (0, 7), (0, 360)))
    sums = jnp.concatenate([sums[:320].reshape(8, 40, 480), lines], axis=1)
    for item in moved:
        grad_hid += item.astype(f32)
    wide = x_rows.astype(f32)
    inverse = lax.rsqrt(jnp.mean(wide * wide, axis=1, keepdims=True) + 1e-06)
    grad_in = (grad_mid + norm_back(grad_hid, wide * inverse, inverse, gain_one)).astype(bf16)

    sums = lax.all_to_all(sums, ("y", "core", "x"), split_axis=0, concat_axis=0, tiled=True)
    big_sums = lax.psum_scatter(kept, "z", scatter_dimension=0, tiled=True)[0].astype(f32)
    qkv_sums = sums[:, :40].reshape(8, 40, 3, 160).transpose(2, 1, 0, 3).reshape(3, 40, width).astype(f32)
    line_sums = jnp.sum(sums[:, 40, :120].astype(f32), axis=0).reshape(3, 40)
    scale_low = query_scale.astype(bf16).astype(f32)
    scale_sum = LOG2E / math.sqrt(HD) * jax.nn.sigmoid(scale_low) * line_sums[2]

    rows = grad_in.reshape(4, 4, 8, width).transpose(1, 0, 2, 3)
    grad_home = [pick(rows, z)] + [ring_shift(pick(rows, (z + k) % 4), k) for k in (1, 2, 3)]
    grad_home = by_source(grad_home, z, 0).reshape(16, 8, width)

    return (
        outputs, grad_home, qkv_sums[0], qkv_sums[1], qkv_sums[2],
        big_sums[0], big_sums[1], big_sums[2], line_sums[0], line_sums[1], scale_sum,
    )


def solution(mesh):
    names = ("dp", "ctx")
    body = per_device
    if dict(mesh.shape) == {"dp": 16, "ctx": 2}:
        mesh = Mesh(mesh.devices.reshape(4, 2, 2, 2), ("z", "y", "core", "x"))
        names = mesh.axis_names
        body = planes
    seq, mat, line = P(None, names, None), P(names, None), P(names)
    return jax.shard_map(
        body,
        mesh=mesh,
        in_specs=(seq,) * 2 + (mat,) * 6 + (line,) * 3 + (P(), P()),
        out_specs=(seq,) * 2 + (mat,) * 6 + (line,) * 3,
        check_vma=False,
    )
```

```python
import math

import jax
import jax.numpy as jnp
from jax import lax
from jax.experimental import pallas as pl
from jax.experimental.pallas import tpu as pltpu
from jax.sharding import Mesh, PartitionSpec as P

H = 16
HD = 80


def mult_trans(left, right):
    return lax.dot_general(
        left, right, (((1,), (1,)), ((), ())), preferred_element_type=jnp.float32
    )


def trans_mult(left, right):
    return lax.dot_general(
        left, right, (((0,), (0,)), ((), ())), preferred_element_type=jnp.float32
    )


def position_of(index, local_rows, piece_rows, groups):
    column = index // local_rows
    within = index % local_rows
    return (within // piece_rows * groups + column) * piece_rows + within % piece_rows


def norm_back(grad_hidden, normed, inverse, gain_value):
    grad_normed = grad_hidden * gain_value
    return inverse * (grad_normed - normed * jnp.mean(grad_normed * normed, axis=1, keepdims=True))


def per_device(
    inputs,
    cotangent,
    w_query,
    w_key,
    w_value,
    w_output,
    w_up,
    w_down,
    attn_gain,
    mlp_gain,
    query_scale,
    deal,
    lengths,
):
    groups = lax.axis_size("ctx")
    group_index = lax.axis_index("dp")
    ctx_index = lax.axis_index("ctx")
    head_count = H
    head_dim = HD
    piece_rows = inputs.shape[1]
    seq_numbers = jnp.arange(inputs.shape[0], dtype=jnp.int32)
    seq_lengths = jnp.sum(
        jnp.where(deal[None, :] == seq_numbers[:, None], lengths[None, :], 0), axis=1
    )
    local_in, local_cot = (
        lax.all_to_all(inputs, "dp", split_axis=0, concat_axis=1, tiled=True),
        lax.all_to_all(cotangent, "dp", split_axis=0, concat_axis=1, tiled=True),
    )
    seq_count, local_rows, model_width = local_in.shape
    padded = local_rows * groups
    token_count = seq_count * local_rows
    my_lengths = lax.dynamic_slice_in_dim(seq_lengths, group_index * seq_count, seq_count, 0)
    query_pos = position_of(
        ctx_index * local_rows + jnp.arange(local_rows, dtype=jnp.int32),
        local_rows,
        piece_rows,
        groups,
    )
    flat_in = local_in.reshape(token_count, model_width).astype(jnp.float32)
    flat_cot = local_cot.reshape(token_count, model_width)
    lowered = (
        w_query.astype(jnp.bfloat16),
        w_key.astype(jnp.bfloat16),
        w_value.astype(jnp.bfloat16),
        w_output.astype(jnp.bfloat16),
        w_up.astype(jnp.bfloat16),
        w_down.astype(jnp.bfloat16),
        attn_gain.astype(jnp.bfloat16),
        mlp_gain.astype(jnp.bfloat16),
        query_scale.astype(jnp.bfloat16),
    )
    gathered = (
        lax.all_gather(lowered[0], ("dp", "ctx"), axis=0, tiled=True),
        lax.all_gather(lowered[1], ("dp", "ctx"), axis=0, tiled=True),
        lax.all_gather(lowered[2], ("dp", "ctx"), axis=0, tiled=True),
        lax.all_gather(lowered[3], ("dp", "ctx"), axis=0, tiled=True),
        lax.all_gather(lowered[4], ("dp", "ctx"), axis=0, tiled=True),
        lax.all_gather(lowered[5], ("dp", "ctx"), axis=0, tiled=True),
        lax.all_gather(lowered[6], ("dp", "ctx"), axis=0, tiled=True),
        lax.all_gather(lowered[7], ("dp", "ctx"), axis=0, tiled=True),
        lax.all_gather(lowered[8], ("dp", "ctx"), axis=0, tiled=True),
    )
    (
        query_full,
        key_full,
        value_full,
        output_full,
        up_full,
        down_full,
        gain_one,
        gain_two,
        scale_raw,
    ) = gathered
    inv_one = lax.rsqrt(jnp.mean(flat_in * flat_in, axis=1, keepdims=True) + 1e-06)
    normed_one = flat_in * inv_one
    hidden_one = (normed_one * gain_one.astype(jnp.float32)).astype(jnp.bfloat16)
    scale_param = scale_raw.astype(jnp.float32)
    query_mult = 1.442695041 / math.sqrt(head_dim) * jax.nn.softplus(scale_param)
    query_pre = jnp.dot(hidden_one, query_full, preferred_element_type=jnp.float32)
    queries = (query_pre * query_mult).astype(jnp.bfloat16)
    keys_local = jnp.dot(hidden_one, key_full, preferred_element_type=jnp.float32).astype(
        jnp.bfloat16
    )
    values_local = jnp.dot(hidden_one, value_full, preferred_element_type=jnp.float32).astype(
        jnp.bfloat16
    )
    four_shape = (seq_count, local_rows, head_count, head_dim)
    query_four = queries.reshape(four_shape)
    keys_three = keys_local.reshape(seq_count, local_rows, model_width)
    values_three = values_local.reshape(seq_count, local_rows, model_width)

    def live_between(row_pos, key_pos):
        allowed = (key_pos[None, None, :] <= row_pos[None, :, None]) & (
            key_pos[None, None, :] < my_lengths[:, None, None]
        )
        return allowed[:, :, None, :]

    def live_mask(key_pos):
        return live_between(query_pos, key_pos)

    def attend_block(state_now, key_block, value_block, first_row):
        run_max, run_sum, run_acc = state_now
        block_len = key_block.shape[1]
        key_pos = position_of(
            first_row + jnp.arange(block_len, dtype=jnp.int32), local_rows, piece_rows, groups
        )
        key_four = key_block.reshape(seq_count, block_len, head_count, head_dim)
        value_four = value_block.reshape(seq_count, block_len, head_count, head_dim)
        scores = jnp.einsum(
            "srhd,skhd->srhk", query_four, key_four, preferred_element_type=jnp.float32
        )
        allowed = live_mask(key_pos)
        masked = jnp.where(allowed, scores, -1e30)
        new_max = jnp.maximum(run_max, jnp.max(masked, axis=3))
        weights_now = jnp.exp(jnp.where(allowed, masked - new_max[..., None], -1e30))
        factor = jnp.exp(run_max - new_max)
        new_sum = run_sum * factor + jnp.sum(weights_now, axis=3)
        added = jnp.einsum(
            "srhk,skhd->srhd",
            weights_now.astype(jnp.bfloat16),
            value_four,
            preferred_element_type=jnp.float32,
        )
        return (new_max, new_sum, run_acc * factor[..., None] + added)

    start_state = (
        jnp.full((seq_count, local_rows, head_count), -1e30, jnp.float32),
        jnp.zeros((seq_count, local_rows, head_count), jnp.float32),
        jnp.zeros(four_shape, jnp.float32),
    )
    key_piece = lax.all_gather(keys_three, "ctx", axis=1, tiled=True)
    value_piece = lax.all_gather(values_three, "ctx", axis=1, tiled=True)
    piece_len = key_piece.shape[1]
    fold_block_len = 512 if piece_len % 512 == 0 else piece_len

    def one_block(state_now, block_index):
        offset = block_index * fold_block_len
        key_block = lax.dynamic_slice_in_dim(key_piece, offset, fold_block_len, 1)
        value_block = lax.dynamic_slice_in_dim(value_piece, offset, fold_block_len, 1)
        return (attend_block(state_now, key_block, value_block, offset), None)

    result_state, unused = lax.scan(
        one_block, start_state, jnp.arange(piece_len // fold_block_len, dtype=jnp.int32)
    )
    run_max, run_sum, run_acc = result_state
    log_total = run_max + jnp.log(run_sum)
    attn_exact = run_acc / run_sum[..., None]
    attended = attn_exact.reshape(token_count, model_width).astype(jnp.bfloat16)
    middle = flat_in + jnp.dot(attended, output_full, preferred_element_type=jnp.float32)
    inv_two = lax.rsqrt(jnp.mean(middle * middle, axis=1, keepdims=True) + 1e-06)
    normed_two = middle * inv_two
    hidden_two = (normed_two * gain_two.astype(jnp.float32)).astype(jnp.bfloat16)
    up_pre = jnp.dot(hidden_two, up_full, preferred_element_type=jnp.float32)
    active = jax.nn.silu(up_pre).astype(jnp.bfloat16)
    result = (middle + jnp.dot(active, down_full, preferred_element_type=jnp.float32)).astype(
        jnp.bfloat16
    )
    back_weights = (
        lax.all_gather(lowered[0], ("dp", "ctx"), axis=0, tiled=True),
        lax.all_gather(lowered[1], ("dp", "ctx"), axis=0, tiled=True),
        lax.all_gather(lowered[2], ("dp", "ctx"), axis=0, tiled=True),
        lax.all_gather(lowered[3], ("dp", "ctx"), axis=0, tiled=True),
        lax.all_gather(lowered[4], ("dp", "ctx"), axis=0, tiled=True),
        lax.all_gather(lowered[5], ("dp", "ctx"), axis=0, tiled=True),
        lax.all_gather(lowered[6], ("dp", "ctx"), axis=0, tiled=True),
        lax.all_gather(lowered[7], ("dp", "ctx"), axis=0, tiled=True),
        lax.all_gather(lowered[8], ("dp", "ctx"), axis=0, tiled=True),
    )
    (
        query_back,
        key_back,
        value_back,
        output_back,
        up_back,
        down_back,
        gain_one_back,
        gain_two_back,
        scale_back,
    ) = back_weights
    cot_wide = flat_cot.astype(jnp.float32)
    grad_down = trans_mult(active, flat_cot)
    grad_active = mult_trans(flat_cot, down_back)
    sigma_up = jax.nn.sigmoid(up_pre)
    grad_up_pre = (grad_active * sigma_up * (1.0 + up_pre * (1.0 - sigma_up))).astype(jnp.bfloat16)
    grad_up = trans_mult(hidden_two, grad_up_pre)
    grad_hidden_two = mult_trans(grad_up_pre, up_back)
    grad_gain_two = jnp.sum(grad_hidden_two * normed_two, axis=0)
    grad_middle = cot_wide + norm_back(
        grad_hidden_two, normed_two, inv_two, gain_two_back.astype(jnp.float32)
    )
    grad_middle_low = grad_middle.astype(jnp.bfloat16)
    grad_output = trans_mult(attended, grad_middle_low)
    grad_attended = mult_trans(grad_middle_low, output_back).astype(jnp.bfloat16)
    grad_att_four = grad_attended.reshape(four_shape)
    delta_rows = jnp.sum(grad_att_four.astype(jnp.float32) * attn_exact, axis=3)
    key_all, value_all = (
        lax.all_gather(keys_three, "ctx", axis=1, tiled=True),
        lax.all_gather(values_three, "ctx", axis=1, tiled=True),
    )
    block_len = min(512, padded)

    def back_block(block_index, state_now):
        grad_query, grad_key_all, grad_value_all = state_now
        offset = block_index * block_len
        key_block = lax.dynamic_slice_in_dim(key_all, offset, block_len, 1).reshape(
            seq_count, block_len, head_count, head_dim
        )
        value_block = lax.dynamic_slice_in_dim(value_all, offset, block_len, 1).reshape(
            seq_count, block_len, head_count, head_dim
        )
        key_pos = position_of(
            offset + jnp.arange(block_len, dtype=jnp.int32), local_rows, piece_rows, groups
        )
        scores = jnp.einsum(
            "srhd,skhd->srhk", query_four, key_block, preferred_element_type=jnp.float32
        )
        probs = jnp.exp(jnp.where(live_mask(key_pos), scores - log_total[..., None], -1e30))
        grad_value_block = jnp.einsum(
            "srhk,srhd->skhd",
            probs.astype(jnp.bfloat16),
            grad_att_four,
            preferred_element_type=jnp.float32,
        )
        grad_probs = jnp.einsum(
            "srhd,skhd->srhk", grad_att_four, value_block, preferred_element_type=jnp.float32
        )
        grad_scores = (probs * (grad_probs - delta_rows[..., None])).astype(jnp.bfloat16)
        grad_query = grad_query + jnp.einsum(
            "srhk,skhd->srhd", grad_scores, key_block, preferred_element_type=jnp.float32
        )
        grad_key_block = jnp.einsum(
            "srhk,srhd->skhd", grad_scores, query_four, preferred_element_type=jnp.float32
        )
        grad_key_all = lax.dynamic_update_slice_in_dim(
            grad_key_all, grad_key_block.reshape(seq_count, block_len, model_width), offset, 1
        )
        grad_value_all = lax.dynamic_update_slice_in_dim(
            grad_value_all, grad_value_block.reshape(seq_count, block_len, model_width), offset, 1
        )
        return (grad_query, grad_key_all, grad_value_all)

    zero_all = jnp.zeros((seq_count, padded, model_width), jnp.float32)
    grad_query, grad_key_all, grad_value_all = lax.fori_loop(
        0, padded // block_len, back_block, (jnp.zeros(four_shape, jnp.float32), zero_all, zero_all)
    )
    grad_key_mine, grad_value_mine = (
        lax.psum_scatter(
            grad_key_all.astype(jnp.bfloat16), "ctx", scatter_dimension=1, tiled=True
        ).astype(jnp.float32),
        lax.psum_scatter(
            grad_value_all.astype(jnp.bfloat16), "ctx", scatter_dimension=1, tiled=True
        ).astype(jnp.float32),
    )
    grad_query_flat = grad_query.reshape(token_count, model_width)
    grad_query_pre = (grad_query_flat * query_mult).astype(jnp.bfloat16)
    grad_scale = (
        1.442695041
        / math.sqrt(head_dim)
        * jax.nn.sigmoid(scale_back.astype(jnp.float32))
        * jnp.sum(grad_query_flat * query_pre, axis=0)
    )
    grad_key_low = grad_key_mine.reshape(token_count, model_width).astype(jnp.bfloat16)
    grad_value_low = grad_value_mine.reshape(token_count, model_width).astype(jnp.bfloat16)
    grad_wq = trans_mult(hidden_one, grad_query_pre)
    grad_wk = trans_mult(hidden_one, grad_key_low)
    grad_wv = trans_mult(hidden_one, grad_value_low)
    grad_hidden_one = (
        mult_trans(grad_query_pre, query_back)
        + mult_trans(grad_key_low, key_back)
        + mult_trans(grad_value_low, value_back)
    )
    grad_gain_one = jnp.sum(grad_hidden_one * normed_one, axis=0)
    grad_in = grad_middle + norm_back(
        grad_hidden_one, normed_one, inv_one, gain_one_back.astype(jnp.float32)
    )
    matrix_stack = jnp.stack([grad_wq, grad_wk, grad_wv, grad_output, grad_up, grad_down], axis=0)
    vector_stack = jnp.stack([grad_gain_one, grad_gain_two, grad_scale], axis=0)
    matrix_sums, vector_sums = (
        lax.psum_scatter(matrix_stack, ("dp", "ctx"), scatter_dimension=1, tiled=True),
        lax.psum_scatter(vector_stack, ("dp", "ctx"), scatter_dimension=1, tiled=True),
    )
    out_local = result.reshape(seq_count, local_rows, model_width)
    grad_local = grad_in.astype(jnp.bfloat16).reshape(seq_count, local_rows, model_width)
    back_out, back_grad = (
        lax.all_to_all(out_local, "dp", split_axis=1, concat_axis=0, tiled=True),
        lax.all_to_all(grad_local, "dp", split_axis=1, concat_axis=0, tiled=True),
    )
    return (
        back_out,
        back_grad,
        matrix_sums[0],
        matrix_sums[1],
        matrix_sums[2],
        matrix_sums[3],
        matrix_sums[4],
        matrix_sums[5],
        vector_sums[0],
        vector_sums[1],
        vector_sums[2],
    )


LOG2E = 1.442695041
CODES = (0, 1, 4, 5)


def plane_shift(value, step):
    if step == 1:
        return lax.ppermute(value, "x", [(0, 1), (1, 0)])
    if step == 2:
        return lax.ppermute(value, "y", [(0, 1), (1, 0)])
    return lax.ppermute(value, ("y", "x"), [(0, 3), (1, 2), (2, 1), (3, 0)])


def core_swap(value):
    return lax.ppermute(value, "core", [(0, 1), (1, 0)])


def ring_shift(value, step):
    return lax.ppermute(value, "z", [(i, (i + step) % 4) for i in range(4)])


def pick(array, index):
    return lax.dynamic_index_in_dim(array, index, 0, keepdims=False)


def by_source(pieces, z_index, axis):
    pieces = [jnp.expand_dims(item, axis) for item in pieces]
    shape = [1] * pieces[0].ndim
    shape[axis] = 4
    hop = ((z_index - jnp.arange(4, dtype=jnp.int32)) % 4).reshape(shape)
    made = pieces[0]
    for k in (1, 2, 3):
        made = jnp.where(hop == k, pieces[k], made)
    return made


def pair(mine, other, index, axis):
    shape = [1] * (mine.ndim + 1)
    shape[axis] = 2
    slot = jnp.arange(2, dtype=jnp.int32).reshape(shape)
    return jnp.where(slot == index, jnp.expand_dims(mine, axis), jnp.expand_dims(other, axis))


def row_positions(shape, dim, plane_index):
    row = lax.broadcasted_iota(jnp.int32, shape, dim)
    chip = (row // 32) % 4
    code = (chip % 2) + 4 * (chip // 2) + 2 * (row // 128)
    return 64 * ((row % 32) // 8) + 8 * (plane_index ^ code) + row % 8


def live_pairs(info_ref, seq):
    shape = (256, 256)
    query_pos = row_positions(shape, 0, info_ref[1])
    key_pos = row_positions(shape, 1, info_ref[1])
    return (key_pos <= query_pos) & (key_pos < info_ref[2 + seq])


def block_rows(near_ref, far_ref):
    return jnp.concatenate([near_ref[...], far_ref[...]], axis=0).reshape(256, near_ref.shape[2])


def soft_probs(query, key, live):
    scores = mult_trans(query, key)
    scores = jnp.where(live, scores, -1e30)
    top = jnp.max(scores, axis=1, keepdims=True)
    weights = jnp.where(live, jnp.exp(scores - top), 0.0)
    return weights / jnp.sum(weights, axis=1, keepdims=True)


def set_weights(info_ref, parts, w_ref):
    @pl.when(pl.program_id(0) == 0)
    def _():
        for hop, part in enumerate(parts):
            w_ref[pl.ds(pl.multiple_of(((info_ref[0] - hop) & 3) * 320, 320), 320), :] = part[...]


def attend_kernel(
    info_ref, near_ref, far_ref, gain_ref, mult_ref, w_0, w_1, w_2, w_3, pre_ref, att_near, att_far, w_ref
):
    seq = pl.program_id(0)
    set_weights(info_ref, (w_0, w_1, w_2, w_3), w_ref)
    live = live_pairs(info_ref, seq)
    wide = block_rows(near_ref, far_ref).astype(jnp.float32)
    inverse = lax.rsqrt(jnp.mean(wide * wide, axis=1, keepdims=True) + 1e-06)
    hidden = (wide * inverse * gain_ref[...]).astype(jnp.bfloat16)
    pre = jnp.dot(hidden, w_ref[...], preferred_element_type=jnp.float32)
    pre_ref[...] = pre.reshape(2, 4, 32, 480)
    query = (pre[:, 0:160] * mult_ref[...]).astype(jnp.bfloat16)
    key = pre[:, 160:320].astype(jnp.bfloat16)
    value = pre[:, 320:480].astype(jnp.bfloat16)
    heads = []
    for head in range(2):
        part = slice(80 * head, 80 * head + 80)
        probs = soft_probs(query[:, part], key[:, part], live).astype(jnp.bfloat16)
        heads.append(jnp.dot(probs, value[:, part], preferred_element_type=jnp.float32))
    att = jnp.concatenate(heads, axis=1).astype(jnp.bfloat16).reshape(2, 4, 32, 160)
    att_near[...] = att[0]
    att_far[...] = att[1]


def attend_back_kernel(
    info_ref, near_ref, far_ref, gain_ref, mult_ref, w_0, w_1, w_2, w_3, pre_ref, grad_near, grad_far, gain_two_ref,
    hid_near, hid_far, send_0, send_1, send_2, send_3, w_ref, w_acc, gain_acc, scale_acc, lines,
):
    seq = pl.program_id(0)
    set_weights(info_ref, (w_0, w_1, w_2, w_3), w_ref)

    @pl.when(seq == 0)
    def _():
        w_acc[...] = jnp.zeros_like(w_acc)
        gain_acc[...] = jnp.zeros_like(gain_acc)
        scale_acc[...] = jnp.zeros_like(scale_acc)

    live = live_pairs(info_ref, seq)
    wide = block_rows(near_ref, far_ref).astype(jnp.float32)
    inverse = lax.rsqrt(jnp.mean(wide * wide, axis=1, keepdims=True) + 1e-06)
    normed = wide * inverse
    hidden = (normed * gain_ref[...]).astype(jnp.bfloat16)
    pre = pre_ref[...].reshape(256, 480)
    mult = mult_ref[...]
    query = (pre[:, 0:160] * mult).astype(jnp.bfloat16)
    key = pre[:, 160:320].astype(jnp.bfloat16)
    value = pre[:, 320:480].astype(jnp.bfloat16)
    grad_att = block_rows(grad_near, grad_far)
    grad_q, grad_k, grad_v = [], [], []
    for head in range(2):
        part = slice(80 * head, 80 * head + 80)
        probs = soft_probs(query[:, part], key[:, part], live)
        grad_probs = mult_trans(grad_att[:, part], value[:, part])
        delta = jnp.sum(probs * grad_probs, axis=1, keepdims=True)
        grad_scores = (probs * (grad_probs - delta)).astype(jnp.bfloat16)
        grad_v.append(trans_mult(probs.astype(jnp.bfloat16), grad_att[:, part]))
        grad_q.append(jnp.dot(grad_scores, key[:, part], preferred_element_type=jnp.float32))
        grad_k.append(trans_mult(grad_scores, query[:, part]))
    grad_query = jnp.concatenate(grad_q, axis=1)
    scale_acc[...] += jnp.sum(grad_query * pre[:, 0:160], axis=0, keepdims=True)
    joined = jnp.concatenate([grad_query * mult] + grad_k + grad_v, axis=1).astype(jnp.bfloat16)
    w_acc[...] += trans_mult(hidden, joined)
    grad_hidden = mult_trans(joined, w_ref[...])
    gain_acc[...] += jnp.sum(grad_hidden * normed, axis=0, keepdims=True)
    low = grad_hidden.astype(jnp.bfloat16).reshape(2, 4, 32, 1280)
    hid_near[...] = low[0]
    hid_far[...] = low[1]

    @pl.when(seq == 3)
    def _():
        lines[...] = jnp.zeros_like(lines)
        for which, source in enumerate((gain_acc, gain_two_ref)):
            for owner in range(32):
                lane = 120 * (owner % 4) + 40 * which
                lines[owner // 4, :, lane : lane + 40] = source[:, 40 * owner : 40 * owner + 40]
        for part in range(4):
            lane = 120 * part + 80
            lines[info_ref[1], :, lane : lane + 40] = scale_acc[:, 40 * part : 40 * part + 40]
        blank = jnp.zeros((14, 480), jnp.float32)
        for hop, send in enumerate((send_0, send_1, send_2, send_3)):
            target = (info_ref[0] + hop) & 3
            rows = w_acc[pl.ds(pl.multiple_of(target * 320, 320), 320), :]
            block = jnp.concatenate([rows, lines[2 * target], lines[2 * target + 1], blank], axis=0)
            send[...] = block.astype(jnp.bfloat16)


def block_index(z_index, y_index, core):
    return pl.ds(pl.multiple_of((4 * z_index + 2 * y_index + core) * 80, 80), 80)


def source_rows(info_ref, chip, core):
    source = info_ref[1] ^ (CODES[chip] + 2 * core)
    return pl.ds(pl.multiple_of(source * 160, 160), 160)


def feed_kernel(
    info_ref, x_ref, g_ref, atts, gain_ref,
    near_a, across_a, all_b, far_near_a, far_across_a, far_b,
    out_ref, pack_ref, dmid_ref, datt_0, datt_1, datt_2, datt_3, gain_grad,
    weights, sems,
):
    y_index, core_index = info_ref[1] // 4, (info_ref[1] // 2) % 2
    copies = []
    for w in range(3):
        moved = []
        for core, refs in ((core_index, (near_a, across_a, all_b)), (1 - core_index, (far_near_a, far_across_a, far_b))):
            for half in range(2):
                moved.append((refs[0].at[half, w], half, y_index, core))
                moved.append((refs[1].at[half, w], half, 1 - y_index, core))
                for row in range(2):
                    moved.append((refs[2].at[half, w, row], 2 + half, row, core))
        copies.append([
            pltpu.make_async_copy(src, weights.at[w, block_index(*place)], sems.at[w, i])
            for i, (src, *place) in enumerate(moved)
        ])
    for group in copies:
        for copy in group:
            copy.start()
    datts = (datt_0, datt_1, datt_2, datt_3)

    for copy in copies[0]:
        copy.wait()
    middle = x_ref[...].astype(jnp.float32)
    for chip in range(4):
        for core in range(2):
            middle += jnp.dot(
                atts[chip, core], weights[0, source_rows(info_ref, chip, core), :],
                preferred_element_type=jnp.float32,
            )
    inverse = lax.rsqrt(jnp.mean(middle * middle, axis=1, keepdims=True) + 1e-06)
    normed = middle * inverse
    gain = gain_ref[...]
    hidden = (normed * gain).astype(jnp.bfloat16)
    pack_ref[1] = hidden
    for copy in copies[1]:
        copy.wait()
    up = jnp.dot(hidden, weights[1], preferred_element_type=jnp.float32)
    sigma = jax.nn.sigmoid(up)
    active = (up * sigma).astype(jnp.bfloat16)
    pack_ref[0] = active
    for copy in copies[2]:
        copy.wait()
    down = jnp.dot(active, weights[2], preferred_element_type=jnp.float32)
    result = middle + down
    for seq in range(4):
        for plane_z in range(4):
            row = 32 * seq + 8 * plane_z
            out_ref[plane_z, seq] = result[row : row + 8].astype(jnp.bfloat16)
    cot = g_ref[...]
    grad_act = mult_trans(cot, weights[2])
    grad_up = (grad_act * sigma * (1.0 + up * (1.0 - sigma))).astype(jnp.bfloat16)
    pack_ref[2] = grad_up
    grad_hidden = mult_trans(grad_up, weights[1])
    gain_grad[...] = jnp.sum(grad_hidden * normed, axis=0, keepdims=True)
    grad_mid = cot.astype(jnp.float32) + norm_back(grad_hidden, normed, inverse, gain)
    dmid_ref[...] = grad_mid
    low = grad_mid.astype(jnp.bfloat16)
    pack_ref[3] = low
    for chip in range(4):
        for core in range(2):
            datts[chip][core] = mult_trans(low, weights[0, source_rows(info_ref, chip, core), :]).astype(jnp.bfloat16)


def grads_kernel(
    info_ref, pack_ref, far_pack, atts, far_atts, cot_ref, far_cot, half_a, kept_b, away_b, stage, sems
):
    y_index, core_index = info_ref[1] // 4, (info_ref[1] // 2) % 2
    copies = []

    def leave(w):
        for half in range(2):
            targets = [(half, row, half_a.at[half, w, row]) for row in range(2)]
            targets += [(2 + half, y_index, kept_b.at[half, w]), (2 + half, 1 - y_index, away_b.at[half, w])]
            for i, (z_index, row, target) in enumerate(targets):
                copy = pltpu.make_async_copy(
                    stage.at[w, block_index(z_index, row, core_index)], target, sems.at[w, 4 * half + i]
                )
                copy.start()
                copies.append(copy)

    def both(near, far):
        return jnp.concatenate([near, far], axis=0)

    cots = both(cot_ref[...], far_cot[...])
    for w, left, grads in ((2, 0, cots), (1, 1, both(pack_ref[2], far_pack[2]))):
        for chunk in range(5):
            part = slice(256 * chunk, 256 * chunk + 256)
            acts = both(pack_ref[left, :, part], far_pack[left, :, part])
            stage[w, part, :] = trans_mult(acts, grads).astype(jnp.bfloat16)
        leave(w)
    grads = both(pack_ref[3], far_pack[3])
    for chip in range(4):
        for core in range(2):
            att = both(atts[chip, core], far_atts[chip, 1 - core])
            stage[0, source_rows(info_ref, chip, core), :] = trans_mult(att, grads).astype(jnp.bfloat16)
    leave(0)
    for copy in copies:
        copy.wait()


def norm_kernel(info_ref, hid_0, hid_1, hid_2, hid_3, x_ref, dmid_ref, gain_ref, out_0, out_1, out_2, out_3, rows):
    grad = hid_0[...].astype(jnp.float32)
    for item in (hid_1, hid_2, hid_3):
        grad += item[...].astype(jnp.float32)
    wide = x_ref[...].astype(jnp.float32)
    inverse = lax.rsqrt(jnp.mean(wide * wide, axis=1, keepdims=True) + 1e-06)
    grad = dmid_ref[...] + norm_back(grad, wide * inverse, inverse, gain_ref[...])
    for seq in range(4):
        for plane_z in range(4):
            row = 32 * seq + 8 * plane_z
            rows[plane_z, seq] = grad[row : row + 8]
    for hop, out in enumerate((out_0, out_1, out_2, out_3)):
        out[...] = rows[(info_ref[0] + hop) & 3].astype(jnp.bfloat16)


def fold_kernel(part_0, part_1, part_2, part_3, out_ref, line):
    total = part_0[...].astype(jnp.float32)
    for item in (part_1, part_2, part_3):
        total += item[...].astype(jnp.float32)
    line[...] = jnp.zeros_like(line)
    for owner in range(8):
        lane = 120 * (owner % 4)
        line[0:1, 0:120] = total[320 + owner // 4 : 321 + owner // 4, lane : lane + 120]
        block = jnp.concatenate([total[40 * owner : 40 * owner + 40], line[...]], axis=0)
        out_ref[owner] = block.astype(jnp.bfloat16)


def spread_kernel(in_ref, *outs):
    for which, out in enumerate(outs):
        for owner in range(8):
            part = in_ref[owner, 0:40, 160 * which : 160 * which + 160]
            out[:, 160 * owner : 160 * owner + 160] = part.astype(jnp.float32)


def widen_kernel(in_ref, *outs):
    for which, out in enumerate(outs):
        out[...] = in_ref[which].astype(jnp.float32)


def whole(shape):
    return pl.BlockSpec(shape, lambda *_: (0,) * len(shape))


def seq_block(*lead, width):
    count = len(lead)
    return pl.BlockSpec((*lead, 32, width), lambda s, info: (*(0,) * count, s, 0))


def planes(
    inputs, cotangent, w_query, w_key, w_value, w_output, w_up, w_down,
    attn_gain, mlp_gain, query_scale, deal, lengths,
):
    f32, bf16 = jnp.float32, jnp.bfloat16
    z, y, c, x = (lax.axis_index(name) for name in ("z", "y", "core", "x"))
    plane = 4 * y + 2 * c + x
    width = 1280
    seqs = jnp.arange(16, dtype=jnp.int32)
    seq_lengths = jnp.sum(jnp.where(deal[None, :] == seqs[:, None], lengths[None, :], 0), axis=1)
    my_lengths = lax.dynamic_slice_in_dim(seq_lengths, 4 * z, 4, 0)
    info = jnp.concatenate([jnp.stack([z, plane]), my_lengths]).astype(jnp.int32)

    vec = jnp.concatenate([attn_gain, mlp_gain, query_scale]).astype(bf16)
    vec_block = jnp.zeros((1, 8, width), bf16).at[0, 0, :120].set(vec)
    in_four = inputs.reshape(4, 4, 8, width)
    sent = [jnp.concatenate([pick(in_four, (z + k) % 4), vec_block]) for k in range(4)]
    got = [sent[0]] + [ring_shift(sent[k], k) for k in (1, 2, 3)]
    x_rows = by_source([item[:4] for item in got], z, 1).reshape(128, width)
    vec_rows = by_source([item[4, 0] for item in got], z, 0)
    vec_rows = jnp.concatenate([vec_rows, jnp.zeros((4, width), bf16)])
    own = jnp.concatenate([x_rows, vec_rows])

    big = jnp.stack([w_output, w_up, w_down]).astype(bf16)
    big = lax.all_gather(big, "z", axis=0)

    qkv = jnp.stack([w_query, w_key, w_value]).astype(bf16)
    own, qkv = lax.optimization_barrier((own, qkv))
    near = [own] + [plane_shift(own, step) for step in (1, 2, 3)]
    qkv = qkv.reshape(3, 40, 8, 160).transpose(2, 1, 0, 3).reshape(8, 40, 480)
    qkv = lax.all_to_all(qkv, ("y", "core", "x"), split_axis=0, concat_axis=0, tiled=True)
    qkv = qkv.reshape(320, 480)

    late = qkv
    *near, qkv = lax.optimization_barrier((*near, qkv))
    near = jnp.stack(near)
    one, three, late = lax.optimization_barrier((ring_shift(qkv, 1), ring_shift(qkv, 3), late))
    w_parts = [qkv, one, ring_shift(late, 2), three]
    big, near = lax.optimization_barrier((big, near))
    far = core_swap(near)
    part_a, part_b = big[:2], big[2:]
    near_a = pair(part_a, plane_shift(part_a, 1), x, 2).reshape(2, 3, 80, width)
    part_b = pair(part_b, plane_shift(part_b, 2), y, 2)
    near_a, part_b, far = lax.optimization_barrier((near_a, part_b, far))
    across_a = plane_shift(near_a, 2)
    across_b = plane_shift(part_b, 1)

    vecs = jnp.stack([near[:, 128:132, :120], far[:, 128:132, :120]])
    vecs = vecs.astype(f32).reshape(2, 2, 2, 4, 120)
    vecs = jnp.where(c == 0, vecs, vecs[::-1])
    vecs = jnp.where(y == 0, vecs, vecs[:, ::-1])
    vecs = jnp.where(x == 0, vecs, vecs[:, :, ::-1])
    vecs = vecs.reshape(2, 2, 2, 4, 3, 40).transpose(4, 3, 1, 0, 2, 5).reshape(3, width)
    gain_one, gain_two = vecs[0:1], vecs[1:2]
    my_scale = lax.dynamic_slice_in_dim(vecs[2:3], 160 * plane, 160, 1)
    query_mult = LOG2E / math.sqrt(HD) * jax.nn.softplus(my_scale)

    limit = pltpu.CompilerParams(vmem_limit_bytes=50 * 1024 * 1024)
    pre, att_near, att_far = pl.pallas_call(
        attend_kernel,
        grid_spec=pltpu.PrefetchScalarGridSpec(
            num_scalar_prefetch=1,
            grid=(4,),
            in_specs=[
                seq_block(4, width=width), seq_block(4, width=width),
                whole((1, width)), whole((1, 160)), *[whole((320, 480))] * 4,
            ],
            out_specs=[seq_block(2, 4, width=480), seq_block(4, width=160), seq_block(4, width=160)],
            scratch_shapes=[pltpu.VMEM((width, 480), bf16)],
        ),
        out_shape=[
            jax.ShapeDtypeStruct((2, 4, 128, 480), f32),
            jax.ShapeDtypeStruct((4, 128, 160), bf16),
            jax.ShapeDtypeStruct((4, 128, 160), bf16),
        ],
        compiler_params=limit,
        cost_estimate=pl.CostEstimate(flops=9_000_000_000, bytes_accessed=8_000_000, transcendentals=600_000),
        name="attend",
    )(info, near, far, gain_one, query_mult, *w_parts)

    att_near, att_far, near_a = lax.optimization_barrier((att_near, att_far, near_a))
    far_near_a = core_swap(near_a)
    att_pair = jnp.stack([att_near, core_swap(att_far)], axis=1)
    att_pair, cotangent = lax.optimization_barrier((att_pair, cotangent))
    cot_rows = lax.all_to_all(cotangent.reshape(4, 4, 8, width), "z", split_axis=0, concat_axis=0, tiled=True)
    cot_rows = cot_rows.transpose(1, 0, 2, 3).reshape(128, width)
    atts = [att_pair[0]] + [plane_shift(att_pair[step], step) for step in (1, 2, 3)]
    atts = jnp.stack(atts)
    far_atts, far_cot = core_swap(atts), core_swap(cot_rows)
    atts, far_near_a, across_a, across_b, cot_rows, far_atts, far_cot = lax.optimization_barrier(
        (atts, far_near_a, across_a, across_b, cot_rows, far_atts, far_cot)
    )
    far_across_a = core_swap(across_a)
    all_b = pair(part_b, across_b, x, 3).reshape(2, 3, 2, 80, width)
    far_b = core_swap(all_b)

    datt_shape = jax.ShapeDtypeStruct((2, 128, 160), bf16)
    smem = pl.BlockSpec(memory_space=pltpu.SMEM)
    vmem = pl.BlockSpec(memory_space=pltpu.VMEM)
    hbm = pl.BlockSpec(memory_space=pl.ANY)
    out_rows, pack, grad_mid, *datts, gain_two_grad = pl.pallas_call(
        feed_kernel,
        in_specs=[smem] + [vmem] * 4 + [hbm] * 6,
        out_specs=[vmem] * 8,
        out_shape=[
            jax.ShapeDtypeStruct((4, 4, 8, width), bf16),
            jax.ShapeDtypeStruct((4, 128, width), bf16),
            jax.ShapeDtypeStruct((128, width), f32),
        ]
        + [datt_shape] * 4
        + [jax.ShapeDtypeStruct((1, width), f32)],
        scratch_shapes=[pltpu.VMEM((3, width, width), bf16), pltpu.SemaphoreType.DMA((3, 16))],
        compiler_params=limit,
        cost_estimate=pl.CostEstimate(flops=12_000_000_000, bytes_accessed=13_000_000, transcendentals=200_000),
        name="feed",
    )(info, x_rows, cot_rows, atts, gain_two, near_a, across_a, all_b, far_near_a, far_across_a, far_b)

    back = [datts[0]] + [plane_shift(datts[step], step) for step in (1, 2, 3)]
    outputs = lax.all_to_all(out_rows, "z", split_axis=0, concat_axis=0, tiled=True).reshape(16, 8, width)
    grad_att_near = jnp.stack([item[0] for item in back])
    grad_att_far = core_swap(jnp.stack([item[1] for item in back]))

    part_shape = jax.ShapeDtypeStruct((2, 3, 80, width), bf16)
    half_a, kept_b, away_b = pl.pallas_call(
        grads_kernel,
        in_specs=[smem] + [vmem] * 6,
        out_specs=[hbm] * 3,
        out_shape=[jax.ShapeDtypeStruct((2, 3, 2, 80, width), bf16), part_shape, part_shape],
        scratch_shapes=[pltpu.VMEM((3, width, width), bf16), pltpu.SemaphoreType.DMA((3, 8))],
        compiler_params=limit,
        cost_estimate=pl.CostEstimate(flops=6_000_000_000, bytes_accessed=8_000_000, transcendentals=0),
        name="grads",
    )(info, pack, core_swap(pack), atts, far_atts, cot_rows, far_cot)

    def added(left, right):
        return (left.astype(f32) + right.astype(f32)).astype(bf16)

    def halves(array, index, axis):
        first, second = (lax.index_in_dim(array, i, axis, keepdims=False) for i in (0, 1))
        return jnp.where(index == 0, first, second), jnp.where(index == 0, second, first)

    half_a, kept_b, away_b, grad_att_near, grad_att_far, outputs = lax.optimization_barrier(
        (half_a, kept_b, away_b, grad_att_near, grad_att_far, outputs)
    )
    kept_a, away_a = halves(half_a.reshape(2, 3, 2, 2, 40, width), x, 3)
    kept_a = added(kept_a, plane_shift(away_a, 1))
    kept_b = added(kept_b, plane_shift(away_b, 2)).reshape(2, 3, 2, 40, width)
    hid_near, hid_far, *send = pl.pallas_call(
        attend_back_kernel,
        grid_spec=pltpu.PrefetchScalarGridSpec(
            num_scalar_prefetch=1,
            grid=(4,),
            in_specs=[
                seq_block(4, width=width), seq_block(4, width=width),
                whole((1, width)), whole((1, 160)), *[whole((320, 480))] * 4,
                seq_block(2, 4, width=480), seq_block(4, width=160), seq_block(4, width=160), whole((1, width)),
            ],
            out_specs=[
                seq_block(4, width=width), seq_block(4, width=width),
                *[whole((336, 480))] * 4,
            ],
            scratch_shapes=[
                pltpu.VMEM((width, 480), bf16), pltpu.VMEM((width, 480), f32), pltpu.VMEM((1, width), f32),
                pltpu.VMEM((1, 160), f32), pltpu.VMEM((8, 1, 480), f32),
            ],
        ),
        out_shape=[
            jax.ShapeDtypeStruct((4, 128, width), bf16),
            jax.ShapeDtypeStruct((4, 128, width), bf16),
            *[jax.ShapeDtypeStruct((336, 480), bf16)] * 4,
        ],
        compiler_params=limit,
        cost_estimate=pl.CostEstimate(flops=15_000_000_000, bytes_accessed=12_000_000, transcendentals=600_000),
        name="attend_back",
    )(info, near, far, gain_one, query_mult, *w_parts, pre, grad_att_near, grad_att_far, gain_two_grad)

    one, three = ring_shift(send[1], 1), ring_shift(send[3], 3)
    swapped = core_swap(hid_far)
    hid = [added(hid_near[i], swapped[i]) for i in range(4)]
    kept_a, kept_b, one, three, later = lax.optimization_barrier((kept_a, kept_b, one, three, send[2]))
    two = ring_shift(later, 2)
    kept_a, away_a = halves(kept_a, y, 2)
    kept_b, away_b = halves(kept_b, x, 2)
    kept_a = added(kept_a, plane_shift(away_a, 2))
    kept_b = added(kept_b, plane_shift(away_b, 1))
    kept = jnp.concatenate([kept_a, kept_b])
    *hid, kept, two = lax.optimization_barrier((*hid, kept, two))
    moved = [plane_shift(hid[step], step) for step in (1, 2, 3)]
    *moved, mine = lax.optimization_barrier((*moved, send[0]))
    big_sums = lax.psum_scatter(kept, "z", scatter_dimension=0, tiled=True)[0]
    grad_home = pl.pallas_call(
        norm_kernel,
        in_specs=[smem] + [vmem] * 7,
        out_specs=[vmem] * 4,
        out_shape=[jax.ShapeDtypeStruct((4, 8, width), bf16)] * 4,
        scratch_shapes=[pltpu.VMEM((4, 4, 8, width), f32)],
        compiler_params=limit,
        cost_estimate=pl.CostEstimate(flops=2_000_000_000, bytes_accessed=2_500_000, transcendentals=128),
        name="norm",
    )(info, hid[0], *moved, x_rows, grad_mid, gain_one)
    sums = pl.pallas_call(
        fold_kernel,
        in_specs=[vmem] * 4,
        out_specs=vmem,
        out_shape=jax.ShapeDtypeStruct((8, 48, 480), bf16),
        scratch_shapes=[pltpu.VMEM((8, 480), f32)],
        compiler_params=limit,
        cost_estimate=pl.CostEstimate(flops=2_000_000_000, bytes_accessed=1_600_000, transcendentals=0),
        name="fold",
    )(mine, one, two, three)
    sums = lax.all_to_all(sums, ("y", "core", "x"), split_axis=0, concat_axis=0, tiled=True)
    rows_shape = [jax.ShapeDtypeStruct((40, width), f32)] * 3
    qkv_sums = pl.pallas_call(
        spread_kernel, in_specs=[vmem], out_specs=[vmem] * 3, out_shape=rows_shape, compiler_params=limit, name="spread"
    )(sums)
    big_sums = pl.pallas_call(
        widen_kernel, in_specs=[vmem], out_specs=[vmem] * 3, out_shape=rows_shape, compiler_params=limit, name="widen"
    )(big_sums)
    line_sums = jnp.sum(sums[:, 40, :120].astype(f32), axis=0).reshape(3, 40)
    scale_low = query_scale.astype(bf16).astype(f32)
    scale_sum = LOG2E / math.sqrt(HD) * jax.nn.sigmoid(scale_low) * line_sums[2]
    grad_home = [grad_home[0]] + [ring_shift(grad_home[k], k) for k in (1, 2, 3)]
    grad_home = by_source(grad_home, z, 0).reshape(16, 8, width)

    return (
        outputs, grad_home, qkv_sums[0], qkv_sums[1], qkv_sums[2],
        big_sums[0], big_sums[1], big_sums[2], line_sums[0], line_sums[1], scale_sum,
    )


def solution(mesh):
    names = ("dp", "ctx")
    body = per_device
    if dict(mesh.shape) == {"dp": 16, "ctx": 2}:
        mesh = Mesh(mesh.devices.reshape(4, 2, 2, 2), ("z", "y", "core", "x"))
        names = mesh.axis_names
        body = planes
    seq, mat, line = P(None, names, None), P(names, None), P(names)
    return jax.shard_map(
        body,
        mesh=mesh,
        in_specs=(seq,) * 2 + (mat,) * 6 + (line,) * 3 + (P(), P()),
        out_specs=(seq,) * 2 + (mat,) * 6 + (line,) * 3,
        check_vma=False,
    )
```

```python
import math

import jax
import jax.numpy as jnp
from jax import lax
from jax.experimental import pallas as pl
from jax.experimental.pallas import tpu as pltpu
from jax.sharding import Mesh, PartitionSpec as P

H = 16
HD = 80


def mult_trans(left, right):
    return lax.dot_general(
        left, right, (((1,), (1,)), ((), ())), preferred_element_type=jnp.float32
    )


def trans_mult(left, right):
    return lax.dot_general(
        left, right, (((0,), (0,)), ((), ())), preferred_element_type=jnp.float32
    )


def position_of(index, local_rows, piece_rows, groups):
    column = index // local_rows
    within = index % local_rows
    return (within // piece_rows * groups + column) * piece_rows + within % piece_rows


def norm_back(grad_hidden, normed, inverse, gain_value):
    grad_normed = grad_hidden * gain_value
    return inverse * (grad_normed - normed * jnp.mean(grad_normed * normed, axis=1, keepdims=True))


def per_device(
    inputs,
    cotangent,
    w_query,
    w_key,
    w_value,
    w_output,
    w_up,
    w_down,
    attn_gain,
    mlp_gain,
    query_scale,
    deal,
    lengths,
):
    groups = lax.axis_size("ctx")
    group_index = lax.axis_index("dp")
    ctx_index = lax.axis_index("ctx")
    head_count = H
    head_dim = HD
    piece_rows = inputs.shape[1]
    seq_numbers = jnp.arange(inputs.shape[0], dtype=jnp.int32)
    seq_lengths = jnp.sum(
        jnp.where(deal[None, :] == seq_numbers[:, None], lengths[None, :], 0), axis=1
    )
    local_in, local_cot = (
        lax.all_to_all(inputs, "dp", split_axis=0, concat_axis=1, tiled=True),
        lax.all_to_all(cotangent, "dp", split_axis=0, concat_axis=1, tiled=True),
    )
    seq_count, local_rows, model_width = local_in.shape
    padded = local_rows * groups
    token_count = seq_count * local_rows
    my_lengths = lax.dynamic_slice_in_dim(seq_lengths, group_index * seq_count, seq_count, 0)
    query_pos = position_of(
        ctx_index * local_rows + jnp.arange(local_rows, dtype=jnp.int32),
        local_rows,
        piece_rows,
        groups,
    )
    flat_in = local_in.reshape(token_count, model_width).astype(jnp.float32)
    flat_cot = local_cot.reshape(token_count, model_width)
    lowered = (
        w_query.astype(jnp.bfloat16),
        w_key.astype(jnp.bfloat16),
        w_value.astype(jnp.bfloat16),
        w_output.astype(jnp.bfloat16),
        w_up.astype(jnp.bfloat16),
        w_down.astype(jnp.bfloat16),
        attn_gain.astype(jnp.bfloat16),
        mlp_gain.astype(jnp.bfloat16),
        query_scale.astype(jnp.bfloat16),
    )
    gathered = (
        lax.all_gather(lowered[0], ("dp", "ctx"), axis=0, tiled=True),
        lax.all_gather(lowered[1], ("dp", "ctx"), axis=0, tiled=True),
        lax.all_gather(lowered[2], ("dp", "ctx"), axis=0, tiled=True),
        lax.all_gather(lowered[3], ("dp", "ctx"), axis=0, tiled=True),
        lax.all_gather(lowered[4], ("dp", "ctx"), axis=0, tiled=True),
        lax.all_gather(lowered[5], ("dp", "ctx"), axis=0, tiled=True),
        lax.all_gather(lowered[6], ("dp", "ctx"), axis=0, tiled=True),
        lax.all_gather(lowered[7], ("dp", "ctx"), axis=0, tiled=True),
        lax.all_gather(lowered[8], ("dp", "ctx"), axis=0, tiled=True),
    )
    (
        query_full,
        key_full,
        value_full,
        output_full,
        up_full,
        down_full,
        gain_one,
        gain_two,
        scale_raw,
    ) = gathered
    inv_one = lax.rsqrt(jnp.mean(flat_in * flat_in, axis=1, keepdims=True) + 1e-06)
    normed_one = flat_in * inv_one
    hidden_one = (normed_one * gain_one.astype(jnp.float32)).astype(jnp.bfloat16)
    scale_param = scale_raw.astype(jnp.float32)
    query_mult = 1.442695041 / math.sqrt(head_dim) * jax.nn.softplus(scale_param)
    query_pre = jnp.dot(hidden_one, query_full, preferred_element_type=jnp.float32)
    queries = (query_pre * query_mult).astype(jnp.bfloat16)
    keys_local = jnp.dot(hidden_one, key_full, preferred_element_type=jnp.float32).astype(
        jnp.bfloat16
    )
    values_local = jnp.dot(hidden_one, value_full, preferred_element_type=jnp.float32).astype(
        jnp.bfloat16
    )
    four_shape = (seq_count, local_rows, head_count, head_dim)
    query_four = queries.reshape(four_shape)
    keys_three = keys_local.reshape(seq_count, local_rows, model_width)
    values_three = values_local.reshape(seq_count, local_rows, model_width)

    def live_between(row_pos, key_pos):
        allowed = (key_pos[None, None, :] <= row_pos[None, :, None]) & (
            key_pos[None, None, :] < my_lengths[:, None, None]
        )
        return allowed[:, :, None, :]

    def live_mask(key_pos):
        return live_between(query_pos, key_pos)

    def attend_block(state_now, key_block, value_block, first_row):
        run_max, run_sum, run_acc = state_now
        block_len = key_block.shape[1]
        key_pos = position_of(
            first_row + jnp.arange(block_len, dtype=jnp.int32), local_rows, piece_rows, groups
        )
        key_four = key_block.reshape(seq_count, block_len, head_count, head_dim)
        value_four = value_block.reshape(seq_count, block_len, head_count, head_dim)
        scores = jnp.einsum(
            "srhd,skhd->srhk", query_four, key_four, preferred_element_type=jnp.float32
        )
        allowed = live_mask(key_pos)
        masked = jnp.where(allowed, scores, -1e30)
        new_max = jnp.maximum(run_max, jnp.max(masked, axis=3))
        weights_now = jnp.exp(jnp.where(allowed, masked - new_max[..., None], -1e30))
        factor = jnp.exp(run_max - new_max)
        new_sum = run_sum * factor + jnp.sum(weights_now, axis=3)
        added = jnp.einsum(
            "srhk,skhd->srhd",
            weights_now.astype(jnp.bfloat16),
            value_four,
            preferred_element_type=jnp.float32,
        )
        return (new_max, new_sum, run_acc * factor[..., None] + added)

    start_state = (
        jnp.full((seq_count, local_rows, head_count), -1e30, jnp.float32),
        jnp.zeros((seq_count, local_rows, head_count), jnp.float32),
        jnp.zeros(four_shape, jnp.float32),
    )
    key_piece = lax.all_gather(keys_three, "ctx", axis=1, tiled=True)
    value_piece = lax.all_gather(values_three, "ctx", axis=1, tiled=True)
    piece_len = key_piece.shape[1]
    fold_block_len = 512 if piece_len % 512 == 0 else piece_len

    def one_block(state_now, block_index):
        offset = block_index * fold_block_len
        key_block = lax.dynamic_slice_in_dim(key_piece, offset, fold_block_len, 1)
        value_block = lax.dynamic_slice_in_dim(value_piece, offset, fold_block_len, 1)
        return (attend_block(state_now, key_block, value_block, offset), None)

    result_state, unused = lax.scan(
        one_block, start_state, jnp.arange(piece_len // fold_block_len, dtype=jnp.int32)
    )
    run_max, run_sum, run_acc = result_state
    log_total = run_max + jnp.log(run_sum)
    attn_exact = run_acc / run_sum[..., None]
    attended = attn_exact.reshape(token_count, model_width).astype(jnp.bfloat16)
    middle = flat_in + jnp.dot(attended, output_full, preferred_element_type=jnp.float32)
    inv_two = lax.rsqrt(jnp.mean(middle * middle, axis=1, keepdims=True) + 1e-06)
    normed_two = middle * inv_two
    hidden_two = (normed_two * gain_two.astype(jnp.float32)).astype(jnp.bfloat16)
    up_pre = jnp.dot(hidden_two, up_full, preferred_element_type=jnp.float32)
    active = jax.nn.silu(up_pre).astype(jnp.bfloat16)
    result = (middle + jnp.dot(active, down_full, preferred_element_type=jnp.float32)).astype(
        jnp.bfloat16
    )
    back_weights = (
        lax.all_gather(lowered[0], ("dp", "ctx"), axis=0, tiled=True),
        lax.all_gather(lowered[1], ("dp", "ctx"), axis=0, tiled=True),
        lax.all_gather(lowered[2], ("dp", "ctx"), axis=0, tiled=True),
        lax.all_gather(lowered[3], ("dp", "ctx"), axis=0, tiled=True),
        lax.all_gather(lowered[4], ("dp", "ctx"), axis=0, tiled=True),
        lax.all_gather(lowered[5], ("dp", "ctx"), axis=0, tiled=True),
        lax.all_gather(lowered[6], ("dp", "ctx"), axis=0, tiled=True),
        lax.all_gather(lowered[7], ("dp", "ctx"), axis=0, tiled=True),
        lax.all_gather(lowered[8], ("dp", "ctx"), axis=0, tiled=True),
    )
    (
        query_back,
        key_back,
        value_back,
        output_back,
        up_back,
        down_back,
        gain_one_back,
        gain_two_back,
        scale_back,
    ) = back_weights
    cot_wide = flat_cot.astype(jnp.float32)
    grad_down = trans_mult(active, flat_cot)
    grad_active = mult_trans(flat_cot, down_back)
    sigma_up = jax.nn.sigmoid(up_pre)
    grad_up_pre = (grad_active * sigma_up * (1.0 + up_pre * (1.0 - sigma_up))).astype(jnp.bfloat16)
    grad_up = trans_mult(hidden_two, grad_up_pre)
    grad_hidden_two = mult_trans(grad_up_pre, up_back)
    grad_gain_two = jnp.sum(grad_hidden_two * normed_two, axis=0)
    grad_middle = cot_wide + norm_back(
        grad_hidden_two, normed_two, inv_two, gain_two_back.astype(jnp.float32)
    )
    grad_middle_low = grad_middle.astype(jnp.bfloat16)
    grad_output = trans_mult(attended, grad_middle_low)
    grad_attended = mult_trans(grad_middle_low, output_back).astype(jnp.bfloat16)
    grad_att_four = grad_attended.reshape(four_shape)
    delta_rows = jnp.sum(grad_att_four.astype(jnp.float32) * attn_exact, axis=3)
    key_all, value_all = (
        lax.all_gather(keys_three, "ctx", axis=1, tiled=True),
        lax.all_gather(values_three, "ctx", axis=1, tiled=True),
    )
    block_len = min(512, padded)

    def back_block(block_index, state_now):
        grad_query, grad_key_all, grad_value_all = state_now
        offset = block_index * block_len
        key_block = lax.dynamic_slice_in_dim(key_all, offset, block_len, 1).reshape(
            seq_count, block_len, head_count, head_dim
        )
        value_block = lax.dynamic_slice_in_dim(value_all, offset, block_len, 1).reshape(
            seq_count, block_len, head_count, head_dim
        )
        key_pos = position_of(
            offset + jnp.arange(block_len, dtype=jnp.int32), local_rows, piece_rows, groups
        )
        scores = jnp.einsum(
            "srhd,skhd->srhk", query_four, key_block, preferred_element_type=jnp.float32
        )
        probs = jnp.exp(jnp.where(live_mask(key_pos), scores - log_total[..., None], -1e30))
        grad_value_block = jnp.einsum(
            "srhk,srhd->skhd",
            probs.astype(jnp.bfloat16),
            grad_att_four,
            preferred_element_type=jnp.float32,
        )
        grad_probs = jnp.einsum(
            "srhd,skhd->srhk", grad_att_four, value_block, preferred_element_type=jnp.float32
        )
        grad_scores = (probs * (grad_probs - delta_rows[..., None])).astype(jnp.bfloat16)
        grad_query = grad_query + jnp.einsum(
            "srhk,skhd->srhd", grad_scores, key_block, preferred_element_type=jnp.float32
        )
        grad_key_block = jnp.einsum(
            "srhk,srhd->skhd", grad_scores, query_four, preferred_element_type=jnp.float32
        )
        grad_key_all = lax.dynamic_update_slice_in_dim(
            grad_key_all, grad_key_block.reshape(seq_count, block_len, model_width), offset, 1
        )
        grad_value_all = lax.dynamic_update_slice_in_dim(
            grad_value_all, grad_value_block.reshape(seq_count, block_len, model_width), offset, 1
        )
        return (grad_query, grad_key_all, grad_value_all)

    zero_all = jnp.zeros((seq_count, padded, model_width), jnp.float32)
    grad_query, grad_key_all, grad_value_all = lax.fori_loop(
        0, padded // block_len, back_block, (jnp.zeros(four_shape, jnp.float32), zero_all, zero_all)
    )
    grad_key_mine, grad_value_mine = (
        lax.psum_scatter(
            grad_key_all.astype(jnp.bfloat16), "ctx", scatter_dimension=1, tiled=True
        ).astype(jnp.float32),
        lax.psum_scatter(
            grad_value_all.astype(jnp.bfloat16), "ctx", scatter_dimension=1, tiled=True
        ).astype(jnp.float32),
    )
    grad_query_flat = grad_query.reshape(token_count, model_width)
    grad_query_pre = (grad_query_flat * query_mult).astype(jnp.bfloat16)
    grad_scale = (
        1.442695041
        / math.sqrt(head_dim)
        * jax.nn.sigmoid(scale_back.astype(jnp.float32))
        * jnp.sum(grad_query_flat * query_pre, axis=0)
    )
    grad_key_low = grad_key_mine.reshape(token_count, model_width).astype(jnp.bfloat16)
    grad_value_low = grad_value_mine.reshape(token_count, model_width).astype(jnp.bfloat16)
    grad_wq = trans_mult(hidden_one, grad_query_pre)
    grad_wk = trans_mult(hidden_one, grad_key_low)
    grad_wv = trans_mult(hidden_one, grad_value_low)
    grad_hidden_one = (
        mult_trans(grad_query_pre, query_back)
        + mult_trans(grad_key_low, key_back)
        + mult_trans(grad_value_low, value_back)
    )
    grad_gain_one = jnp.sum(grad_hidden_one * normed_one, axis=0)
    grad_in = grad_middle + norm_back(
        grad_hidden_one, normed_one, inv_one, gain_one_back.astype(jnp.float32)
    )
    matrix_stack = jnp.stack([grad_wq, grad_wk, grad_wv, grad_output, grad_up, grad_down], axis=0)
    vector_stack = jnp.stack([grad_gain_one, grad_gain_two, grad_scale], axis=0)
    matrix_sums, vector_sums = (
        lax.psum_scatter(matrix_stack, ("dp", "ctx"), scatter_dimension=1, tiled=True),
        lax.psum_scatter(vector_stack, ("dp", "ctx"), scatter_dimension=1, tiled=True),
    )
    out_local = result.reshape(seq_count, local_rows, model_width)
    grad_local = grad_in.astype(jnp.bfloat16).reshape(seq_count, local_rows, model_width)
    back_out, back_grad = (
        lax.all_to_all(out_local, "dp", split_axis=1, concat_axis=0, tiled=True),
        lax.all_to_all(grad_local, "dp", split_axis=1, concat_axis=0, tiled=True),
    )
    return (
        back_out,
        back_grad,
        matrix_sums[0],
        matrix_sums[1],
        matrix_sums[2],
        matrix_sums[3],
        matrix_sums[4],
        matrix_sums[5],
        vector_sums[0],
        vector_sums[1],
        vector_sums[2],
    )


LOG2E = 1.442695041
CODES = (0, 1, 4, 5)


def plane_shift(value, step):
    if step == 1:
        return lax.ppermute(value, "x", [(0, 1), (1, 0)])
    if step == 2:
        return lax.ppermute(value, "y", [(0, 1), (1, 0)])
    return lax.ppermute(value, ("y", "x"), [(0, 3), (1, 2), (2, 1), (3, 0)])


def core_swap(value):
    return lax.ppermute(value, "core", [(0, 1), (1, 0)])


def ring_shift(value, step):
    return lax.ppermute(value, "z", [(i, (i + step) % 4) for i in range(4)])


def pick(array, index):
    return lax.dynamic_index_in_dim(array, index, 0, keepdims=False)


def by_source(pieces, z_index, axis):
    pieces = [jnp.expand_dims(item, axis) for item in pieces]
    shape = [1] * pieces[0].ndim
    shape[axis] = 4
    hop = ((z_index - jnp.arange(4, dtype=jnp.int32)) % 4).reshape(shape)
    made = pieces[0]
    for k in (1, 2, 3):
        made = jnp.where(hop == k, pieces[k], made)
    return made


def pair(mine, other, index, axis):
    shape = [1] * (mine.ndim + 1)
    shape[axis] = 2
    slot = jnp.arange(2, dtype=jnp.int32).reshape(shape)
    return jnp.where(slot == index, jnp.expand_dims(mine, axis), jnp.expand_dims(other, axis))


def row_positions(shape, dim, plane_index):
    row = lax.broadcasted_iota(jnp.int32, shape, dim)
    chip = (row // 32) % 4
    code = (chip % 2) + 4 * (chip // 2) + 2 * (row // 128)
    return 64 * ((row % 32) // 8) + 8 * (plane_index ^ code) + row % 8


def live_pairs(info_ref, seq):
    shape = (256, 256)
    query_pos = row_positions(shape, 0, info_ref[1])
    key_pos = row_positions(shape, 1, info_ref[1])
    return (key_pos <= query_pos) & (key_pos < info_ref[2 + seq])


def block_rows(near_ref, far_ref):
    return jnp.concatenate([near_ref[...], far_ref[...]], axis=0).reshape(256, near_ref.shape[2])


def soft_probs(query, key, live):
    scores = mult_trans(query, key)
    scores = jnp.where(live, scores, -1e30)
    top = jnp.max(scores, axis=1, keepdims=True)
    weights = jnp.where(live, jnp.exp(scores - top), 0.0)
    return weights / jnp.sum(weights, axis=1, keepdims=True)


def set_weights(info_ref, parts, w_ref):
    @pl.when(pl.program_id(0) == 0)
    def _():
        for hop, part in enumerate(parts):
            w_ref[pl.ds(pl.multiple_of(((info_ref[0] - hop) & 3) * 320, 320), 320), :] = part[...]


def attend_kernel(
    info_ref, near_ref, far_ref, gain_ref, mult_ref, w_0, w_1, w_2, w_3, pre_ref, att_near, att_far, w_ref
):
    seq = pl.program_id(0)
    set_weights(info_ref, (w_0, w_1, w_2, w_3), w_ref)
    live = live_pairs(info_ref, seq)
    wide = block_rows(near_ref, far_ref).astype(jnp.float32)
    inverse = lax.rsqrt(jnp.mean(wide * wide, axis=1, keepdims=True) + 1e-06)
    hidden = (wide * inverse * gain_ref[...]).astype(jnp.bfloat16)
    pre = jnp.dot(hidden, w_ref[...], preferred_element_type=jnp.float32)
    pre_ref[...] = pre.reshape(2, 4, 32, 480)
    query = (pre[:, 0:160] * mult_ref[...]).astype(jnp.bfloat16)
    key = pre[:, 160:320].astype(jnp.bfloat16)
    value = pre[:, 320:480].astype(jnp.bfloat16)
    heads = []
    for head in range(2):
        part = slice(80 * head, 80 * head + 80)
        probs = soft_probs(query[:, part], key[:, part], live).astype(jnp.bfloat16)
        heads.append(jnp.dot(probs, value[:, part], preferred_element_type=jnp.float32))
    att = jnp.concatenate(heads, axis=1).astype(jnp.bfloat16).reshape(2, 4, 32, 160)
    att_near[...] = att[0]
    att_far[...] = att[1]


def attend_back_kernel(
    info_ref, near_ref, far_ref, gain_ref, mult_ref, w_0, w_1, w_2, w_3, pre_ref, grad_near, grad_far, gain_two_ref,
    hid_near, hid_far, send_0, send_1, send_2, send_3, w_ref, w_acc, gain_acc, scale_acc, lines,
):
    seq = pl.program_id(0)
    set_weights(info_ref, (w_0, w_1, w_2, w_3), w_ref)

    @pl.when(seq == 0)
    def _():
        w_acc[...] = jnp.zeros_like(w_acc)
        gain_acc[...] = jnp.zeros_like(gain_acc)
        scale_acc[...] = jnp.zeros_like(scale_acc)

    live = live_pairs(info_ref, seq)
    wide = block_rows(near_ref, far_ref).astype(jnp.float32)
    inverse = lax.rsqrt(jnp.mean(wide * wide, axis=1, keepdims=True) + 1e-06)
    normed = wide * inverse
    hidden = (normed * gain_ref[...]).astype(jnp.bfloat16)
    pre = pre_ref[...].reshape(256, 480)
    mult = mult_ref[...]
    query = (pre[:, 0:160] * mult).astype(jnp.bfloat16)
    key = pre[:, 160:320].astype(jnp.bfloat16)
    value = pre[:, 320:480].astype(jnp.bfloat16)
    grad_att = block_rows(grad_near, grad_far)
    grad_q, grad_k, grad_v = [], [], []
    for head in range(2):
        part = slice(80 * head, 80 * head + 80)
        probs = soft_probs(query[:, part], key[:, part], live)
        grad_probs = mult_trans(grad_att[:, part], value[:, part])
        delta = jnp.sum(probs * grad_probs, axis=1, keepdims=True)
        grad_scores = (probs * (grad_probs - delta)).astype(jnp.bfloat16)
        grad_v.append(trans_mult(probs.astype(jnp.bfloat16), grad_att[:, part]))
        grad_q.append(jnp.dot(grad_scores, key[:, part], preferred_element_type=jnp.float32))
        grad_k.append(trans_mult(grad_scores, query[:, part]))
    grad_query = jnp.concatenate(grad_q, axis=1)
    scale_acc[...] += jnp.sum(grad_query * pre[:, 0:160], axis=0, keepdims=True)
    joined = jnp.concatenate([grad_query * mult] + grad_k + grad_v, axis=1).astype(jnp.bfloat16)
    w_acc[...] += trans_mult(hidden, joined)
    grad_hidden = mult_trans(joined, w_ref[...])
    gain_acc[...] += jnp.sum(grad_hidden * normed, axis=0, keepdims=True)
    low = grad_hidden.astype(jnp.bfloat16).reshape(2, 4, 32, 1280)
    hid_near[...] = low[0]
    hid_far[...] = low[1]

    @pl.when(seq == 3)
    def _():
        lines[...] = jnp.zeros_like(lines)
        for which, source in enumerate((gain_acc, gain_two_ref)):
            for owner in range(32):
                lane = 120 * (owner % 4) + 40 * which
                lines[owner // 4, :, lane : lane + 40] = source[:, 40 * owner : 40 * owner + 40]
        for part in range(4):
            lane = 120 * part + 80
            lines[info_ref[1], :, lane : lane + 40] = scale_acc[:, 40 * part : 40 * part + 40]
        blank = jnp.zeros((14, 480), jnp.float32)
        for hop, send in enumerate((send_0, send_1, send_2, send_3)):
            target = (info_ref[0] + hop) & 3
            rows = w_acc[pl.ds(pl.multiple_of(target * 320, 320), 320), :]
            block = jnp.concatenate([rows, lines[2 * target], lines[2 * target + 1], blank], axis=0)
            send[...] = block.astype(jnp.bfloat16)


def block_index(z_index, y_index, core):
    return pl.ds(pl.multiple_of((4 * z_index + 2 * y_index + core) * 80, 80), 80)


def source_rows(info_ref, chip, core):
    source = info_ref[1] ^ (CODES[chip] + 2 * core)
    return pl.ds(pl.multiple_of(source * 160, 160), 160)


def feed_kernel(
    info_ref, x_ref, g_ref, atts, gain_ref,
    near_rows, across_a, across_b, far_near_rows, far_across_a, far_across_b,
    out_ref, pack_ref, dmid_ref, datt_0, datt_1, datt_2, datt_3, gain_grad,
    weights, sems,
):
    y_index, core_index = info_ref[1] // 4, (info_ref[1] // 2) % 2
    copies = []
    for w in range(3):
        moved = []
        for core, own, others in (
            (core_index, near_rows, (across_a, across_b)),
            (1 - core_index, far_near_rows, (far_across_a, far_across_b)),
        ):
            for z_index in range(4):
                moved.append((own.at[z_index, w], z_index, y_index, core))
                moved.append((others[z_index // 2].at[z_index % 2, w], z_index, 1 - y_index, core))
        copies.append([
            pltpu.make_async_copy(src, weights.at[w, block_index(*place)], sems.at[w, i])
            for i, (src, *place) in enumerate(moved)
        ])
    for group in copies:
        for copy in group:
            copy.start()
    datts = (datt_0, datt_1, datt_2, datt_3)

    for copy in copies[0]:
        copy.wait()
    middle = x_ref[...].astype(jnp.float32)
    for chip in range(4):
        for core in range(2):
            middle += jnp.dot(
                atts[chip, core], weights[0, source_rows(info_ref, chip, core), :],
                preferred_element_type=jnp.float32,
            )
    inverse = lax.rsqrt(jnp.mean(middle * middle, axis=1, keepdims=True) + 1e-06)
    normed = middle * inverse
    gain = gain_ref[...]
    hidden = (normed * gain).astype(jnp.bfloat16)
    pack_ref[1] = hidden
    for copy in copies[1]:
        copy.wait()
    up = jnp.dot(hidden, weights[1], preferred_element_type=jnp.float32)
    sigma = jax.nn.sigmoid(up)
    active = (up * sigma).astype(jnp.bfloat16)
    pack_ref[0] = active
    for copy in copies[2]:
        copy.wait()
    down = jnp.dot(active, weights[2], preferred_element_type=jnp.float32)
    result = middle + down
    for seq in range(4):
        for plane_z in range(4):
            row = 32 * seq + 8 * plane_z
            out_ref[plane_z, seq] = result[row : row + 8].astype(jnp.bfloat16)
    cot = g_ref[...]
    grad_act = mult_trans(cot, weights[2])
    grad_up = (grad_act * sigma * (1.0 + up * (1.0 - sigma))).astype(jnp.bfloat16)
    pack_ref[2] = grad_up
    grad_hidden = mult_trans(grad_up, weights[1])
    gain_grad[...] = jnp.sum(grad_hidden * normed, axis=0, keepdims=True)
    grad_mid = cot.astype(jnp.float32) + norm_back(grad_hidden, normed, inverse, gain)
    dmid_ref[...] = grad_mid
    low = grad_mid.astype(jnp.bfloat16)
    pack_ref[3] = low
    for chip in range(4):
        for core in range(2):
            datts[chip][core] = mult_trans(low, weights[0, source_rows(info_ref, chip, core), :]).astype(jnp.bfloat16)


def grads_kernel(
    info_ref, pack_ref, far_pack, atts, far_atts, cot_ref, far_cot, half_a, kept_b, away_b, stage, sems
):
    y_index, core_index = info_ref[1] // 4, (info_ref[1] // 2) % 2
    copies = []

    def leave(w):
        for half in range(2):
            targets = [(half, row, half_a.at[half, w, row]) for row in range(2)]
            targets += [(2 + half, y_index, kept_b.at[half, w]), (2 + half, 1 - y_index, away_b.at[half, w])]
            for i, (z_index, row, target) in enumerate(targets):
                copy = pltpu.make_async_copy(
                    stage.at[w, block_index(z_index, row, core_index)], target, sems.at[w, 4 * half + i]
                )
                copy.start()
                copies.append(copy)

    def both(near, far):
        return jnp.concatenate([near, far], axis=0)

    cots = both(cot_ref[...], far_cot[...])
    for w, left, grads in ((2, 0, cots), (1, 1, both(pack_ref[2], far_pack[2]))):
        for chunk in range(5):
            part = slice(256 * chunk, 256 * chunk + 256)
            acts = both(pack_ref[left, :, part], far_pack[left, :, part])
            stage[w, part, :] = trans_mult(acts, grads).astype(jnp.bfloat16)
        leave(w)
    grads = both(pack_ref[3], far_pack[3])
    for chip in range(4):
        for core in range(2):
            att = both(atts[chip, core], far_atts[chip, 1 - core])
            stage[0, source_rows(info_ref, chip, core), :] = trans_mult(att, grads).astype(jnp.bfloat16)
    leave(0)
    for copy in copies:
        copy.wait()


def norm_kernel(info_ref, hid_0, hid_1, hid_2, hid_3, x_ref, dmid_ref, gain_ref, out_0, out_1, out_2, out_3, rows):
    grad = hid_0[...].astype(jnp.float32)
    for item in (hid_1, hid_2, hid_3):
        grad += item[...].astype(jnp.float32)
    wide = x_ref[...].astype(jnp.float32)
    inverse = lax.rsqrt(jnp.mean(wide * wide, axis=1, keepdims=True) + 1e-06)
    grad = dmid_ref[...] + norm_back(grad, wide * inverse, inverse, gain_ref[...])
    for seq in range(4):
        for plane_z in range(4):
            row = 32 * seq + 8 * plane_z
            rows[plane_z, seq] = grad[row : row + 8]
    for hop, out in enumerate((out_0, out_1, out_2, out_3)):
        out[...] = rows[(info_ref[0] + hop) & 3].astype(jnp.bfloat16)


def fold_kernel(part_0, part_1, part_2, part_3, out_ref, line):
    total = part_0[...].astype(jnp.float32)
    for item in (part_1, part_2, part_3):
        total += item[...].astype(jnp.float32)
    line[...] = jnp.zeros_like(line)
    for owner in range(8):
        lane = 120 * (owner % 4)
        line[0:1, 0:120] = total[320 + owner // 4 : 321 + owner // 4, lane : lane + 120]
        block = jnp.concatenate([total[40 * owner : 40 * owner + 40], line[...]], axis=0)
        out_ref[owner] = block.astype(jnp.bfloat16)


def spread_kernel(in_ref, *outs):
    for which, out in enumerate(outs):
        for owner in range(8):
            part = in_ref[owner, 0:40, 160 * which : 160 * which + 160]
            out[:, 160 * owner : 160 * owner + 160] = part.astype(jnp.float32)


def widen_kernel(in_ref, *outs):
    for which, out in enumerate(outs):
        out[...] = in_ref[which].astype(jnp.float32)


def whole(shape):
    return pl.BlockSpec(shape, lambda *_: (0,) * len(shape))


def seq_block(*lead, width):
    count = len(lead)
    return pl.BlockSpec((*lead, 32, width), lambda s, info: (*(0,) * count, s, 0))


def planes(
    inputs, cotangent, w_query, w_key, w_value, w_output, w_up, w_down,
    attn_gain, mlp_gain, query_scale, deal, lengths,
):
    f32, bf16 = jnp.float32, jnp.bfloat16
    z, y, c, x = (lax.axis_index(name) for name in ("z", "y", "core", "x"))
    plane = 4 * y + 2 * c + x
    width = 1280
    seqs = jnp.arange(16, dtype=jnp.int32)
    seq_lengths = jnp.sum(jnp.where(deal[None, :] == seqs[:, None], lengths[None, :], 0), axis=1)
    my_lengths = lax.dynamic_slice_in_dim(seq_lengths, 4 * z, 4, 0)
    info = jnp.concatenate([jnp.stack([z, plane]), my_lengths]).astype(jnp.int32)

    vec = jnp.concatenate([attn_gain, mlp_gain, query_scale]).astype(bf16)
    vec_block = jnp.zeros((1, 8, width), bf16).at[0, 0, :120].set(vec)
    in_four = inputs.reshape(4, 4, 8, width)
    sent = [jnp.concatenate([pick(in_four, (z + k) % 4), vec_block]) for k in range(4)]
    got = [sent[0]] + [ring_shift(sent[k], k) for k in (1, 2, 3)]
    x_rows = by_source([item[:4] for item in got], z, 1).reshape(128, width)
    vec_rows = by_source([item[4, 0] for item in got], z, 0)
    vec_rows = jnp.concatenate([vec_rows, jnp.zeros((4, width), bf16)])
    own = jnp.concatenate([x_rows, vec_rows])

    big = jnp.stack([w_output, w_up, w_down]).astype(bf16)
    big = lax.all_gather(big, "z", axis=0)

    qkv = jnp.stack([w_query, w_key, w_value]).astype(bf16)
    own, qkv = lax.optimization_barrier((own, qkv))
    near = [own] + [plane_shift(own, step) for step in (1, 2, 3)]
    qkv = qkv.reshape(3, 40, 8, 160).transpose(2, 1, 0, 3).reshape(8, 40, 480)
    qkv = lax.all_to_all(qkv, ("y", "core", "x"), split_axis=0, concat_axis=0, tiled=True)
    qkv = qkv.reshape(320, 480)

    late = qkv
    *near, qkv = lax.optimization_barrier((*near, qkv))
    near = jnp.stack(near)
    one, three, late = lax.optimization_barrier((ring_shift(qkv, 1), ring_shift(qkv, 3), late))
    w_parts = [qkv, one, ring_shift(late, 2), three]
    big, near = lax.optimization_barrier((big, near))
    far = core_swap(near)
    beside, across = plane_shift(big, 1), plane_shift(big, 2)
    beside, across, w_parts[1] = lax.optimization_barrier((beside, across, w_parts[1]))
    across_a = plane_shift(beside[:2], 2)
    across_b = plane_shift(across[2:], 1)
    near_rows = pair(big, beside, x, 2).reshape(4, 3, 80, width)

    vecs = jnp.stack([near[:, 128:132, :120], far[:, 128:132, :120]])
    vecs = vecs.astype(f32).reshape(2, 2, 2, 4, 120)
    vecs = jnp.where(c == 0, vecs, vecs[::-1])
    vecs = jnp.where(y == 0, vecs, vecs[:, ::-1])
    vecs = jnp.where(x == 0, vecs, vecs[:, :, ::-1])
    vecs = vecs.reshape(2, 2, 2, 4, 3, 40).transpose(4, 3, 1, 0, 2, 5).reshape(3, width)
    gain_one, gain_two = vecs[0:1], vecs[1:2]
    my_scale = lax.dynamic_slice_in_dim(vecs[2:3], 160 * plane, 160, 1)
    query_mult = LOG2E / math.sqrt(HD) * jax.nn.softplus(my_scale)

    limit = pltpu.CompilerParams(vmem_limit_bytes=50 * 1024 * 1024)
    pre, att_near, att_far = pl.pallas_call(
        attend_kernel,
        grid_spec=pltpu.PrefetchScalarGridSpec(
            num_scalar_prefetch=1,
            grid=(4,),
            in_specs=[
                seq_block(4, width=width), seq_block(4, width=width),
                whole((1, width)), whole((1, 160)), *[whole((320, 480))] * 4,
            ],
            out_specs=[seq_block(2, 4, width=480), seq_block(4, width=160), seq_block(4, width=160)],
            scratch_shapes=[pltpu.VMEM((width, 480), bf16)],
        ),
        out_shape=[
            jax.ShapeDtypeStruct((2, 4, 128, 480), f32),
            jax.ShapeDtypeStruct((4, 128, 160), bf16),
            jax.ShapeDtypeStruct((4, 128, 160), bf16),
        ],
        compiler_params=limit,
        cost_estimate=pl.CostEstimate(flops=9_000_000_000, bytes_accessed=8_000_000, transcendentals=600_000),
        name="attend",
    )(info, near, far, gain_one, query_mult, *w_parts)

    att_near, att_far, near_rows, across_a, across_b = lax.optimization_barrier(
        (att_near, att_far, near_rows, across_a, across_b)
    )
    far_near_rows = core_swap(near_rows)
    across_a = pair(across[:2], across_a, x, 2).reshape(2, 3, 80, width)
    across_b = pair(across[2:], across_b, x, 2).reshape(2, 3, 80, width)
    far_across_a, far_across_b = core_swap(across_a), core_swap(across_b)
    att_pair = jnp.stack([att_near, core_swap(att_far)], axis=1)
    att_pair, cotangent = lax.optimization_barrier((att_pair, cotangent))
    cot_rows = lax.all_to_all(cotangent.reshape(4, 4, 8, width), "z", split_axis=0, concat_axis=0, tiled=True)
    cot_rows = cot_rows.transpose(1, 0, 2, 3).reshape(128, width)
    atts = [att_pair[0]] + [plane_shift(att_pair[step], step) for step in (1, 2, 3)]
    atts = jnp.stack(atts)
    far_atts, far_cot = core_swap(atts), core_swap(cot_rows)
    atts, cot_rows, far_atts, far_cot = lax.optimization_barrier((atts, cot_rows, far_atts, far_cot))

    datt_shape = jax.ShapeDtypeStruct((2, 128, 160), bf16)
    smem = pl.BlockSpec(memory_space=pltpu.SMEM)
    vmem = pl.BlockSpec(memory_space=pltpu.VMEM)
    hbm = pl.BlockSpec(memory_space=pl.ANY)
    out_rows, pack, grad_mid, *datts, gain_two_grad = pl.pallas_call(
        feed_kernel,
        in_specs=[smem] + [vmem] * 4 + [hbm] * 6,
        out_specs=[vmem] * 8,
        out_shape=[
            jax.ShapeDtypeStruct((4, 4, 8, width), bf16),
            jax.ShapeDtypeStruct((4, 128, width), bf16),
            jax.ShapeDtypeStruct((128, width), f32),
        ]
        + [datt_shape] * 4
        + [jax.ShapeDtypeStruct((1, width), f32)],
        scratch_shapes=[pltpu.VMEM((3, width, width), bf16), pltpu.SemaphoreType.DMA((3, 16))],
        compiler_params=limit,
        cost_estimate=pl.CostEstimate(flops=12_000_000_000, bytes_accessed=13_000_000, transcendentals=200_000),
        name="feed",
    )(info, x_rows, cot_rows, atts, gain_two, near_rows, across_a, across_b, far_near_rows, far_across_a, far_across_b)

    back = [datts[0]] + [plane_shift(datts[step], step) for step in (1, 2, 3)]

    part_shape = jax.ShapeDtypeStruct((2, 3, 80, width), bf16)
    half_a, kept_b, away_b = pl.pallas_call(
        grads_kernel,
        in_specs=[smem] + [vmem] * 6,
        out_specs=[hbm] * 3,
        out_shape=[jax.ShapeDtypeStruct((2, 3, 2, 80, width), bf16), part_shape, part_shape],
        scratch_shapes=[pltpu.VMEM((3, width, width), bf16), pltpu.SemaphoreType.DMA((3, 8))],
        compiler_params=limit,
        cost_estimate=pl.CostEstimate(flops=6_000_000_000, bytes_accessed=8_000_000, transcendentals=0),
        name="grads",
    )(info, pack, core_swap(pack), atts, far_atts, cot_rows, far_cot)

    def added(left, right):
        return (left.astype(f32) + right.astype(f32)).astype(bf16)

    def halves(array, index, axis):
        first, second = (lax.index_in_dim(array, i, axis, keepdims=False) for i in (0, 1))
        return jnp.where(index == 0, first, second), jnp.where(index == 0, second, first)

    half_a, kept_b, away_b, out_rows, *back = lax.optimization_barrier((half_a, kept_b, away_b, out_rows, *back))
    outputs = lax.all_to_all(out_rows, "z", split_axis=0, concat_axis=0, tiled=True).reshape(16, 8, width)
    grad_att_near = jnp.stack([item[0] for item in back])
    grad_att_far = core_swap(jnp.stack([item[1] for item in back]))
    kept_a, away_a = halves(half_a.reshape(2, 3, 2, 2, 40, width), x, 3)
    kept_a = added(kept_a, plane_shift(away_a, 1))
    kept_b = added(kept_b, plane_shift(away_b, 2)).reshape(2, 3, 2, 40, width)
    hid_near, hid_far, *send = pl.pallas_call(
        attend_back_kernel,
        grid_spec=pltpu.PrefetchScalarGridSpec(
            num_scalar_prefetch=1,
            grid=(4,),
            in_specs=[
                seq_block(4, width=width), seq_block(4, width=width),
                whole((1, width)), whole((1, 160)), *[whole((320, 480))] * 4,
                seq_block(2, 4, width=480), seq_block(4, width=160), seq_block(4, width=160), whole((1, width)),
            ],
            out_specs=[
                seq_block(4, width=width), seq_block(4, width=width),
                *[whole((336, 480))] * 4,
            ],
            scratch_shapes=[
                pltpu.VMEM((width, 480), bf16), pltpu.VMEM((width, 480), f32), pltpu.VMEM((1, width), f32),
                pltpu.VMEM((1, 160), f32), pltpu.VMEM((8, 1, 480), f32),
            ],
        ),
        out_shape=[
            jax.ShapeDtypeStruct((4, 128, width), bf16),
            jax.ShapeDtypeStruct((4, 128, width), bf16),
            *[jax.ShapeDtypeStruct((336, 480), bf16)] * 4,
        ],
        compiler_params=limit,
        cost_estimate=pl.CostEstimate(flops=15_000_000_000, bytes_accessed=12_000_000, transcendentals=600_000),
        name="attend_back",
    )(info, near, far, gain_one, query_mult, *w_parts, pre, grad_att_near, grad_att_far, gain_two_grad)

    one = ring_shift(send[1], 1)
    swapped = core_swap(hid_far)
    hid = [added(hid_near[i], swapped[i]) for i in range(4)]
    kept_a, kept_b, one, outputs, *later = lax.optimization_barrier((kept_a, kept_b, one, outputs, send[2], send[3]))
    two, three = ring_shift(later[0], 2), ring_shift(later[1], 3)
    kept_a, away_a = halves(kept_a, y, 2)
    kept_b, away_b = halves(kept_b, x, 2)
    kept_a = added(kept_a, plane_shift(away_a, 2))
    kept_b = added(kept_b, plane_shift(away_b, 1))
    kept = jnp.concatenate([kept_a, kept_b])
    *hid, kept, two, three = lax.optimization_barrier((*hid, kept, two, three))
    moved = [plane_shift(hid[step], step) for step in (1, 2, 3)]
    *moved, mine = lax.optimization_barrier((*moved, send[0]))
    big_sums = lax.psum_scatter(kept, "z", scatter_dimension=0, tiled=True)[0]
    grad_home = pl.pallas_call(
        norm_kernel,
        in_specs=[smem] + [vmem] * 7,
        out_specs=[vmem] * 4,
        out_shape=[jax.ShapeDtypeStruct((4, 8, width), bf16)] * 4,
        scratch_shapes=[pltpu.VMEM((4, 4, 8, width), f32)],
        compiler_params=limit,
        cost_estimate=pl.CostEstimate(flops=2_000_000_000, bytes_accessed=2_500_000, transcendentals=128),
        name="norm",
    )(info, hid[0], *moved, x_rows, grad_mid, gain_one)
    sums = pl.pallas_call(
        fold_kernel,
        in_specs=[vmem] * 4,
        out_specs=vmem,
        out_shape=jax.ShapeDtypeStruct((8, 48, 480), bf16),
        scratch_shapes=[pltpu.VMEM((8, 480), f32)],
        compiler_params=limit,
        cost_estimate=pl.CostEstimate(flops=2_000_000_000, bytes_accessed=1_600_000, transcendentals=0),
        name="fold",
    )(mine, one, two, three)
    sums = lax.all_to_all(sums, ("y", "core", "x"), split_axis=0, concat_axis=0, tiled=True)
    rows_shape = [jax.ShapeDtypeStruct((40, width), f32)] * 3
    qkv_sums = pl.pallas_call(
        spread_kernel, in_specs=[vmem], out_specs=[vmem] * 3, out_shape=rows_shape, compiler_params=limit, name="spread"
    )(sums)
    big_sums = pl.pallas_call(
        widen_kernel, in_specs=[vmem], out_specs=[vmem] * 3, out_shape=rows_shape, compiler_params=limit, name="widen"
    )(big_sums)
    line_sums = jnp.sum(sums[:, 40, :120].astype(f32), axis=0).reshape(3, 40)
    scale_low = query_scale.astype(bf16).astype(f32)
    scale_sum = LOG2E / math.sqrt(HD) * jax.nn.sigmoid(scale_low) * line_sums[2]
    grad_home = [grad_home[0]] + [ring_shift(grad_home[k], k) for k in (1, 2, 3)]
    grad_home = by_source(grad_home, z, 0).reshape(16, 8, width)

    return (
        outputs, grad_home, qkv_sums[0], qkv_sums[1], qkv_sums[2],
        big_sums[0], big_sums[1], big_sums[2], line_sums[0], line_sums[1], scale_sum,
    )


def solution(mesh):
    names = ("dp", "ctx")
    body = per_device
    if dict(mesh.shape) == {"dp": 16, "ctx": 2}:
        mesh = Mesh(mesh.devices.reshape(4, 2, 2, 2), ("z", "y", "core", "x"))
        names = mesh.axis_names
        body = planes
    seq, mat, line = P(None, names, None), P(names, None), P(names)
    return jax.shard_map(
        body,
        mesh=mesh,
        in_specs=(seq,) * 2 + (mat,) * 6 + (line,) * 3 + (P(), P()),
        out_specs=(seq,) * 2 + (mat,) * 6 + (line,) * 3,
        check_vma=False,
    )
```

```python
import math

import jax
import jax.numpy as jnp
from jax import lax
from jax.experimental import pallas as pl
from jax.experimental.pallas import tpu as pltpu
from jax.sharding import Mesh, PartitionSpec as P

H = 16
HD = 80


def mult_trans(left, right):
    return lax.dot_general(
        left, right, (((1,), (1,)), ((), ())), preferred_element_type=jnp.float32
    )


def trans_mult(left, right):
    return lax.dot_general(
        left, right, (((0,), (0,)), ((), ())), preferred_element_type=jnp.float32
    )


def position_of(index, local_rows, piece_rows, groups):
    column = index // local_rows
    within = index % local_rows
    return (within // piece_rows * groups + column) * piece_rows + within % piece_rows


def norm_back(grad_hidden, normed, inverse, gain_value):
    grad_normed = grad_hidden * gain_value
    return inverse * (grad_normed - normed * jnp.mean(grad_normed * normed, axis=1, keepdims=True))


def per_device(
    inputs,
    cotangent,
    w_query,
    w_key,
    w_value,
    w_output,
    w_up,
    w_down,
    attn_gain,
    mlp_gain,
    query_scale,
    deal,
    lengths,
):
    groups = lax.axis_size("ctx")
    group_index = lax.axis_index("dp")
    ctx_index = lax.axis_index("ctx")
    head_count = H
    head_dim = HD
    piece_rows = inputs.shape[1]
    seq_numbers = jnp.arange(inputs.shape[0], dtype=jnp.int32)
    seq_lengths = jnp.sum(
        jnp.where(deal[None, :] == seq_numbers[:, None], lengths[None, :], 0), axis=1
    )
    local_in, local_cot = (
        lax.all_to_all(inputs, "dp", split_axis=0, concat_axis=1, tiled=True),
        lax.all_to_all(cotangent, "dp", split_axis=0, concat_axis=1, tiled=True),
    )
    seq_count, local_rows, model_width = local_in.shape
    padded = local_rows * groups
    token_count = seq_count * local_rows
    my_lengths = lax.dynamic_slice_in_dim(seq_lengths, group_index * seq_count, seq_count, 0)
    query_pos = position_of(
        ctx_index * local_rows + jnp.arange(local_rows, dtype=jnp.int32),
        local_rows,
        piece_rows,
        groups,
    )
    flat_in = local_in.reshape(token_count, model_width).astype(jnp.float32)
    flat_cot = local_cot.reshape(token_count, model_width)
    lowered = (
        w_query.astype(jnp.bfloat16),
        w_key.astype(jnp.bfloat16),
        w_value.astype(jnp.bfloat16),
        w_output.astype(jnp.bfloat16),
        w_up.astype(jnp.bfloat16),
        w_down.astype(jnp.bfloat16),
        attn_gain.astype(jnp.bfloat16),
        mlp_gain.astype(jnp.bfloat16),
        query_scale.astype(jnp.bfloat16),
    )
    gathered = (
        lax.all_gather(lowered[0], ("dp", "ctx"), axis=0, tiled=True),
        lax.all_gather(lowered[1], ("dp", "ctx"), axis=0, tiled=True),
        lax.all_gather(lowered[2], ("dp", "ctx"), axis=0, tiled=True),
        lax.all_gather(lowered[3], ("dp", "ctx"), axis=0, tiled=True),
        lax.all_gather(lowered[4], ("dp", "ctx"), axis=0, tiled=True),
        lax.all_gather(lowered[5], ("dp", "ctx"), axis=0, tiled=True),
        lax.all_gather(lowered[6], ("dp", "ctx"), axis=0, tiled=True),
        lax.all_gather(lowered[7], ("dp", "ctx"), axis=0, tiled=True),
        lax.all_gather(lowered[8], ("dp", "ctx"), axis=0, tiled=True),
    )
    (
        query_full,
        key_full,
        value_full,
        output_full,
        up_full,
        down_full,
        gain_one,
        gain_two,
        scale_raw,
    ) = gathered
    inv_one = lax.rsqrt(jnp.mean(flat_in * flat_in, axis=1, keepdims=True) + 1e-06)
    normed_one = flat_in * inv_one
    hidden_one = (normed_one * gain_one.astype(jnp.float32)).astype(jnp.bfloat16)
    scale_param = scale_raw.astype(jnp.float32)
    query_mult = 1.442695041 / math.sqrt(head_dim) * jax.nn.softplus(scale_param)
    query_pre = jnp.dot(hidden_one, query_full, preferred_element_type=jnp.float32)
    queries = (query_pre * query_mult).astype(jnp.bfloat16)
    keys_local = jnp.dot(hidden_one, key_full, preferred_element_type=jnp.float32).astype(
        jnp.bfloat16
    )
    values_local = jnp.dot(hidden_one, value_full, preferred_element_type=jnp.float32).astype(
        jnp.bfloat16
    )
    four_shape = (seq_count, local_rows, head_count, head_dim)
    query_four = queries.reshape(four_shape)
    keys_three = keys_local.reshape(seq_count, local_rows, model_width)
    values_three = values_local.reshape(seq_count, local_rows, model_width)

    def live_between(row_pos, key_pos):
        allowed = (key_pos[None, None, :] <= row_pos[None, :, None]) & (
            key_pos[None, None, :] < my_lengths[:, None, None]
        )
        return allowed[:, :, None, :]

    def live_mask(key_pos):
        return live_between(query_pos, key_pos)

    def attend_block(state_now, key_block, value_block, first_row):
        run_max, run_sum, run_acc = state_now
        block_len = key_block.shape[1]
        key_pos = position_of(
            first_row + jnp.arange(block_len, dtype=jnp.int32), local_rows, piece_rows, groups
        )
        key_four = key_block.reshape(seq_count, block_len, head_count, head_dim)
        value_four = value_block.reshape(seq_count, block_len, head_count, head_dim)
        scores = jnp.einsum(
            "srhd,skhd->srhk", query_four, key_four, preferred_element_type=jnp.float32
        )
        allowed = live_mask(key_pos)
        masked = jnp.where(allowed, scores, -1e30)
        new_max = jnp.maximum(run_max, jnp.max(masked, axis=3))
        weights_now = jnp.exp(jnp.where(allowed, masked - new_max[..., None], -1e30))
        factor = jnp.exp(run_max - new_max)
        new_sum = run_sum * factor + jnp.sum(weights_now, axis=3)
        added = jnp.einsum(
            "srhk,skhd->srhd",
            weights_now.astype(jnp.bfloat16),
            value_four,
            preferred_element_type=jnp.float32,
        )
        return (new_max, new_sum, run_acc * factor[..., None] + added)

    start_state = (
        jnp.full((seq_count, local_rows, head_count), -1e30, jnp.float32),
        jnp.zeros((seq_count, local_rows, head_count), jnp.float32),
        jnp.zeros(four_shape, jnp.float32),
    )
    key_piece = lax.all_gather(keys_three, "ctx", axis=1, tiled=True)
    value_piece = lax.all_gather(values_three, "ctx", axis=1, tiled=True)
    piece_len = key_piece.shape[1]
    fold_block_len = 512 if piece_len % 512 == 0 else piece_len

    def one_block(state_now, block_index):
        offset = block_index * fold_block_len
        key_block = lax.dynamic_slice_in_dim(key_piece, offset, fold_block_len, 1)
        value_block = lax.dynamic_slice_in_dim(value_piece, offset, fold_block_len, 1)
        return (attend_block(state_now, key_block, value_block, offset), None)

    result_state, unused = lax.scan(
        one_block, start_state, jnp.arange(piece_len // fold_block_len, dtype=jnp.int32)
    )
    run_max, run_sum, run_acc = result_state
    log_total = run_max + jnp.log(run_sum)
    attn_exact = run_acc / run_sum[..., None]
    attended = attn_exact.reshape(token_count, model_width).astype(jnp.bfloat16)
    middle = flat_in + jnp.dot(attended, output_full, preferred_element_type=jnp.float32)
    inv_two = lax.rsqrt(jnp.mean(middle * middle, axis=1, keepdims=True) + 1e-06)
    normed_two = middle * inv_two
    hidden_two = (normed_two * gain_two.astype(jnp.float32)).astype(jnp.bfloat16)
    up_pre = jnp.dot(hidden_two, up_full, preferred_element_type=jnp.float32)
    active = jax.nn.silu(up_pre).astype(jnp.bfloat16)
    result = (middle + jnp.dot(active, down_full, preferred_element_type=jnp.float32)).astype(
        jnp.bfloat16
    )
    back_weights = (
        lax.all_gather(lowered[0], ("dp", "ctx"), axis=0, tiled=True),
        lax.all_gather(lowered[1], ("dp", "ctx"), axis=0, tiled=True),
        lax.all_gather(lowered[2], ("dp", "ctx"), axis=0, tiled=True),
        lax.all_gather(lowered[3], ("dp", "ctx"), axis=0, tiled=True),
        lax.all_gather(lowered[4], ("dp", "ctx"), axis=0, tiled=True),
        lax.all_gather(lowered[5], ("dp", "ctx"), axis=0, tiled=True),
        lax.all_gather(lowered[6], ("dp", "ctx"), axis=0, tiled=True),
        lax.all_gather(lowered[7], ("dp", "ctx"), axis=0, tiled=True),
        lax.all_gather(lowered[8], ("dp", "ctx"), axis=0, tiled=True),
    )
    (
        query_back,
        key_back,
        value_back,
        output_back,
        up_back,
        down_back,
        gain_one_back,
        gain_two_back,
        scale_back,
    ) = back_weights
    cot_wide = flat_cot.astype(jnp.float32)
    grad_down = trans_mult(active, flat_cot)
    grad_active = mult_trans(flat_cot, down_back)
    sigma_up = jax.nn.sigmoid(up_pre)
    grad_up_pre = (grad_active * sigma_up * (1.0 + up_pre * (1.0 - sigma_up))).astype(jnp.bfloat16)
    grad_up = trans_mult(hidden_two, grad_up_pre)
    grad_hidden_two = mult_trans(grad_up_pre, up_back)
    grad_gain_two = jnp.sum(grad_hidden_two * normed_two, axis=0)
    grad_middle = cot_wide + norm_back(
        grad_hidden_two, normed_two, inv_two, gain_two_back.astype(jnp.float32)
    )
    grad_middle_low = grad_middle.astype(jnp.bfloat16)
    grad_output = trans_mult(attended, grad_middle_low)
    grad_attended = mult_trans(grad_middle_low, output_back).astype(jnp.bfloat16)
    grad_att_four = grad_attended.reshape(four_shape)
    delta_rows = jnp.sum(grad_att_four.astype(jnp.float32) * attn_exact, axis=3)
    key_all, value_all = (
        lax.all_gather(keys_three, "ctx", axis=1, tiled=True),
        lax.all_gather(values_three, "ctx", axis=1, tiled=True),
    )
    block_len = min(512, padded)

    def back_block(block_index, state_now):
        grad_query, grad_key_all, grad_value_all = state_now
        offset = block_index * block_len
        key_block = lax.dynamic_slice_in_dim(key_all, offset, block_len, 1).reshape(
            seq_count, block_len, head_count, head_dim
        )
        value_block = lax.dynamic_slice_in_dim(value_all, offset, block_len, 1).reshape(
            seq_count, block_len, head_count, head_dim
        )
        key_pos = position_of(
            offset + jnp.arange(block_len, dtype=jnp.int32), local_rows, piece_rows, groups
        )
        scores = jnp.einsum(
            "srhd,skhd->srhk", query_four, key_block, preferred_element_type=jnp.float32
        )
        probs = jnp.exp(jnp.where(live_mask(key_pos), scores - log_total[..., None], -1e30))
        grad_value_block = jnp.einsum(
            "srhk,srhd->skhd",
            probs.astype(jnp.bfloat16),
            grad_att_four,
            preferred_element_type=jnp.float32,
        )
        grad_probs = jnp.einsum(
            "srhd,skhd->srhk", grad_att_four, value_block, preferred_element_type=jnp.float32
        )
        grad_scores = (probs * (grad_probs - delta_rows[..., None])).astype(jnp.bfloat16)
        grad_query = grad_query + jnp.einsum(
            "srhk,skhd->srhd", grad_scores, key_block, preferred_element_type=jnp.float32
        )
        grad_key_block = jnp.einsum(
            "srhk,srhd->skhd", grad_scores, query_four, preferred_element_type=jnp.float32
        )
        grad_key_all = lax.dynamic_update_slice_in_dim(
            grad_key_all, grad_key_block.reshape(seq_count, block_len, model_width), offset, 1
        )
        grad_value_all = lax.dynamic_update_slice_in_dim(
            grad_value_all, grad_value_block.reshape(seq_count, block_len, model_width), offset, 1
        )
        return (grad_query, grad_key_all, grad_value_all)

    zero_all = jnp.zeros((seq_count, padded, model_width), jnp.float32)
    grad_query, grad_key_all, grad_value_all = lax.fori_loop(
        0, padded // block_len, back_block, (jnp.zeros(four_shape, jnp.float32), zero_all, zero_all)
    )
    grad_key_mine, grad_value_mine = (
        lax.psum_scatter(
            grad_key_all.astype(jnp.bfloat16), "ctx", scatter_dimension=1, tiled=True
        ).astype(jnp.float32),
        lax.psum_scatter(
            grad_value_all.astype(jnp.bfloat16), "ctx", scatter_dimension=1, tiled=True
        ).astype(jnp.float32),
    )
    grad_query_flat = grad_query.reshape(token_count, model_width)
    grad_query_pre = (grad_query_flat * query_mult).astype(jnp.bfloat16)
    grad_scale = (
        1.442695041
        / math.sqrt(head_dim)
        * jax.nn.sigmoid(scale_back.astype(jnp.float32))
        * jnp.sum(grad_query_flat * query_pre, axis=0)
    )
    grad_key_low = grad_key_mine.reshape(token_count, model_width).astype(jnp.bfloat16)
    grad_value_low = grad_value_mine.reshape(token_count, model_width).astype(jnp.bfloat16)
    grad_wq = trans_mult(hidden_one, grad_query_pre)
    grad_wk = trans_mult(hidden_one, grad_key_low)
    grad_wv = trans_mult(hidden_one, grad_value_low)
    grad_hidden_one = (
        mult_trans(grad_query_pre, query_back)
        + mult_trans(grad_key_low, key_back)
        + mult_trans(grad_value_low, value_back)
    )
    grad_gain_one = jnp.sum(grad_hidden_one * normed_one, axis=0)
    grad_in = grad_middle + norm_back(
        grad_hidden_one, normed_one, inv_one, gain_one_back.astype(jnp.float32)
    )
    matrix_stack = jnp.stack([grad_wq, grad_wk, grad_wv, grad_output, grad_up, grad_down], axis=0)
    vector_stack = jnp.stack([grad_gain_one, grad_gain_two, grad_scale], axis=0)
    matrix_sums, vector_sums = (
        lax.psum_scatter(matrix_stack, ("dp", "ctx"), scatter_dimension=1, tiled=True),
        lax.psum_scatter(vector_stack, ("dp", "ctx"), scatter_dimension=1, tiled=True),
    )
    out_local = result.reshape(seq_count, local_rows, model_width)
    grad_local = grad_in.astype(jnp.bfloat16).reshape(seq_count, local_rows, model_width)
    back_out, back_grad = (
        lax.all_to_all(out_local, "dp", split_axis=1, concat_axis=0, tiled=True),
        lax.all_to_all(grad_local, "dp", split_axis=1, concat_axis=0, tiled=True),
    )
    return (
        back_out,
        back_grad,
        matrix_sums[0],
        matrix_sums[1],
        matrix_sums[2],
        matrix_sums[3],
        matrix_sums[4],
        matrix_sums[5],
        vector_sums[0],
        vector_sums[1],
        vector_sums[2],
    )


LOG2E = 1.442695041
CODES = (0, 1, 4, 5)


def plane_shift(value, step):
    if step == 1:
        return lax.ppermute(value, "x", [(0, 1), (1, 0)])
    if step == 2:
        return lax.ppermute(value, "y", [(0, 1), (1, 0)])
    return lax.ppermute(value, ("y", "x"), [(0, 3), (1, 2), (2, 1), (3, 0)])


def core_swap(value):
    return lax.ppermute(value, "core", [(0, 1), (1, 0)])


def ring_shift(value, step):
    return lax.ppermute(value, "z", [(i, (i + step) % 4) for i in range(4)])


def pick(array, index):
    return lax.dynamic_index_in_dim(array, index, 0, keepdims=False)


def by_source(pieces, z_index, axis):
    pieces = [jnp.expand_dims(item, axis) for item in pieces]
    shape = [1] * pieces[0].ndim
    shape[axis] = 4
    hop = ((z_index - jnp.arange(4, dtype=jnp.int32)) % 4).reshape(shape)
    made = pieces[0]
    for k in (1, 2, 3):
        made = jnp.where(hop == k, pieces[k], made)
    return made


def pair(mine, other, index, axis):
    shape = [1] * (mine.ndim + 1)
    shape[axis] = 2
    slot = jnp.arange(2, dtype=jnp.int32).reshape(shape)
    return jnp.where(slot == index, jnp.expand_dims(mine, axis), jnp.expand_dims(other, axis))


def row_positions(shape, dim, plane_index):
    row = lax.broadcasted_iota(jnp.int32, shape, dim)
    chip = (row // 32) % 4
    code = (chip % 2) + 4 * (chip // 2) + 2 * (row // 128)
    return 64 * ((row % 32) // 8) + 8 * (plane_index ^ code) + row % 8


def live_pairs(info_ref, seq):
    shape = (256, 256)
    query_pos = row_positions(shape, 0, info_ref[1])
    key_pos = row_positions(shape, 1, info_ref[1])
    return (key_pos <= query_pos) & (key_pos < info_ref[2 + seq])


def block_rows(near_ref, far_ref):
    return jnp.concatenate([near_ref[...], far_ref[...]], axis=0).reshape(256, near_ref.shape[2])


def soft_probs(query, key, live):
    scores = mult_trans(query, key)
    scores = jnp.where(live, scores, -1e30)
    top = jnp.max(scores, axis=1, keepdims=True)
    weights = jnp.where(live, jnp.exp(scores - top), 0.0)
    return weights / jnp.sum(weights, axis=1, keepdims=True)


def attend_kernel(
    info_ref, near_ref, far_ref, gain_ref, mult_ref, w_ref, pre_ref, att_ref
):
    seq = pl.program_id(0)
    live = live_pairs(info_ref, seq)
    wide = block_rows(near_ref, far_ref).astype(jnp.float32)
    inverse = lax.rsqrt(jnp.mean(wide * wide, axis=1, keepdims=True) + 1e-06)
    hidden = (wide * inverse * gain_ref[...]).astype(jnp.bfloat16)
    pre = jnp.dot(hidden, w_ref[...], preferred_element_type=jnp.float32)
    pre_ref[...] = pre.reshape(2, 4, 32, 480)
    query = (pre[:, 0:160] * mult_ref[...]).astype(jnp.bfloat16)
    key = pre[:, 160:320].astype(jnp.bfloat16)
    value = pre[:, 320:480].astype(jnp.bfloat16)
    heads = []
    for head in range(2):
        part = slice(80 * head, 80 * head + 80)
        probs = soft_probs(query[:, part], key[:, part], live).astype(jnp.bfloat16)
        heads.append(jnp.dot(probs, value[:, part], preferred_element_type=jnp.float32))
    att = jnp.concatenate(heads, axis=1).astype(jnp.bfloat16).reshape(2, 4, 32, 160)
    for chip in range(4):
        for core in range(2):
            att_ref[chip, core] = att[core, chip]


def attend_back_kernel(
    info_ref, near_ref, far_ref, gain_ref, mult_ref, w_ref, pre_ref, grad_near, grad_far, gain_two_ref,
    hid_near, hid_far, send_0, send_1, send_2, send_3, w_acc, gain_acc, scale_acc, lines,
):
    seq = pl.program_id(0)

    @pl.when(seq == 0)
    def _():
        w_acc[...] = jnp.zeros_like(w_acc)
        gain_acc[...] = jnp.zeros_like(gain_acc)
        scale_acc[...] = jnp.zeros_like(scale_acc)

    live = live_pairs(info_ref, seq)
    wide = block_rows(near_ref, far_ref).astype(jnp.float32)
    inverse = lax.rsqrt(jnp.mean(wide * wide, axis=1, keepdims=True) + 1e-06)
    normed = wide * inverse
    hidden = (normed * gain_ref[...]).astype(jnp.bfloat16)
    pre = pre_ref[...].reshape(256, 480)
    mult = mult_ref[...]
    query = (pre[:, 0:160] * mult).astype(jnp.bfloat16)
    key = pre[:, 160:320].astype(jnp.bfloat16)
    value = pre[:, 320:480].astype(jnp.bfloat16)
    grad_att = jnp.concatenate([grad_near[:, 0], grad_far[:, 0]], axis=0).reshape(256, 160)
    grad_q, grad_k, grad_v = [], [], []
    for head in range(2):
        part = slice(80 * head, 80 * head + 80)
        probs = soft_probs(query[:, part], key[:, part], live)
        grad_probs = mult_trans(grad_att[:, part], value[:, part])
        delta = jnp.sum(probs * grad_probs, axis=1, keepdims=True)
        grad_scores = (probs * (grad_probs - delta)).astype(jnp.bfloat16)
        grad_v.append(trans_mult(probs.astype(jnp.bfloat16), grad_att[:, part]))
        grad_q.append(jnp.dot(grad_scores, key[:, part], preferred_element_type=jnp.float32))
        grad_k.append(trans_mult(grad_scores, query[:, part]))
    grad_query = jnp.concatenate(grad_q, axis=1)
    scale_acc[...] += jnp.sum(grad_query * pre[:, 0:160], axis=0, keepdims=True)
    joined = jnp.concatenate([grad_query * mult] + grad_k + grad_v, axis=1).astype(jnp.bfloat16)
    w_acc[...] += trans_mult(hidden, joined)
    grad_hidden = mult_trans(joined, w_ref[...])
    gain_acc[...] += jnp.sum(grad_hidden * normed, axis=0, keepdims=True)
    low = grad_hidden.astype(jnp.bfloat16).reshape(2, 4, 32, 1280)
    hid_near[...] = low[0]
    hid_far[...] = low[1]

    @pl.when(seq == 3)
    def _():
        lines[...] = jnp.zeros_like(lines)
        for which, source in enumerate((gain_acc, gain_two_ref)):
            for owner in range(32):
                lane = 120 * (owner % 4) + 40 * which
                lines[owner // 4, :, lane : lane + 40] = source[:, 40 * owner : 40 * owner + 40]
        for part in range(4):
            lane = 120 * part + 80
            lines[info_ref[1], :, lane : lane + 40] = scale_acc[:, 40 * part : 40 * part + 40]
        blank = jnp.zeros((14, 480), jnp.float32)
        for hop, send in enumerate((send_0, send_1, send_2, send_3)):
            target = (info_ref[0] + hop) & 3
            rows = w_acc[pl.ds(pl.multiple_of(target * 320, 320), 320), :]
            block = jnp.concatenate([rows, lines[2 * target], lines[2 * target + 1], blank], axis=0)
            send[...] = block.astype(jnp.bfloat16)


def block_index(z_index, y_index, core):
    return pl.ds(pl.multiple_of((4 * z_index + 2 * y_index + core) * 80, 80), 80)


def source_rows(info_ref, chip, core):
    source = info_ref[1] ^ (CODES[chip] + 2 * core)
    return pl.ds(pl.multiple_of(source * 160, 160), 160)


def feed_kernel(
    info_ref, x_ref, g_ref, atts, far_atts, gain_ref,
    near_rows, across_a, across_b, far_near_rows, far_across_a, far_across_b,
    out_ref, pack_ref, dmid_ref, datt_0, datt_1, datt_2, datt_3, gain_grad,
    weights, sems,
):
    y_index, core_index = info_ref[1] // 4, (info_ref[1] // 2) % 2
    copies = []
    for w in range(3):
        moved = []
        for core, own, others in (
            (core_index, near_rows, (across_a, across_b)),
            (1 - core_index, far_near_rows, (far_across_a, far_across_b)),
        ):
            for z_index in range(4):
                moved.append((own.at[z_index, w], z_index, y_index, core))
                moved.append((others[z_index // 2].at[z_index % 2, w], z_index, 1 - y_index, core))
        copies.append([
            pltpu.make_async_copy(src, weights.at[w, block_index(*place)], sems.at[w, i])
            for i, (src, *place) in enumerate(moved)
        ])
    for group in copies:
        for copy in group:
            copy.start()
    datts = (datt_0, datt_1, datt_2, datt_3)

    for copy in copies[0]:
        copy.wait()
    middle = x_ref[...].astype(jnp.float32)
    for chip in range(4):
        for core in range(2):
            middle += jnp.dot(
                (far_atts if core else atts)[chip, core], weights[0, source_rows(info_ref, chip, core), :],
                preferred_element_type=jnp.float32,
            )
    inverse = lax.rsqrt(jnp.mean(middle * middle, axis=1, keepdims=True) + 1e-06)
    normed = middle * inverse
    gain = gain_ref[...]
    hidden = (normed * gain).astype(jnp.bfloat16)
    pack_ref[1] = hidden
    for copy in copies[1]:
        copy.wait()
    up = jnp.dot(hidden, weights[1], preferred_element_type=jnp.float32)
    sigma = jax.nn.sigmoid(up)
    active = (up * sigma).astype(jnp.bfloat16)
    pack_ref[0] = active
    for copy in copies[2]:
        copy.wait()
    down = jnp.dot(active, weights[2], preferred_element_type=jnp.float32)
    result = middle + down
    for seq in range(4):
        for plane_z in range(4):
            row = 32 * seq + 8 * plane_z
            out_ref[plane_z, seq] = result[row : row + 8].astype(jnp.bfloat16)
    cot = g_ref[...]
    grad_act = mult_trans(cot, weights[2])
    grad_up = (grad_act * sigma * (1.0 + up * (1.0 - sigma))).astype(jnp.bfloat16)
    pack_ref[2] = grad_up
    grad_hidden = mult_trans(grad_up, weights[1])
    gain_grad[...] = jnp.sum(grad_hidden * normed, axis=0, keepdims=True)
    grad_mid = cot.astype(jnp.float32) + norm_back(grad_hidden, normed, inverse, gain)
    dmid_ref[...] = grad_mid
    low = grad_mid.astype(jnp.bfloat16)
    pack_ref[3] = low
    for chip in range(4):
        for core in range(2):
            datts[chip][core] = mult_trans(low, weights[0, source_rows(info_ref, chip, core), :]).astype(jnp.bfloat16)


def grads_kernel(
    info_ref, pack_ref, far_pack, atts, far_atts, cot_ref, far_cot, half_a, kept_b, away_b, stage, sems
):
    y_index, core_index = info_ref[1] // 4, (info_ref[1] // 2) % 2
    copies = []

    def leave(w):
        for half in range(2):
            targets = [(half, row, half_a.at[half, w, row]) for row in range(2)]
            targets += [(2 + half, y_index, kept_b.at[half, w]), (2 + half, 1 - y_index, away_b.at[half, w])]
            for i, (z_index, row, target) in enumerate(targets):
                copy = pltpu.make_async_copy(
                    stage.at[w, block_index(z_index, row, core_index)], target, sems.at[w, 4 * half + i]
                )
                copy.start()
                copies.append(copy)

    def both(near, far):
        return jnp.concatenate([near, far], axis=0)

    cots = both(cot_ref[...], far_cot[...])
    for w, left, grads in ((2, 0, cots), (1, 1, both(pack_ref[2], far_pack[2]))):
        for chunk in range(5):
            part = slice(256 * chunk, 256 * chunk + 256)
            acts = both(pack_ref[left, :, part], far_pack[left, :, part])
            stage[w, part, :] = trans_mult(acts, grads).astype(jnp.bfloat16)
        leave(w)
    grads = both(pack_ref[3], far_pack[3])
    for chip in range(4):
        for core in range(2):
            near, far = (far_atts, far_atts) if core else (atts, atts)
            att = both(near[chip, core], far[chip, 1 - core])
            stage[0, source_rows(info_ref, chip, core), :] = trans_mult(att, grads).astype(jnp.bfloat16)
    leave(0)
    for copy in copies:
        copy.wait()


def meet_kernel(info_ref, half_a, from_a, half_b, from_b, keep_a, away_a, keep_b, away_b):
    y_index, x_index = info_ref[1] // 4, info_ref[1] % 2
    for half in range(2):
        for w in range(3):
            for row, out in ((y_index, keep_a), (1 - y_index, away_a)):
                out[half, w] = sum_low(half_a[half, w, row, x_index], from_a[half, w, row])
            for row, out in ((x_index, keep_b), (1 - x_index, away_b)):
                out[half, w] = sum_low(half_b[half, w, row], from_b[half, w, row])


def join_kernel(keep_a, from_a, keep_b, from_b, out_ref):
    for half in range(2):
        for w in range(3):
            out_ref[half, w] = sum_low(keep_a[half, w], from_a[half, w])
            out_ref[2 + half, w] = sum_low(keep_b[half, w], from_b[half, w])


def sum_low(left, right):
    return (left.astype(jnp.float32) + right.astype(jnp.float32)).astype(jnp.bfloat16)


def norm_kernel(info_ref, hid_0, hid_1, hid_2, hid_3, x_ref, dmid_ref, gain_ref, out_0, out_1, out_2, out_3, rows):
    grad = hid_0[...].astype(jnp.float32)
    for item in (hid_1, hid_2, hid_3):
        grad += item[...].astype(jnp.float32)
    wide = x_ref[...].astype(jnp.float32)
    inverse = lax.rsqrt(jnp.mean(wide * wide, axis=1, keepdims=True) + 1e-06)
    grad = dmid_ref[...] + norm_back(grad, wide * inverse, inverse, gain_ref[...])
    for seq in range(4):
        for plane_z in range(4):
            row = 32 * seq + 8 * plane_z
            rows[plane_z, seq] = grad[row : row + 8]
    for hop, out in enumerate((out_0, out_1, out_2, out_3)):
        out[...] = rows[(info_ref[0] + hop) & 3].astype(jnp.bfloat16)


def fold_kernel(part_0, part_1, part_2, part_3, out_ref, line):
    total = part_0[...].astype(jnp.float32)
    for item in (part_1, part_2, part_3):
        total += item[...].astype(jnp.float32)
    line[...] = jnp.zeros_like(line)
    for owner in range(8):
        lane = 120 * (owner % 4)
        line[0:1, 0:120] = total[320 + owner // 4 : 321 + owner // 4, lane : lane + 120]
        block = jnp.concatenate([total[40 * owner : 40 * owner + 40], line[...]], axis=0)
        out_ref[owner] = block.astype(jnp.bfloat16)


def spread_kernel(in_ref, *outs):
    for which, out in enumerate(outs):
        for owner in range(8):
            part = in_ref[owner, 0:40, 160 * which : 160 * which + 160]
            out[:, 160 * owner : 160 * owner + 160] = part.astype(jnp.float32)


def widen_kernel(in_ref, *outs):
    for which, out in enumerate(outs):
        out[...] = in_ref[which].astype(jnp.float32)


def whole(shape):
    return pl.BlockSpec(shape, lambda *_: (0,) * len(shape))


def seq_block(*lead, width):
    count = len(lead)
    return pl.BlockSpec((*lead, 32, width), lambda s, info: (*(0,) * count, s, 0))


def planes(
    inputs, cotangent, w_query, w_key, w_value, w_output, w_up, w_down,
    attn_gain, mlp_gain, query_scale, deal, lengths,
):
    f32, bf16 = jnp.float32, jnp.bfloat16
    z, y, c, x = (lax.axis_index(name) for name in ("z", "y", "core", "x"))
    plane = 4 * y + 2 * c + x
    width = 1280
    seqs = jnp.arange(16, dtype=jnp.int32)
    seq_lengths = jnp.sum(jnp.where(deal[None, :] == seqs[:, None], lengths[None, :], 0), axis=1)
    my_lengths = lax.dynamic_slice_in_dim(seq_lengths, 4 * z, 4, 0)
    info = jnp.concatenate([jnp.stack([z, plane]), my_lengths]).astype(jnp.int32)

    vec = jnp.concatenate([attn_gain, mlp_gain, query_scale]).astype(bf16)
    vec_block = jnp.zeros((1, 8, width), bf16).at[0, 0, :120].set(vec)
    in_four = inputs.reshape(4, 4, 8, width)
    sent = [jnp.concatenate([pick(in_four, (z + k) % 4), vec_block]) for k in range(4)]
    qkv = jnp.stack([w_query, w_key, w_value]).astype(bf16)
    *sent, qkv = lax.optimization_barrier((*sent, qkv))
    got = [sent[0]] + [ring_shift(sent[k], k) for k in (1, 2, 3)]
    x_rows = by_source([item[:4] for item in got], z, 1).reshape(128, width)
    vec_rows = by_source([item[4, 0] for item in got], z, 0)
    vec_rows = jnp.concatenate([vec_rows, jnp.zeros((4, width), bf16)])
    own = jnp.concatenate([x_rows, vec_rows])

    big = jnp.stack([w_output, w_up, w_down]).astype(bf16)
    big = lax.all_gather(big, "z", axis=0)

    qkv = qkv.reshape(3, 40, 8, 160).transpose(2, 1, 0, 3).reshape(8, 40, 480)
    qkv = lax.all_to_all(qkv, ("y", "core", "x"), split_axis=0, concat_axis=0, tiled=True)
    own, qkv = lax.optimization_barrier((own, qkv.reshape(320, 480)))
    w_qkv = lax.all_gather(qkv, "z", axis=0, tiled=True)
    near = jnp.stack([own] + [plane_shift(own, step) for step in (1, 2, 3)])
    big, near = lax.optimization_barrier((big, near))
    far = core_swap(near)
    beside, across = plane_shift(big, 1), plane_shift(big, 2)
    relay_a, relay_b = beside[:2], across[2:]
    relay_a, relay_b, cotangent = lax.optimization_barrier((relay_a, relay_b, cotangent))
    across_a, across_b = plane_shift(relay_a, 2), plane_shift(relay_b, 1)

    vecs = jnp.stack([near[:, 128:132, :120], far[:, 128:132, :120]])
    vecs = vecs.astype(f32).reshape(2, 2, 2, 4, 120)
    vecs = jnp.where(c == 0, vecs, vecs[::-1])
    vecs = jnp.where(y == 0, vecs, vecs[:, ::-1])
    vecs = jnp.where(x == 0, vecs, vecs[:, :, ::-1])
    vecs = vecs.reshape(2, 2, 2, 4, 3, 40).transpose(4, 3, 1, 0, 2, 5).reshape(3, width)
    gain_one, gain_two = vecs[0:1], vecs[1:2]
    my_scale = lax.dynamic_slice_in_dim(vecs[2:3], 160 * plane, 160, 1)
    query_mult = LOG2E / math.sqrt(HD) * jax.nn.softplus(my_scale)

    limit = pltpu.CompilerParams(vmem_limit_bytes=50 * 1024 * 1024)
    pre, att_made = pl.pallas_call(
        attend_kernel,
        grid_spec=pltpu.PrefetchScalarGridSpec(
            num_scalar_prefetch=1,
            grid=(4,),
            in_specs=[
                seq_block(4, width=width), seq_block(4, width=width),
                whole((1, width)), whole((1, 160)), whole((width, 480)),
            ],
            out_specs=[seq_block(2, 4, width=480), seq_block(4, 2, width=160)],
        ),
        out_shape=[
            jax.ShapeDtypeStruct((2, 4, 128, 480), f32),
            jax.ShapeDtypeStruct((4, 2, 128, 160), bf16),
        ],
        compiler_params=limit,
        cost_estimate=pl.CostEstimate(flops=9_000_000_000, bytes_accessed=8_000_000, transcendentals=600_000),
        name="attend",
    )(info, near, far, gain_one, query_mult, w_qkv)

    cot_rows = lax.all_to_all(cotangent.reshape(4, 4, 8, width), "z", split_axis=0, concat_axis=0, tiled=True)
    near_rows = pair(big, beside, x, 2).reshape(4, 3, 80, width)
    att_made, near_rows, across_a, across_b, cot_rows = lax.optimization_barrier(
        (att_made, near_rows, across_a, across_b, cot_rows)
    )
    far_near_rows = core_swap(near_rows)
    atts = [att_made[0]] + [plane_shift(att_made[step], step) for step in (1, 2, 3)]
    atts = jnp.stack(atts)
    far_atts = core_swap(atts)
    across_a = pair(across[:2], across_a, x, 2).reshape(2, 3, 80, width)
    across_b = pair(across[2:], across_b, x, 2).reshape(2, 3, 80, width)
    far_across_a, far_across_b = core_swap(across_a), core_swap(across_b)
    cot_rows = cot_rows.transpose(1, 0, 2, 3).reshape(128, width)
    far_cot = core_swap(cot_rows)
    far_cot, far_atts, cot_rows = lax.optimization_barrier((far_cot, far_atts, cot_rows))
    datt_shape = jax.ShapeDtypeStruct((2, 128, 160), bf16)
    smem = pl.BlockSpec(memory_space=pltpu.SMEM)
    vmem = pl.BlockSpec(memory_space=pltpu.VMEM)
    hbm = pl.BlockSpec(memory_space=pl.ANY)
    out_rows, pack, grad_mid, *datts, gain_two_grad = pl.pallas_call(
        feed_kernel,
        in_specs=[smem] + [vmem] * 5 + [hbm] * 6,
        out_specs=[vmem] * 8,
        out_shape=[
            jax.ShapeDtypeStruct((4, 4, 8, width), bf16),
            jax.ShapeDtypeStruct((4, 128, width), bf16),
            jax.ShapeDtypeStruct((128, width), f32),
        ]
        + [datt_shape] * 4
        + [jax.ShapeDtypeStruct((1, width), f32)],
        scratch_shapes=[pltpu.VMEM((3, width, width), bf16), pltpu.SemaphoreType.DMA((3, 16))],
        compiler_params=limit,
        cost_estimate=pl.CostEstimate(flops=12_000_000_000, bytes_accessed=13_000_000, transcendentals=200_000),
        name="feed",
    )(info, x_rows, cot_rows, atts, far_atts, gain_two, near_rows, across_a, across_b, far_near_rows, far_across_a, far_across_b)

    back = [datts[0]] + [plane_shift(datts[step], step) for step in (1, 2, 3)]

    part_shape = jax.ShapeDtypeStruct((2, 3, 80, width), bf16)
    half_a, kept_b, away_b = pl.pallas_call(
        grads_kernel,
        in_specs=[smem] + [vmem] * 6,
        out_specs=[hbm] * 3,
        out_shape=[jax.ShapeDtypeStruct((2, 3, 2, 80, width), bf16), part_shape, part_shape],
        scratch_shapes=[pltpu.VMEM((3, width, width), bf16), pltpu.SemaphoreType.DMA((3, 8))],
        compiler_params=limit,
        cost_estimate=pl.CostEstimate(flops=6_000_000_000, bytes_accessed=8_000_000, transcendentals=0),
        name="grads",
    )(info, pack, core_swap(pack), atts, far_atts, cot_rows, far_cot)

    half_a, kept_b, away_b, *back = lax.optimization_barrier((half_a, kept_b, away_b, *back))
    half_a = half_a.reshape(2, 3, 2, 2, 40, width)
    away_a = lax.dynamic_index_in_dim(half_a, 1 - x, 3, keepdims=False)
    away_a, away_b, grad_atts = lax.optimization_barrier((away_a, away_b, jnp.stack(back)))
    from_a, from_b = plane_shift(away_a, 1), plane_shift(away_b, 2)
    hid_near, hid_far, *send = pl.pallas_call(
        attend_back_kernel,
        grid_spec=pltpu.PrefetchScalarGridSpec(
            num_scalar_prefetch=1,
            grid=(4,),
            in_specs=[
                seq_block(4, width=width), seq_block(4, width=width),
                whole((1, width)), whole((1, 160)), whole((width, 480)),
                seq_block(2, 4, width=480),
                *[pl.BlockSpec((4, 1, 32, 160), lambda s, info, core=core: (0, core, s, 0)) for core in range(2)],
                whole((1, width)),
            ],
            out_specs=[
                seq_block(4, width=width), seq_block(4, width=width),
                *[whole((336, 480))] * 4,
            ],
            scratch_shapes=[
                pltpu.VMEM((width, 480), f32), pltpu.VMEM((1, width), f32),
                pltpu.VMEM((1, 160), f32), pltpu.VMEM((8, 1, 480), f32),
            ],
        ),
        out_shape=[
            jax.ShapeDtypeStruct((4, 128, width), bf16),
            jax.ShapeDtypeStruct((4, 128, width), bf16),
            *[jax.ShapeDtypeStruct((336, 480), bf16)] * 4,
        ],
        compiler_params=limit,
        cost_estimate=pl.CostEstimate(flops=15_000_000_000, bytes_accessed=12_000_000, transcendentals=600_000),
        name="attend_back",
    )(info, near, far, gain_one, query_mult, w_qkv, pre, grad_atts, core_swap(grad_atts), gain_two_grad)

    *send, out_rows = lax.optimization_barrier((*send, out_rows))
    outputs = lax.all_to_all(out_rows, "z", split_axis=0, concat_axis=0, tiled=True).reshape(16, 8, width)
    one = ring_shift(send[1], 1)
    swapped = core_swap(hid_far)
    hid = [sum_low(hid_near[i], swapped[i]) for i in range(4)]
    from_a, from_b, one, outputs, *later = lax.optimization_barrier(
        (from_a, from_b, one, outputs, send[2], send[3])
    )
    two, three = ring_shift(later[0], 2), ring_shift(later[1], 3)
    split = (2, 3, 2, 40, width)
    keep_a, away_a, keep_b, away_b = pl.pallas_call(
        meet_kernel,
        in_specs=[smem] + [vmem] * 4,
        out_specs=[vmem] * 4,
        out_shape=[jax.ShapeDtypeStruct((2, 3, 40, width), bf16)] * 4,
        compiler_params=limit,
        cost_estimate=pl.CostEstimate(flops=3_000_000_000, bytes_accessed=8_000_000, transcendentals=0),
        name="meet",
    )(info, half_a, from_a, kept_b.reshape(split), from_b.reshape(split))
    kept = pl.pallas_call(
        join_kernel,
        in_specs=[vmem] * 4,
        out_specs=vmem,
        out_shape=jax.ShapeDtypeStruct((4, 3, 40, width), bf16),
        compiler_params=limit,
        cost_estimate=pl.CostEstimate(flops=2_000_000_000, bytes_accessed=4_000_000, transcendentals=0),
        name="join",
    )(keep_a, plane_shift(away_a, 2), keep_b, plane_shift(away_b, 1))
    *hid, kept, two, three = lax.optimization_barrier((*hid, kept, two, three))
    moved = [plane_shift(hid[step], step) for step in (1, 2, 3)]
    *moved, mine = lax.optimization_barrier((*moved, send[0]))
    big_sums = lax.psum_scatter(kept, "z", scatter_dimension=0, tiled=True)[0]
    grad_home = pl.pallas_call(
        norm_kernel,
        in_specs=[smem] + [vmem] * 7,
        out_specs=[vmem] * 4,
        out_shape=[jax.ShapeDtypeStruct((4, 8, width), bf16)] * 4,
        scratch_shapes=[pltpu.VMEM((4, 4, 8, width), f32)],
        compiler_params=limit,
        cost_estimate=pl.CostEstimate(flops=2_000_000_000, bytes_accessed=2_500_000, transcendentals=128),
        name="norm",
    )(info, hid[0], *moved, x_rows, grad_mid, gain_one)
    sums = pl.pallas_call(
        fold_kernel,
        in_specs=[vmem] * 4,
        out_specs=vmem,
        out_shape=jax.ShapeDtypeStruct((8, 48, 480), bf16),
        scratch_shapes=[pltpu.VMEM((8, 480), f32)],
        compiler_params=limit,
        cost_estimate=pl.CostEstimate(flops=2_000_000_000, bytes_accessed=1_600_000, transcendentals=0),
        name="fold",
    )(mine, one, two, three)
    sums = lax.all_to_all(sums, ("y", "core", "x"), split_axis=0, concat_axis=0, tiled=True)
    rows_shape = [jax.ShapeDtypeStruct((40, width), f32)] * 3
    qkv_sums = pl.pallas_call(
        spread_kernel, in_specs=[vmem], out_specs=[vmem] * 3, out_shape=rows_shape, compiler_params=limit, name="spread"
    )(sums)
    big_sums = pl.pallas_call(
        widen_kernel, in_specs=[vmem], out_specs=[vmem] * 3, out_shape=rows_shape, compiler_params=limit, name="widen"
    )(big_sums)
    line_sums = jnp.sum(sums[:, 40, :120].astype(f32), axis=0).reshape(3, 40)
    scale_low = query_scale.astype(bf16).astype(f32)
    scale_sum = LOG2E / math.sqrt(HD) * jax.nn.sigmoid(scale_low) * line_sums[2]
    grad_home = [grad_home[0]] + [ring_shift(grad_home[k], k) for k in (1, 2, 3)]
    grad_home = by_source(grad_home, z, 0).reshape(16, 8, width)

    return (
        outputs, grad_home, qkv_sums[0], qkv_sums[1], qkv_sums[2],
        big_sums[0], big_sums[1], big_sums[2], line_sums[0], line_sums[1], scale_sum,
    )


def solution(mesh):
    names = ("dp", "ctx")
    body = per_device
    if dict(mesh.shape) == {"dp": 16, "ctx": 2}:
        mesh = Mesh(mesh.devices.reshape(4, 2, 2, 2), ("z", "y", "core", "x"))
        names = mesh.axis_names
        body = planes
    seq, mat, line = P(None, names, None), P(names, None), P(names)
    return jax.shard_map(
        body,
        mesh=mesh,
        in_specs=(seq,) * 2 + (mat,) * 6 + (line,) * 3 + (P(), P()),
        out_specs=(seq,) * 2 + (mat,) * 6 + (line,) * 3,
        check_vma=False,
    )
```

```python
import math

import jax
import jax.numpy as jnp
from jax import lax
from jax.experimental import pallas as pl
from jax.experimental.pallas import tpu as pltpu
from jax.sharding import Mesh, PartitionSpec as P

H = 16
HD = 80


def mult_trans(left, right):
    return lax.dot_general(
        left, right, (((1,), (1,)), ((), ())), preferred_element_type=jnp.float32
    )


def trans_mult(left, right):
    return lax.dot_general(
        left, right, (((0,), (0,)), ((), ())), preferred_element_type=jnp.float32
    )


def position_of(index, local_rows, piece_rows, groups):
    column = index // local_rows
    within = index % local_rows
    return (within // piece_rows * groups + column) * piece_rows + within % piece_rows


def norm_back(grad_hidden, normed, inverse, gain_value):
    grad_normed = grad_hidden * gain_value
    return inverse * (grad_normed - normed * jnp.mean(grad_normed * normed, axis=1, keepdims=True))


def per_device(
    inputs,
    cotangent,
    w_query,
    w_key,
    w_value,
    w_output,
    w_up,
    w_down,
    attn_gain,
    mlp_gain,
    query_scale,
    deal,
    lengths,
):
    groups = lax.axis_size("ctx")
    group_index = lax.axis_index("dp")
    ctx_index = lax.axis_index("ctx")
    head_count = H
    head_dim = HD
    piece_rows = inputs.shape[1]
    seq_numbers = jnp.arange(inputs.shape[0], dtype=jnp.int32)
    seq_lengths = jnp.sum(
        jnp.where(deal[None, :] == seq_numbers[:, None], lengths[None, :], 0), axis=1
    )
    local_in, local_cot = (
        lax.all_to_all(inputs, "dp", split_axis=0, concat_axis=1, tiled=True),
        lax.all_to_all(cotangent, "dp", split_axis=0, concat_axis=1, tiled=True),
    )
    seq_count, local_rows, model_width = local_in.shape
    padded = local_rows * groups
    token_count = seq_count * local_rows
    my_lengths = lax.dynamic_slice_in_dim(seq_lengths, group_index * seq_count, seq_count, 0)
    query_pos = position_of(
        ctx_index * local_rows + jnp.arange(local_rows, dtype=jnp.int32),
        local_rows,
        piece_rows,
        groups,
    )
    flat_in = local_in.reshape(token_count, model_width).astype(jnp.float32)
    flat_cot = local_cot.reshape(token_count, model_width)
    lowered = (
        w_query.astype(jnp.bfloat16),
        w_key.astype(jnp.bfloat16),
        w_value.astype(jnp.bfloat16),
        w_output.astype(jnp.bfloat16),
        w_up.astype(jnp.bfloat16),
        w_down.astype(jnp.bfloat16),
        attn_gain.astype(jnp.bfloat16),
        mlp_gain.astype(jnp.bfloat16),
        query_scale.astype(jnp.bfloat16),
    )
    gathered = (
        lax.all_gather(lowered[0], ("dp", "ctx"), axis=0, tiled=True),
        lax.all_gather(lowered[1], ("dp", "ctx"), axis=0, tiled=True),
        lax.all_gather(lowered[2], ("dp", "ctx"), axis=0, tiled=True),
        lax.all_gather(lowered[3], ("dp", "ctx"), axis=0, tiled=True),
        lax.all_gather(lowered[4], ("dp", "ctx"), axis=0, tiled=True),
        lax.all_gather(lowered[5], ("dp", "ctx"), axis=0, tiled=True),
        lax.all_gather(lowered[6], ("dp", "ctx"), axis=0, tiled=True),
        lax.all_gather(lowered[7], ("dp", "ctx"), axis=0, tiled=True),
        lax.all_gather(lowered[8], ("dp", "ctx"), axis=0, tiled=True),
    )
    (
        query_full,
        key_full,
        value_full,
        output_full,
        up_full,
        down_full,
        gain_one,
        gain_two,
        scale_raw,
    ) = gathered
    inv_one = lax.rsqrt(jnp.mean(flat_in * flat_in, axis=1, keepdims=True) + 1e-06)
    normed_one = flat_in * inv_one
    hidden_one = (normed_one * gain_one.astype(jnp.float32)).astype(jnp.bfloat16)
    scale_param = scale_raw.astype(jnp.float32)
    query_mult = 1.442695041 / math.sqrt(head_dim) * jax.nn.softplus(scale_param)
    query_pre = jnp.dot(hidden_one, query_full, preferred_element_type=jnp.float32)
    queries = (query_pre * query_mult).astype(jnp.bfloat16)
    keys_local = jnp.dot(hidden_one, key_full, preferred_element_type=jnp.float32).astype(
        jnp.bfloat16
    )
    values_local = jnp.dot(hidden_one, value_full, preferred_element_type=jnp.float32).astype(
        jnp.bfloat16
    )
    four_shape = (seq_count, local_rows, head_count, head_dim)
    query_four = queries.reshape(four_shape)
    keys_three = keys_local.reshape(seq_count, local_rows, model_width)
    values_three = values_local.reshape(seq_count, local_rows, model_width)

    def live_between(row_pos, key_pos):
        allowed = (key_pos[None, None, :] <= row_pos[None, :, None]) & (
            key_pos[None, None, :] < my_lengths[:, None, None]
        )
        return allowed[:, :, None, :]

    def live_mask(key_pos):
        return live_between(query_pos, key_pos)

    def attend_block(state_now, key_block, value_block, first_row):
        run_max, run_sum, run_acc = state_now
        block_len = key_block.shape[1]
        key_pos = position_of(
            first_row + jnp.arange(block_len, dtype=jnp.int32), local_rows, piece_rows, groups
        )
        key_four = key_block.reshape(seq_count, block_len, head_count, head_dim)
        value_four = value_block.reshape(seq_count, block_len, head_count, head_dim)
        scores = jnp.einsum(
            "srhd,skhd->srhk", query_four, key_four, preferred_element_type=jnp.float32
        )
        allowed = live_mask(key_pos)
        masked = jnp.where(allowed, scores, -1e30)
        new_max = jnp.maximum(run_max, jnp.max(masked, axis=3))
        weights_now = jnp.exp(jnp.where(allowed, masked - new_max[..., None], -1e30))
        factor = jnp.exp(run_max - new_max)
        new_sum = run_sum * factor + jnp.sum(weights_now, axis=3)
        added = jnp.einsum(
            "srhk,skhd->srhd",
            weights_now.astype(jnp.bfloat16),
            value_four,
            preferred_element_type=jnp.float32,
        )
        return (new_max, new_sum, run_acc * factor[..., None] + added)

    start_state = (
        jnp.full((seq_count, local_rows, head_count), -1e30, jnp.float32),
        jnp.zeros((seq_count, local_rows, head_count), jnp.float32),
        jnp.zeros(four_shape, jnp.float32),
    )
    key_piece = lax.all_gather(keys_three, "ctx", axis=1, tiled=True)
    value_piece = lax.all_gather(values_three, "ctx", axis=1, tiled=True)
    piece_len = key_piece.shape[1]
    fold_block_len = 512 if piece_len % 512 == 0 else piece_len

    def one_block(state_now, block_index):
        offset = block_index * fold_block_len
        key_block = lax.dynamic_slice_in_dim(key_piece, offset, fold_block_len, 1)
        value_block = lax.dynamic_slice_in_dim(value_piece, offset, fold_block_len, 1)
        return (attend_block(state_now, key_block, value_block, offset), None)

    result_state, unused = lax.scan(
        one_block, start_state, jnp.arange(piece_len // fold_block_len, dtype=jnp.int32)
    )
    run_max, run_sum, run_acc = result_state
    log_total = run_max + jnp.log(run_sum)
    attn_exact = run_acc / run_sum[..., None]
    attended = attn_exact.reshape(token_count, model_width).astype(jnp.bfloat16)
    middle = flat_in + jnp.dot(attended, output_full, preferred_element_type=jnp.float32)
    inv_two = lax.rsqrt(jnp.mean(middle * middle, axis=1, keepdims=True) + 1e-06)
    normed_two = middle * inv_two
    hidden_two = (normed_two * gain_two.astype(jnp.float32)).astype(jnp.bfloat16)
    up_pre = jnp.dot(hidden_two, up_full, preferred_element_type=jnp.float32)
    active = jax.nn.silu(up_pre).astype(jnp.bfloat16)
    result = (middle + jnp.dot(active, down_full, preferred_element_type=jnp.float32)).astype(
        jnp.bfloat16
    )
    back_weights = (
        lax.all_gather(lowered[0], ("dp", "ctx"), axis=0, tiled=True),
        lax.all_gather(lowered[1], ("dp", "ctx"), axis=0, tiled=True),
        lax.all_gather(lowered[2], ("dp", "ctx"), axis=0, tiled=True),
        lax.all_gather(lowered[3], ("dp", "ctx"), axis=0, tiled=True),
        lax.all_gather(lowered[4], ("dp", "ctx"), axis=0, tiled=True),
        lax.all_gather(lowered[5], ("dp", "ctx"), axis=0, tiled=True),
        lax.all_gather(lowered[6], ("dp", "ctx"), axis=0, tiled=True),
        lax.all_gather(lowered[7], ("dp", "ctx"), axis=0, tiled=True),
        lax.all_gather(lowered[8], ("dp", "ctx"), axis=0, tiled=True),
    )
    (
        query_back,
        key_back,
        value_back,
        output_back,
        up_back,
        down_back,
        gain_one_back,
        gain_two_back,
        scale_back,
    ) = back_weights
    cot_wide = flat_cot.astype(jnp.float32)
    grad_down = trans_mult(active, flat_cot)
    grad_active = mult_trans(flat_cot, down_back)
    sigma_up = jax.nn.sigmoid(up_pre)
    grad_up_pre = (grad_active * sigma_up * (1.0 + up_pre * (1.0 - sigma_up))).astype(jnp.bfloat16)
    grad_up = trans_mult(hidden_two, grad_up_pre)
    grad_hidden_two = mult_trans(grad_up_pre, up_back)
    grad_gain_two = jnp.sum(grad_hidden_two * normed_two, axis=0)
    grad_middle = cot_wide + norm_back(
        grad_hidden_two, normed_two, inv_two, gain_two_back.astype(jnp.float32)
    )
    grad_middle_low = grad_middle.astype(jnp.bfloat16)
    grad_output = trans_mult(attended, grad_middle_low)
    grad_attended = mult_trans(grad_middle_low, output_back).astype(jnp.bfloat16)
    grad_att_four = grad_attended.reshape(four_shape)
    delta_rows = jnp.sum(grad_att_four.astype(jnp.float32) * attn_exact, axis=3)
    key_all, value_all = (
        lax.all_gather(keys_three, "ctx", axis=1, tiled=True),
        lax.all_gather(values_three, "ctx", axis=1, tiled=True),
    )
    block_len = min(512, padded)

    def back_block(block_index, state_now):
        grad_query, grad_key_all, grad_value_all = state_now
        offset = block_index * block_len
        key_block = lax.dynamic_slice_in_dim(key_all, offset, block_len, 1).reshape(
            seq_count, block_len, head_count, head_dim
        )
        value_block = lax.dynamic_slice_in_dim(value_all, offset, block_len, 1).reshape(
            seq_count, block_len, head_count, head_dim
        )
        key_pos = position_of(
            offset + jnp.arange(block_len, dtype=jnp.int32), local_rows, piece_rows, groups
        )
        scores = jnp.einsum(
            "srhd,skhd->srhk", query_four, key_block, preferred_element_type=jnp.float32
        )
        probs = jnp.exp(jnp.where(live_mask(key_pos), scores - log_total[..., None], -1e30))
        grad_value_block = jnp.einsum(
            "srhk,srhd->skhd",
            probs.astype(jnp.bfloat16),
            grad_att_four,
            preferred_element_type=jnp.float32,
        )
        grad_probs = jnp.einsum(
            "srhd,skhd->srhk", grad_att_four, value_block, preferred_element_type=jnp.float32
        )
        grad_scores = (probs * (grad_probs - delta_rows[..., None])).astype(jnp.bfloat16)
        grad_query = grad_query + jnp.einsum(
            "srhk,skhd->srhd", grad_scores, key_block, preferred_element_type=jnp.float32
        )
        grad_key_block = jnp.einsum(
            "srhk,srhd->skhd", grad_scores, query_four, preferred_element_type=jnp.float32
        )
        grad_key_all = lax.dynamic_update_slice_in_dim(
            grad_key_all, grad_key_block.reshape(seq_count, block_len, model_width), offset, 1
        )
        grad_value_all = lax.dynamic_update_slice_in_dim(
            grad_value_all, grad_value_block.reshape(seq_count, block_len, model_width), offset, 1
        )
        return (grad_query, grad_key_all, grad_value_all)

    zero_all = jnp.zeros((seq_count, padded, model_width), jnp.float32)
    grad_query, grad_key_all, grad_value_all = lax.fori_loop(
        0, padded // block_len, back_block, (jnp.zeros(four_shape, jnp.float32), zero_all, zero_all)
    )
    grad_key_mine, grad_value_mine = (
        lax.psum_scatter(
            grad_key_all.astype(jnp.bfloat16), "ctx", scatter_dimension=1, tiled=True
        ).astype(jnp.float32),
        lax.psum_scatter(
            grad_value_all.astype(jnp.bfloat16), "ctx", scatter_dimension=1, tiled=True
        ).astype(jnp.float32),
    )
    grad_query_flat = grad_query.reshape(token_count, model_width)
    grad_query_pre = (grad_query_flat * query_mult).astype(jnp.bfloat16)
    grad_scale = (
        1.442695041
        / math.sqrt(head_dim)
        * jax.nn.sigmoid(scale_back.astype(jnp.float32))
        * jnp.sum(grad_query_flat * query_pre, axis=0)
    )
    grad_key_low = grad_key_mine.reshape(token_count, model_width).astype(jnp.bfloat16)
    grad_value_low = grad_value_mine.reshape(token_count, model_width).astype(jnp.bfloat16)
    grad_wq = trans_mult(hidden_one, grad_query_pre)
    grad_wk = trans_mult(hidden_one, grad_key_low)
    grad_wv = trans_mult(hidden_one, grad_value_low)
    grad_hidden_one = (
        mult_trans(grad_query_pre, query_back)
        + mult_trans(grad_key_low, key_back)
        + mult_trans(grad_value_low, value_back)
    )
    grad_gain_one = jnp.sum(grad_hidden_one * normed_one, axis=0)
    grad_in = grad_middle + norm_back(
        grad_hidden_one, normed_one, inv_one, gain_one_back.astype(jnp.float32)
    )
    matrix_stack = jnp.stack([grad_wq, grad_wk, grad_wv, grad_output, grad_up, grad_down], axis=0)
    vector_stack = jnp.stack([grad_gain_one, grad_gain_two, grad_scale], axis=0)
    matrix_sums, vector_sums = (
        lax.psum_scatter(matrix_stack, ("dp", "ctx"), scatter_dimension=1, tiled=True),
        lax.psum_scatter(vector_stack, ("dp", "ctx"), scatter_dimension=1, tiled=True),
    )
    out_local = result.reshape(seq_count, local_rows, model_width)
    grad_local = grad_in.astype(jnp.bfloat16).reshape(seq_count, local_rows, model_width)
    back_out, back_grad = (
        lax.all_to_all(out_local, "dp", split_axis=1, concat_axis=0, tiled=True),
        lax.all_to_all(grad_local, "dp", split_axis=1, concat_axis=0, tiled=True),
    )
    return (
        back_out,
        back_grad,
        matrix_sums[0],
        matrix_sums[1],
        matrix_sums[2],
        matrix_sums[3],
        matrix_sums[4],
        matrix_sums[5],
        vector_sums[0],
        vector_sums[1],
        vector_sums[2],
    )


LOG2E = 1.442695041
CODES = (0, 1, 4, 5)


def plane_shift(value, step):
    if step == 1:
        return lax.ppermute(value, "x", [(0, 1), (1, 0)])
    if step == 2:
        return lax.ppermute(value, "y", [(0, 1), (1, 0)])
    return lax.ppermute(value, ("y", "x"), [(0, 3), (1, 2), (2, 1), (3, 0)])


def core_swap(value):
    return lax.ppermute(value, "core", [(0, 1), (1, 0)])


def ring_shift(value, step):
    return lax.ppermute(value, "z", [(i, (i + step) % 4) for i in range(4)])


def pick(array, index):
    return lax.dynamic_index_in_dim(array, index, 0, keepdims=False)


def by_source(pieces, z_index, axis):
    pieces = [jnp.expand_dims(item, axis) for item in pieces]
    shape = [1] * pieces[0].ndim
    shape[axis] = 4
    hop = ((z_index - jnp.arange(4, dtype=jnp.int32)) % 4).reshape(shape)
    made = pieces[0]
    for k in (1, 2, 3):
        made = jnp.where(hop == k, pieces[k], made)
    return made


def pair(mine, other, index, axis):
    shape = [1] * (mine.ndim + 1)
    shape[axis] = 2
    slot = jnp.arange(2, dtype=jnp.int32).reshape(shape)
    return jnp.where(slot == index, jnp.expand_dims(mine, axis), jnp.expand_dims(other, axis))


def row_positions(shape, dim, plane_index):
    row = lax.broadcasted_iota(jnp.int32, shape, dim)
    chip = (row // 32) % 4
    code = (chip % 2) + 4 * (chip // 2) + 2 * (row // 128)
    return 64 * ((row % 32) // 8) + 8 * (plane_index ^ code) + row % 8


def live_pairs(info_ref, seq):
    shape = (256, 256)
    query_pos = row_positions(shape, 0, info_ref[1])
    key_pos = row_positions(shape, 1, info_ref[1])
    return (key_pos <= query_pos) & (key_pos < info_ref[2 + seq])


def block_rows(near_ref, far_ref):
    return jnp.concatenate([near_ref[...], far_ref[...]], axis=0).reshape(256, near_ref.shape[2])


def soft_probs(query, key, live):
    scores = mult_trans(query, key)
    scores = jnp.where(live, scores, -1e30)
    top = jnp.max(scores, axis=1, keepdims=True)
    weights = jnp.where(live, jnp.exp(scores - top), 0.0)
    return weights / jnp.sum(weights, axis=1, keepdims=True)


def attend_kernel(
    info_ref, near_ref, far_ref, gain_ref, mult_ref, w_ref, pre_ref, att_ref
):
    seq = pl.program_id(0)
    live = live_pairs(info_ref, seq)
    wide = block_rows(near_ref, far_ref).astype(jnp.float32)
    inverse = lax.rsqrt(jnp.mean(wide * wide, axis=1, keepdims=True) + 1e-06)
    hidden = (wide * inverse * gain_ref[...]).astype(jnp.bfloat16)
    pre = jnp.dot(hidden, w_ref[...], preferred_element_type=jnp.float32)
    pre_ref[...] = pre.reshape(2, 4, 32, 480)
    query = (pre[:, 0:160] * mult_ref[...]).astype(jnp.bfloat16)
    key = pre[:, 160:320].astype(jnp.bfloat16)
    value = pre[:, 320:480].astype(jnp.bfloat16)
    heads = []
    for head in range(2):
        part = slice(80 * head, 80 * head + 80)
        probs = soft_probs(query[:, part], key[:, part], live).astype(jnp.bfloat16)
        heads.append(jnp.dot(probs, value[:, part], preferred_element_type=jnp.float32))
    att = jnp.concatenate(heads, axis=1).astype(jnp.bfloat16).reshape(2, 4, 32, 160)
    for chip in range(4):
        for core in range(2):
            att_ref[chip, core] = att[core, chip]


def attend_back_kernel(
    info_ref, near_ref, far_ref, gain_ref, mult_ref, w_ref, pre_ref, grad_near, grad_far, gain_two_ref,
    hid_near, hid_far, send_0, send_1, send_2, send_3, w_acc, gain_acc, scale_acc, lines,
):
    seq = pl.program_id(0)

    @pl.when(seq == 0)
    def _():
        w_acc[...] = jnp.zeros_like(w_acc)
        gain_acc[...] = jnp.zeros_like(gain_acc)
        scale_acc[...] = jnp.zeros_like(scale_acc)

    live = live_pairs(info_ref, seq)
    wide = block_rows(near_ref, far_ref).astype(jnp.float32)
    inverse = lax.rsqrt(jnp.mean(wide * wide, axis=1, keepdims=True) + 1e-06)
    normed = wide * inverse
    hidden = (normed * gain_ref[...]).astype(jnp.bfloat16)
    pre = pre_ref[...].reshape(256, 480)
    mult = mult_ref[...]
    query = (pre[:, 0:160] * mult).astype(jnp.bfloat16)
    key = pre[:, 160:320].astype(jnp.bfloat16)
    value = pre[:, 320:480].astype(jnp.bfloat16)
    grad_att = jnp.concatenate([grad_near[:, 0], grad_far[:, 0]], axis=0).reshape(256, 160)
    grad_q, grad_k, grad_v = [], [], []
    for head in range(2):
        part = slice(80 * head, 80 * head + 80)
        probs = soft_probs(query[:, part], key[:, part], live)
        grad_probs = mult_trans(grad_att[:, part], value[:, part])
        delta = jnp.sum(probs * grad_probs, axis=1, keepdims=True)
        grad_scores = (probs * (grad_probs - delta)).astype(jnp.bfloat16)
        grad_v.append(trans_mult(probs.astype(jnp.bfloat16), grad_att[:, part]))
        grad_q.append(jnp.dot(grad_scores, key[:, part], preferred_element_type=jnp.float32))
        grad_k.append(trans_mult(grad_scores, query[:, part]))
    grad_query = jnp.concatenate(grad_q, axis=1)
    scale_acc[...] += jnp.sum(grad_query * pre[:, 0:160], axis=0, keepdims=True)
    joined = jnp.concatenate([grad_query * mult] + grad_k + grad_v, axis=1).astype(jnp.bfloat16)
    w_acc[...] += trans_mult(hidden, joined)
    grad_hidden = mult_trans(joined, w_ref[...])
    gain_acc[...] += jnp.sum(grad_hidden * normed, axis=0, keepdims=True)
    low = grad_hidden.astype(jnp.bfloat16).reshape(2, 4, 32, 1280)
    hid_near[...] = low[0]
    hid_far[...] = low[1]

    @pl.when(seq == 3)
    def _():
        lines[...] = jnp.zeros_like(lines)
        for which, source in enumerate((gain_acc, gain_two_ref)):
            for owner in range(32):
                lane = 120 * (owner % 4) + 40 * which
                lines[owner // 4, :, lane : lane + 40] = source[:, 40 * owner : 40 * owner + 40]
        for part in range(4):
            lane = 120 * part + 80
            lines[info_ref[1], :, lane : lane + 40] = scale_acc[:, 40 * part : 40 * part + 40]
        blank = jnp.zeros((14, 480), jnp.float32)
        for hop, send in enumerate((send_0, send_1, send_2, send_3)):
            target = (info_ref[0] + hop) & 3
            rows = w_acc[pl.ds(pl.multiple_of(target * 320, 320), 320), :]
            block = jnp.concatenate([rows, lines[2 * target], lines[2 * target + 1], blank], axis=0)
            send[...] = block.astype(jnp.bfloat16)


def block_index(z_index, y_index, core):
    return pl.ds(pl.multiple_of((4 * z_index + 2 * y_index + core) * 80, 80), 80)


def source_rows(info_ref, chip, core):
    source = info_ref[1] ^ (CODES[chip] + 2 * core)
    return pl.ds(pl.multiple_of(source * 160, 160), 160)


def feed_kernel(
    info_ref, x_ref, g_ref, atts, far_atts, gain_ref,
    near_rows, across_a, across_b, far_near_rows, far_across_a, far_across_b,
    out_ref, pack_ref, dmid_ref, datt_0, datt_1, datt_2, datt_3, gain_grad,
    weights, sems,
):
    y_index, core_index = info_ref[1] // 4, (info_ref[1] // 2) % 2
    copies = []
    for w in range(3):
        moved = []
        for core, own, others in (
            (core_index, near_rows, (across_a, across_b)),
            (1 - core_index, far_near_rows, (far_across_a, far_across_b)),
        ):
            for z_index in range(4):
                moved.append((own.at[z_index, w], z_index, y_index, core))
                moved.append((others[z_index // 2].at[z_index % 2, w], z_index, 1 - y_index, core))
        copies.append([
            pltpu.make_async_copy(src, weights.at[w, block_index(*place)], sems.at[w, i])
            for i, (src, *place) in enumerate(moved)
        ])
    for group in copies:
        for copy in group:
            copy.start()
    datts = (datt_0, datt_1, datt_2, datt_3)

    for copy in copies[0]:
        copy.wait()
    middle = x_ref[...].astype(jnp.float32)
    for chip in range(4):
        for core in range(2):
            middle += jnp.dot(
                (far_atts if core else atts)[chip, core], weights[0, source_rows(info_ref, chip, core), :],
                preferred_element_type=jnp.float32,
            )
    inverse = lax.rsqrt(jnp.mean(middle * middle, axis=1, keepdims=True) + 1e-06)
    normed = middle * inverse
    gain = gain_ref[...]
    hidden = (normed * gain).astype(jnp.bfloat16)
    pack_ref[1] = hidden
    for copy in copies[1]:
        copy.wait()
    up = jnp.dot(hidden, weights[1], preferred_element_type=jnp.float32)
    sigma = jax.nn.sigmoid(up)
    active = (up * sigma).astype(jnp.bfloat16)
    pack_ref[0] = active
    for copy in copies[2]:
        copy.wait()
    down = jnp.dot(active, weights[2], preferred_element_type=jnp.float32)
    result = middle + down
    for seq in range(4):
        for plane_z in range(4):
            row = 32 * seq + 8 * plane_z
            out_ref[plane_z, seq] = result[row : row + 8].astype(jnp.bfloat16)
    cot = g_ref[...]
    grad_act = mult_trans(cot, weights[2])
    grad_up = (grad_act * sigma * (1.0 + up * (1.0 - sigma))).astype(jnp.bfloat16)
    pack_ref[2] = grad_up
    grad_hidden = mult_trans(grad_up, weights[1])
    gain_grad[...] = jnp.sum(grad_hidden * normed, axis=0, keepdims=True)
    grad_mid = cot.astype(jnp.float32) + norm_back(grad_hidden, normed, inverse, gain)
    dmid_ref[...] = grad_mid
    low = grad_mid.astype(jnp.bfloat16)
    pack_ref[3] = low
    for chip in range(4):
        for core in range(2):
            datts[chip][core] = mult_trans(low, weights[0, source_rows(info_ref, chip, core), :]).astype(jnp.bfloat16)


def grads_kernel(
    info_ref, pack_ref, far_pack, atts, far_atts, cot_ref, far_cot, half_a, kept_b, away_b, stage, sems
):
    y_index, core_index = info_ref[1] // 4, (info_ref[1] // 2) % 2

    def leave(w):
        copies = []
        for half in range(2):
            targets = [(half, row, half_a.at[half, w, row]) for row in range(2)]
            targets += [(2 + half, y_index, kept_b.at[half, w]), (2 + half, 1 - y_index, away_b.at[half, w])]
            for i, (z_index, row, target) in enumerate(targets):
                block = pl.ds(pl.multiple_of(160 * z_index + 80 * row, 80), 80)
                copies.append(pltpu.make_async_copy(stage.at[w, block], target, sems.at[w, 4 * half + i]))
        return copies

    def both(near, far):
        return jnp.concatenate([near, far], axis=0)

    cots = both(cot_ref[...], far_cot[...])
    for core in range(2):

        @pl.when(core_index == core)
        def _():
            def own_columns(near, far):
                return both(*(
                    jnp.concatenate([ref[:, 160 * i + 80 * core : 160 * i + 80 * core + 80] for i in range(8)], axis=1)
                    for ref in (near, far)
                ))

            acts = own_columns(pack_ref.at[0], far_pack.at[0])
            stage[2] = trans_mult(acts, cots).astype(jnp.bfloat16)
            for copy in leave(2):
                copy.start()
            acts = own_columns(pack_ref.at[1], far_pack.at[1])
            stage[1] = trans_mult(acts, both(pack_ref[2], far_pack[2])).astype(jnp.bfloat16)
            for copy in leave(1):
                copy.start()
            grads = both(pack_ref[3], far_pack[3])
            for chip in range(4):
                for source in range(2):
                    near, far = (far_atts, far_atts) if source else (atts, atts)
                    att = both(near[chip, source], far[chip, 1 - source])[:, 80 * core : 80 * core + 80]
                    place = (info_ref[1] ^ (CODES[chip] + 2 * source)) * 80
                    stage[0, pl.ds(pl.multiple_of(place, 80), 80), :] = trans_mult(att, grads).astype(jnp.bfloat16)
            for copy in leave(0):
                copy.start()

    for w in range(3):
        for copy in leave(w):
            copy.wait()


def meet_kernel(info_ref, half_a, from_a, half_b, from_b, keep_a, away_a, keep_b, away_b):
    y_index, x_index = info_ref[1] // 4, info_ref[1] % 2
    for half in range(2):
        for w in range(3):
            for row, out in ((y_index, keep_a), (1 - y_index, away_a)):
                out[half, w] = sum_low(half_a[half, w, row, x_index], from_a[half, w, row])
            for row, out in ((x_index, keep_b), (1 - x_index, away_b)):
                out[half, w] = sum_low(half_b[half, w, row], from_b[half, w, row])


def join_kernel(keep_a, from_a, keep_b, from_b, out_ref):
    for half in range(2):
        for w in range(3):
            out_ref[half, w] = sum_low(keep_a[half, w], from_a[half, w])
            out_ref[2 + half, w] = sum_low(keep_b[half, w], from_b[half, w])


def sum_low(left, right):
    return (left.astype(jnp.float32) + right.astype(jnp.float32)).astype(jnp.bfloat16)


def norm_kernel(info_ref, hid_0, hid_1, hid_2, hid_3, x_ref, dmid_ref, gain_ref, out_0, out_1, out_2, out_3, rows):
    grad = hid_0[...].astype(jnp.float32)
    for item in (hid_1, hid_2, hid_3):
        grad += item[...].astype(jnp.float32)
    wide = x_ref[...].astype(jnp.float32)
    inverse = lax.rsqrt(jnp.mean(wide * wide, axis=1, keepdims=True) + 1e-06)
    grad = dmid_ref[...] + norm_back(grad, wide * inverse, inverse, gain_ref[...])
    for seq in range(4):
        for plane_z in range(4):
            row = 32 * seq + 8 * plane_z
            rows[plane_z, seq] = grad[row : row + 8]
    for hop, out in enumerate((out_0, out_1, out_2, out_3)):
        out[...] = rows[(info_ref[0] + hop) & 3].astype(jnp.bfloat16)


def fold_kernel(part_0, part_1, part_2, part_3, out_ref, line):
    total = part_0[...].astype(jnp.float32)
    for item in (part_1, part_2, part_3):
        total += item[...].astype(jnp.float32)
    line[...] = jnp.zeros_like(line)
    for owner in range(8):
        lane = 120 * (owner % 4)
        line[0:1, 0:120] = total[320 + owner // 4 : 321 + owner // 4, lane : lane + 120]
        block = jnp.concatenate([total[40 * owner : 40 * owner + 40], line[...]], axis=0)
        out_ref[owner] = block.astype(jnp.bfloat16)


def spread_kernel(in_ref, *outs):
    for which, out in enumerate(outs):
        for owner in range(8):
            part = in_ref[owner, 0:40, 160 * which : 160 * which + 160]
            out[:, 160 * owner : 160 * owner + 160] = part.astype(jnp.float32)


def widen_kernel(in_ref, *outs):
    for which, out in enumerate(outs):
        out[...] = in_ref[which].astype(jnp.float32)


def whole(shape):
    return pl.BlockSpec(shape, lambda *_: (0,) * len(shape))


def seq_block(*lead, width):
    count = len(lead)
    return pl.BlockSpec((*lead, 32, width), lambda s, info: (*(0,) * count, s, 0))


def planes(
    inputs, cotangent, w_query, w_key, w_value, w_output, w_up, w_down,
    attn_gain, mlp_gain, query_scale, deal, lengths,
):
    f32, bf16 = jnp.float32, jnp.bfloat16
    z, y, c, x = (lax.axis_index(name) for name in ("z", "y", "core", "x"))
    plane = 4 * y + 2 * c + x
    width = 1280
    seqs = jnp.arange(16, dtype=jnp.int32)
    seq_lengths = jnp.sum(jnp.where(deal[None, :] == seqs[:, None], lengths[None, :], 0), axis=1)
    my_lengths = lax.dynamic_slice_in_dim(seq_lengths, 4 * z, 4, 0)
    info = jnp.concatenate([jnp.stack([z, plane]), my_lengths]).astype(jnp.int32)

    vec = jnp.concatenate([attn_gain, mlp_gain, query_scale]).astype(bf16)
    vec_block = jnp.zeros((1, 8, width), bf16).at[0, 0, :120].set(vec)
    in_four = inputs.reshape(4, 4, 8, width)
    sent = [jnp.concatenate([pick(in_four, (z + k) % 4), vec_block]) for k in range(4)]
    qkv = jnp.stack([w_query, w_key, w_value]).astype(bf16)
    *sent, qkv = lax.optimization_barrier((*sent, qkv))
    got = [sent[0]] + [ring_shift(sent[k], k) for k in (1, 2, 3)]
    x_rows = by_source([item[:4] for item in got], z, 1).reshape(128, width)
    vec_rows = by_source([item[4, 0] for item in got], z, 0)
    vec_rows = jnp.concatenate([vec_rows, jnp.zeros((4, width), bf16)])
    own = jnp.concatenate([x_rows, vec_rows])

    big = jnp.stack([w_output, w_up, w_down]).astype(bf16)
    big = lax.all_gather(big, "z", axis=0)

    qkv = qkv.reshape(3, 40, 8, 160).transpose(2, 1, 0, 3).reshape(8, 40, 480)
    qkv = lax.all_to_all(qkv, ("y", "core", "x"), split_axis=0, concat_axis=0, tiled=True)
    own, qkv = lax.optimization_barrier((own, qkv.reshape(320, 480)))
    w_qkv = lax.all_gather(qkv, "z", axis=0, tiled=True)
    near = jnp.stack([own] + [plane_shift(own, step) for step in (1, 2, 3)])
    big, near, cotangent = lax.optimization_barrier((big, near, cotangent))
    far = core_swap(near)
    beside, across = plane_shift(big, 1), plane_shift(big, 2)
    relay_a, relay_b = beside[:2], across[2:]
    cot_rows = lax.all_to_all(cotangent.reshape(4, 4, 8, width), "z", split_axis=0, concat_axis=0, tiled=True)
    relay_a, relay_b, cot_rows = lax.optimization_barrier((relay_a, relay_b, cot_rows))
    across_a, across_b = plane_shift(relay_a, 2), plane_shift(relay_b, 1)

    vecs = jnp.stack([near[:, 128:132, :120], far[:, 128:132, :120]])
    vecs = vecs.astype(f32).reshape(2, 2, 2, 4, 120)
    vecs = jnp.where(c == 0, vecs, vecs[::-1])
    vecs = jnp.where(y == 0, vecs, vecs[:, ::-1])
    vecs = jnp.where(x == 0, vecs, vecs[:, :, ::-1])
    vecs = vecs.reshape(2, 2, 2, 4, 3, 40).transpose(4, 3, 1, 0, 2, 5).reshape(3, width)
    gain_one, gain_two = vecs[0:1], vecs[1:2]
    my_scale = lax.dynamic_slice_in_dim(vecs[2:3], 160 * plane, 160, 1)
    query_mult = LOG2E / math.sqrt(HD) * jax.nn.softplus(my_scale)

    limit = pltpu.CompilerParams(vmem_limit_bytes=50 * 1024 * 1024)
    pre, att_made = pl.pallas_call(
        attend_kernel,
        grid_spec=pltpu.PrefetchScalarGridSpec(
            num_scalar_prefetch=1,
            grid=(4,),
            in_specs=[
                seq_block(4, width=width), seq_block(4, width=width),
                whole((1, width)), whole((1, 160)), whole((width, 480)),
            ],
            out_specs=[seq_block(2, 4, width=480), seq_block(4, 2, width=160)],
        ),
        out_shape=[
            jax.ShapeDtypeStruct((2, 4, 128, 480), f32),
            jax.ShapeDtypeStruct((4, 2, 128, 160), bf16),
        ],
        compiler_params=limit,
        cost_estimate=pl.CostEstimate(flops=9_000_000_000, bytes_accessed=8_000_000, transcendentals=600_000),
        name="attend",
    )(info, near, far, gain_one, query_mult, w_qkv)

    near_rows = pair(big, beside, x, 2).reshape(4, 3, 80, width)
    att_made, near_rows, across_a, across_b = lax.optimization_barrier((att_made, near_rows, across_a, across_b))
    far_near_rows = core_swap(near_rows)
    atts = [att_made[0]] + [plane_shift(att_made[step], step) for step in (1, 2, 3)]
    atts = jnp.stack(atts)
    far_atts = core_swap(atts)
    across_a = pair(across[:2], across_a, x, 2).reshape(2, 3, 80, width)
    across_b = pair(across[2:], across_b, x, 2).reshape(2, 3, 80, width)
    far_across_a, far_across_b = core_swap(across_a), core_swap(across_b)
    cot_rows = cot_rows.transpose(1, 0, 2, 3).reshape(128, width)
    far_cot = core_swap(cot_rows)
    far_cot, far_atts, cot_rows = lax.optimization_barrier((far_cot, far_atts, cot_rows))
    datt_shape = jax.ShapeDtypeStruct((2, 128, 160), bf16)
    smem = pl.BlockSpec(memory_space=pltpu.SMEM)
    vmem = pl.BlockSpec(memory_space=pltpu.VMEM)
    hbm = pl.BlockSpec(memory_space=pl.ANY)
    out_rows, pack, grad_mid, *datts, gain_two_grad = pl.pallas_call(
        feed_kernel,
        in_specs=[smem] + [vmem] * 5 + [hbm] * 6,
        out_specs=[vmem] * 8,
        out_shape=[
            jax.ShapeDtypeStruct((4, 4, 8, width), bf16),
            jax.ShapeDtypeStruct((4, 128, width), bf16),
            jax.ShapeDtypeStruct((128, width), f32),
        ]
        + [datt_shape] * 4
        + [jax.ShapeDtypeStruct((1, width), f32)],
        scratch_shapes=[pltpu.VMEM((3, width, width), bf16), pltpu.SemaphoreType.DMA((3, 16))],
        compiler_params=limit,
        cost_estimate=pl.CostEstimate(flops=12_000_000_000, bytes_accessed=13_000_000, transcendentals=200_000),
        name="feed",
    )(info, x_rows, cot_rows, atts, far_atts, gain_two, near_rows, across_a, across_b, far_near_rows, far_across_a, far_across_b)

    back = [datts[0]] + [plane_shift(datts[step], step) for step in (1, 2, 3)]

    part_shape = jax.ShapeDtypeStruct((2, 3, 80, width), bf16)
    half_a, kept_b, away_b = pl.pallas_call(
        grads_kernel,
        in_specs=[smem] + [vmem] * 6,
        out_specs=[hbm] * 3,
        out_shape=[jax.ShapeDtypeStruct((2, 3, 2, 80, width), bf16), part_shape, part_shape],
        scratch_shapes=[pltpu.VMEM((3, 640, width), bf16), pltpu.SemaphoreType.DMA((3, 8))],
        compiler_params=limit,
        cost_estimate=pl.CostEstimate(flops=6_000_000_000, bytes_accessed=8_000_000, transcendentals=0),
        name="grads",
    )(info, pack, core_swap(pack), atts, far_atts, cot_rows, far_cot)

    half_a, kept_b, away_b, *back = lax.optimization_barrier((half_a, kept_b, away_b, *back))
    half_a = half_a.reshape(2, 3, 2, 2, 40, width)
    away_a = lax.dynamic_index_in_dim(half_a, 1 - x, 3, keepdims=False)
    away_a, away_b, grad_atts = lax.optimization_barrier((away_a, away_b, jnp.stack(back)))
    from_a, from_b = plane_shift(away_a, 1), plane_shift(away_b, 2)
    hid_near, hid_far, *send = pl.pallas_call(
        attend_back_kernel,
        grid_spec=pltpu.PrefetchScalarGridSpec(
            num_scalar_prefetch=1,
            grid=(4,),
            in_specs=[
                seq_block(4, width=width), seq_block(4, width=width),
                whole((1, width)), whole((1, 160)), whole((width, 480)),
                seq_block(2, 4, width=480),
                *[pl.BlockSpec((4, 1, 32, 160), lambda s, info, core=core: (0, core, s, 0)) for core in range(2)],
                whole((1, width)),
            ],
            out_specs=[
                seq_block(4, width=width), seq_block(4, width=width),
                *[whole((336, 480))] * 4,
            ],
            scratch_shapes=[
                pltpu.VMEM((width, 480), f32), pltpu.VMEM((1, width), f32),
                pltpu.VMEM((1, 160), f32), pltpu.VMEM((8, 1, 480), f32),
            ],
        ),
        out_shape=[
            jax.ShapeDtypeStruct((4, 128, width), bf16),
            jax.ShapeDtypeStruct((4, 128, width), bf16),
            *[jax.ShapeDtypeStruct((336, 480), bf16)] * 4,
        ],
        compiler_params=limit,
        cost_estimate=pl.CostEstimate(flops=15_000_000_000, bytes_accessed=12_000_000, transcendentals=600_000),
        name="attend_back",
    )(info, near, far, gain_one, query_mult, w_qkv, pre, grad_atts, core_swap(grad_atts), gain_two_grad)

    send[0], out_rows = lax.optimization_barrier((send[0], out_rows))
    outputs = lax.all_to_all(out_rows, "z", split_axis=0, concat_axis=0, tiled=True).reshape(16, 8, width)
    swapped = core_swap(hid_far)
    from_a, from_b, outputs, hid_near, *early = lax.optimization_barrier(
        (from_a, from_b, outputs, hid_near, send[1], send[3])
    )
    one, three = ring_shift(early[0], 1), ring_shift(early[1], 3)
    hid = [sum_low(hid_near[i], swapped[i]) for i in range(4)]
    split = (2, 3, 2, 40, width)
    keep_a, away_a, keep_b, away_b = pl.pallas_call(
        meet_kernel,
        in_specs=[smem] + [vmem] * 4,
        out_specs=[vmem] * 4,
        out_shape=[jax.ShapeDtypeStruct((2, 3, 40, width), bf16)] * 4,
        compiler_params=limit,
        cost_estimate=pl.CostEstimate(flops=3_000_000_000, bytes_accessed=8_000_000, transcendentals=0),
        name="meet",
    )(info, half_a, from_a, kept_b.reshape(split), from_b.reshape(split))
    kept = pl.pallas_call(
        join_kernel,
        in_specs=[vmem] * 4,
        out_specs=vmem,
        out_shape=jax.ShapeDtypeStruct((4, 3, 40, width), bf16),
        compiler_params=limit,
        cost_estimate=pl.CostEstimate(flops=2_000_000_000, bytes_accessed=4_000_000, transcendentals=0),
        name="join",
    )(keep_a, plane_shift(away_a, 2), keep_b, plane_shift(away_b, 1))
    *hid, kept, one, three, late = lax.optimization_barrier((*hid, kept, one, three, send[2]))
    two = ring_shift(late, 2)
    moved = [plane_shift(hid[step], step) for step in (1, 2, 3)]
    *moved, mine = lax.optimization_barrier((*moved, send[0]))
    big_sums = lax.psum_scatter(kept, "z", scatter_dimension=0, tiled=True)[0]
    grad_home = pl.pallas_call(
        norm_kernel,
        in_specs=[smem] + [vmem] * 7,
        out_specs=[vmem] * 4,
        out_shape=[jax.ShapeDtypeStruct((4, 8, width), bf16)] * 4,
        scratch_shapes=[pltpu.VMEM((4, 4, 8, width), f32)],
        compiler_params=limit,
        cost_estimate=pl.CostEstimate(flops=2_000_000_000, bytes_accessed=2_500_000, transcendentals=128),
        name="norm",
    )(info, hid[0], *moved, x_rows, grad_mid, gain_one)
    sums = pl.pallas_call(
        fold_kernel,
        in_specs=[vmem] * 4,
        out_specs=vmem,
        out_shape=jax.ShapeDtypeStruct((8, 48, 480), bf16),
        scratch_shapes=[pltpu.VMEM((8, 480), f32)],
        compiler_params=limit,
        cost_estimate=pl.CostEstimate(flops=2_000_000_000, bytes_accessed=1_600_000, transcendentals=0),
        name="fold",
    )(mine, one, two, three)
    sums = lax.all_to_all(sums, ("y", "core", "x"), split_axis=0, concat_axis=0, tiled=True)
    rows_shape = [jax.ShapeDtypeStruct((40, width), f32)] * 3
    qkv_sums = pl.pallas_call(
        spread_kernel, in_specs=[vmem], out_specs=[vmem] * 3, out_shape=rows_shape, compiler_params=limit, name="spread"
    )(sums)
    big_sums = pl.pallas_call(
        widen_kernel, in_specs=[vmem], out_specs=[vmem] * 3, out_shape=rows_shape, compiler_params=limit, name="widen"
    )(big_sums)
    line_sums = jnp.sum(sums[:, 40, :120].astype(f32), axis=0).reshape(3, 40)
    scale_low = query_scale.astype(bf16).astype(f32)
    scale_sum = LOG2E / math.sqrt(HD) * jax.nn.sigmoid(scale_low) * line_sums[2]
    grad_home = [grad_home[0]] + [ring_shift(grad_home[k], k) for k in (1, 2, 3)]
    grad_home = by_source(grad_home, z, 0).reshape(16, 8, width)

    return (
        outputs, grad_home, qkv_sums[0], qkv_sums[1], qkv_sums[2],
        big_sums[0], big_sums[1], big_sums[2], line_sums[0], line_sums[1], scale_sum,
    )


def solution(mesh):
    names = ("dp", "ctx")
    body = per_device
    if dict(mesh.shape) == {"dp": 16, "ctx": 2}:
        mesh = Mesh(mesh.devices.reshape(4, 2, 2, 2), ("z", "y", "core", "x"))
        names = mesh.axis_names
        body = planes
    seq, mat, line = P(None, names, None), P(names, None), P(names)
    return jax.shard_map(
        body,
        mesh=mesh,
        in_specs=(seq,) * 2 + (mat,) * 6 + (line,) * 3 + (P(), P()),
        out_specs=(seq,) * 2 + (mat,) * 6 + (line,) * 3,
        check_vma=False,
    )
```

```python
import math

import jax
import jax.numpy as jnp
from jax import lax
from jax.experimental import pallas as pl
from jax.experimental.pallas import tpu as pltpu
from jax.sharding import Mesh, PartitionSpec as P

H = 16
HD = 80


def mult_trans(left, right):
    return lax.dot_general(
        left, right, (((1,), (1,)), ((), ())), preferred_element_type=jnp.float32
    )


def trans_mult(left, right):
    return lax.dot_general(
        left, right, (((0,), (0,)), ((), ())), preferred_element_type=jnp.float32
    )


def position_of(index, local_rows, piece_rows, groups):
    column = index // local_rows
    within = index % local_rows
    return (within // piece_rows * groups + column) * piece_rows + within % piece_rows


def norm_back(grad_hidden, normed, inverse, gain_value):
    grad_normed = grad_hidden * gain_value
    return inverse * (grad_normed - normed * jnp.mean(grad_normed * normed, axis=1, keepdims=True))


def per_device(
    inputs,
    cotangent,
    w_query,
    w_key,
    w_value,
    w_output,
    w_up,
    w_down,
    attn_gain,
    mlp_gain,
    query_scale,
    deal,
    lengths,
):
    groups = lax.axis_size("ctx")
    group_index = lax.axis_index("dp")
    ctx_index = lax.axis_index("ctx")
    head_count = H
    head_dim = HD
    piece_rows = inputs.shape[1]
    seq_numbers = jnp.arange(inputs.shape[0], dtype=jnp.int32)
    seq_lengths = jnp.sum(
        jnp.where(deal[None, :] == seq_numbers[:, None], lengths[None, :], 0), axis=1
    )
    local_in, local_cot = (
        lax.all_to_all(inputs, "dp", split_axis=0, concat_axis=1, tiled=True),
        lax.all_to_all(cotangent, "dp", split_axis=0, concat_axis=1, tiled=True),
    )
    seq_count, local_rows, model_width = local_in.shape
    padded = local_rows * groups
    token_count = seq_count * local_rows
    my_lengths = lax.dynamic_slice_in_dim(seq_lengths, group_index * seq_count, seq_count, 0)
    query_pos = position_of(
        ctx_index * local_rows + jnp.arange(local_rows, dtype=jnp.int32),
        local_rows,
        piece_rows,
        groups,
    )
    flat_in = local_in.reshape(token_count, model_width).astype(jnp.float32)
    flat_cot = local_cot.reshape(token_count, model_width)
    lowered = (
        w_query.astype(jnp.bfloat16),
        w_key.astype(jnp.bfloat16),
        w_value.astype(jnp.bfloat16),
        w_output.astype(jnp.bfloat16),
        w_up.astype(jnp.bfloat16),
        w_down.astype(jnp.bfloat16),
        attn_gain.astype(jnp.bfloat16),
        mlp_gain.astype(jnp.bfloat16),
        query_scale.astype(jnp.bfloat16),
    )
    gathered = (
        lax.all_gather(lowered[0], ("dp", "ctx"), axis=0, tiled=True),
        lax.all_gather(lowered[1], ("dp", "ctx"), axis=0, tiled=True),
        lax.all_gather(lowered[2], ("dp", "ctx"), axis=0, tiled=True),
        lax.all_gather(lowered[3], ("dp", "ctx"), axis=0, tiled=True),
        lax.all_gather(lowered[4], ("dp", "ctx"), axis=0, tiled=True),
        lax.all_gather(lowered[5], ("dp", "ctx"), axis=0, tiled=True),
        lax.all_gather(lowered[6], ("dp", "ctx"), axis=0, tiled=True),
        lax.all_gather(lowered[7], ("dp", "ctx"), axis=0, tiled=True),
        lax.all_gather(lowered[8], ("dp", "ctx"), axis=0, tiled=True),
    )
    (
        query_full,
        key_full,
        value_full,
        output_full,
        up_full,
        down_full,
        gain_one,
        gain_two,
        scale_raw,
    ) = gathered
    inv_one = lax.rsqrt(jnp.mean(flat_in * flat_in, axis=1, keepdims=True) + 1e-06)
    normed_one = flat_in * inv_one
    hidden_one = (normed_one * gain_one.astype(jnp.float32)).astype(jnp.bfloat16)
    scale_param = scale_raw.astype(jnp.float32)
    query_mult = 1.442695041 / math.sqrt(head_dim) * jax.nn.softplus(scale_param)
    query_pre = jnp.dot(hidden_one, query_full, preferred_element_type=jnp.float32)
    queries = (query_pre * query_mult).astype(jnp.bfloat16)
    keys_local = jnp.dot(hidden_one, key_full, preferred_element_type=jnp.float32).astype(
        jnp.bfloat16
    )
    values_local = jnp.dot(hidden_one, value_full, preferred_element_type=jnp.float32).astype(
        jnp.bfloat16
    )
    four_shape = (seq_count, local_rows, head_count, head_dim)
    query_four = queries.reshape(four_shape)
    keys_three = keys_local.reshape(seq_count, local_rows, model_width)
    values_three = values_local.reshape(seq_count, local_rows, model_width)

    def live_between(row_pos, key_pos):
        allowed = (key_pos[None, None, :] <= row_pos[None, :, None]) & (
            key_pos[None, None, :] < my_lengths[:, None, None]
        )
        return allowed[:, :, None, :]

    def live_mask(key_pos):
        return live_between(query_pos, key_pos)

    def attend_block(state_now, key_block, value_block, first_row):
        run_max, run_sum, run_acc = state_now
        block_len = key_block.shape[1]
        key_pos = position_of(
            first_row + jnp.arange(block_len, dtype=jnp.int32), local_rows, piece_rows, groups
        )
        key_four = key_block.reshape(seq_count, block_len, head_count, head_dim)
        value_four = value_block.reshape(seq_count, block_len, head_count, head_dim)
        scores = jnp.einsum(
            "srhd,skhd->srhk", query_four, key_four, preferred_element_type=jnp.float32
        )
        allowed = live_mask(key_pos)
        masked = jnp.where(allowed, scores, -1e30)
        new_max = jnp.maximum(run_max, jnp.max(masked, axis=3))
        weights_now = jnp.exp(jnp.where(allowed, masked - new_max[..., None], -1e30))
        factor = jnp.exp(run_max - new_max)
        new_sum = run_sum * factor + jnp.sum(weights_now, axis=3)
        added = jnp.einsum(
            "srhk,skhd->srhd",
            weights_now.astype(jnp.bfloat16),
            value_four,
            preferred_element_type=jnp.float32,
        )
        return (new_max, new_sum, run_acc * factor[..., None] + added)

    start_state = (
        jnp.full((seq_count, local_rows, head_count), -1e30, jnp.float32),
        jnp.zeros((seq_count, local_rows, head_count), jnp.float32),
        jnp.zeros(four_shape, jnp.float32),
    )
    key_piece = lax.all_gather(keys_three, "ctx", axis=1, tiled=True)
    value_piece = lax.all_gather(values_three, "ctx", axis=1, tiled=True)
    piece_len = key_piece.shape[1]
    fold_block_len = 512 if piece_len % 512 == 0 else piece_len

    def one_block(state_now, block_index):
        offset = block_index * fold_block_len
        key_block = lax.dynamic_slice_in_dim(key_piece, offset, fold_block_len, 1)
        value_block = lax.dynamic_slice_in_dim(value_piece, offset, fold_block_len, 1)
        return (attend_block(state_now, key_block, value_block, offset), None)

    result_state, unused = lax.scan(
        one_block, start_state, jnp.arange(piece_len // fold_block_len, dtype=jnp.int32)
    )
    run_max, run_sum, run_acc = result_state
    log_total = run_max + jnp.log(run_sum)
    attn_exact = run_acc / run_sum[..., None]
    attended = attn_exact.reshape(token_count, model_width).astype(jnp.bfloat16)
    middle = flat_in + jnp.dot(attended, output_full, preferred_element_type=jnp.float32)
    inv_two = lax.rsqrt(jnp.mean(middle * middle, axis=1, keepdims=True) + 1e-06)
    normed_two = middle * inv_two
    hidden_two = (normed_two * gain_two.astype(jnp.float32)).astype(jnp.bfloat16)
    up_pre = jnp.dot(hidden_two, up_full, preferred_element_type=jnp.float32)
    active = jax.nn.silu(up_pre).astype(jnp.bfloat16)
    result = (middle + jnp.dot(active, down_full, preferred_element_type=jnp.float32)).astype(
        jnp.bfloat16
    )
    back_weights = (
        lax.all_gather(lowered[0], ("dp", "ctx"), axis=0, tiled=True),
        lax.all_gather(lowered[1], ("dp", "ctx"), axis=0, tiled=True),
        lax.all_gather(lowered[2], ("dp", "ctx"), axis=0, tiled=True),
        lax.all_gather(lowered[3], ("dp", "ctx"), axis=0, tiled=True),
        lax.all_gather(lowered[4], ("dp", "ctx"), axis=0, tiled=True),
        lax.all_gather(lowered[5], ("dp", "ctx"), axis=0, tiled=True),
        lax.all_gather(lowered[6], ("dp", "ctx"), axis=0, tiled=True),
        lax.all_gather(lowered[7], ("dp", "ctx"), axis=0, tiled=True),
        lax.all_gather(lowered[8], ("dp", "ctx"), axis=0, tiled=True),
    )
    (
        query_back,
        key_back,
        value_back,
        output_back,
        up_back,
        down_back,
        gain_one_back,
        gain_two_back,
        scale_back,
    ) = back_weights
    cot_wide = flat_cot.astype(jnp.float32)
    grad_down = trans_mult(active, flat_cot)
    grad_active = mult_trans(flat_cot, down_back)
    sigma_up = jax.nn.sigmoid(up_pre)
    grad_up_pre = (grad_active * sigma_up * (1.0 + up_pre * (1.0 - sigma_up))).astype(jnp.bfloat16)
    grad_up = trans_mult(hidden_two, grad_up_pre)
    grad_hidden_two = mult_trans(grad_up_pre, up_back)
    grad_gain_two = jnp.sum(grad_hidden_two * normed_two, axis=0)
    grad_middle = cot_wide + norm_back(
        grad_hidden_two, normed_two, inv_two, gain_two_back.astype(jnp.float32)
    )
    grad_middle_low = grad_middle.astype(jnp.bfloat16)
    grad_output = trans_mult(attended, grad_middle_low)
    grad_attended = mult_trans(grad_middle_low, output_back).astype(jnp.bfloat16)
    grad_att_four = grad_attended.reshape(four_shape)
    delta_rows = jnp.sum(grad_att_four.astype(jnp.float32) * attn_exact, axis=3)
    key_all, value_all = (
        lax.all_gather(keys_three, "ctx", axis=1, tiled=True),
        lax.all_gather(values_three, "ctx", axis=1, tiled=True),
    )
    block_len = min(512, padded)

    def back_block(block_index, state_now):
        grad_query, grad_key_all, grad_value_all = state_now
        offset = block_index * block_len
        key_block = lax.dynamic_slice_in_dim(key_all, offset, block_len, 1).reshape(
            seq_count, block_len, head_count, head_dim
        )
        value_block = lax.dynamic_slice_in_dim(value_all, offset, block_len, 1).reshape(
            seq_count, block_len, head_count, head_dim
        )
        key_pos = position_of(
            offset + jnp.arange(block_len, dtype=jnp.int32), local_rows, piece_rows, groups
        )
        scores = jnp.einsum(
            "srhd,skhd->srhk", query_four, key_block, preferred_element_type=jnp.float32
        )
        probs = jnp.exp(jnp.where(live_mask(key_pos), scores - log_total[..., None], -1e30))
        grad_value_block = jnp.einsum(
            "srhk,srhd->skhd",
            probs.astype(jnp.bfloat16),
            grad_att_four,
            preferred_element_type=jnp.float32,
        )
        grad_probs = jnp.einsum(
            "srhd,skhd->srhk", grad_att_four, value_block, preferred_element_type=jnp.float32
        )
        grad_scores = (probs * (grad_probs - delta_rows[..., None])).astype(jnp.bfloat16)
        grad_query = grad_query + jnp.einsum(
            "srhk,skhd->srhd", grad_scores, key_block, preferred_element_type=jnp.float32
        )
        grad_key_block = jnp.einsum(
            "srhk,srhd->skhd", grad_scores, query_four, preferred_element_type=jnp.float32
        )
        grad_key_all = lax.dynamic_update_slice_in_dim(
            grad_key_all, grad_key_block.reshape(seq_count, block_len, model_width), offset, 1
        )
        grad_value_all = lax.dynamic_update_slice_in_dim(
            grad_value_all, grad_value_block.reshape(seq_count, block_len, model_width), offset, 1
        )
        return (grad_query, grad_key_all, grad_value_all)

    zero_all = jnp.zeros((seq_count, padded, model_width), jnp.float32)
    grad_query, grad_key_all, grad_value_all = lax.fori_loop(
        0, padded // block_len, back_block, (jnp.zeros(four_shape, jnp.float32), zero_all, zero_all)
    )
    grad_key_mine, grad_value_mine = (
        lax.psum_scatter(
            grad_key_all.astype(jnp.bfloat16), "ctx", scatter_dimension=1, tiled=True
        ).astype(jnp.float32),
        lax.psum_scatter(
            grad_value_all.astype(jnp.bfloat16), "ctx", scatter_dimension=1, tiled=True
        ).astype(jnp.float32),
    )
    grad_query_flat = grad_query.reshape(token_count, model_width)
    grad_query_pre = (grad_query_flat * query_mult).astype(jnp.bfloat16)
    grad_scale = (
        1.442695041
        / math.sqrt(head_dim)
        * jax.nn.sigmoid(scale_back.astype(jnp.float32))
        * jnp.sum(grad_query_flat * query_pre, axis=0)
    )
    grad_key_low = grad_key_mine.reshape(token_count, model_width).astype(jnp.bfloat16)
    grad_value_low = grad_value_mine.reshape(token_count, model_width).astype(jnp.bfloat16)
    grad_wq = trans_mult(hidden_one, grad_query_pre)
    grad_wk = trans_mult(hidden_one, grad_key_low)
    grad_wv = trans_mult(hidden_one, grad_value_low)
    grad_hidden_one = (
        mult_trans(grad_query_pre, query_back)
        + mult_trans(grad_key_low, key_back)
        + mult_trans(grad_value_low, value_back)
    )
    grad_gain_one = jnp.sum(grad_hidden_one * normed_one, axis=0)
    grad_in = grad_middle + norm_back(
        grad_hidden_one, normed_one, inv_one, gain_one_back.astype(jnp.float32)
    )
    matrix_stack = jnp.stack([grad_wq, grad_wk, grad_wv, grad_output, grad_up, grad_down], axis=0)
    vector_stack = jnp.stack([grad_gain_one, grad_gain_two, grad_scale], axis=0)
    matrix_sums, vector_sums = (
        lax.psum_scatter(matrix_stack, ("dp", "ctx"), scatter_dimension=1, tiled=True),
        lax.psum_scatter(vector_stack, ("dp", "ctx"), scatter_dimension=1, tiled=True),
    )
    out_local = result.reshape(seq_count, local_rows, model_width)
    grad_local = grad_in.astype(jnp.bfloat16).reshape(seq_count, local_rows, model_width)
    back_out, back_grad = (
        lax.all_to_all(out_local, "dp", split_axis=1, concat_axis=0, tiled=True),
        lax.all_to_all(grad_local, "dp", split_axis=1, concat_axis=0, tiled=True),
    )
    return (
        back_out,
        back_grad,
        matrix_sums[0],
        matrix_sums[1],
        matrix_sums[2],
        matrix_sums[3],
        matrix_sums[4],
        matrix_sums[5],
        vector_sums[0],
        vector_sums[1],
        vector_sums[2],
    )


LOG2E = 1.442695041
CODES = (0, 1, 4, 5)


def plane_shift(value, step):
    if step == 1:
        return lax.ppermute(value, "x", [(0, 1), (1, 0)])
    if step == 2:
        return lax.ppermute(value, "y", [(0, 1), (1, 0)])
    return lax.ppermute(value, ("y", "x"), [(0, 3), (1, 2), (2, 1), (3, 0)])


def core_swap(value):
    return lax.ppermute(value, "core", [(0, 1), (1, 0)])


def ring_shift(value, step):
    return lax.ppermute(value, "z", [(i, (i + step) % 4) for i in range(4)])


def pick(array, index):
    return lax.dynamic_index_in_dim(array, index, 0, keepdims=False)


def by_source(pieces, z_index, axis):
    pieces = [jnp.expand_dims(item, axis) for item in pieces]
    shape = [1] * pieces[0].ndim
    shape[axis] = 4
    hop = ((z_index - jnp.arange(4, dtype=jnp.int32)) % 4).reshape(shape)
    made = pieces[0]
    for k in (1, 2, 3):
        made = jnp.where(hop == k, pieces[k], made)
    return made


def pair(mine, other, index, axis):
    shape = [1] * (mine.ndim + 1)
    shape[axis] = 2
    slot = jnp.arange(2, dtype=jnp.int32).reshape(shape)
    return jnp.where(slot == index, jnp.expand_dims(mine, axis), jnp.expand_dims(other, axis))


def row_positions(shape, dim, plane_index):
    row = lax.broadcasted_iota(jnp.int32, shape, dim)
    chip = (row // 32) % 4
    code = (chip % 2) + 4 * (chip // 2) + 2 * (row // 128)
    return 64 * ((row % 32) // 8) + 8 * (plane_index ^ code) + row % 8


def live_pairs(info_ref, seq):
    shape = (256, 256)
    query_pos = row_positions(shape, 0, info_ref[1])
    key_pos = row_positions(shape, 1, info_ref[1])
    return (key_pos <= query_pos) & (key_pos < info_ref[2 + seq])


def block_rows(near_ref, far_ref):
    return jnp.concatenate([near_ref[...], far_ref[...]], axis=0).reshape(256, near_ref.shape[2])


def soft_probs(query, key, live):
    scores = mult_trans(query, key)
    scores = jnp.where(live, scores, -1e30)
    top = jnp.max(scores, axis=1, keepdims=True)
    weights = jnp.where(live, jnp.exp(scores - top), 0.0)
    return weights / jnp.sum(weights, axis=1, keepdims=True)


def attend_kernel(
    info_ref, near_ref, far_ref, gain_ref, mult_ref, w_ref, pre_ref, att_ref
):
    seq = pl.program_id(0)
    live = live_pairs(info_ref, seq)
    wide = block_rows(near_ref, far_ref).astype(jnp.float32)
    inverse = lax.rsqrt(jnp.mean(wide * wide, axis=1, keepdims=True) + 1e-06)
    hidden = (wide * inverse * gain_ref[...]).astype(jnp.bfloat16)
    pre = jnp.dot(hidden, w_ref[...], preferred_element_type=jnp.float32)
    pre_ref[...] = pre.reshape(2, 4, 32, 480)
    query = (pre[:, 0:160] * mult_ref[...]).astype(jnp.bfloat16)
    key = pre[:, 160:320].astype(jnp.bfloat16)
    value = pre[:, 320:480].astype(jnp.bfloat16)
    heads = []
    for head in range(2):
        part = slice(80 * head, 80 * head + 80)
        probs = soft_probs(query[:, part], key[:, part], live).astype(jnp.bfloat16)
        heads.append(jnp.dot(probs, value[:, part], preferred_element_type=jnp.float32))
    att = jnp.concatenate(heads, axis=1).astype(jnp.bfloat16).reshape(2, 4, 32, 160)
    for chip in range(4):
        for core in range(2):
            att_ref[chip, core] = att[core, chip]


def attend_back_kernel(
    info_ref, near_ref, far_ref, gain_ref, mult_ref, w_ref, pre_ref, grad_near, grad_far, gain_two_ref, result_ref,
    hid_near, hid_far, send_0, send_1, send_2, send_3, w_acc, gain_acc, scale_acc, lines,
):
    seq = pl.program_id(0)

    @pl.when(seq == 0)
    def _():
        w_acc[...] = jnp.zeros_like(w_acc)
        gain_acc[...] = jnp.zeros_like(gain_acc)
        scale_acc[...] = jnp.zeros_like(scale_acc)

    live = live_pairs(info_ref, seq)
    wide = block_rows(near_ref, far_ref).astype(jnp.float32)
    inverse = lax.rsqrt(jnp.mean(wide * wide, axis=1, keepdims=True) + 1e-06)
    normed = wide * inverse
    hidden = (normed * gain_ref[...]).astype(jnp.bfloat16)
    pre = pre_ref[...].reshape(256, 480)
    mult = mult_ref[...]
    query = (pre[:, 0:160] * mult).astype(jnp.bfloat16)
    key = pre[:, 160:320].astype(jnp.bfloat16)
    value = pre[:, 320:480].astype(jnp.bfloat16)
    grad_att = jnp.concatenate([grad_near[:, 0], grad_far[:, 0]], axis=0).reshape(256, 160)
    grad_q, grad_k, grad_v = [], [], []
    for head in range(2):
        part = slice(80 * head, 80 * head + 80)
        probs = soft_probs(query[:, part], key[:, part], live)
        grad_probs = mult_trans(grad_att[:, part], value[:, part])
        delta = jnp.sum(probs * grad_probs, axis=1, keepdims=True)
        grad_scores = (probs * (grad_probs - delta)).astype(jnp.bfloat16)
        grad_v.append(trans_mult(probs.astype(jnp.bfloat16), grad_att[:, part]))
        grad_q.append(jnp.dot(grad_scores, key[:, part], preferred_element_type=jnp.float32))
        grad_k.append(trans_mult(grad_scores, query[:, part]))
    grad_query = jnp.concatenate(grad_q, axis=1)
    scale_acc[...] += jnp.sum(grad_query * pre[:, 0:160], axis=0, keepdims=True)
    joined = jnp.concatenate([grad_query * mult] + grad_k + grad_v, axis=1).astype(jnp.bfloat16)
    w_acc[...] += trans_mult(hidden, joined)
    grad_hidden = mult_trans(joined, w_ref[...])
    gain_acc[...] += jnp.sum(grad_hidden * normed, axis=0, keepdims=True)
    low = grad_hidden.astype(jnp.bfloat16).reshape(2, 4, 32, 1280)
    hid_near[...] = low[0]
    hid_far[...] = low[1]

    @pl.when(seq == 3)
    def _():
        lines[...] = jnp.zeros_like(lines)
        for which, source in enumerate((gain_acc, gain_two_ref)):
            for owner in range(32):
                lane = 120 * (owner % 4) + 40 * which
                lines[owner // 4, :, lane : lane + 40] = source[:, 40 * owner : 40 * owner + 40]
        for part in range(4):
            lane = 120 * part + 80
            lines[info_ref[1], :, lane : lane + 40] = scale_acc[:, 40 * part : 40 * part + 40]
        blank = jnp.zeros((14, 480), jnp.float32)
        for hop, send in enumerate((send_0, send_1, send_2, send_3)):
            target = (info_ref[0] + hop) & 3
            rows = w_acc[pl.ds(pl.multiple_of(target * 320, 320), 320), :]
            block = jnp.concatenate([rows, lines[2 * target], lines[2 * target + 1], blank], axis=0)
            send[0:336, :] = block.astype(jnp.bfloat16)
            result = result_ref[target].reshape(32, 1280).astype(jnp.bfloat16)
            send[336:368, :] = result[:, 0:480]
            send[368:400, :] = result[:, 480:960]
            send[400:432, 0:320] = result[:, 960:1280]
            send[400:432, 320:480] = jnp.zeros((32, 160), jnp.bfloat16)


def block_index(z_index, y_index, core):
    return pl.ds(pl.multiple_of((4 * z_index + 2 * y_index + core) * 80, 80), 80)


def arrival_rows(info_ref, w, z_index, y_index, core):
    if w > 0:
        return block_index(z_index, y_index, core)
    block = 4 * z_index + 2 * y_index + core
    code = info_ref[1] ^ (block // 2)
    arrival = 2 * ((code & 1) + 2 * (code // 4)) + ((code // 2) & 1)
    return pl.ds(pl.multiple_of(160 * arrival + 80 * (block & 1), 80), 80)


def feed_kernel(
    info_ref, x_ref, g_ref, atts, far_atts, gain_ref,
    near_rows, across_a, across_b, far_near_rows, far_across_a, far_across_b,
    out_ref, pack_ref, dmid_ref, datt_0, datt_1, datt_2, datt_3, gain_grad,
    weights, sems,
):
    y_index, core_index = info_ref[1] // 4, (info_ref[1] // 2) % 2
    copies = []
    for w in range(3):
        moved = []
        for core, own, others in (
            (core_index, near_rows, (across_a, across_b)),
            (1 - core_index, far_near_rows, (far_across_a, far_across_b)),
        ):
            for z_index in range(4):
                moved.append((own.at[z_index, w], z_index, y_index, core))
                moved.append((others[z_index // 2].at[z_index % 2, w], z_index, 1 - y_index, core))
        copies.append([
            pltpu.make_async_copy(src, weights.at[w, arrival_rows(info_ref, w, *place)], sems.at[w, i])
            for i, (src, *place) in enumerate(moved)
        ])
    for group in copies:
        for copy in group:
            copy.start()
    datts = (datt_0, datt_1, datt_2, datt_3)

    for copy in copies[0]:
        copy.wait()
    att = jnp.concatenate(
        [(far_atts if core else atts)[chip, core] for chip in range(4) for core in range(2)], axis=1
    )
    middle = x_ref[...].astype(jnp.float32)
    middle += jnp.dot(att, weights[0], preferred_element_type=jnp.float32)
    inverse = lax.rsqrt(jnp.mean(middle * middle, axis=1, keepdims=True) + 1e-06)
    normed = middle * inverse
    gain = gain_ref[...]
    hidden = (normed * gain).astype(jnp.bfloat16)
    pack_ref[1] = hidden
    for copy in copies[1]:
        copy.wait()
    up = jnp.dot(hidden, weights[1], preferred_element_type=jnp.float32)
    sigma = jax.nn.sigmoid(up)
    active = (up * sigma).astype(jnp.bfloat16)
    pack_ref[0] = active
    for copy in copies[2]:
        copy.wait()
    down = jnp.dot(active, weights[2], preferred_element_type=jnp.float32)
    result = middle + down
    for seq in range(4):
        for plane_z in range(4):
            row = 32 * seq + 8 * plane_z
            out_ref[plane_z, seq] = result[row : row + 8]
    cot = g_ref[...]
    grad_act = mult_trans(cot, weights[2])
    grad_up = (grad_act * sigma * (1.0 + up * (1.0 - sigma))).astype(jnp.bfloat16)
    pack_ref[2] = grad_up
    grad_hidden = mult_trans(grad_up, weights[1])
    gain_grad[...] = jnp.sum(grad_hidden * normed, axis=0, keepdims=True)
    grad_mid = cot.astype(jnp.float32) + norm_back(grad_hidden, normed, inverse, gain)
    dmid_ref[...] = grad_mid
    low = grad_mid.astype(jnp.bfloat16)
    pack_ref[3] = low
    grad_att = mult_trans(low, weights[0]).astype(jnp.bfloat16)
    for chip in range(4):
        for core in range(2):
            lane = 160 * (2 * chip + core)
            datts[chip][core] = grad_att[:, lane : lane + 160]


def grads_kernel(
    info_ref, pack_ref, far_pack, atts, far_atts, cot_ref, far_cot, half_a, kept_b, away_b, stage, sems
):
    y_index, core_index = info_ref[1] // 4, (info_ref[1] // 2) % 2

    def leave(w):
        copies = []
        for half in range(2):
            targets = [(half, row, half_a.at[half, w, row]) for row in range(2)]
            targets += [(2 + half, y_index, kept_b.at[half, w]), (2 + half, 1 - y_index, away_b.at[half, w])]
            for i, (z_index, row, target) in enumerate(targets):
                block = pl.ds(pl.multiple_of(160 * z_index + 80 * row, 80), 80)
                copies.append(pltpu.make_async_copy(stage.at[w, block], target, sems.at[w, 4 * half + i]))
        return copies

    def both(near, far):
        return jnp.concatenate([near, far], axis=0)

    cots = both(cot_ref[...], far_cot[...])
    for core in range(2):

        @pl.when(core_index == core)
        def _():
            def own_columns(near, far):
                return both(*(
                    jnp.concatenate([ref[:, 160 * i + 80 * core : 160 * i + 80 * core + 80] for i in range(8)], axis=1)
                    for ref in (near, far)
                ))

            acts = own_columns(pack_ref.at[0], far_pack.at[0])
            stage[2] = trans_mult(acts, cots).astype(jnp.bfloat16)
            for copy in leave(2):
                copy.start()
            acts = own_columns(pack_ref.at[1], far_pack.at[1])
            stage[1] = trans_mult(acts, both(pack_ref[2], far_pack[2])).astype(jnp.bfloat16)
            for copy in leave(1):
                copy.start()
            grads = both(pack_ref[3], far_pack[3])
            pieces = []
            for chip in range(4):
                for source in range(2):
                    near, far = (far_atts, far_atts) if source else (atts, atts)
                    pieces.append(both(near[chip, source], far[chip, 1 - source])[:, 80 * core : 80 * core + 80])
            made = trans_mult(jnp.concatenate(pieces, axis=1), grads).astype(jnp.bfloat16)
            for i in range(8):
                place = (info_ref[1] ^ (CODES[i // 2] + 2 * (i % 2))) * 80
                stage[0, pl.ds(pl.multiple_of(place, 80), 80), :] = made[80 * i : 80 * i + 80]
            for copy in leave(0):
                copy.start()

    for w in range(3):
        for copy in leave(w):
            copy.wait()


def meet_kernel(info_ref, half_a, from_a, half_b, from_b, keep_a, away_a, keep_b, away_b):
    y_index, x_index = info_ref[1] // 4, info_ref[1] % 2
    for half in range(2):
        for w in range(3):
            for row, out in ((y_index, keep_a), (1 - y_index, away_a)):
                out[half, w] = sum_low(half_a[half, w, row, x_index], from_a[half, w, row])
            for row, out in ((x_index, keep_b), (1 - x_index, away_b)):
                out[half, w] = sum_low(half_b[half, w, row], from_b[half, w, row])


def join_kernel(keep_a, from_a, keep_b, from_b, out_ref):
    for half in range(2):
        for w in range(3):
            out_ref[half, w] = sum_low(keep_a[half, w], from_a[half, w])
            out_ref[2 + half, w] = sum_low(keep_b[half, w], from_b[half, w])


def sum_low(left, right):
    return (left.astype(jnp.float32) + right.astype(jnp.float32)).astype(jnp.bfloat16)


def norm_kernel(info_ref, hid_0, hid_1, hid_2, hid_3, x_ref, dmid_ref, gain_ref, out_0, out_1, out_2, out_3, rows):
    grad = hid_0[...].astype(jnp.float32)
    for item in (hid_1, hid_2, hid_3):
        grad += item[...].astype(jnp.float32)
    wide = x_ref[...].astype(jnp.float32)
    inverse = lax.rsqrt(jnp.mean(wide * wide, axis=1, keepdims=True) + 1e-06)
    grad = dmid_ref[...] + norm_back(grad, wide * inverse, inverse, gain_ref[...])
    for seq in range(4):
        for plane_z in range(4):
            row = 32 * seq + 8 * plane_z
            rows[plane_z, seq] = grad[row : row + 8]
    for hop, out in enumerate((out_0, out_1, out_2, out_3)):
        out[...] = rows[(info_ref[0] + hop) & 3].astype(jnp.bfloat16)


def fold_kernel(info_ref, part_0, part_1, part_2, part_3, out_ref, home_ref, line):
    parts = (part_0, part_1, part_2, part_3)
    total = sum(item[0:336, :].astype(jnp.float32) for item in parts)
    line[...] = jnp.zeros_like(line)
    for owner in range(8):
        lane = 120 * (owner % 4)
        line[0:1, 0:120] = total[320 + owner // 4 : 321 + owner // 4, lane : lane + 120]
        block = jnp.concatenate([total[40 * owner : 40 * owner + 40], line[...]], axis=0)
        out_ref[owner] = block.astype(jnp.bfloat16)
    for hop, item in enumerate(parts):
        source = (info_ref[0] - hop) & 3
        rows = item[336:432, :].astype(jnp.float32)
        for i, lanes in enumerate((480, 480, 320)):
            part = rows[32 * i : 32 * i + 32, 0:lanes].reshape(4, 8, lanes).astype(jnp.bfloat16)
            home_ref[source, :, :, 480 * i : 480 * i + lanes] = part


def spread_kernel(in_ref, *outs):
    for which, out in enumerate(outs):
        for owner in range(8):
            part = in_ref[owner, 0:40, 160 * which : 160 * which + 160]
            out[:, 160 * owner : 160 * owner + 160] = part.astype(jnp.float32)


def widen_kernel(in_ref, *outs):
    for which, out in enumerate(outs):
        out[...] = in_ref[which].astype(jnp.float32)


def whole(shape):
    return pl.BlockSpec(shape, lambda *_: (0,) * len(shape))


def seq_block(*lead, width):
    count = len(lead)
    return pl.BlockSpec((*lead, 32, width), lambda s, info: (*(0,) * count, s, 0))


def planes(
    inputs, cotangent, w_query, w_key, w_value, w_output, w_up, w_down,
    attn_gain, mlp_gain, query_scale, deal, lengths,
):
    f32, bf16 = jnp.float32, jnp.bfloat16
    z, y, c, x = (lax.axis_index(name) for name in ("z", "y", "core", "x"))
    plane = 4 * y + 2 * c + x
    width = 1280
    seqs = jnp.arange(16, dtype=jnp.int32)
    seq_lengths = jnp.sum(jnp.where(deal[None, :] == seqs[:, None], lengths[None, :], 0), axis=1)
    my_lengths = lax.dynamic_slice_in_dim(seq_lengths, 4 * z, 4, 0)
    info = jnp.concatenate([jnp.stack([z, plane]), my_lengths]).astype(jnp.int32)

    vec = jnp.concatenate([attn_gain, mlp_gain, query_scale]).astype(bf16)
    vec_block = jnp.zeros((1, 8, width), bf16).at[0, 0, :120].set(vec)
    in_four = inputs.reshape(4, 4, 8, width)
    sent = [jnp.concatenate([pick(in_four, (z + k) % 4), vec_block]) for k in range(4)]
    qkv = jnp.stack([w_query, w_key, w_value]).astype(bf16)
    *sent, qkv = lax.optimization_barrier((*sent, qkv))
    got = [sent[0]] + [ring_shift(sent[k], k) for k in (1, 2, 3)]
    x_rows = by_source([item[:4] for item in got], z, 1).reshape(128, width)
    vec_rows = by_source([item[4, 0] for item in got], z, 0)
    vec_rows = jnp.concatenate([vec_rows, jnp.zeros((4, width), bf16)])
    own = jnp.concatenate([x_rows, vec_rows])

    big = jnp.stack([w_output, w_up, w_down]).astype(bf16)
    big = lax.all_gather(big, "z", axis=0)

    qkv = qkv.reshape(3, 40, 8, 160).transpose(2, 1, 0, 3).reshape(8, 40, 480)
    qkv = lax.all_to_all(qkv, ("y", "core", "x"), split_axis=0, concat_axis=0, tiled=True)
    own, qkv = lax.optimization_barrier((own, qkv.reshape(320, 480)))
    w_qkv = lax.all_gather(qkv, "z", axis=0, tiled=True)
    near = jnp.stack([own] + [plane_shift(own, step) for step in (1, 2, 3)])
    big, near, cotangent = lax.optimization_barrier((big, near, cotangent))
    far = core_swap(near)
    beside, across = plane_shift(big, 1), plane_shift(big, 2)
    relay_a, relay_b = beside[:2], across[2:]
    cot_rows = lax.all_to_all(cotangent.reshape(4, 4, 8, width), "z", split_axis=0, concat_axis=0, tiled=True)
    relay_a, relay_b, cot_rows = lax.optimization_barrier((relay_a, relay_b, cot_rows))
    across_a, across_b = plane_shift(relay_a, 2), plane_shift(relay_b, 1)

    vecs = jnp.stack([near[:, 128:132, :120], far[:, 128:132, :120]])
    vecs = vecs.astype(f32).reshape(2, 2, 2, 4, 120)
    vecs = jnp.where(c == 0, vecs, vecs[::-1])
    vecs = jnp.where(y == 0, vecs, vecs[:, ::-1])
    vecs = jnp.where(x == 0, vecs, vecs[:, :, ::-1])
    vecs = vecs.reshape(2, 2, 2, 4, 3, 40).transpose(4, 3, 1, 0, 2, 5).reshape(3, width)
    gain_one, gain_two = vecs[0:1], vecs[1:2]
    my_scale = lax.dynamic_slice_in_dim(vecs[2:3], 160 * plane, 160, 1)
    query_mult = LOG2E / math.sqrt(HD) * jax.nn.softplus(my_scale)

    limit = pltpu.CompilerParams(vmem_limit_bytes=50 * 1024 * 1024)
    pre, att_made = pl.pallas_call(
        attend_kernel,
        grid_spec=pltpu.PrefetchScalarGridSpec(
            num_scalar_prefetch=1,
            grid=(4,),
            in_specs=[
                seq_block(4, width=width), seq_block(4, width=width),
                whole((1, width)), whole((1, 160)), whole((width, 480)),
            ],
            out_specs=[seq_block(2, 4, width=480), seq_block(4, 2, width=160)],
        ),
        out_shape=[
            jax.ShapeDtypeStruct((2, 4, 128, 480), f32),
            jax.ShapeDtypeStruct((4, 2, 128, 160), bf16),
        ],
        compiler_params=limit,
        cost_estimate=pl.CostEstimate(flops=9_000_000_000, bytes_accessed=8_000_000, transcendentals=600_000),
        name="attend",
    )(info, near, far, gain_one, query_mult, w_qkv)

    near_rows = pair(big, beside, x, 2).reshape(4, 3, 80, width)
    att_made, near_rows, across_a, across_b = lax.optimization_barrier((att_made, near_rows, across_a, across_b))
    far_near_rows = core_swap(near_rows)
    atts = [att_made[0]] + [plane_shift(att_made[step], step) for step in (1, 2, 3)]
    atts = jnp.stack(atts)
    far_atts = core_swap(atts)
    across_a = pair(across[:2], across_a, x, 2).reshape(2, 3, 80, width)
    across_b = pair(across[2:], across_b, x, 2).reshape(2, 3, 80, width)
    far_across_a, far_across_b = core_swap(across_a), core_swap(across_b)
    cot_rows = cot_rows.transpose(1, 0, 2, 3).reshape(128, width)
    far_cot = core_swap(cot_rows)
    far_cot, far_atts, cot_rows = lax.optimization_barrier((far_cot, far_atts, cot_rows))
    datt_shape = jax.ShapeDtypeStruct((2, 128, 160), bf16)
    smem = pl.BlockSpec(memory_space=pltpu.SMEM)
    vmem = pl.BlockSpec(memory_space=pltpu.VMEM)
    hbm = pl.BlockSpec(memory_space=pl.ANY)
    out_rows, pack, grad_mid, *datts, gain_two_grad = pl.pallas_call(
        feed_kernel,
        in_specs=[smem] + [vmem] * 5 + [hbm] * 6,
        out_specs=[vmem] * 8,
        out_shape=[
            jax.ShapeDtypeStruct((4, 4, 8, width), f32),
            jax.ShapeDtypeStruct((4, 128, width), bf16),
            jax.ShapeDtypeStruct((128, width), f32),
        ]
        + [datt_shape] * 4
        + [jax.ShapeDtypeStruct((1, width), f32)],
        scratch_shapes=[pltpu.VMEM((3, width, width), bf16), pltpu.SemaphoreType.DMA((3, 16))],
        compiler_params=limit,
        cost_estimate=pl.CostEstimate(flops=12_000_000_000, bytes_accessed=13_000_000, transcendentals=200_000),
        name="feed",
    )(info, x_rows, cot_rows, atts, far_atts, gain_two, near_rows, across_a, across_b, far_near_rows, far_across_a, far_across_b)

    back = [datts[0]] + [plane_shift(datts[step], step) for step in (1, 2, 3)]

    part_shape = jax.ShapeDtypeStruct((2, 3, 80, width), bf16)
    half_a, kept_b, away_b = pl.pallas_call(
        grads_kernel,
        in_specs=[smem] + [vmem] * 6,
        out_specs=[hbm] * 3,
        out_shape=[jax.ShapeDtypeStruct((2, 3, 2, 80, width), bf16), part_shape, part_shape],
        scratch_shapes=[pltpu.VMEM((3, 640, width), bf16), pltpu.SemaphoreType.DMA((3, 8))],
        compiler_params=limit,
        cost_estimate=pl.CostEstimate(flops=6_000_000_000, bytes_accessed=8_000_000, transcendentals=0),
        name="grads",
    )(info, pack, core_swap(pack), atts, far_atts, cot_rows, far_cot)

    half_a, kept_b, away_b, *back = lax.optimization_barrier((half_a, kept_b, away_b, *back))
    half_a = half_a.reshape(2, 3, 2, 2, 40, width)
    away_a = lax.dynamic_index_in_dim(half_a, 1 - x, 3, keepdims=False)
    away_a, away_b, grad_atts = lax.optimization_barrier((away_a, away_b, jnp.stack(back)))
    from_a, from_b = plane_shift(away_a, 1), plane_shift(away_b, 2)
    hid_near, hid_far, *send = pl.pallas_call(
        attend_back_kernel,
        grid_spec=pltpu.PrefetchScalarGridSpec(
            num_scalar_prefetch=1,
            grid=(4,),
            in_specs=[
                seq_block(4, width=width), seq_block(4, width=width),
                whole((1, width)), whole((1, 160)), whole((width, 480)),
                seq_block(2, 4, width=480),
                *[pl.BlockSpec((4, 1, 32, 160), lambda s, info, core=core: (0, core, s, 0)) for core in range(2)],
                whole((1, width)), whole((4, 4, 8, width)),
            ],
            out_specs=[
                seq_block(4, width=width), seq_block(4, width=width),
                *[whole((432, 480))] * 4,
            ],
            scratch_shapes=[
                pltpu.VMEM((width, 480), f32), pltpu.VMEM((1, width), f32),
                pltpu.VMEM((1, 160), f32), pltpu.VMEM((8, 1, 480), f32),
            ],
        ),
        out_shape=[
            jax.ShapeDtypeStruct((4, 128, width), bf16),
            jax.ShapeDtypeStruct((4, 128, width), bf16),
            *[jax.ShapeDtypeStruct((432, 480), bf16)] * 4,
        ],
        compiler_params=limit,
        cost_estimate=pl.CostEstimate(flops=15_000_000_000, bytes_accessed=12_000_000, transcendentals=600_000),
        name="attend_back",
    )(info, near, far, gain_one, query_mult, w_qkv, pre, grad_atts, core_swap(grad_atts), gain_two_grad, out_rows)

    one, three = ring_shift(send[1], 1), ring_shift(send[3], 3)
    swapped = core_swap(hid_far)
    from_a, from_b, one, three, late = lax.optimization_barrier((from_a, from_b, one, three, send[2]))
    two = ring_shift(late, 2)
    hid = [sum_low(hid_near[i], swapped[i]) for i in range(4)]
    split = (2, 3, 2, 40, width)
    keep_a, away_a, keep_b, away_b = pl.pallas_call(
        meet_kernel,
        in_specs=[smem] + [vmem] * 4,
        out_specs=[vmem] * 4,
        out_shape=[jax.ShapeDtypeStruct((2, 3, 40, width), bf16)] * 4,
        compiler_params=limit,
        cost_estimate=pl.CostEstimate(flops=3_000_000_000, bytes_accessed=8_000_000, transcendentals=0),
        name="meet",
    )(info, half_a, from_a, kept_b.reshape(split), from_b.reshape(split))
    kept = pl.pallas_call(
        join_kernel,
        in_specs=[vmem] * 4,
        out_specs=vmem,
        out_shape=jax.ShapeDtypeStruct((4, 3, 40, width), bf16),
        compiler_params=limit,
        cost_estimate=pl.CostEstimate(flops=2_000_000_000, bytes_accessed=4_000_000, transcendentals=0),
        name="join",
    )(keep_a, plane_shift(away_a, 2), keep_b, plane_shift(away_b, 1))
    *hid, kept, two = lax.optimization_barrier((*hid, kept, two))
    moved = [plane_shift(hid[step], step) for step in (1, 2, 3)]
    moved[0], mine = lax.optimization_barrier((moved[0], send[0]))
    big_sums = lax.psum_scatter(kept, "z", scatter_dimension=0, tiled=True)[0]
    grad_home = pl.pallas_call(
        norm_kernel,
        in_specs=[smem] + [vmem] * 7,
        out_specs=[vmem] * 4,
        out_shape=[jax.ShapeDtypeStruct((4, 8, width), bf16)] * 4,
        scratch_shapes=[pltpu.VMEM((4, 4, 8, width), f32)],
        compiler_params=limit,
        cost_estimate=pl.CostEstimate(flops=2_000_000_000, bytes_accessed=2_500_000, transcendentals=128),
        name="norm",
    )(info, hid[0], *moved, x_rows, grad_mid, gain_one)
    sums, outputs = pl.pallas_call(
        fold_kernel,
        in_specs=[smem] + [vmem] * 4,
        out_specs=[vmem] * 2,
        out_shape=[jax.ShapeDtypeStruct((8, 48, 480), bf16), jax.ShapeDtypeStruct((4, 4, 8, width), bf16)],
        scratch_shapes=[pltpu.VMEM((8, 480), f32)],
        compiler_params=limit,
        cost_estimate=pl.CostEstimate(flops=2_000_000_000, bytes_accessed=1_600_000, transcendentals=0),
        name="fold",
    )(info, mine, one, two, three)
    sums = lax.all_to_all(sums, ("y", "core", "x"), split_axis=0, concat_axis=0, tiled=True)
    rows_shape = [jax.ShapeDtypeStruct((40, width), f32)] * 3
    qkv_sums = pl.pallas_call(
        spread_kernel, in_specs=[vmem], out_specs=[vmem] * 3, out_shape=rows_shape, compiler_params=limit, name="spread"
    )(sums)
    big_sums = pl.pallas_call(
        widen_kernel, in_specs=[vmem], out_specs=[vmem] * 3, out_shape=rows_shape, compiler_params=limit, name="widen"
    )(big_sums)
    line_sums = jnp.sum(sums[:, 40, :120].astype(f32), axis=0).reshape(3, 40)
    scale_low = query_scale.astype(bf16).astype(f32)
    scale_sum = LOG2E / math.sqrt(HD) * jax.nn.sigmoid(scale_low) * line_sums[2]
    grad_home = [grad_home[0]] + [ring_shift(grad_home[k], k) for k in (1, 2, 3)]
    grad_home = by_source(grad_home, z, 0).reshape(16, 8, width)

    return (
        outputs.reshape(16, 8, width), grad_home, qkv_sums[0], qkv_sums[1], qkv_sums[2],
        big_sums[0], big_sums[1], big_sums[2], line_sums[0], line_sums[1], scale_sum,
    )


def solution(mesh):
    names = ("dp", "ctx")
    body = per_device
    if dict(mesh.shape) == {"dp": 16, "ctx": 2}:
        mesh = Mesh(mesh.devices.reshape(4, 2, 2, 2), ("z", "y", "core", "x"))
        names = mesh.axis_names
        body = planes
    seq, mat, line = P(None, names, None), P(names, None), P(names)
    return jax.shard_map(
        body,
        mesh=mesh,
        in_specs=(seq,) * 2 + (mat,) * 6 + (line,) * 3 + (P(), P()),
        out_specs=(seq,) * 2 + (mat,) * 6 + (line,) * 3,
        check_vma=False,
    )
```

```python
import math

import jax
import jax.numpy as jnp
from jax import lax
from jax.experimental import pallas as pl
from jax.experimental.pallas import tpu as pltpu
from jax.sharding import Mesh, PartitionSpec as P

H = 16
HD = 80


def mult_trans(left, right):
    return lax.dot_general(
        left, right, (((1,), (1,)), ((), ())), preferred_element_type=jnp.float32
    )


def trans_mult(left, right):
    return lax.dot_general(
        left, right, (((0,), (0,)), ((), ())), preferred_element_type=jnp.float32
    )


def position_of(index, local_rows, piece_rows, groups):
    column = index // local_rows
    within = index % local_rows
    return (within // piece_rows * groups + column) * piece_rows + within % piece_rows


def norm_back(grad_hidden, normed, inverse, gain_value):
    grad_normed = grad_hidden * gain_value
    return inverse * (grad_normed - normed * jnp.mean(grad_normed * normed, axis=1, keepdims=True))


def per_device(
    inputs,
    cotangent,
    w_query,
    w_key,
    w_value,
    w_output,
    w_up,
    w_down,
    attn_gain,
    mlp_gain,
    query_scale,
    deal,
    lengths,
):
    groups = lax.axis_size("ctx")
    group_index = lax.axis_index("dp")
    ctx_index = lax.axis_index("ctx")
    head_count = H
    head_dim = HD
    piece_rows = inputs.shape[1]
    seq_numbers = jnp.arange(inputs.shape[0], dtype=jnp.int32)
    seq_lengths = jnp.sum(
        jnp.where(deal[None, :] == seq_numbers[:, None], lengths[None, :], 0), axis=1
    )
    local_in, local_cot = (
        lax.all_to_all(inputs, "dp", split_axis=0, concat_axis=1, tiled=True),
        lax.all_to_all(cotangent, "dp", split_axis=0, concat_axis=1, tiled=True),
    )
    seq_count, local_rows, model_width = local_in.shape
    padded = local_rows * groups
    token_count = seq_count * local_rows
    my_lengths = lax.dynamic_slice_in_dim(seq_lengths, group_index * seq_count, seq_count, 0)
    query_pos = position_of(
        ctx_index * local_rows + jnp.arange(local_rows, dtype=jnp.int32),
        local_rows,
        piece_rows,
        groups,
    )
    flat_in = local_in.reshape(token_count, model_width).astype(jnp.float32)
    flat_cot = local_cot.reshape(token_count, model_width)
    lowered = (
        w_query.astype(jnp.bfloat16),
        w_key.astype(jnp.bfloat16),
        w_value.astype(jnp.bfloat16),
        w_output.astype(jnp.bfloat16),
        w_up.astype(jnp.bfloat16),
        w_down.astype(jnp.bfloat16),
        attn_gain.astype(jnp.bfloat16),
        mlp_gain.astype(jnp.bfloat16),
        query_scale.astype(jnp.bfloat16),
    )
    gathered = (
        lax.all_gather(lowered[0], ("dp", "ctx"), axis=0, tiled=True),
        lax.all_gather(lowered[1], ("dp", "ctx"), axis=0, tiled=True),
        lax.all_gather(lowered[2], ("dp", "ctx"), axis=0, tiled=True),
        lax.all_gather(lowered[3], ("dp", "ctx"), axis=0, tiled=True),
        lax.all_gather(lowered[4], ("dp", "ctx"), axis=0, tiled=True),
        lax.all_gather(lowered[5], ("dp", "ctx"), axis=0, tiled=True),
        lax.all_gather(lowered[6], ("dp", "ctx"), axis=0, tiled=True),
        lax.all_gather(lowered[7], ("dp", "ctx"), axis=0, tiled=True),
        lax.all_gather(lowered[8], ("dp", "ctx"), axis=0, tiled=True),
    )
    (
        query_full,
        key_full,
        value_full,
        output_full,
        up_full,
        down_full,
        gain_one,
        gain_two,
        scale_raw,
    ) = gathered
    inv_one = lax.rsqrt(jnp.mean(flat_in * flat_in, axis=1, keepdims=True) + 1e-06)
    normed_one = flat_in * inv_one
    hidden_one = (normed_one * gain_one.astype(jnp.float32)).astype(jnp.bfloat16)
    scale_param = scale_raw.astype(jnp.float32)
    query_mult = 1.442695041 / math.sqrt(head_dim) * jax.nn.softplus(scale_param)
    query_pre = jnp.dot(hidden_one, query_full, preferred_element_type=jnp.float32)
    queries = (query_pre * query_mult).astype(jnp.bfloat16)
    keys_local = jnp.dot(hidden_one, key_full, preferred_element_type=jnp.float32).astype(
        jnp.bfloat16
    )
    values_local = jnp.dot(hidden_one, value_full, preferred_element_type=jnp.float32).astype(
        jnp.bfloat16
    )
    four_shape = (seq_count, local_rows, head_count, head_dim)
    query_four = queries.reshape(four_shape)
    keys_three = keys_local.reshape(seq_count, local_rows, model_width)
    values_three = values_local.reshape(seq_count, local_rows, model_width)

    def live_between(row_pos, key_pos):
        allowed = (key_pos[None, None, :] <= row_pos[None, :, None]) & (
            key_pos[None, None, :] < my_lengths[:, None, None]
        )
        return allowed[:, :, None, :]

    def live_mask(key_pos):
        return live_between(query_pos, key_pos)

    def attend_block(state_now, key_block, value_block, first_row):
        run_max, run_sum, run_acc = state_now
        block_len = key_block.shape[1]
        key_pos = position_of(
            first_row + jnp.arange(block_len, dtype=jnp.int32), local_rows, piece_rows, groups
        )
        key_four = key_block.reshape(seq_count, block_len, head_count, head_dim)
        value_four = value_block.reshape(seq_count, block_len, head_count, head_dim)
        scores = jnp.einsum(
            "srhd,skhd->srhk", query_four, key_four, preferred_element_type=jnp.float32
        )
        allowed = live_mask(key_pos)
        masked = jnp.where(allowed, scores, -1e30)
        new_max = jnp.maximum(run_max, jnp.max(masked, axis=3))
        weights_now = jnp.exp(jnp.where(allowed, masked - new_max[..., None], -1e30))
        factor = jnp.exp(run_max - new_max)
        new_sum = run_sum * factor + jnp.sum(weights_now, axis=3)
        added = jnp.einsum(
            "srhk,skhd->srhd",
            weights_now.astype(jnp.bfloat16),
            value_four,
            preferred_element_type=jnp.float32,
        )
        return (new_max, new_sum, run_acc * factor[..., None] + added)

    start_state = (
        jnp.full((seq_count, local_rows, head_count), -1e30, jnp.float32),
        jnp.zeros((seq_count, local_rows, head_count), jnp.float32),
        jnp.zeros(four_shape, jnp.float32),
    )
    key_piece = lax.all_gather(keys_three, "ctx", axis=1, tiled=True)
    value_piece = lax.all_gather(values_three, "ctx", axis=1, tiled=True)
    piece_len = key_piece.shape[1]
    fold_block_len = 512 if piece_len % 512 == 0 else piece_len

    def one_block(state_now, block_index):
        offset = block_index * fold_block_len
        key_block = lax.dynamic_slice_in_dim(key_piece, offset, fold_block_len, 1)
        value_block = lax.dynamic_slice_in_dim(value_piece, offset, fold_block_len, 1)
        return (attend_block(state_now, key_block, value_block, offset), None)

    result_state, unused = lax.scan(
        one_block, start_state, jnp.arange(piece_len // fold_block_len, dtype=jnp.int32)
    )
    run_max, run_sum, run_acc = result_state
    log_total = run_max + jnp.log(run_sum)
    attn_exact = run_acc / run_sum[..., None]
    attended = attn_exact.reshape(token_count, model_width).astype(jnp.bfloat16)
    middle = flat_in + jnp.dot(attended, output_full, preferred_element_type=jnp.float32)
    inv_two = lax.rsqrt(jnp.mean(middle * middle, axis=1, keepdims=True) + 1e-06)
    normed_two = middle * inv_two
    hidden_two = (normed_two * gain_two.astype(jnp.float32)).astype(jnp.bfloat16)
    up_pre = jnp.dot(hidden_two, up_full, preferred_element_type=jnp.float32)
    active = jax.nn.silu(up_pre).astype(jnp.bfloat16)
    result = (middle + jnp.dot(active, down_full, preferred_element_type=jnp.float32)).astype(
        jnp.bfloat16
    )
    back_weights = (
        lax.all_gather(lowered[0], ("dp", "ctx"), axis=0, tiled=True),
        lax.all_gather(lowered[1], ("dp", "ctx"), axis=0, tiled=True),
        lax.all_gather(lowered[2], ("dp", "ctx"), axis=0, tiled=True),
        lax.all_gather(lowered[3], ("dp", "ctx"), axis=0, tiled=True),
        lax.all_gather(lowered[4], ("dp", "ctx"), axis=0, tiled=True),
        lax.all_gather(lowered[5], ("dp", "ctx"), axis=0, tiled=True),
        lax.all_gather(lowered[6], ("dp", "ctx"), axis=0, tiled=True),
        lax.all_gather(lowered[7], ("dp", "ctx"), axis=0, tiled=True),
        lax.all_gather(lowered[8], ("dp", "ctx"), axis=0, tiled=True),
    )
    (
        query_back,
        key_back,
        value_back,
        output_back,
        up_back,
        down_back,
        gain_one_back,
        gain_two_back,
        scale_back,
    ) = back_weights
    cot_wide = flat_cot.astype(jnp.float32)
    grad_down = trans_mult(active, flat_cot)
    grad_active = mult_trans(flat_cot, down_back)
    sigma_up = jax.nn.sigmoid(up_pre)
    grad_up_pre = (grad_active * sigma_up * (1.0 + up_pre * (1.0 - sigma_up))).astype(jnp.bfloat16)
    grad_up = trans_mult(hidden_two, grad_up_pre)
    grad_hidden_two = mult_trans(grad_up_pre, up_back)
    grad_gain_two = jnp.sum(grad_hidden_two * normed_two, axis=0)
    grad_middle = cot_wide + norm_back(
        grad_hidden_two, normed_two, inv_two, gain_two_back.astype(jnp.float32)
    )
    grad_middle_low = grad_middle.astype(jnp.bfloat16)
    grad_output = trans_mult(attended, grad_middle_low)
    grad_attended = mult_trans(grad_middle_low, output_back).astype(jnp.bfloat16)
    grad_att_four = grad_attended.reshape(four_shape)
    delta_rows = jnp.sum(grad_att_four.astype(jnp.float32) * attn_exact, axis=3)
    key_all, value_all = (
        lax.all_gather(keys_three, "ctx", axis=1, tiled=True),
        lax.all_gather(values_three, "ctx", axis=1, tiled=True),
    )
    block_len = min(512, padded)

    def back_block(block_index, state_now):
        grad_query, grad_key_all, grad_value_all = state_now
        offset = block_index * block_len
        key_block = lax.dynamic_slice_in_dim(key_all, offset, block_len, 1).reshape(
            seq_count, block_len, head_count, head_dim
        )
        value_block = lax.dynamic_slice_in_dim(value_all, offset, block_len, 1).reshape(
            seq_count, block_len, head_count, head_dim
        )
        key_pos = position_of(
            offset + jnp.arange(block_len, dtype=jnp.int32), local_rows, piece_rows, groups
        )
        scores = jnp.einsum(
            "srhd,skhd->srhk", query_four, key_block, preferred_element_type=jnp.float32
        )
        probs = jnp.exp(jnp.where(live_mask(key_pos), scores - log_total[..., None], -1e30))
        grad_value_block = jnp.einsum(
            "srhk,srhd->skhd",
            probs.astype(jnp.bfloat16),
            grad_att_four,
            preferred_element_type=jnp.float32,
        )
        grad_probs = jnp.einsum(
            "srhd,skhd->srhk", grad_att_four, value_block, preferred_element_type=jnp.float32
        )
        grad_scores = (probs * (grad_probs - delta_rows[..., None])).astype(jnp.bfloat16)
        grad_query = grad_query + jnp.einsum(
            "srhk,skhd->srhd", grad_scores, key_block, preferred_element_type=jnp.float32
        )
        grad_key_block = jnp.einsum(
            "srhk,srhd->skhd", grad_scores, query_four, preferred_element_type=jnp.float32
        )
        grad_key_all = lax.dynamic_update_slice_in_dim(
            grad_key_all, grad_key_block.reshape(seq_count, block_len, model_width), offset, 1
        )
        grad_value_all = lax.dynamic_update_slice_in_dim(
            grad_value_all, grad_value_block.reshape(seq_count, block_len, model_width), offset, 1
        )
        return (grad_query, grad_key_all, grad_value_all)

    zero_all = jnp.zeros((seq_count, padded, model_width), jnp.float32)
    grad_query, grad_key_all, grad_value_all = lax.fori_loop(
        0, padded // block_len, back_block, (jnp.zeros(four_shape, jnp.float32), zero_all, zero_all)
    )
    grad_key_mine, grad_value_mine = (
        lax.psum_scatter(
            grad_key_all.astype(jnp.bfloat16), "ctx", scatter_dimension=1, tiled=True
        ).astype(jnp.float32),
        lax.psum_scatter(
            grad_value_all.astype(jnp.bfloat16), "ctx", scatter_dimension=1, tiled=True
        ).astype(jnp.float32),
    )
    grad_query_flat = grad_query.reshape(token_count, model_width)
    grad_query_pre = (grad_query_flat * query_mult).astype(jnp.bfloat16)
    grad_scale = (
        1.442695041
        / math.sqrt(head_dim)
        * jax.nn.sigmoid(scale_back.astype(jnp.float32))
        * jnp.sum(grad_query_flat * query_pre, axis=0)
    )
    grad_key_low = grad_key_mine.reshape(token_count, model_width).astype(jnp.bfloat16)
    grad_value_low = grad_value_mine.reshape(token_count, model_width).astype(jnp.bfloat16)
    grad_wq = trans_mult(hidden_one, grad_query_pre)
    grad_wk = trans_mult(hidden_one, grad_key_low)
    grad_wv = trans_mult(hidden_one, grad_value_low)
    grad_hidden_one = (
        mult_trans(grad_query_pre, query_back)
        + mult_trans(grad_key_low, key_back)
        + mult_trans(grad_value_low, value_back)
    )
    grad_gain_one = jnp.sum(grad_hidden_one * normed_one, axis=0)
    grad_in = grad_middle + norm_back(
        grad_hidden_one, normed_one, inv_one, gain_one_back.astype(jnp.float32)
    )
    matrix_stack = jnp.stack([grad_wq, grad_wk, grad_wv, grad_output, grad_up, grad_down], axis=0)
    vector_stack = jnp.stack([grad_gain_one, grad_gain_two, grad_scale], axis=0)
    matrix_sums, vector_sums = (
        lax.psum_scatter(matrix_stack, ("dp", "ctx"), scatter_dimension=1, tiled=True),
        lax.psum_scatter(vector_stack, ("dp", "ctx"), scatter_dimension=1, tiled=True),
    )
    out_local = result.reshape(seq_count, local_rows, model_width)
    grad_local = grad_in.astype(jnp.bfloat16).reshape(seq_count, local_rows, model_width)
    back_out, back_grad = (
        lax.all_to_all(out_local, "dp", split_axis=1, concat_axis=0, tiled=True),
        lax.all_to_all(grad_local, "dp", split_axis=1, concat_axis=0, tiled=True),
    )
    return (
        back_out,
        back_grad,
        matrix_sums[0],
        matrix_sums[1],
        matrix_sums[2],
        matrix_sums[3],
        matrix_sums[4],
        matrix_sums[5],
        vector_sums[0],
        vector_sums[1],
        vector_sums[2],
    )


LOG2E = 1.442695041
CODES = (0, 1, 4, 5)


def plane_shift(value, step):
    if step == 1:
        return lax.ppermute(value, "x", [(0, 1), (1, 0)])
    if step == 2:
        return lax.ppermute(value, "y", [(0, 1), (1, 0)])
    return lax.ppermute(value, ("y", "x"), [(0, 3), (1, 2), (2, 1), (3, 0)])


def core_swap(value):
    return lax.ppermute(value, "core", [(0, 1), (1, 0)])


def ring_shift(value, step):
    return lax.ppermute(value, "z", [(i, (i + step) % 4) for i in range(4)])


def pick(array, index):
    return lax.dynamic_index_in_dim(array, index, 0, keepdims=False)


def by_source(pieces, z_index, axis):
    pieces = [jnp.expand_dims(item, axis) for item in pieces]
    shape = [1] * pieces[0].ndim
    shape[axis] = 4
    hop = ((z_index - jnp.arange(4, dtype=jnp.int32)) % 4).reshape(shape)
    made = pieces[0]
    for k in (1, 2, 3):
        made = jnp.where(hop == k, pieces[k], made)
    return made


def pair(mine, other, index, axis):
    shape = [1] * (mine.ndim + 1)
    shape[axis] = 2
    slot = jnp.arange(2, dtype=jnp.int32).reshape(shape)
    return jnp.where(slot == index, jnp.expand_dims(mine, axis), jnp.expand_dims(other, axis))


def row_positions(shape, dim, plane_index):
    row = lax.broadcasted_iota(jnp.int32, shape, dim)
    chip = (row // 32) % 4
    code = (chip % 2) + 4 * (chip // 2) + 2 * (row // 128)
    return 64 * ((row % 32) // 8) + 8 * (plane_index ^ code) + row % 8


def live_pairs(info_ref, seq):
    shape = (256, 256)
    query_pos = row_positions(shape, 0, info_ref[1])
    key_pos = row_positions(shape, 1, info_ref[1])
    return (key_pos <= query_pos) & (key_pos < info_ref[2 + seq])


def block_rows(near_ref, far_ref):
    return jnp.concatenate([near_ref[...], far_ref[...]], axis=0).reshape(256, near_ref.shape[2])


def soft_probs(query, key, live):
    scores = mult_trans(query, key)
    scores = jnp.where(live, scores, -1e30)
    top = jnp.max(scores, axis=1, keepdims=True)
    weights = jnp.where(live, jnp.exp(scores - top), 0.0)
    return weights / jnp.sum(weights, axis=1, keepdims=True)


def attend_kernel(
    info_ref, near_ref, far_ref, gain_ref, mult_ref, w_ref, pre_ref, att_ref
):
    seq = pl.program_id(0)
    live = live_pairs(info_ref, seq)
    wide = block_rows(near_ref, far_ref).astype(jnp.float32)
    inverse = lax.rsqrt(jnp.mean(wide * wide, axis=1, keepdims=True) + 1e-06)
    hidden = (wide * inverse * gain_ref[...]).astype(jnp.bfloat16)
    pre = jnp.dot(hidden, w_ref[...], preferred_element_type=jnp.float32)
    pre_ref[...] = pre.reshape(2, 4, 32, 480)
    query = (pre[:, 0:160] * mult_ref[...]).astype(jnp.bfloat16)
    key = pre[:, 160:320].astype(jnp.bfloat16)
    value = pre[:, 320:480].astype(jnp.bfloat16)
    heads = []
    for head in range(2):
        part = slice(80 * head, 80 * head + 80)
        probs = soft_probs(query[:, part], key[:, part], live).astype(jnp.bfloat16)
        heads.append(jnp.dot(probs, value[:, part], preferred_element_type=jnp.float32))
    att = jnp.concatenate(heads, axis=1).astype(jnp.bfloat16).reshape(2, 4, 32, 160)
    for chip in range(4):
        for core in range(2):
            att_ref[chip, core] = att[core, chip]


def attend_back_kernel(
    info_ref, near_ref, far_ref, gain_ref, mult_ref, w_ref, pre_ref, grad_near, grad_far, gain_two_ref,
    hid_near, hid_far, send_ref, w_acc, gain_acc, scale_acc, lines,
):
    seq = pl.program_id(0)

    @pl.when(seq == 0)
    def _():
        w_acc[...] = jnp.zeros_like(w_acc)
        gain_acc[...] = jnp.zeros_like(gain_acc)
        scale_acc[...] = jnp.zeros_like(scale_acc)

    live = live_pairs(info_ref, seq)
    wide = block_rows(near_ref, far_ref).astype(jnp.float32)
    inverse = lax.rsqrt(jnp.mean(wide * wide, axis=1, keepdims=True) + 1e-06)
    normed = wide * inverse
    hidden = (normed * gain_ref[...]).astype(jnp.bfloat16)
    pre = pre_ref[...].reshape(256, 480)
    mult = mult_ref[...]
    query = (pre[:, 0:160] * mult).astype(jnp.bfloat16)
    key = pre[:, 160:320].astype(jnp.bfloat16)
    value = pre[:, 320:480].astype(jnp.bfloat16)
    grad_att = jnp.concatenate([grad_near[:, 0], grad_far[:, 0]], axis=0).reshape(256, 160)
    grad_q, grad_k, grad_v = [], [], []
    for head in range(2):
        part = slice(80 * head, 80 * head + 80)
        probs = soft_probs(query[:, part], key[:, part], live)
        grad_probs = mult_trans(grad_att[:, part], value[:, part])
        delta = jnp.sum(probs * grad_probs, axis=1, keepdims=True)
        grad_scores = (probs * (grad_probs - delta)).astype(jnp.bfloat16)
        grad_v.append(trans_mult(probs.astype(jnp.bfloat16), grad_att[:, part]))
        grad_q.append(jnp.dot(grad_scores, key[:, part], preferred_element_type=jnp.float32))
        grad_k.append(trans_mult(grad_scores, query[:, part]))
    grad_query = jnp.concatenate(grad_q, axis=1)
    scale_acc[...] += jnp.sum(grad_query * pre[:, 0:160], axis=0, keepdims=True)
    joined = jnp.concatenate([grad_query * mult] + grad_k + grad_v, axis=1).astype(jnp.bfloat16)
    w_acc[...] += trans_mult(hidden, joined)
    grad_hidden = mult_trans(joined, w_ref[...])
    gain_acc[...] += jnp.sum(grad_hidden * normed, axis=0, keepdims=True)
    low = grad_hidden.astype(jnp.bfloat16).reshape(2, 4, 32, 1280)
    hid_near[...] = low[0]
    hid_far[...] = low[1]

    @pl.when(seq == 3)
    def _():
        lines[...] = jnp.zeros_like(lines)
        for which, source in enumerate((gain_acc, gain_two_ref)):
            for owner in range(32):
                lane = 120 * (owner % 4) + 40 * which
                lines[owner // 4, :, lane : lane + 40] = source[:, 40 * owner : 40 * owner + 40]
        for part in range(4):
            lane = 120 * part + 80
            lines[info_ref[1], :, lane : lane + 40] = scale_acc[:, 40 * part : 40 * part + 40]
        blank = jnp.zeros((14, 480), jnp.float32)
        for target in range(4):
            rows = w_acc[320 * target : 320 * target + 320, :]
            block = jnp.concatenate([rows, lines[2 * target], lines[2 * target + 1], blank], axis=0)
            send_ref[target] = block.astype(jnp.bfloat16)


def block_index(z_index, y_index, core):
    return pl.ds(pl.multiple_of((4 * z_index + 2 * y_index + core) * 80, 80), 80)


def arrival_rows(info_ref, w, z_index, y_index, core):
    if w > 0:
        return block_index(z_index, y_index, core)
    block = 4 * z_index + 2 * y_index + core
    code = info_ref[1] ^ (block // 2)
    arrival = 2 * ((code & 1) + 2 * (code // 4)) + ((code // 2) & 1)
    return pl.ds(pl.multiple_of(160 * arrival + 80 * (block & 1), 80), 80)


def feed_kernel(
    info_ref, x_ref, g_ref, atts, far_atts, gain_ref,
    near_rows, across_a, across_b, far_near_rows, far_across_a, far_across_b,
    out_ref, pack_ref, dmid_ref, datt_0, datt_1, datt_2, datt_3, gain_grad,
    weights, sems,
):
    y_index, core_index = info_ref[1] // 4, (info_ref[1] // 2) % 2
    copies = []
    for w in range(3):
        moved = []
        for core, own, others in (
            (core_index, near_rows, (across_a, across_b)),
            (1 - core_index, far_near_rows, (far_across_a, far_across_b)),
        ):
            for z_index in range(4):
                moved.append((own.at[z_index, w], z_index, y_index, core))
                moved.append((others[z_index // 2].at[z_index % 2, w], z_index, 1 - y_index, core))
        copies.append([
            pltpu.make_async_copy(src, weights.at[w, arrival_rows(info_ref, w, *place)], sems.at[w, i])
            for i, (src, *place) in enumerate(moved)
        ])
    for group in copies:
        for copy in group:
            copy.start()
    datts = (datt_0, datt_1, datt_2, datt_3)

    for copy in copies[0]:
        copy.wait()
    att = jnp.concatenate(
        [(far_atts if core else atts)[chip, core] for chip in range(4) for core in range(2)], axis=1
    )
    middle = x_ref[...].astype(jnp.float32)
    middle += jnp.dot(att, weights[0], preferred_element_type=jnp.float32)
    inverse = lax.rsqrt(jnp.mean(middle * middle, axis=1, keepdims=True) + 1e-06)
    normed = middle * inverse
    gain = gain_ref[...]
    hidden = (normed * gain).astype(jnp.bfloat16)
    pack_ref[1] = hidden
    for copy in copies[1]:
        copy.wait()
    up = jnp.dot(hidden, weights[1], preferred_element_type=jnp.float32)
    sigma = jax.nn.sigmoid(up)
    active = (up * sigma).astype(jnp.bfloat16)
    pack_ref[0] = active
    for copy in copies[2]:
        copy.wait()
    down = jnp.dot(active, weights[2], preferred_element_type=jnp.float32)
    result = middle + down
    for seq in range(4):
        for plane_z in range(4):
            row = 32 * seq + 8 * plane_z
            out_ref[plane_z, seq] = result[row : row + 8].astype(jnp.bfloat16)
    cot = g_ref[...]
    grad_act = mult_trans(cot, weights[2])
    grad_up = (grad_act * sigma * (1.0 + up * (1.0 - sigma))).astype(jnp.bfloat16)
    pack_ref[2] = grad_up
    grad_hidden = mult_trans(grad_up, weights[1])
    gain_grad[...] = jnp.sum(grad_hidden * normed, axis=0, keepdims=True)
    grad_mid = cot.astype(jnp.float32) + norm_back(grad_hidden, normed, inverse, gain)
    dmid_ref[...] = grad_mid
    low = grad_mid.astype(jnp.bfloat16)
    pack_ref[3] = low
    grad_att = mult_trans(low, weights[0]).astype(jnp.bfloat16)
    for chip in range(4):
        for core in range(2):
            lane = 160 * (2 * chip + core)
            datts[chip][core] = grad_att[:, lane : lane + 160]


def grads_kernel(
    info_ref, pack_ref, far_pack, atts, far_atts, cot_ref, far_cot, half_a, kept_b, away_b, stage, sems
):
    y_index, core_index = info_ref[1] // 4, (info_ref[1] // 2) % 2

    def leave(w):
        copies = []
        for half in range(2):
            targets = [(half, row, half_a.at[half, w, row]) for row in range(2)]
            targets += [(2 + half, y_index, kept_b.at[half, w]), (2 + half, 1 - y_index, away_b.at[half, w])]
            for i, (z_index, row, target) in enumerate(targets):
                block = pl.ds(pl.multiple_of(160 * z_index + 80 * row, 80), 80)
                copies.append(pltpu.make_async_copy(stage.at[w, block], target, sems.at[w, 4 * half + i]))
        return copies

    def both(near, far):
        return jnp.concatenate([near, far], axis=0)

    cots = both(cot_ref[...], far_cot[...])
    for core in range(2):

        @pl.when(core_index == core)
        def _():
            def own_columns(near, far):
                return both(*(
                    jnp.concatenate([ref[:, 160 * i + 80 * core : 160 * i + 80 * core + 80] for i in range(8)], axis=1)
                    for ref in (near, far)
                ))

            acts = own_columns(pack_ref.at[0], far_pack.at[0])
            stage[2] = trans_mult(acts, cots).astype(jnp.bfloat16)
            for copy in leave(2):
                copy.start()
            acts = own_columns(pack_ref.at[1], far_pack.at[1])
            stage[1] = trans_mult(acts, both(pack_ref[2], far_pack[2])).astype(jnp.bfloat16)
            for copy in leave(1):
                copy.start()
            grads = both(pack_ref[3], far_pack[3])
            pieces = []
            for chip in range(4):
                for source in range(2):
                    near, far = (far_atts, far_atts) if source else (atts, atts)
                    pieces.append(both(near[chip, source], far[chip, 1 - source])[:, 80 * core : 80 * core + 80])
            made = trans_mult(jnp.concatenate(pieces, axis=1), grads).astype(jnp.bfloat16)
            for i in range(8):
                place = (info_ref[1] ^ (CODES[i // 2] + 2 * (i % 2))) * 80
                stage[0, pl.ds(pl.multiple_of(place, 80), 80), :] = made[80 * i : 80 * i + 80]
            for copy in leave(0):
                copy.start()

    for w in range(3):
        for copy in leave(w):
            copy.wait()


def meet_kernel(info_ref, half_a, from_a, half_b, from_b, keep_a, away_a, keep_b, away_b):
    y_index, x_index = info_ref[1] // 4, info_ref[1] % 2
    for half in range(2):
        for w in range(3):
            for row, out in ((y_index, keep_a), (1 - y_index, away_a)):
                out[half, w] = sum_low(half_a[half, w, row, x_index], from_a[half, w, row])
            for row, out in ((x_index, keep_b), (1 - x_index, away_b)):
                out[half, w] = sum_low(half_b[half, w, row], from_b[half, w, row])


def join_kernel(keep_a, from_a, keep_b, from_b, out_ref):
    for half in range(2):
        for w in range(3):
            out_ref[half, w] = sum_low(keep_a[half, w], from_a[half, w])
            out_ref[2 + half, w] = sum_low(keep_b[half, w], from_b[half, w])


def sum_low(left, right):
    return (left.astype(jnp.float32) + right.astype(jnp.float32)).astype(jnp.bfloat16)


def norm_kernel(info_ref, hid_0, hid_1, hid_2, hid_3, x_ref, dmid_ref, gain_ref, out_0, out_1, out_2, out_3, rows):
    grad = hid_0[...].astype(jnp.float32)
    for item in (hid_1, hid_2, hid_3):
        grad += item[...].astype(jnp.float32)
    wide = x_ref[...].astype(jnp.float32)
    inverse = lax.rsqrt(jnp.mean(wide * wide, axis=1, keepdims=True) + 1e-06)
    grad = dmid_ref[...] + norm_back(grad, wide * inverse, inverse, gain_ref[...])
    for seq in range(4):
        for plane_z in range(4):
            row = 32 * seq + 8 * plane_z
            rows[plane_z, seq] = grad[row : row + 8]
    for hop, out in enumerate((out_0, out_1, out_2, out_3)):
        out[...] = rows[(info_ref[0] + hop) & 3].astype(jnp.bfloat16)


def fold_kernel(in_ref, out_ref, line):
    total = in_ref[0].astype(jnp.float32)
    line[...] = jnp.zeros_like(line)
    for owner in range(8):
        lane = 120 * (owner % 4)
        line[0:1, 0:120] = total[320 + owner // 4 : 321 + owner // 4, lane : lane + 120]
        block = jnp.concatenate([total[40 * owner : 40 * owner + 40], line[...]], axis=0)
        out_ref[owner] = block.astype(jnp.bfloat16)


def spread_kernel(in_ref, *outs):
    for which, out in enumerate(outs):
        for owner in range(8):
            part = in_ref[owner, 0:40, 160 * which : 160 * which + 160]
            out[:, 160 * owner : 160 * owner + 160] = part.astype(jnp.float32)


def widen_kernel(in_ref, *outs):
    for which, out in enumerate(outs):
        out[...] = in_ref[which].astype(jnp.float32)


def whole(shape):
    return pl.BlockSpec(shape, lambda *_: (0,) * len(shape))


def seq_block(*lead, width):
    count = len(lead)
    return pl.BlockSpec((*lead, 32, width), lambda s, info: (*(0,) * count, s, 0))


def planes(
    inputs, cotangent, w_query, w_key, w_value, w_output, w_up, w_down,
    attn_gain, mlp_gain, query_scale, deal, lengths,
):
    f32, bf16 = jnp.float32, jnp.bfloat16
    z, y, c, x = (lax.axis_index(name) for name in ("z", "y", "core", "x"))
    plane = 4 * y + 2 * c + x
    width = 1280
    seqs = jnp.arange(16, dtype=jnp.int32)
    seq_lengths = jnp.sum(jnp.where(deal[None, :] == seqs[:, None], lengths[None, :], 0), axis=1)
    my_lengths = lax.dynamic_slice_in_dim(seq_lengths, 4 * z, 4, 0)
    info = jnp.concatenate([jnp.stack([z, plane]), my_lengths]).astype(jnp.int32)

    vec = jnp.concatenate([attn_gain, mlp_gain, query_scale]).astype(bf16)
    vec_block = jnp.zeros((1, 8, width), bf16).at[0, 0, :120].set(vec)
    in_four = inputs.reshape(4, 4, 8, width)
    sent = [jnp.concatenate([pick(in_four, (z + k) % 4), vec_block]) for k in range(4)]
    qkv = jnp.stack([w_query, w_key, w_value]).astype(bf16)
    *sent, qkv = lax.optimization_barrier((*sent, qkv))
    got = [sent[0]] + [ring_shift(sent[k], k) for k in (1, 2, 3)]
    x_rows = by_source([item[:4] for item in got], z, 1).reshape(128, width)
    vec_rows = by_source([item[4, 0] for item in got], z, 0)
    vec_rows = jnp.concatenate([vec_rows, jnp.zeros((4, width), bf16)])
    own = jnp.concatenate([x_rows, vec_rows])

    big = jnp.stack([w_output, w_up, w_down]).astype(bf16)
    big = lax.all_gather(big, "z", axis=0)

    qkv = qkv.reshape(3, 40, 8, 160).transpose(2, 1, 0, 3).reshape(8, 40, 480)
    qkv = lax.all_to_all(qkv, ("y", "core", "x"), split_axis=0, concat_axis=0, tiled=True)
    near = jnp.stack([own] + [plane_shift(own, step) for step in (1, 2, 3)])
    big, near, cotangent, qkv = lax.optimization_barrier((big, near, cotangent, qkv.reshape(320, 480)))
    w_qkv = lax.all_gather(qkv, "z", axis=0, tiled=True)
    far = core_swap(near)
    beside, across = plane_shift(big, 1), plane_shift(big, 2)
    relay_a, relay_b = beside[:2], across[2:]
    cot_rows = lax.all_to_all(cotangent.reshape(4, 4, 8, width), "z", split_axis=0, concat_axis=0, tiled=True)
    relay_a, relay_b, cot_rows = lax.optimization_barrier((relay_a, relay_b, cot_rows))
    across_a, across_b = plane_shift(relay_a, 2), plane_shift(relay_b, 1)

    vecs = jnp.stack([near[:, 128:132, :120], far[:, 128:132, :120]])
    vecs = vecs.astype(f32).reshape(2, 2, 2, 4, 120)
    vecs = jnp.where(c == 0, vecs, vecs[::-1])
    vecs = jnp.where(y == 0, vecs, vecs[:, ::-1])
    vecs = jnp.where(x == 0, vecs, vecs[:, :, ::-1])
    vecs = vecs.reshape(2, 2, 2, 4, 3, 40).transpose(4, 3, 1, 0, 2, 5).reshape(3, width)
    gain_one, gain_two = vecs[0:1], vecs[1:2]
    my_scale = lax.dynamic_slice_in_dim(vecs[2:3], 160 * plane, 160, 1)
    query_mult = LOG2E / math.sqrt(HD) * jax.nn.softplus(my_scale)

    limit = pltpu.CompilerParams(vmem_limit_bytes=50 * 1024 * 1024)
    pre, att_made = pl.pallas_call(
        attend_kernel,
        grid_spec=pltpu.PrefetchScalarGridSpec(
            num_scalar_prefetch=1,
            grid=(4,),
            in_specs=[
                seq_block(4, width=width), seq_block(4, width=width),
                whole((1, width)), whole((1, 160)), whole((width, 480)),
            ],
            out_specs=[seq_block(2, 4, width=480), seq_block(4, 2, width=160)],
        ),
        out_shape=[
            jax.ShapeDtypeStruct((2, 4, 128, 480), f32),
            jax.ShapeDtypeStruct((4, 2, 128, 160), bf16),
        ],
        compiler_params=limit,
        cost_estimate=pl.CostEstimate(flops=9_000_000_000, bytes_accessed=8_000_000, transcendentals=600_000),
        name="attend",
    )(info, near, far, gain_one, query_mult, w_qkv)

    near_rows = pair(big, beside, x, 2).reshape(4, 3, 80, width)
    att_made, near_rows, across_a, across_b = lax.optimization_barrier((att_made, near_rows, across_a, across_b))
    far_near_rows = core_swap(near_rows)
    atts = [att_made[0]] + [plane_shift(att_made[step], step) for step in (1, 2, 3)]
    atts = jnp.stack(atts)
    far_atts = core_swap(atts)
    across_a = pair(across[:2], across_a, x, 2).reshape(2, 3, 80, width)
    across_b = pair(across[2:], across_b, x, 2).reshape(2, 3, 80, width)
    far_across_a, far_across_b = core_swap(across_a), core_swap(across_b)
    cot_rows = cot_rows.transpose(1, 0, 2, 3).reshape(128, width)
    far_cot = core_swap(cot_rows)
    far_cot, far_atts, cot_rows = lax.optimization_barrier((far_cot, far_atts, cot_rows))
    datt_shape = jax.ShapeDtypeStruct((2, 128, 160), bf16)
    smem = pl.BlockSpec(memory_space=pltpu.SMEM)
    vmem = pl.BlockSpec(memory_space=pltpu.VMEM)
    hbm = pl.BlockSpec(memory_space=pl.ANY)
    out_rows, pack, grad_mid, *datts, gain_two_grad = pl.pallas_call(
        feed_kernel,
        in_specs=[smem] + [vmem] * 5 + [hbm] * 6,
        out_specs=[vmem] * 8,
        out_shape=[
            jax.ShapeDtypeStruct((4, 4, 8, width), bf16),
            jax.ShapeDtypeStruct((4, 128, width), bf16),
            jax.ShapeDtypeStruct((128, width), f32),
        ]
        + [datt_shape] * 4
        + [jax.ShapeDtypeStruct((1, width), f32)],
        scratch_shapes=[pltpu.VMEM((3, width, width), bf16), pltpu.SemaphoreType.DMA((3, 16))],
        compiler_params=limit,
        cost_estimate=pl.CostEstimate(flops=12_000_000_000, bytes_accessed=13_000_000, transcendentals=200_000),
        name="feed",
    )(info, x_rows, cot_rows, atts, far_atts, gain_two, near_rows, across_a, across_b, far_near_rows, far_across_a, far_across_b)

    back = [datts[0]] + [plane_shift(datts[step], step) for step in (1, 2, 3)]

    part_shape = jax.ShapeDtypeStruct((2, 3, 80, width), bf16)
    half_a, kept_b, away_b = pl.pallas_call(
        grads_kernel,
        in_specs=[smem] + [vmem] * 6,
        out_specs=[hbm] * 3,
        out_shape=[jax.ShapeDtypeStruct((2, 3, 2, 80, width), bf16), part_shape, part_shape],
        scratch_shapes=[pltpu.VMEM((3, 640, width), bf16), pltpu.SemaphoreType.DMA((3, 8))],
        compiler_params=limit,
        cost_estimate=pl.CostEstimate(flops=6_000_000_000, bytes_accessed=8_000_000, transcendentals=0),
        name="grads",
    )(info, pack, core_swap(pack), atts, far_atts, cot_rows, far_cot)

    half_a, kept_b, away_b, *back = lax.optimization_barrier((half_a, kept_b, away_b, *back))
    half_a = half_a.reshape(2, 3, 2, 2, 40, width)
    away_a = lax.dynamic_index_in_dim(half_a, 1 - x, 3, keepdims=False)
    away_a, away_b, grad_atts = lax.optimization_barrier((away_a, away_b, jnp.stack(back)))
    from_a, from_b = plane_shift(away_a, 1), plane_shift(away_b, 2)
    hid_near, hid_far, send = pl.pallas_call(
        attend_back_kernel,
        grid_spec=pltpu.PrefetchScalarGridSpec(
            num_scalar_prefetch=1,
            grid=(4,),
            in_specs=[
                seq_block(4, width=width), seq_block(4, width=width),
                whole((1, width)), whole((1, 160)), whole((width, 480)),
                seq_block(2, 4, width=480),
                *[pl.BlockSpec((4, 1, 32, 160), lambda s, info, core=core: (0, core, s, 0)) for core in range(2)],
                whole((1, width)),
            ],
            out_specs=[
                seq_block(4, width=width), seq_block(4, width=width),
                whole((4, 336, 480)),
            ],
            scratch_shapes=[
                pltpu.VMEM((width, 480), f32), pltpu.VMEM((1, width), f32),
                pltpu.VMEM((1, 160), f32), pltpu.VMEM((8, 1, 480), f32),
            ],
        ),
        out_shape=[
            jax.ShapeDtypeStruct((4, 128, width), bf16),
            jax.ShapeDtypeStruct((4, 128, width), bf16),
            jax.ShapeDtypeStruct((4, 336, 480), bf16),
        ],
        compiler_params=limit,
        cost_estimate=pl.CostEstimate(flops=15_000_000_000, bytes_accessed=12_000_000, transcendentals=600_000),
        name="attend_back",
    )(info, near, far, gain_one, query_mult, w_qkv, pre, grad_atts, core_swap(grad_atts), gain_two_grad)

    send, out_rows = lax.optimization_barrier((send, out_rows))
    sums = lax.psum_scatter(send, "z", scatter_dimension=0, tiled=True)
    out_sent = [pick(out_rows, (z + k) % 4) for k in range(4)]
    out_one, out_three = ring_shift(out_sent[1], 1), ring_shift(out_sent[3], 3)
    from_a, from_b, hid_far, out_one, out_three = lax.optimization_barrier(
        (from_a, from_b, hid_far, out_one, out_three)
    )
    swapped = core_swap(hid_far)
    outputs = by_source([out_sent[0], out_one, ring_shift(out_sent[2], 2), out_three], z, 0).reshape(16, 8, width)
    hid = [sum_low(hid_near[i], swapped[i]) for i in range(4)]
    split = (2, 3, 2, 40, width)
    keep_a, away_a, keep_b, away_b = pl.pallas_call(
        meet_kernel,
        in_specs=[smem] + [vmem] * 4,
        out_specs=[vmem] * 4,
        out_shape=[jax.ShapeDtypeStruct((2, 3, 40, width), bf16)] * 4,
        compiler_params=limit,
        cost_estimate=pl.CostEstimate(flops=3_000_000_000, bytes_accessed=8_000_000, transcendentals=0),
        name="meet",
    )(info, half_a, from_a, kept_b.reshape(split), from_b.reshape(split))
    kept = pl.pallas_call(
        join_kernel,
        in_specs=[vmem] * 4,
        out_specs=vmem,
        out_shape=jax.ShapeDtypeStruct((4, 3, 40, width), bf16),
        compiler_params=limit,
        cost_estimate=pl.CostEstimate(flops=2_000_000_000, bytes_accessed=4_000_000, transcendentals=0),
        name="join",
    )(keep_a, plane_shift(away_a, 2), keep_b, plane_shift(away_b, 1))
    *hid, kept, outputs = lax.optimization_barrier((*hid, kept, outputs))
    moved = [plane_shift(hid[step], step) for step in (1, 2, 3)]
    moved[0], sums = lax.optimization_barrier((moved[0], sums))
    big_sums = lax.psum_scatter(kept, "z", scatter_dimension=0, tiled=True)[0]
    grad_home = pl.pallas_call(
        norm_kernel,
        in_specs=[smem] + [vmem] * 7,
        out_specs=[vmem] * 4,
        out_shape=[jax.ShapeDtypeStruct((4, 8, width), bf16)] * 4,
        scratch_shapes=[pltpu.VMEM((4, 4, 8, width), f32)],
        compiler_params=limit,
        cost_estimate=pl.CostEstimate(flops=2_000_000_000, bytes_accessed=2_500_000, transcendentals=128),
        name="norm",
    )(info, hid[0], *moved, x_rows, grad_mid, gain_one)
    sums = pl.pallas_call(
        fold_kernel,
        in_specs=[vmem],
        out_specs=vmem,
        out_shape=jax.ShapeDtypeStruct((8, 48, 480), bf16),
        scratch_shapes=[pltpu.VMEM((8, 480), f32)],
        compiler_params=limit,
        cost_estimate=pl.CostEstimate(flops=2_000_000_000, bytes_accessed=1_600_000, transcendentals=0),
        name="fold",
    )(sums)
    sums = lax.all_to_all(sums, ("y", "core", "x"), split_axis=0, concat_axis=0, tiled=True)
    rows_shape = [jax.ShapeDtypeStruct((40, width), f32)] * 3
    qkv_sums = pl.pallas_call(
        spread_kernel, in_specs=[vmem], out_specs=[vmem] * 3, out_shape=rows_shape, compiler_params=limit, name="spread"
    )(sums)
    big_sums = pl.pallas_call(
        widen_kernel, in_specs=[vmem], out_specs=[vmem] * 3, out_shape=rows_shape, compiler_params=limit, name="widen"
    )(big_sums)
    line_sums = jnp.sum(sums[:, 40, :120].astype(f32), axis=0).reshape(3, 40)
    scale_low = query_scale.astype(bf16).astype(f32)
    scale_sum = LOG2E / math.sqrt(HD) * jax.nn.sigmoid(scale_low) * line_sums[2]
    grad_home = [grad_home[0]] + [ring_shift(grad_home[k], k) for k in (1, 2, 3)]
    grad_home = by_source(grad_home, z, 0).reshape(16, 8, width)

    return (
        outputs, grad_home, qkv_sums[0], qkv_sums[1], qkv_sums[2],
        big_sums[0], big_sums[1], big_sums[2], line_sums[0], line_sums[1], scale_sum,
    )


def solution(mesh):
    names = ("dp", "ctx")
    body = per_device
    if dict(mesh.shape) == {"dp": 16, "ctx": 2}:
        mesh = Mesh(mesh.devices.reshape(4, 2, 2, 2), ("z", "y", "core", "x"))
        names = mesh.axis_names
        body = planes
    seq, mat, line = P(None, names, None), P(names, None), P(names)
    return jax.shard_map(
        body,
        mesh=mesh,
        in_specs=(seq,) * 2 + (mat,) * 6 + (line,) * 3 + (P(), P()),
        out_specs=(seq,) * 2 + (mat,) * 6 + (line,) * 3,
        check_vma=False,
    )
```

```python
import math

import jax
import jax.numpy as jnp
from jax import lax
from jax.experimental import pallas as pl
from jax.experimental.pallas import tpu as pltpu
from jax.sharding import Mesh, PartitionSpec as P

H = 16
HD = 80


def mult_trans(left, right):
    return lax.dot_general(
        left, right, (((1,), (1,)), ((), ())), preferred_element_type=jnp.float32
    )


def trans_mult(left, right):
    return lax.dot_general(
        left, right, (((0,), (0,)), ((), ())), preferred_element_type=jnp.float32
    )


def position_of(index, local_rows, piece_rows, groups):
    column = index // local_rows
    within = index % local_rows
    return (within // piece_rows * groups + column) * piece_rows + within % piece_rows


def norm_back(grad_hidden, normed, inverse, gain_value):
    grad_normed = grad_hidden * gain_value
    return inverse * (grad_normed - normed * jnp.mean(grad_normed * normed, axis=1, keepdims=True))


def per_device(
    inputs,
    cotangent,
    w_query,
    w_key,
    w_value,
    w_output,
    w_up,
    w_down,
    attn_gain,
    mlp_gain,
    query_scale,
    deal,
    lengths,
):
    groups = lax.axis_size("ctx")
    group_index = lax.axis_index("dp")
    ctx_index = lax.axis_index("ctx")
    head_count = H
    head_dim = HD
    piece_rows = inputs.shape[1]
    seq_numbers = jnp.arange(inputs.shape[0], dtype=jnp.int32)
    seq_lengths = jnp.sum(
        jnp.where(deal[None, :] == seq_numbers[:, None], lengths[None, :], 0), axis=1
    )
    local_in, local_cot = (
        lax.all_to_all(inputs, "dp", split_axis=0, concat_axis=1, tiled=True),
        lax.all_to_all(cotangent, "dp", split_axis=0, concat_axis=1, tiled=True),
    )
    seq_count, local_rows, model_width = local_in.shape
    padded = local_rows * groups
    token_count = seq_count * local_rows
    my_lengths = lax.dynamic_slice_in_dim(seq_lengths, group_index * seq_count, seq_count, 0)
    query_pos = position_of(
        ctx_index * local_rows + jnp.arange(local_rows, dtype=jnp.int32),
        local_rows,
        piece_rows,
        groups,
    )
    flat_in = local_in.reshape(token_count, model_width).astype(jnp.float32)
    flat_cot = local_cot.reshape(token_count, model_width)
    lowered = (
        w_query.astype(jnp.bfloat16),
        w_key.astype(jnp.bfloat16),
        w_value.astype(jnp.bfloat16),
        w_output.astype(jnp.bfloat16),
        w_up.astype(jnp.bfloat16),
        w_down.astype(jnp.bfloat16),
        attn_gain.astype(jnp.bfloat16),
        mlp_gain.astype(jnp.bfloat16),
        query_scale.astype(jnp.bfloat16),
    )
    gathered = (
        lax.all_gather(lowered[0], ("dp", "ctx"), axis=0, tiled=True),
        lax.all_gather(lowered[1], ("dp", "ctx"), axis=0, tiled=True),
        lax.all_gather(lowered[2], ("dp", "ctx"), axis=0, tiled=True),
        lax.all_gather(lowered[3], ("dp", "ctx"), axis=0, tiled=True),
        lax.all_gather(lowered[4], ("dp", "ctx"), axis=0, tiled=True),
        lax.all_gather(lowered[5], ("dp", "ctx"), axis=0, tiled=True),
        lax.all_gather(lowered[6], ("dp", "ctx"), axis=0, tiled=True),
        lax.all_gather(lowered[7], ("dp", "ctx"), axis=0, tiled=True),
        lax.all_gather(lowered[8], ("dp", "ctx"), axis=0, tiled=True),
    )
    (
        query_full,
        key_full,
        value_full,
        output_full,
        up_full,
        down_full,
        gain_one,
        gain_two,
        scale_raw,
    ) = gathered
    inv_one = lax.rsqrt(jnp.mean(flat_in * flat_in, axis=1, keepdims=True) + 1e-06)
    normed_one = flat_in * inv_one
    hidden_one = (normed_one * gain_one.astype(jnp.float32)).astype(jnp.bfloat16)
    scale_param = scale_raw.astype(jnp.float32)
    query_mult = 1.442695041 / math.sqrt(head_dim) * jax.nn.softplus(scale_param)
    query_pre = jnp.dot(hidden_one, query_full, preferred_element_type=jnp.float32)
    queries = (query_pre * query_mult).astype(jnp.bfloat16)
    keys_local = jnp.dot(hidden_one, key_full, preferred_element_type=jnp.float32).astype(
        jnp.bfloat16
    )
    values_local = jnp.dot(hidden_one, value_full, preferred_element_type=jnp.float32).astype(
        jnp.bfloat16
    )
    four_shape = (seq_count, local_rows, head_count, head_dim)
    query_four = queries.reshape(four_shape)
    keys_three = keys_local.reshape(seq_count, local_rows, model_width)
    values_three = values_local.reshape(seq_count, local_rows, model_width)

    def live_between(row_pos, key_pos):
        allowed = (key_pos[None, None, :] <= row_pos[None, :, None]) & (
            key_pos[None, None, :] < my_lengths[:, None, None]
        )
        return allowed[:, :, None, :]

    def live_mask(key_pos):
        return live_between(query_pos, key_pos)

    def attend_block(state_now, key_block, value_block, first_row):
        run_max, run_sum, run_acc = state_now
        block_len = key_block.shape[1]
        key_pos = position_of(
            first_row + jnp.arange(block_len, dtype=jnp.int32), local_rows, piece_rows, groups
        )
        key_four = key_block.reshape(seq_count, block_len, head_count, head_dim)
        value_four = value_block.reshape(seq_count, block_len, head_count, head_dim)
        scores = jnp.einsum(
            "srhd,skhd->srhk", query_four, key_four, preferred_element_type=jnp.float32
        )
        allowed = live_mask(key_pos)
        masked = jnp.where(allowed, scores, -1e30)
        new_max = jnp.maximum(run_max, jnp.max(masked, axis=3))
        weights_now = jnp.exp(jnp.where(allowed, masked - new_max[..., None], -1e30))
        factor = jnp.exp(run_max - new_max)
        new_sum = run_sum * factor + jnp.sum(weights_now, axis=3)
        added = jnp.einsum(
            "srhk,skhd->srhd",
            weights_now.astype(jnp.bfloat16),
            value_four,
            preferred_element_type=jnp.float32,
        )
        return (new_max, new_sum, run_acc * factor[..., None] + added)

    start_state = (
        jnp.full((seq_count, local_rows, head_count), -1e30, jnp.float32),
        jnp.zeros((seq_count, local_rows, head_count), jnp.float32),
        jnp.zeros(four_shape, jnp.float32),
    )
    key_piece = lax.all_gather(keys_three, "ctx", axis=1, tiled=True)
    value_piece = lax.all_gather(values_three, "ctx", axis=1, tiled=True)
    piece_len = key_piece.shape[1]
    fold_block_len = 512 if piece_len % 512 == 0 else piece_len

    def one_block(state_now, block_index):
        offset = block_index * fold_block_len
        key_block = lax.dynamic_slice_in_dim(key_piece, offset, fold_block_len, 1)
        value_block = lax.dynamic_slice_in_dim(value_piece, offset, fold_block_len, 1)
        return (attend_block(state_now, key_block, value_block, offset), None)

    result_state, unused = lax.scan(
        one_block, start_state, jnp.arange(piece_len // fold_block_len, dtype=jnp.int32)
    )
    run_max, run_sum, run_acc = result_state
    log_total = run_max + jnp.log(run_sum)
    attn_exact = run_acc / run_sum[..., None]
    attended = attn_exact.reshape(token_count, model_width).astype(jnp.bfloat16)
    middle = flat_in + jnp.dot(attended, output_full, preferred_element_type=jnp.float32)
    inv_two = lax.rsqrt(jnp.mean(middle * middle, axis=1, keepdims=True) + 1e-06)
    normed_two = middle * inv_two
    hidden_two = (normed_two * gain_two.astype(jnp.float32)).astype(jnp.bfloat16)
    up_pre = jnp.dot(hidden_two, up_full, preferred_element_type=jnp.float32)
    active = jax.nn.silu(up_pre).astype(jnp.bfloat16)
    result = (middle + jnp.dot(active, down_full, preferred_element_type=jnp.float32)).astype(
        jnp.bfloat16
    )
    back_weights = (
        lax.all_gather(lowered[0], ("dp", "ctx"), axis=0, tiled=True),
        lax.all_gather(lowered[1], ("dp", "ctx"), axis=0, tiled=True),
        lax.all_gather(lowered[2], ("dp", "ctx"), axis=0, tiled=True),
        lax.all_gather(lowered[3], ("dp", "ctx"), axis=0, tiled=True),
        lax.all_gather(lowered[4], ("dp", "ctx"), axis=0, tiled=True),
        lax.all_gather(lowered[5], ("dp", "ctx"), axis=0, tiled=True),
        lax.all_gather(lowered[6], ("dp", "ctx"), axis=0, tiled=True),
        lax.all_gather(lowered[7], ("dp", "ctx"), axis=0, tiled=True),
        lax.all_gather(lowered[8], ("dp", "ctx"), axis=0, tiled=True),
    )
    (
        query_back,
        key_back,
        value_back,
        output_back,
        up_back,
        down_back,
        gain_one_back,
        gain_two_back,
        scale_back,
    ) = back_weights
    cot_wide = flat_cot.astype(jnp.float32)
    grad_down = trans_mult(active, flat_cot)
    grad_active = mult_trans(flat_cot, down_back)
    sigma_up = jax.nn.sigmoid(up_pre)
    grad_up_pre = (grad_active * sigma_up * (1.0 + up_pre * (1.0 - sigma_up))).astype(jnp.bfloat16)
    grad_up = trans_mult(hidden_two, grad_up_pre)
    grad_hidden_two = mult_trans(grad_up_pre, up_back)
    grad_gain_two = jnp.sum(grad_hidden_two * normed_two, axis=0)
    grad_middle = cot_wide + norm_back(
        grad_hidden_two, normed_two, inv_two, gain_two_back.astype(jnp.float32)
    )
    grad_middle_low = grad_middle.astype(jnp.bfloat16)
    grad_output = trans_mult(attended, grad_middle_low)
    grad_attended = mult_trans(grad_middle_low, output_back).astype(jnp.bfloat16)
    grad_att_four = grad_attended.reshape(four_shape)
    delta_rows = jnp.sum(grad_att_four.astype(jnp.float32) * attn_exact, axis=3)
    key_all, value_all = (
        lax.all_gather(keys_three, "ctx", axis=1, tiled=True),
        lax.all_gather(values_three, "ctx", axis=1, tiled=True),
    )
    block_len = min(512, padded)

    def back_block(block_index, state_now):
        grad_query, grad_key_all, grad_value_all = state_now
        offset = block_index * block_len
        key_block = lax.dynamic_slice_in_dim(key_all, offset, block_len, 1).reshape(
            seq_count, block_len, head_count, head_dim
        )
        value_block = lax.dynamic_slice_in_dim(value_all, offset, block_len, 1).reshape(
            seq_count, block_len, head_count, head_dim
        )
        key_pos = position_of(
            offset + jnp.arange(block_len, dtype=jnp.int32), local_rows, piece_rows, groups
        )
        scores = jnp.einsum(
            "srhd,skhd->srhk", query_four, key_block, preferred_element_type=jnp.float32
        )
        probs = jnp.exp(jnp.where(live_mask(key_pos), scores - log_total[..., None], -1e30))
        grad_value_block = jnp.einsum(
            "srhk,srhd->skhd",
            probs.astype(jnp.bfloat16),
            grad_att_four,
            preferred_element_type=jnp.float32,
        )
        grad_probs = jnp.einsum(
            "srhd,skhd->srhk", grad_att_four, value_block, preferred_element_type=jnp.float32
        )
        grad_scores = (probs * (grad_probs - delta_rows[..., None])).astype(jnp.bfloat16)
        grad_query = grad_query + jnp.einsum(
            "srhk,skhd->srhd", grad_scores, key_block, preferred_element_type=jnp.float32
        )
        grad_key_block = jnp.einsum(
            "srhk,srhd->skhd", grad_scores, query_four, preferred_element_type=jnp.float32
        )
        grad_key_all = lax.dynamic_update_slice_in_dim(
            grad_key_all, grad_key_block.reshape(seq_count, block_len, model_width), offset, 1
        )
        grad_value_all = lax.dynamic_update_slice_in_dim(
            grad_value_all, grad_value_block.reshape(seq_count, block_len, model_width), offset, 1
        )
        return (grad_query, grad_key_all, grad_value_all)

    zero_all = jnp.zeros((seq_count, padded, model_width), jnp.float32)
    grad_query, grad_key_all, grad_value_all = lax.fori_loop(
        0, padded // block_len, back_block, (jnp.zeros(four_shape, jnp.float32), zero_all, zero_all)
    )
    grad_key_mine, grad_value_mine = (
        lax.psum_scatter(
            grad_key_all.astype(jnp.bfloat16), "ctx", scatter_dimension=1, tiled=True
        ).astype(jnp.float32),
        lax.psum_scatter(
            grad_value_all.astype(jnp.bfloat16), "ctx", scatter_dimension=1, tiled=True
        ).astype(jnp.float32),
    )
    grad_query_flat = grad_query.reshape(token_count, model_width)
    grad_query_pre = (grad_query_flat * query_mult).astype(jnp.bfloat16)
    grad_scale = (
        1.442695041
        / math.sqrt(head_dim)
        * jax.nn.sigmoid(scale_back.astype(jnp.float32))
        * jnp.sum(grad_query_flat * query_pre, axis=0)
    )
    grad_key_low = grad_key_mine.reshape(token_count, model_width).astype(jnp.bfloat16)
    grad_value_low = grad_value_mine.reshape(token_count, model_width).astype(jnp.bfloat16)
    grad_wq = trans_mult(hidden_one, grad_query_pre)
    grad_wk = trans_mult(hidden_one, grad_key_low)
    grad_wv = trans_mult(hidden_one, grad_value_low)
    grad_hidden_one = (
        mult_trans(grad_query_pre, query_back)
        + mult_trans(grad_key_low, key_back)
        + mult_trans(grad_value_low, value_back)
    )
    grad_gain_one = jnp.sum(grad_hidden_one * normed_one, axis=0)
    grad_in = grad_middle + norm_back(
        grad_hidden_one, normed_one, inv_one, gain_one_back.astype(jnp.float32)
    )
    matrix_stack = jnp.stack([grad_wq, grad_wk, grad_wv, grad_output, grad_up, grad_down], axis=0)
    vector_stack = jnp.stack([grad_gain_one, grad_gain_two, grad_scale], axis=0)
    matrix_sums, vector_sums = (
        lax.psum_scatter(matrix_stack, ("dp", "ctx"), scatter_dimension=1, tiled=True),
        lax.psum_scatter(vector_stack, ("dp", "ctx"), scatter_dimension=1, tiled=True),
    )
    out_local = result.reshape(seq_count, local_rows, model_width)
    grad_local = grad_in.astype(jnp.bfloat16).reshape(seq_count, local_rows, model_width)
    back_out, back_grad = (
        lax.all_to_all(out_local, "dp", split_axis=1, concat_axis=0, tiled=True),
        lax.all_to_all(grad_local, "dp", split_axis=1, concat_axis=0, tiled=True),
    )
    return (
        back_out,
        back_grad,
        matrix_sums[0],
        matrix_sums[1],
        matrix_sums[2],
        matrix_sums[3],
        matrix_sums[4],
        matrix_sums[5],
        vector_sums[0],
        vector_sums[1],
        vector_sums[2],
    )


LOG2E = 1.442695041
CODES = (0, 1, 4, 5)


def plane_shift(value, step):
    if step == 1:
        return lax.ppermute(value, "x", [(0, 1), (1, 0)])
    if step == 2:
        return lax.ppermute(value, "y", [(0, 1), (1, 0)])
    return lax.ppermute(value, ("y", "x"), [(0, 3), (1, 2), (2, 1), (3, 0)])


def core_swap(value):
    return lax.ppermute(value, "core", [(0, 1), (1, 0)])


def ring_shift(value, step):
    return lax.ppermute(value, "z", [(i, (i + step) % 4) for i in range(4)])


def pick(array, index):
    return lax.dynamic_index_in_dim(array, index, 0, keepdims=False)


def by_source(pieces, z_index, axis):
    pieces = [jnp.expand_dims(item, axis) for item in pieces]
    shape = [1] * pieces[0].ndim
    shape[axis] = 4
    hop = ((z_index - jnp.arange(4, dtype=jnp.int32)) % 4).reshape(shape)
    made = pieces[0]
    for k in (1, 2, 3):
        made = jnp.where(hop == k, pieces[k], made)
    return made


def pair(mine, other, index, axis):
    shape = [1] * (mine.ndim + 1)
    shape[axis] = 2
    slot = jnp.arange(2, dtype=jnp.int32).reshape(shape)
    return jnp.where(slot == index, jnp.expand_dims(mine, axis), jnp.expand_dims(other, axis))


def row_positions(shape, dim, plane_index):
    row = lax.broadcasted_iota(jnp.int32, shape, dim)
    chip = (row // 32) % 4
    code = (chip % 2) + 4 * (chip // 2) + 2 * (row // 128)
    return 64 * ((row % 32) // 8) + 8 * (plane_index ^ code) + row % 8


def live_pairs(info_ref, seq):
    shape = (256, 256)
    query_pos = row_positions(shape, 0, info_ref[1])
    key_pos = row_positions(shape, 1, info_ref[1])
    return (key_pos <= query_pos) & (key_pos < info_ref[2 + seq])


def block_rows(near_ref, far_ref):
    return jnp.concatenate([near_ref[...], far_ref[...]], axis=0).reshape(256, near_ref.shape[2])


def soft_probs(query, key, live):
    scores = mult_trans(query, key)
    scores = jnp.where(live, scores, -1e30)
    top = jnp.max(scores, axis=1, keepdims=True)
    weights = jnp.where(live, jnp.exp(scores - top), 0.0)
    return weights / jnp.sum(weights, axis=1, keepdims=True)


def attend_kernel(
    info_ref, near_ref, far_ref, gain_ref, mult_ref, w_ref, pre_ref, att_ref
):
    seq = pl.program_id(0)
    live = live_pairs(info_ref, seq)
    wide = block_rows(near_ref, far_ref).astype(jnp.float32)
    inverse = lax.rsqrt(jnp.mean(wide * wide, axis=1, keepdims=True) + 1e-06)
    hidden = (wide * inverse * gain_ref[...]).astype(jnp.bfloat16)
    pre = jnp.dot(hidden, w_ref[...], preferred_element_type=jnp.float32)
    pre_ref[...] = pre.reshape(2, 4, 32, 480)
    query = (pre[:, 0:160] * mult_ref[...]).astype(jnp.bfloat16)
    key = pre[:, 160:320].astype(jnp.bfloat16)
    value = pre[:, 320:480].astype(jnp.bfloat16)
    heads = []
    for head in range(2):
        part = slice(80 * head, 80 * head + 80)
        probs = soft_probs(query[:, part], key[:, part], live).astype(jnp.bfloat16)
        heads.append(jnp.dot(probs, value[:, part], preferred_element_type=jnp.float32))
    att = jnp.concatenate(heads, axis=1).astype(jnp.bfloat16).reshape(2, 4, 32, 160)
    for chip in range(4):
        for core in range(2):
            att_ref[chip, core] = att[core, chip]


def attend_back_kernel(
    info_ref, near_ref, far_ref, gain_ref, mult_ref, w_ref, pre_ref, grad_near, grad_far, gain_two_ref,
    hid_near, hid_far, send_ref, w_acc, gain_acc, scale_acc, lines,
):
    seq = pl.program_id(0)

    @pl.when(seq == 0)
    def _():
        w_acc[...] = jnp.zeros_like(w_acc)
        gain_acc[...] = jnp.zeros_like(gain_acc)
        scale_acc[...] = jnp.zeros_like(scale_acc)

    live = live_pairs(info_ref, seq)
    wide = block_rows(near_ref, far_ref).astype(jnp.float32)
    inverse = lax.rsqrt(jnp.mean(wide * wide, axis=1, keepdims=True) + 1e-06)
    normed = wide * inverse
    hidden = (normed * gain_ref[...]).astype(jnp.bfloat16)
    pre = pre_ref[...].reshape(256, 480)
    mult = mult_ref[...]
    query = (pre[:, 0:160] * mult).astype(jnp.bfloat16)
    key = pre[:, 160:320].astype(jnp.bfloat16)
    value = pre[:, 320:480].astype(jnp.bfloat16)
    grad_att = jnp.concatenate([grad_near[:, 0], grad_far[:, 0]], axis=0).reshape(256, 160)
    grad_q, grad_k, grad_v = [], [], []
    for head in range(2):
        part = slice(80 * head, 80 * head + 80)
        probs = soft_probs(query[:, part], key[:, part], live)
        grad_probs = mult_trans(grad_att[:, part], value[:, part])
        delta = jnp.sum(probs * grad_probs, axis=1, keepdims=True)
        grad_scores = (probs * (grad_probs - delta)).astype(jnp.bfloat16)
        grad_v.append(trans_mult(probs.astype(jnp.bfloat16), grad_att[:, part]))
        grad_q.append(jnp.dot(grad_scores, key[:, part], preferred_element_type=jnp.float32))
        grad_k.append(trans_mult(grad_scores, query[:, part]))
    grad_query = jnp.concatenate(grad_q, axis=1)
    scale_acc[...] += jnp.sum(grad_query * pre[:, 0:160], axis=0, keepdims=True)
    joined = jnp.concatenate([grad_query * mult] + grad_k + grad_v, axis=1).astype(jnp.bfloat16)
    w_acc[...] += trans_mult(hidden, joined)
    grad_hidden = mult_trans(joined, w_ref[...])
    gain_acc[...] += jnp.sum(grad_hidden * normed, axis=0, keepdims=True)
    low = grad_hidden.astype(jnp.bfloat16).reshape(2, 4, 32, 1280)
    hid_near[...] = low[0]
    hid_far[...] = low[1]

    @pl.when(seq == 3)
    def _():
        lines[...] = jnp.zeros_like(lines)
        for which, source in enumerate((gain_acc, gain_two_ref)):
            for owner in range(32):
                lane = 120 * (owner % 4) + 40 * which
                lines[owner // 4, :, lane : lane + 40] = source[:, 40 * owner : 40 * owner + 40]
        for part in range(4):
            lane = 120 * part + 80
            lines[info_ref[1], :, lane : lane + 40] = scale_acc[:, 40 * part : 40 * part + 40]
        blank = jnp.zeros((14, 480), jnp.float32)
        for target in range(4):
            rows = w_acc[320 * target : 320 * target + 320, :]
            block = jnp.concatenate([rows, lines[2 * target], lines[2 * target + 1], blank], axis=0)
            send_ref[target] = block.astype(jnp.bfloat16)


def block_index(z_index, y_index, core):
    return pl.ds(pl.multiple_of((4 * z_index + 2 * y_index + core) * 80, 80), 80)


def arrival_rows(info_ref, w, z_index, y_index, core):
    if w > 0:
        return block_index(z_index, y_index, core)
    block = 4 * z_index + 2 * y_index + core
    code = info_ref[1] ^ (block // 2)
    arrival = 2 * ((code & 1) + 2 * (code // 4)) + ((code // 2) & 1)
    return pl.ds(pl.multiple_of(160 * arrival + 80 * (block & 1), 80), 80)


def feed_kernel(
    info_ref, x_ref, g_ref, atts, far_atts, gain_ref,
    near_rows, across_a, across_b, far_near_rows, far_across_a, far_across_b,
    out_ref, pack_ref, dmid_ref, datt_0, datt_1, datt_2, datt_3, gain_grad,
    weights, sems,
):
    y_index, core_index = info_ref[1] // 4, (info_ref[1] // 2) % 2
    copies = []
    for w in range(3):
        moved = []
        for core, own, others in (
            (core_index, near_rows, (across_a, across_b)),
            (1 - core_index, far_near_rows, (far_across_a, far_across_b)),
        ):
            for z_index in range(4):
                moved.append((own.at[z_index, w], z_index, y_index, core))
                moved.append((others[z_index // 2].at[z_index % 2, w], z_index, 1 - y_index, core))
        copies.append([
            pltpu.make_async_copy(src, weights.at[w, arrival_rows(info_ref, w, *place)], sems.at[w, i])
            for i, (src, *place) in enumerate(moved)
        ])
    for group in copies:
        for copy in group:
            copy.start()
    datts = (datt_0, datt_1, datt_2, datt_3)

    for copy in copies[0]:
        copy.wait()
    att = jnp.concatenate(
        [(far_atts if core else atts)[chip, core] for chip in range(4) for core in range(2)], axis=1
    )
    middle = x_ref[...].astype(jnp.float32)
    middle += jnp.dot(att, weights[0], preferred_element_type=jnp.float32)
    inverse = lax.rsqrt(jnp.mean(middle * middle, axis=1, keepdims=True) + 1e-06)
    normed = middle * inverse
    gain = gain_ref[...]
    hidden = (normed * gain).astype(jnp.bfloat16)
    pack_ref[1] = hidden
    for copy in copies[1]:
        copy.wait()
    up = jnp.dot(hidden, weights[1], preferred_element_type=jnp.float32)
    sigma = jax.nn.sigmoid(up)
    active = (up * sigma).astype(jnp.bfloat16)
    pack_ref[0] = active
    for copy in copies[2]:
        copy.wait()
    down = jnp.dot(active, weights[2], preferred_element_type=jnp.float32)
    result = middle + down
    for seq in range(4):
        for plane_z in range(4):
            row = 32 * seq + 8 * plane_z
            out_ref[plane_z, seq] = result[row : row + 8].astype(jnp.bfloat16)
    cot = g_ref[...]
    grad_act = mult_trans(cot, weights[2])
    grad_up = (grad_act * sigma * (1.0 + up * (1.0 - sigma))).astype(jnp.bfloat16)
    pack_ref[2] = grad_up
    grad_hidden = mult_trans(grad_up, weights[1])
    gain_grad[...] = jnp.sum(grad_hidden * normed, axis=0, keepdims=True)
    grad_mid = cot.astype(jnp.float32) + norm_back(grad_hidden, normed, inverse, gain)
    dmid_ref[...] = grad_mid
    low = grad_mid.astype(jnp.bfloat16)
    pack_ref[3] = low
    grad_att = mult_trans(low, weights[0]).astype(jnp.bfloat16)
    for chip in range(4):
        for core in range(2):
            lane = 160 * (2 * chip + core)
            datts[chip][core] = grad_att[:, lane : lane + 160]


def grads_kernel(
    info_ref, pack_ref, far_pack, atts, far_atts, cot_ref, far_cot, keep_a, away_a, keep_b, away_b, stage, sems
):
    y_index, core_index, x_index = info_ref[1] // 4, (info_ref[1] // 2) % 2, info_ref[1] % 2

    def leave(w):
        copies = []
        for half in range(2):
            for i in range(2):
                moves = (
                    (stage.at[w, half, i, x_index], keep_a),
                    (stage.at[w, half, i, 1 - x_index], away_a),
                    (stage.at[w, 2 + half, y_index, i], keep_b),
                    (stage.at[w, 2 + half, 1 - y_index, i], away_b),
                )
                for j, (block, target) in enumerate(moves):
                    sem = sems.at[w, 8 * half + 4 * i + j]
                    copies.append(pltpu.make_async_copy(block, target.at[half, w, i], sem))
        return copies

    def store(w, made):
        for i in range(16):
            stage[w, i // 4, (i // 2) % 2, i % 2] = made[40 * i : 40 * i + 40].astype(jnp.bfloat16)

    def both(near, far):
        return jnp.concatenate([near, far], axis=0)

    cots = both(cot_ref[...], far_cot[...])
    for core in range(2):

        @pl.when(core_index == core)
        def _():
            def own_columns(near, far):
                return both(*(
                    jnp.concatenate([ref[:, 160 * i + 80 * core : 160 * i + 80 * core + 80] for i in range(8)], axis=1)
                    for ref in (near, far)
                ))

            acts = own_columns(pack_ref.at[0], far_pack.at[0])
            store(2, trans_mult(acts, cots))
            for copy in leave(2):
                copy.start()
            acts = own_columns(pack_ref.at[1], far_pack.at[1])
            store(1, trans_mult(acts, both(pack_ref[2], far_pack[2])))
            for copy in leave(1):
                copy.start()
            grads = both(pack_ref[3], far_pack[3])
            pieces = []
            for chip in range(4):
                for source in range(2):
                    near, far = (far_atts, far_atts) if source else (atts, atts)
                    pieces.append(both(near[chip, source], far[chip, 1 - source])[:, 80 * core : 80 * core + 80])
            made = trans_mult(jnp.concatenate(pieces, axis=1), grads)
            for i in range(8):
                source = info_ref[1] ^ (CODES[i // 2] + 2 * (i % 2))
                for part in range(2):
                    row = 80 * i + 40 * part
                    stage[0, source // 2, source & 1, part] = made[row : row + 40].astype(jnp.bfloat16)
            for copy in leave(0):
                copy.start()

    for w in range(3):
        for copy in leave(w):
            copy.wait()


def meet_kernel(info_ref, mine_a, from_a, mine_b, from_b, keep_a, away_a, keep_b, away_b):
    y_index, x_index = info_ref[1] // 4, info_ref[1] % 2
    for half in range(2):
        for w in range(3):
            for row, out in ((y_index, keep_a), (1 - y_index, away_a)):
                out[half, w] = sum_low(mine_a[half, w, row], from_a[half, w, row])
            for row, out in ((x_index, keep_b), (1 - x_index, away_b)):
                out[half, w] = sum_low(mine_b[half, w, row], from_b[half, w, row])


def join_kernel(keep_a, from_a, keep_b, from_b, out_ref):
    for half in range(2):
        for w in range(3):
            out_ref[half, w] = sum_low(keep_a[half, w], from_a[half, w])
            out_ref[2 + half, w] = sum_low(keep_b[half, w], from_b[half, w])


def sum_low(left, right):
    return (left.astype(jnp.float32) + right.astype(jnp.float32)).astype(jnp.bfloat16)


def norm_kernel(info_ref, hid_0, hid_1, hid_2, hid_3, x_ref, dmid_ref, gain_ref, out_0, out_1, out_2, out_3, rows):
    grad = hid_0[...].astype(jnp.float32)
    for item in (hid_1, hid_2, hid_3):
        grad += item[...].astype(jnp.float32)
    wide = x_ref[...].astype(jnp.float32)
    inverse = lax.rsqrt(jnp.mean(wide * wide, axis=1, keepdims=True) + 1e-06)
    grad = dmid_ref[...] + norm_back(grad, wide * inverse, inverse, gain_ref[...])
    for seq in range(4):
        for plane_z in range(4):
            row = 32 * seq + 8 * plane_z
            rows[plane_z, seq] = grad[row : row + 8]
    for hop, out in enumerate((out_0, out_1, out_2, out_3)):
        out[...] = rows[(info_ref[0] + hop) & 3].astype(jnp.bfloat16)


def fold_kernel(in_ref, out_ref, line):
    total = in_ref[0].astype(jnp.float32)
    line[...] = jnp.zeros_like(line)
    for owner in range(8):
        lane = 120 * (owner % 4)
        line[0:1, 0:120] = total[320 + owner // 4 : 321 + owner // 4, lane : lane + 120]
        block = jnp.concatenate([total[40 * owner : 40 * owner + 40], line[...]], axis=0)
        out_ref[owner] = block.astype(jnp.bfloat16)


def spread_kernel(in_ref, *outs):
    for which, out in enumerate(outs):
        for owner in range(8):
            part = in_ref[owner, 0:40, 160 * which : 160 * which + 160]
            out[:, 160 * owner : 160 * owner + 160] = part.astype(jnp.float32)


def widen_kernel(in_ref, *outs):
    for which, out in enumerate(outs):
        out[...] = in_ref[which].astype(jnp.float32)


def whole(shape):
    return pl.BlockSpec(shape, lambda *_: (0,) * len(shape))


def seq_block(*lead, width):
    count = len(lead)
    return pl.BlockSpec((*lead, 32, width), lambda s, info: (*(0,) * count, s, 0))


def planes(
    inputs, cotangent, w_query, w_key, w_value, w_output, w_up, w_down,
    attn_gain, mlp_gain, query_scale, deal, lengths,
):
    f32, bf16 = jnp.float32, jnp.bfloat16
    z, y, c, x = (lax.axis_index(name) for name in ("z", "y", "core", "x"))
    plane = 4 * y + 2 * c + x
    width = 1280
    seqs = jnp.arange(16, dtype=jnp.int32)
    seq_lengths = jnp.sum(jnp.where(deal[None, :] == seqs[:, None], lengths[None, :], 0), axis=1)
    my_lengths = lax.dynamic_slice_in_dim(seq_lengths, 4 * z, 4, 0)
    info = jnp.concatenate([jnp.stack([z, plane]), my_lengths]).astype(jnp.int32)

    vec = jnp.concatenate([attn_gain, mlp_gain, query_scale]).astype(bf16)
    vec_block = jnp.zeros((1, 8, width), bf16).at[0, 0, :120].set(vec)
    in_four = inputs.reshape(4, 4, 8, width)
    sent = [jnp.concatenate([pick(in_four, (z + k) % 4), vec_block]) for k in range(4)]
    qkv = jnp.stack([w_query, w_key, w_value]).astype(bf16)
    *sent, qkv = lax.optimization_barrier((*sent, qkv))
    got = [sent[0]] + [ring_shift(sent[k], k) for k in (1, 2, 3)]
    x_rows = by_source([item[:4] for item in got], z, 1).reshape(128, width)
    vec_rows = by_source([item[4, 0] for item in got], z, 0)
    vec_rows = jnp.concatenate([vec_rows, jnp.zeros((4, width), bf16)])
    own = jnp.concatenate([x_rows, vec_rows])

    big = jnp.stack([w_output, w_up, w_down]).astype(bf16)
    big = lax.all_gather(big, "z", axis=0)

    qkv = qkv.reshape(3, 40, 8, 160).transpose(2, 1, 0, 3).reshape(8, 40, 480)
    qkv = lax.all_to_all(qkv, ("y", "core", "x"), split_axis=0, concat_axis=0, tiled=True)
    near = jnp.stack([own] + [plane_shift(own, step) for step in (1, 2, 3)])
    big, near, cotangent, qkv = lax.optimization_barrier((big, near, cotangent, qkv.reshape(320, 480)))
    w_qkv = lax.all_gather(qkv, "z", axis=0, tiled=True)
    far = core_swap(near)
    beside, across = plane_shift(big, 1), plane_shift(big, 2)
    relay_a, relay_b = beside[:2], across[2:]
    cot_rows = lax.all_to_all(cotangent.reshape(4, 4, 8, width), "z", split_axis=0, concat_axis=0, tiled=True)
    relay_a, relay_b, cot_rows = lax.optimization_barrier((relay_a, relay_b, cot_rows))
    across_a, across_b = plane_shift(relay_a, 2), plane_shift(relay_b, 1)

    vecs = jnp.stack([near[:, 128:132, :120], far[:, 128:132, :120]])
    vecs = vecs.astype(f32).reshape(2, 2, 2, 4, 120)
    vecs = jnp.where(c == 0, vecs, vecs[::-1])
    vecs = jnp.where(y == 0, vecs, vecs[:, ::-1])
    vecs = jnp.where(x == 0, vecs, vecs[:, :, ::-1])
    vecs = vecs.reshape(2, 2, 2, 4, 3, 40).transpose(4, 3, 1, 0, 2, 5).reshape(3, width)
    gain_one, gain_two = vecs[0:1], vecs[1:2]
    my_scale = lax.dynamic_slice_in_dim(vecs[2:3], 160 * plane, 160, 1)
    query_mult = LOG2E / math.sqrt(HD) * jax.nn.softplus(my_scale)


    def limit(megabytes):
        return pltpu.CompilerParams(vmem_limit_bytes=megabytes * 1024 * 1024)

    pre, att_made = pl.pallas_call(
        attend_kernel,
        grid_spec=pltpu.PrefetchScalarGridSpec(
            num_scalar_prefetch=1,
            grid=(4,),
            in_specs=[
                seq_block(4, width=width), seq_block(4, width=width),
                whole((1, width)), whole((1, 160)), whole((width, 480)),
            ],
            out_specs=[seq_block(2, 4, width=480), seq_block(4, 2, width=160)],
        ),
        out_shape=[
            jax.ShapeDtypeStruct((2, 4, 128, 480), f32),
            jax.ShapeDtypeStruct((4, 2, 128, 160), bf16),
        ],
        compiler_params=limit(14),
        cost_estimate=pl.CostEstimate(flops=9_000_000_000, bytes_accessed=8_000_000, transcendentals=600_000),
        name="attend",
    )(info, near, far, gain_one, query_mult, w_qkv)

    near_rows = pair(big, beside, x, 2).reshape(4, 3, 80, width)
    att_made, near_rows, across_a, across_b = lax.optimization_barrier((att_made, near_rows, across_a, across_b))
    far_near_rows = core_swap(near_rows)
    atts = [att_made[0]] + [plane_shift(att_made[step], step) for step in (1, 2, 3)]
    atts = jnp.stack(atts)
    far_atts = core_swap(atts)
    across_a = pair(across[:2], across_a, x, 2).reshape(2, 3, 80, width)
    across_b = pair(across[2:], across_b, x, 2).reshape(2, 3, 80, width)
    far_across_a, far_across_b = core_swap(across_a), core_swap(across_b)
    cot_rows = cot_rows.transpose(1, 0, 2, 3).reshape(128, width)
    far_cot = core_swap(cot_rows)
    far_cot, far_atts, cot_rows = lax.optimization_barrier((far_cot, far_atts, cot_rows))
    datt_shape = jax.ShapeDtypeStruct((2, 128, 160), bf16)
    smem = pl.BlockSpec(memory_space=pltpu.SMEM)
    vmem = pl.BlockSpec(memory_space=pltpu.VMEM)
    hbm = pl.BlockSpec(memory_space=pl.ANY)
    out_rows, pack, grad_mid, *datts, gain_two_grad = pl.pallas_call(
        feed_kernel,
        in_specs=[smem] + [vmem] * 5 + [hbm] * 6,
        out_specs=[vmem] * 8,
        out_shape=[
            jax.ShapeDtypeStruct((4, 4, 8, width), bf16),
            jax.ShapeDtypeStruct((4, 128, width), bf16),
            jax.ShapeDtypeStruct((128, width), f32),
        ]
        + [datt_shape] * 4
        + [jax.ShapeDtypeStruct((1, width), f32)],
        scratch_shapes=[pltpu.VMEM((3, width, width), bf16), pltpu.SemaphoreType.DMA((3, 16))],
        compiler_params=limit(28),
        cost_estimate=pl.CostEstimate(flops=12_000_000_000, bytes_accessed=13_000_000, transcendentals=200_000),
        name="feed",
    )(info, x_rows, cot_rows, atts, far_atts, gain_two, near_rows, across_a, across_b, far_near_rows, far_across_a, far_across_b)

    back = [datts[0]] + [plane_shift(datts[step], step) for step in (1, 2, 3)]

    mine_a, away_a, mine_b, away_b = pl.pallas_call(
        grads_kernel,
        in_specs=[smem] + [vmem] * 6,
        out_specs=[hbm] * 4,
        out_shape=[jax.ShapeDtypeStruct((2, 3, 2, 40, width), bf16)] * 4,
        scratch_shapes=[pltpu.VMEM((3, 4, 2, 2, 40, width), bf16), pltpu.SemaphoreType.DMA((3, 16))],
        compiler_params=limit(22),
        cost_estimate=pl.CostEstimate(flops=6_000_000_000, bytes_accessed=8_000_000, transcendentals=0),
        name="grads",
    )(info, pack, core_swap(pack), atts, far_atts, cot_rows, far_cot)

    mine_a, away_a, mine_b, away_b, *back = lax.optimization_barrier((mine_a, away_a, mine_b, away_b, *back))
    away_a, away_b, grad_atts = lax.optimization_barrier((away_a, away_b, jnp.stack(back)))
    from_a, from_b = plane_shift(away_a, 1), plane_shift(away_b, 2)
    hid_near, hid_far, send = pl.pallas_call(
        attend_back_kernel,
        grid_spec=pltpu.PrefetchScalarGridSpec(
            num_scalar_prefetch=1,
            grid=(4,),
            in_specs=[
                seq_block(4, width=width), seq_block(4, width=width),
                whole((1, width)), whole((1, 160)), whole((width, 480)),
                seq_block(2, 4, width=480),
                *[pl.BlockSpec((4, 1, 32, 160), lambda s, info, core=core: (0, core, s, 0)) for core in range(2)],
                whole((1, width)),
            ],
            out_specs=[
                seq_block(4, width=width), seq_block(4, width=width),
                whole((4, 336, 480)),
            ],
            scratch_shapes=[
                pltpu.VMEM((width, 480), f32), pltpu.VMEM((1, width), f32),
                pltpu.VMEM((1, 160), f32), pltpu.VMEM((8, 1, 480), f32),
            ],
        ),
        out_shape=[
            jax.ShapeDtypeStruct((4, 128, width), bf16),
            jax.ShapeDtypeStruct((4, 128, width), bf16),
            jax.ShapeDtypeStruct((4, 336, 480), bf16),
        ],
        compiler_params=limit(22),
        cost_estimate=pl.CostEstimate(flops=15_000_000_000, bytes_accessed=12_000_000, transcendentals=600_000),
        name="attend_back",
    )(info, near, far, gain_one, query_mult, w_qkv, pre, grad_atts, core_swap(grad_atts), gain_two_grad)

    send, out_rows = lax.optimization_barrier((send, out_rows))
    sums = lax.psum_scatter(send, "z", scatter_dimension=0, tiled=True)
    out_sent = [pick(out_rows, (z + k) % 4) for k in range(4)]
    out_one, out_three = ring_shift(out_sent[1], 1), ring_shift(out_sent[3], 3)
    from_a, from_b, hid_far, out_one, out_three = lax.optimization_barrier(
        (from_a, from_b, hid_far, out_one, out_three)
    )
    swapped = core_swap(hid_far)
    hid = [sum_low(hid_near[i], swapped[i]) for i in range(4)]
    outputs = by_source([out_sent[0], out_one, ring_shift(out_sent[2], 2), out_three], z, 0).reshape(16, 8, width)
    keep_a, away_a, keep_b, away_b = pl.pallas_call(
        meet_kernel,
        in_specs=[smem] + [vmem] * 4,
        out_specs=[vmem] * 4,
        out_shape=[jax.ShapeDtypeStruct((2, 3, 40, width), bf16)] * 4,
        compiler_params=limit(18),
        cost_estimate=pl.CostEstimate(flops=3_000_000_000, bytes_accessed=8_000_000, transcendentals=0),
        name="meet",
    )(info, mine_a, from_a, mine_b, from_b)
    from_a, from_b = plane_shift(away_a, 2), plane_shift(away_b, 1)
    *hid, from_a, from_b, outputs = lax.optimization_barrier((*hid, from_a, from_b, outputs))
    kept = pl.pallas_call(
        join_kernel,
        in_specs=[vmem] * 4,
        out_specs=vmem,
        out_shape=jax.ShapeDtypeStruct((4, 3, 40, width), bf16),
        compiler_params=limit(12),
        cost_estimate=pl.CostEstimate(flops=2_000_000_000, bytes_accessed=4_000_000, transcendentals=0),
        name="join",
    )(keep_a, from_a, keep_b, from_b)
    moved = [plane_shift(hid[step], step) for step in (1, 2, 3)]
    moved[0], sums = lax.optimization_barrier((moved[0], sums))
    big_sums = lax.psum_scatter(kept, "z", scatter_dimension=0, tiled=True)[0]
    grad_home = pl.pallas_call(
        norm_kernel,
        in_specs=[smem] + [vmem] * 7,
        out_specs=[vmem] * 4,
        out_shape=[jax.ShapeDtypeStruct((4, 8, width), bf16)] * 4,
        scratch_shapes=[pltpu.VMEM((4, 4, 8, width), f32)],
        compiler_params=limit(10),
        cost_estimate=pl.CostEstimate(flops=2_000_000_000, bytes_accessed=2_500_000, transcendentals=128),
        name="norm",
    )(info, hid[0], *moved, x_rows, grad_mid, gain_one)
    sums = pl.pallas_call(
        fold_kernel,
        in_specs=[vmem],
        out_specs=vmem,
        out_shape=jax.ShapeDtypeStruct((8, 48, 480), bf16),
        scratch_shapes=[pltpu.VMEM((8, 480), f32)],
        compiler_params=limit(8),
        cost_estimate=pl.CostEstimate(flops=2_000_000_000, bytes_accessed=1_600_000, transcendentals=0),
        name="fold",
    )(sums)
    sums = lax.all_to_all(sums, ("y", "core", "x"), split_axis=0, concat_axis=0, tiled=True)
    rows_shape = [jax.ShapeDtypeStruct((40, width), f32)] * 3
    qkv_sums = pl.pallas_call(
        spread_kernel, in_specs=[vmem], out_specs=[vmem] * 3, out_shape=rows_shape, compiler_params=limit(6), name="spread"
    )(sums)
    big_sums = pl.pallas_call(
        widen_kernel, in_specs=[vmem], out_specs=[vmem] * 3, out_shape=rows_shape, compiler_params=limit(6), name="widen"
    )(big_sums)
    line_sums = jnp.sum(sums[:, 40, :120].astype(f32), axis=0).reshape(3, 40)
    scale_low = query_scale.astype(bf16).astype(f32)
    scale_sum = LOG2E / math.sqrt(HD) * jax.nn.sigmoid(scale_low) * line_sums[2]
    grad_home = [grad_home[0]] + [ring_shift(grad_home[k], k) for k in (1, 2, 3)]
    grad_home = by_source(grad_home, z, 0).reshape(16, 8, width)

    return (
        outputs, grad_home, qkv_sums[0], qkv_sums[1], qkv_sums[2],
        big_sums[0], big_sums[1], big_sums[2], line_sums[0], line_sums[1], scale_sum,
    )


def solution(mesh):
    names = ("dp", "ctx")
    body = per_device
    if dict(mesh.shape) == {"dp": 16, "ctx": 2}:
        mesh = Mesh(mesh.devices.reshape(4, 2, 2, 2), ("z", "y", "core", "x"))
        names = mesh.axis_names
        body = planes
    seq, mat, line = P(None, names, None), P(names, None), P(names)
    return jax.shard_map(
        body,
        mesh=mesh,
        in_specs=(seq,) * 2 + (mat,) * 6 + (line,) * 3 + (P(), P()),
        out_specs=(seq,) * 2 + (mat,) * 6 + (line,) * 3,
        check_vma=False,
    )
```

```python
import math

import jax
import jax.numpy as jnp
from jax import lax
from jax.experimental import pallas as pl
from jax.experimental.pallas import tpu as pltpu
from jax.sharding import Mesh, PartitionSpec as P

H = 16
HD = 80


def mult_trans(left, right):
    return lax.dot_general(
        left, right, (((1,), (1,)), ((), ())), preferred_element_type=jnp.float32
    )


def trans_mult(left, right):
    return lax.dot_general(
        left, right, (((0,), (0,)), ((), ())), preferred_element_type=jnp.float32
    )


def position_of(index, local_rows, piece_rows, groups):
    column = index // local_rows
    within = index % local_rows
    return (within // piece_rows * groups + column) * piece_rows + within % piece_rows


def norm_back(grad_hidden, normed, inverse, gain_value):
    grad_normed = grad_hidden * gain_value
    return inverse * (grad_normed - normed * jnp.mean(grad_normed * normed, axis=1, keepdims=True))


def per_device(
    inputs,
    cotangent,
    w_query,
    w_key,
    w_value,
    w_output,
    w_up,
    w_down,
    attn_gain,
    mlp_gain,
    query_scale,
    deal,
    lengths,
):
    groups = lax.axis_size("ctx")
    group_index = lax.axis_index("dp")
    ctx_index = lax.axis_index("ctx")
    head_count = H
    head_dim = HD
    piece_rows = inputs.shape[1]
    seq_numbers = jnp.arange(inputs.shape[0], dtype=jnp.int32)
    seq_lengths = jnp.sum(
        jnp.where(deal[None, :] == seq_numbers[:, None], lengths[None, :], 0), axis=1
    )
    local_in, local_cot = (
        lax.all_to_all(inputs, "dp", split_axis=0, concat_axis=1, tiled=True),
        lax.all_to_all(cotangent, "dp", split_axis=0, concat_axis=1, tiled=True),
    )
    seq_count, local_rows, model_width = local_in.shape
    padded = local_rows * groups
    token_count = seq_count * local_rows
    my_lengths = lax.dynamic_slice_in_dim(seq_lengths, group_index * seq_count, seq_count, 0)
    query_pos = position_of(
        ctx_index * local_rows + jnp.arange(local_rows, dtype=jnp.int32),
        local_rows,
        piece_rows,
        groups,
    )
    flat_in = local_in.reshape(token_count, model_width).astype(jnp.float32)
    flat_cot = local_cot.reshape(token_count, model_width)
    lowered = (
        w_query.astype(jnp.bfloat16),
        w_key.astype(jnp.bfloat16),
        w_value.astype(jnp.bfloat16),
        w_output.astype(jnp.bfloat16),
        w_up.astype(jnp.bfloat16),
        w_down.astype(jnp.bfloat16),
        attn_gain.astype(jnp.bfloat16),
        mlp_gain.astype(jnp.bfloat16),
        query_scale.astype(jnp.bfloat16),
    )
    gathered = (
        lax.all_gather(lowered[0], ("dp", "ctx"), axis=0, tiled=True),
        lax.all_gather(lowered[1], ("dp", "ctx"), axis=0, tiled=True),
        lax.all_gather(lowered[2], ("dp", "ctx"), axis=0, tiled=True),
        lax.all_gather(lowered[3], ("dp", "ctx"), axis=0, tiled=True),
        lax.all_gather(lowered[4], ("dp", "ctx"), axis=0, tiled=True),
        lax.all_gather(lowered[5], ("dp", "ctx"), axis=0, tiled=True),
        lax.all_gather(lowered[6], ("dp", "ctx"), axis=0, tiled=True),
        lax.all_gather(lowered[7], ("dp", "ctx"), axis=0, tiled=True),
        lax.all_gather(lowered[8], ("dp", "ctx"), axis=0, tiled=True),
    )
    (
        query_full,
        key_full,
        value_full,
        output_full,
        up_full,
        down_full,
        gain_one,
        gain_two,
        scale_raw,
    ) = gathered
    inv_one = lax.rsqrt(jnp.mean(flat_in * flat_in, axis=1, keepdims=True) + 1e-06)
    normed_one = flat_in * inv_one
    hidden_one = (normed_one * gain_one.astype(jnp.float32)).astype(jnp.bfloat16)
    scale_param = scale_raw.astype(jnp.float32)
    query_mult = 1.442695041 / math.sqrt(head_dim) * jax.nn.softplus(scale_param)
    query_pre = jnp.dot(hidden_one, query_full, preferred_element_type=jnp.float32)
    queries = (query_pre * query_mult).astype(jnp.bfloat16)
    keys_local = jnp.dot(hidden_one, key_full, preferred_element_type=jnp.float32).astype(
        jnp.bfloat16
    )
    values_local = jnp.dot(hidden_one, value_full, preferred_element_type=jnp.float32).astype(
        jnp.bfloat16
    )
    four_shape = (seq_count, local_rows, head_count, head_dim)
    query_four = queries.reshape(four_shape)
    keys_three = keys_local.reshape(seq_count, local_rows, model_width)
    values_three = values_local.reshape(seq_count, local_rows, model_width)

    def live_between(row_pos, key_pos):
        allowed = (key_pos[None, None, :] <= row_pos[None, :, None]) & (
            key_pos[None, None, :] < my_lengths[:, None, None]
        )
        return allowed[:, :, None, :]

    def live_mask(key_pos):
        return live_between(query_pos, key_pos)

    def attend_block(state_now, key_block, value_block, first_row):
        run_max, run_sum, run_acc = state_now
        block_len = key_block.shape[1]
        key_pos = position_of(
            first_row + jnp.arange(block_len, dtype=jnp.int32), local_rows, piece_rows, groups
        )
        key_four = key_block.reshape(seq_count, block_len, head_count, head_dim)
        value_four = value_block.reshape(seq_count, block_len, head_count, head_dim)
        scores = jnp.einsum(
            "srhd,skhd->srhk", query_four, key_four, preferred_element_type=jnp.float32
        )
        allowed = live_mask(key_pos)
        masked = jnp.where(allowed, scores, -1e30)
        new_max = jnp.maximum(run_max, jnp.max(masked, axis=3))
        weights_now = jnp.exp(jnp.where(allowed, masked - new_max[..., None], -1e30))
        factor = jnp.exp(run_max - new_max)
        new_sum = run_sum * factor + jnp.sum(weights_now, axis=3)
        added = jnp.einsum(
            "srhk,skhd->srhd",
            weights_now.astype(jnp.bfloat16),
            value_four,
            preferred_element_type=jnp.float32,
        )
        return (new_max, new_sum, run_acc * factor[..., None] + added)

    start_state = (
        jnp.full((seq_count, local_rows, head_count), -1e30, jnp.float32),
        jnp.zeros((seq_count, local_rows, head_count), jnp.float32),
        jnp.zeros(four_shape, jnp.float32),
    )
    key_piece = lax.all_gather(keys_three, "ctx", axis=1, tiled=True)
    value_piece = lax.all_gather(values_three, "ctx", axis=1, tiled=True)
    piece_len = key_piece.shape[1]
    fold_block_len = 512 if piece_len % 512 == 0 else piece_len

    def one_block(state_now, block_index):
        offset = block_index * fold_block_len
        key_block = lax.dynamic_slice_in_dim(key_piece, offset, fold_block_len, 1)
        value_block = lax.dynamic_slice_in_dim(value_piece, offset, fold_block_len, 1)
        return (attend_block(state_now, key_block, value_block, offset), None)

    result_state, unused = lax.scan(
        one_block, start_state, jnp.arange(piece_len // fold_block_len, dtype=jnp.int32)
    )
    run_max, run_sum, run_acc = result_state
    log_total = run_max + jnp.log(run_sum)
    attn_exact = run_acc / run_sum[..., None]
    attended = attn_exact.reshape(token_count, model_width).astype(jnp.bfloat16)
    middle = flat_in + jnp.dot(attended, output_full, preferred_element_type=jnp.float32)
    inv_two = lax.rsqrt(jnp.mean(middle * middle, axis=1, keepdims=True) + 1e-06)
    normed_two = middle * inv_two
    hidden_two = (normed_two * gain_two.astype(jnp.float32)).astype(jnp.bfloat16)
    up_pre = jnp.dot(hidden_two, up_full, preferred_element_type=jnp.float32)
    active = jax.nn.silu(up_pre).astype(jnp.bfloat16)
    result = (middle + jnp.dot(active, down_full, preferred_element_type=jnp.float32)).astype(
        jnp.bfloat16
    )
    back_weights = (
        lax.all_gather(lowered[0], ("dp", "ctx"), axis=0, tiled=True),
        lax.all_gather(lowered[1], ("dp", "ctx"), axis=0, tiled=True),
        lax.all_gather(lowered[2], ("dp", "ctx"), axis=0, tiled=True),
        lax.all_gather(lowered[3], ("dp", "ctx"), axis=0, tiled=True),
        lax.all_gather(lowered[4], ("dp", "ctx"), axis=0, tiled=True),
        lax.all_gather(lowered[5], ("dp", "ctx"), axis=0, tiled=True),
        lax.all_gather(lowered[6], ("dp", "ctx"), axis=0, tiled=True),
        lax.all_gather(lowered[7], ("dp", "ctx"), axis=0, tiled=True),
        lax.all_gather(lowered[8], ("dp", "ctx"), axis=0, tiled=True),
    )
    (
        query_back,
        key_back,
        value_back,
        output_back,
        up_back,
        down_back,
        gain_one_back,
        gain_two_back,
        scale_back,
    ) = back_weights
    cot_wide = flat_cot.astype(jnp.float32)
    grad_down = trans_mult(active, flat_cot)
    grad_active = mult_trans(flat_cot, down_back)
    sigma_up = jax.nn.sigmoid(up_pre)
    grad_up_pre = (grad_active * sigma_up * (1.0 + up_pre * (1.0 - sigma_up))).astype(jnp.bfloat16)
    grad_up = trans_mult(hidden_two, grad_up_pre)
    grad_hidden_two = mult_trans(grad_up_pre, up_back)
    grad_gain_two = jnp.sum(grad_hidden_two * normed_two, axis=0)
    grad_middle = cot_wide + norm_back(
        grad_hidden_two, normed_two, inv_two, gain_two_back.astype(jnp.float32)
    )
    grad_middle_low = grad_middle.astype(jnp.bfloat16)
    grad_output = trans_mult(attended, grad_middle_low)
    grad_attended = mult_trans(grad_middle_low, output_back).astype(jnp.bfloat16)
    grad_att_four = grad_attended.reshape(four_shape)
    delta_rows = jnp.sum(grad_att_four.astype(jnp.float32) * attn_exact, axis=3)
    key_all, value_all = (
        lax.all_gather(keys_three, "ctx", axis=1, tiled=True),
        lax.all_gather(values_three, "ctx", axis=1, tiled=True),
    )
    block_len = min(512, padded)

    def back_block(block_index, state_now):
        grad_query, grad_key_all, grad_value_all = state_now
        offset = block_index * block_len
        key_block = lax.dynamic_slice_in_dim(key_all, offset, block_len, 1).reshape(
            seq_count, block_len, head_count, head_dim
        )
        value_block = lax.dynamic_slice_in_dim(value_all, offset, block_len, 1).reshape(
            seq_count, block_len, head_count, head_dim
        )
        key_pos = position_of(
            offset + jnp.arange(block_len, dtype=jnp.int32), local_rows, piece_rows, groups
        )
        scores = jnp.einsum(
            "srhd,skhd->srhk", query_four, key_block, preferred_element_type=jnp.float32
        )
        probs = jnp.exp(jnp.where(live_mask(key_pos), scores - log_total[..., None], -1e30))
        grad_value_block = jnp.einsum(
            "srhk,srhd->skhd",
            probs.astype(jnp.bfloat16),
            grad_att_four,
            preferred_element_type=jnp.float32,
        )
        grad_probs = jnp.einsum(
            "srhd,skhd->srhk", grad_att_four, value_block, preferred_element_type=jnp.float32
        )
        grad_scores = (probs * (grad_probs - delta_rows[..., None])).astype(jnp.bfloat16)
        grad_query = grad_query + jnp.einsum(
            "srhk,skhd->srhd", grad_scores, key_block, preferred_element_type=jnp.float32
        )
        grad_key_block = jnp.einsum(
            "srhk,srhd->skhd", grad_scores, query_four, preferred_element_type=jnp.float32
        )
        grad_key_all = lax.dynamic_update_slice_in_dim(
            grad_key_all, grad_key_block.reshape(seq_count, block_len, model_width), offset, 1
        )
        grad_value_all = lax.dynamic_update_slice_in_dim(
            grad_value_all, grad_value_block.reshape(seq_count, block_len, model_width), offset, 1
        )
        return (grad_query, grad_key_all, grad_value_all)

    zero_all = jnp.zeros((seq_count, padded, model_width), jnp.float32)
    grad_query, grad_key_all, grad_value_all = lax.fori_loop(
        0, padded // block_len, back_block, (jnp.zeros(four_shape, jnp.float32), zero_all, zero_all)
    )
    grad_key_mine, grad_value_mine = (
        lax.psum_scatter(
            grad_key_all.astype(jnp.bfloat16), "ctx", scatter_dimension=1, tiled=True
        ).astype(jnp.float32),
        lax.psum_scatter(
            grad_value_all.astype(jnp.bfloat16), "ctx", scatter_dimension=1, tiled=True
        ).astype(jnp.float32),
    )
    grad_query_flat = grad_query.reshape(token_count, model_width)
    grad_query_pre = (grad_query_flat * query_mult).astype(jnp.bfloat16)
    grad_scale = (
        1.442695041
        / math.sqrt(head_dim)
        * jax.nn.sigmoid(scale_back.astype(jnp.float32))
        * jnp.sum(grad_query_flat * query_pre, axis=0)
    )
    grad_key_low = grad_key_mine.reshape(token_count, model_width).astype(jnp.bfloat16)
    grad_value_low = grad_value_mine.reshape(token_count, model_width).astype(jnp.bfloat16)
    grad_wq = trans_mult(hidden_one, grad_query_pre)
    grad_wk = trans_mult(hidden_one, grad_key_low)
    grad_wv = trans_mult(hidden_one, grad_value_low)
    grad_hidden_one = (
        mult_trans(grad_query_pre, query_back)
        + mult_trans(grad_key_low, key_back)
        + mult_trans(grad_value_low, value_back)
    )
    grad_gain_one = jnp.sum(grad_hidden_one * normed_one, axis=0)
    grad_in = grad_middle + norm_back(
        grad_hidden_one, normed_one, inv_one, gain_one_back.astype(jnp.float32)
    )
    matrix_stack = jnp.stack([grad_wq, grad_wk, grad_wv, grad_output, grad_up, grad_down], axis=0)
    vector_stack = jnp.stack([grad_gain_one, grad_gain_two, grad_scale], axis=0)
    matrix_sums, vector_sums = (
        lax.psum_scatter(matrix_stack, ("dp", "ctx"), scatter_dimension=1, tiled=True),
        lax.psum_scatter(vector_stack, ("dp", "ctx"), scatter_dimension=1, tiled=True),
    )
    out_local = result.reshape(seq_count, local_rows, model_width)
    grad_local = grad_in.astype(jnp.bfloat16).reshape(seq_count, local_rows, model_width)
    back_out, back_grad = (
        lax.all_to_all(out_local, "dp", split_axis=1, concat_axis=0, tiled=True),
        lax.all_to_all(grad_local, "dp", split_axis=1, concat_axis=0, tiled=True),
    )
    return (
        back_out,
        back_grad,
        matrix_sums[0],
        matrix_sums[1],
        matrix_sums[2],
        matrix_sums[3],
        matrix_sums[4],
        matrix_sums[5],
        vector_sums[0],
        vector_sums[1],
        vector_sums[2],
    )


LOG2E = 1.442695041
CODES = (0, 1, 4, 5)


def plane_shift(value, step):
    if step == 1:
        return lax.ppermute(value, "x", [(0, 1), (1, 0)])
    if step == 2:
        return lax.ppermute(value, "y", [(0, 1), (1, 0)])
    return lax.ppermute(value, ("y", "x"), [(0, 3), (1, 2), (2, 1), (3, 0)])


def core_swap(value):
    return lax.ppermute(value, "core", [(0, 1), (1, 0)])


def ring_shift(value, step):
    return lax.ppermute(value, "z", [(i, (i + step) % 4) for i in range(4)])


def pick(array, index):
    return lax.dynamic_index_in_dim(array, index, 0, keepdims=False)


def by_source(pieces, z_index, axis):
    pieces = [jnp.expand_dims(item, axis) for item in pieces]
    shape = [1] * pieces[0].ndim
    shape[axis] = 4
    hop = ((z_index - jnp.arange(4, dtype=jnp.int32)) % 4).reshape(shape)
    made = pieces[0]
    for k in (1, 2, 3):
        made = jnp.where(hop == k, pieces[k], made)
    return made


def pair(mine, other, index, axis):
    shape = [1] * (mine.ndim + 1)
    shape[axis] = 2
    slot = jnp.arange(2, dtype=jnp.int32).reshape(shape)
    return jnp.where(slot == index, jnp.expand_dims(mine, axis), jnp.expand_dims(other, axis))


def row_positions(shape, dim, plane_index):
    row = lax.broadcasted_iota(jnp.int32, shape, dim)
    chip = (row // 32) % 4
    code = (chip % 2) + 4 * (chip // 2) + 2 * (row // 128)
    return 64 * ((row % 32) // 8) + 8 * (plane_index ^ code) + row % 8


def live_pairs(info_ref, seq):
    shape = (256, 256)
    query_pos = row_positions(shape, 0, info_ref[1])
    key_pos = row_positions(shape, 1, info_ref[1])
    return (key_pos <= query_pos) & (key_pos < info_ref[2 + seq])


def block_rows(near_ref, far_ref):
    return jnp.concatenate([near_ref[...], far_ref[...]], axis=0).reshape(256, near_ref.shape[2])


def soft_probs(query, key, live):
    scores = mult_trans(query, key)
    scores = jnp.where(live, scores, -1e30)
    top = jnp.max(scores, axis=1, keepdims=True)
    weights = jnp.where(live, jnp.exp(scores - top), 0.0)
    return weights / jnp.sum(weights, axis=1, keepdims=True)


def attend_kernel(
    info_ref, near_ref, far_ref, gain_ref, mult_ref, w_ref, pre_ref, att_ref
):
    seq = pl.program_id(0)
    live = live_pairs(info_ref, seq)
    wide = block_rows(near_ref, far_ref).astype(jnp.float32)
    inverse = lax.rsqrt(jnp.mean(wide * wide, axis=1, keepdims=True) + 1e-06)
    hidden = (wide * inverse * gain_ref[...]).astype(jnp.bfloat16)
    pre = jnp.dot(hidden, w_ref[...], preferred_element_type=jnp.float32)
    pre_ref[...] = pre.reshape(2, 4, 32, 480)
    query = (pre[:, 0:160] * mult_ref[...]).astype(jnp.bfloat16)
    key = pre[:, 160:320].astype(jnp.bfloat16)
    value = pre[:, 320:480].astype(jnp.bfloat16)
    heads = []
    for head in range(2):
        part = slice(80 * head, 80 * head + 80)
        probs = soft_probs(query[:, part], key[:, part], live).astype(jnp.bfloat16)
        heads.append(jnp.dot(probs, value[:, part], preferred_element_type=jnp.float32))
    att = jnp.concatenate(heads, axis=1).astype(jnp.bfloat16).reshape(2, 4, 32, 160)
    for chip in range(4):
        for core in range(2):
            att_ref[chip, core] = att[core, chip]


def attend_back_kernel(
    info_ref, near_ref, far_ref, gain_ref, mult_ref, w_ref, pre_ref, grad_near, grad_far, gain_two_ref,
    hid_near, hid_far, send_ref, w_acc, gain_acc, scale_acc, lines,
):
    seq = pl.program_id(0)

    @pl.when(seq == 0)
    def _():
        w_acc[...] = jnp.zeros_like(w_acc)
        gain_acc[...] = jnp.zeros_like(gain_acc)
        scale_acc[...] = jnp.zeros_like(scale_acc)

    live = live_pairs(info_ref, seq)
    wide = block_rows(near_ref, far_ref).astype(jnp.float32)
    inverse = lax.rsqrt(jnp.mean(wide * wide, axis=1, keepdims=True) + 1e-06)
    normed = wide * inverse
    hidden = (normed * gain_ref[...]).astype(jnp.bfloat16)
    pre = pre_ref[...].reshape(256, 480)
    mult = mult_ref[...]
    query = (pre[:, 0:160] * mult).astype(jnp.bfloat16)
    key = pre[:, 160:320].astype(jnp.bfloat16)
    value = pre[:, 320:480].astype(jnp.bfloat16)
    grad_att = jnp.concatenate([grad_near[:, 0], grad_far[:, 0]], axis=0).reshape(256, 160)
    grad_q, grad_k, grad_v = [], [], []
    for head in range(2):
        part = slice(80 * head, 80 * head + 80)
        probs = soft_probs(query[:, part], key[:, part], live)
        grad_probs = mult_trans(grad_att[:, part], value[:, part])
        delta = jnp.sum(probs * grad_probs, axis=1, keepdims=True)
        grad_scores = (probs * (grad_probs - delta)).astype(jnp.bfloat16)
        grad_v.append(trans_mult(probs.astype(jnp.bfloat16), grad_att[:, part]))
        grad_q.append(jnp.dot(grad_scores, key[:, part], preferred_element_type=jnp.float32))
        grad_k.append(trans_mult(grad_scores, query[:, part]))
    grad_query = jnp.concatenate(grad_q, axis=1)
    scale_acc[...] += jnp.sum(grad_query * pre[:, 0:160], axis=0, keepdims=True)
    joined = jnp.concatenate([grad_query * mult] + grad_k + grad_v, axis=1).astype(jnp.bfloat16)
    w_acc[...] += trans_mult(hidden, joined)
    grad_hidden = mult_trans(joined, w_ref[...])
    gain_acc[...] += jnp.sum(grad_hidden * normed, axis=0, keepdims=True)
    low = grad_hidden.astype(jnp.bfloat16).reshape(2, 4, 32, 1280)
    hid_near[...] = low[0]
    hid_far[...] = low[1]

    @pl.when(seq == 3)
    def _():
        lines[...] = jnp.zeros_like(lines)
        for which, source in enumerate((gain_acc, gain_two_ref)):
            for owner in range(32):
                lane = 120 * (owner % 4) + 40 * which
                lines[owner // 4, :, lane : lane + 40] = source[:, 40 * owner : 40 * owner + 40]
        for part in range(4):
            lane = 120 * part + 80
            lines[info_ref[1], :, lane : lane + 40] = scale_acc[:, 40 * part : 40 * part + 40]
        blank = jnp.zeros((14, 480), jnp.float32)
        for target in range(4):
            rows = w_acc[320 * target : 320 * target + 320, :]
            block = jnp.concatenate([rows, lines[2 * target], lines[2 * target + 1], blank], axis=0)
            send_ref[target] = block.astype(jnp.bfloat16)


def block_index(z_index, y_index, core):
    return pl.ds(pl.multiple_of((4 * z_index + 2 * y_index + core) * 80, 80), 80)


def arrival_rows(info_ref, w, z_index, y_index, core):
    if w > 0:
        return block_index(z_index, y_index, core)
    block = 4 * z_index + 2 * y_index + core
    code = info_ref[1] ^ (block // 2)
    arrival = 2 * ((code & 1) + 2 * (code // 4)) + ((code // 2) & 1)
    return pl.ds(pl.multiple_of(160 * arrival + 80 * (block & 1), 80), 80)


def feed_kernel(
    info_ref, x_ref, g_ref, atts, far_atts, gain_ref,
    near_rows, across_a, across_b, far_near_rows, far_across_a, far_across_b,
    out_ref, pack_ref, dmid_ref, datt_0, datt_1, datt_2, datt_3, gain_grad,
    weights, sems,
):
    y_index, core_index = info_ref[1] // 4, (info_ref[1] // 2) % 2
    copies = []
    for w in range(3):
        moved = []
        for core, own, others in (
            (core_index, near_rows, (across_a, across_b)),
            (1 - core_index, far_near_rows, (far_across_a, far_across_b)),
        ):
            for z_index in range(4):
                moved.append((own.at[z_index, w], z_index, y_index, core))
                moved.append((others[z_index // 2].at[z_index % 2, w], z_index, 1 - y_index, core))
        copies.append([
            pltpu.make_async_copy(src, weights.at[w, arrival_rows(info_ref, w, *place)], sems.at[w, i])
            for i, (src, *place) in enumerate(moved)
        ])
    for group in copies:
        for copy in group:
            copy.start()
    datts = (datt_0, datt_1, datt_2, datt_3)

    for copy in copies[0]:
        copy.wait()
    att = jnp.concatenate(
        [(far_atts if core else atts)[chip, core] for chip in range(4) for core in range(2)], axis=1
    )
    middle = x_ref[...].astype(jnp.float32)
    middle += jnp.dot(att, weights[0], preferred_element_type=jnp.float32)
    inverse = lax.rsqrt(jnp.mean(middle * middle, axis=1, keepdims=True) + 1e-06)
    normed = middle * inverse
    gain = gain_ref[...]
    hidden = (normed * gain).astype(jnp.bfloat16)
    pack_ref[1] = hidden
    for copy in copies[1]:
        copy.wait()
    up = jnp.dot(hidden, weights[1], preferred_element_type=jnp.float32)
    sigma = jax.nn.sigmoid(up)
    active = (up * sigma).astype(jnp.bfloat16)
    pack_ref[0] = active
    for copy in copies[2]:
        copy.wait()
    down = jnp.dot(active, weights[2], preferred_element_type=jnp.float32)
    result = middle + down
    for seq in range(4):
        for plane_z in range(4):
            row = 32 * seq + 8 * plane_z
            out_ref[plane_z, seq] = result[row : row + 8].astype(jnp.bfloat16)
    cot = g_ref[...]
    grad_act = mult_trans(cot, weights[2])
    grad_up = (grad_act * sigma * (1.0 + up * (1.0 - sigma))).astype(jnp.bfloat16)
    pack_ref[2] = grad_up
    grad_hidden = mult_trans(grad_up, weights[1])
    gain_grad[...] = jnp.sum(grad_hidden * normed, axis=0, keepdims=True)
    grad_mid = cot.astype(jnp.float32) + norm_back(grad_hidden, normed, inverse, gain)
    dmid_ref[...] = grad_mid
    low = grad_mid.astype(jnp.bfloat16)
    pack_ref[3] = low
    grad_att = mult_trans(low, weights[0]).astype(jnp.bfloat16)
    for chip in range(4):
        for core in range(2):
            lane = 160 * (2 * chip + core)
            datts[chip][core] = grad_att[:, lane : lane + 160]


def grads_kernel(
    info_ref, pack_ref, far_pack, atts, far_atts, cot_ref, far_cot, keep_a, away_a, keep_b, away_b, stage, sems
):
    y_index, core_index, x_index = info_ref[1] // 4, (info_ref[1] // 2) % 2, info_ref[1] % 2

    def leave(w):
        copies = []
        for half in range(2):
            for i in range(2):
                moves = ((stage.at[w, half, i, 1 - x_index], away_a), (stage.at[w, 2 + half, 1 - y_index, i], away_b))
                for j, (block, target) in enumerate(moves):
                    sem = sems.at[w, 4 * half + 2 * i + j]
                    copies.append(pltpu.make_async_copy(block, target.at[half, w, i], sem))
        return copies

    def keep():
        for half in range(2):
            for w in range(3):
                for i in range(2):
                    keep_a[half, w, i] = stage[w, half, i, x_index]
                    keep_b[half, w, i] = stage[w, 2 + half, y_index, i]

    def store(w, made):
        for i in range(16):
            stage[w, i // 4, (i // 2) % 2, i % 2] = made[40 * i : 40 * i + 40].astype(jnp.bfloat16)

    def both(near, far):
        return jnp.concatenate([near, far], axis=0)

    cots = both(cot_ref[...], far_cot[...])
    for core in range(2):

        @pl.when(core_index == core)
        def _():
            def own_columns(near, far):
                return both(*(
                    jnp.concatenate([ref[:, 160 * i + 80 * core : 160 * i + 80 * core + 80] for i in range(8)], axis=1)
                    for ref in (near, far)
                ))

            acts = own_columns(pack_ref.at[0], far_pack.at[0])
            store(2, trans_mult(acts, cots))
            for copy in leave(2):
                copy.start()
            acts = own_columns(pack_ref.at[1], far_pack.at[1])
            store(1, trans_mult(acts, both(pack_ref[2], far_pack[2])))
            for copy in leave(1):
                copy.start()
            grads = both(pack_ref[3], far_pack[3])
            pieces = []
            for chip in range(4):
                for source in range(2):
                    near, far = (far_atts, far_atts) if source else (atts, atts)
                    pieces.append(both(near[chip, source], far[chip, 1 - source])[:, 80 * core : 80 * core + 80])
            made = trans_mult(jnp.concatenate(pieces, axis=1), grads)
            for i in range(8):
                source = info_ref[1] ^ (CODES[i // 2] + 2 * (i % 2))
                for part in range(2):
                    row = 80 * i + 40 * part
                    stage[0, source // 2, source & 1, part] = made[row : row + 40].astype(jnp.bfloat16)
            for copy in leave(0):
                copy.start()

    keep()
    for w in range(3):
        for copy in leave(w):
            copy.wait()


def meet_kernel(info_ref, mine_a, from_a, mine_b, from_b, keep_a, away_a, keep_b, away_b):
    y_index, x_index = info_ref[1] // 4, info_ref[1] % 2
    for half in range(2):
        for w in range(3):
            for row, out in ((y_index, keep_a), (1 - y_index, away_a)):
                out[half, w] = sum_low(mine_a[half, w, row], from_a[half, w, row])
            for row, out in ((x_index, keep_b), (1 - x_index, away_b)):
                out[half, w] = sum_low(mine_b[half, w, row], from_b[half, w, row])


def join_kernel(keep_a, from_a, keep_b, from_b, out_ref):
    for half in range(2):
        for w in range(3):
            out_ref[half, w] = sum_low(keep_a[half, w], from_a[half, w])
            out_ref[2 + half, w] = sum_low(keep_b[half, w], from_b[half, w])


def sum_low(left, right):
    return (left.astype(jnp.float32) + right.astype(jnp.float32)).astype(jnp.bfloat16)


def norm_kernel(info_ref, hid_0, hid_1, hid_2, hid_3, x_ref, dmid_ref, gain_ref, out_0, out_1, out_2, out_3, rows):
    grad = hid_0[...].astype(jnp.float32)
    for item in (hid_1, hid_2, hid_3):
        grad += item[...].astype(jnp.float32)
    wide = x_ref[...].astype(jnp.float32)
    inverse = lax.rsqrt(jnp.mean(wide * wide, axis=1, keepdims=True) + 1e-06)
    grad = dmid_ref[...] + norm_back(grad, wide * inverse, inverse, gain_ref[...])
    for seq in range(4):
        for plane_z in range(4):
            row = 32 * seq + 8 * plane_z
            rows[plane_z, seq] = grad[row : row + 8]
    for hop, out in enumerate((out_0, out_1, out_2, out_3)):
        out[...] = rows[(info_ref[0] + hop) & 3].astype(jnp.bfloat16)


def fold_kernel(in_ref, out_ref, line):
    total = in_ref[0].astype(jnp.float32)
    line[...] = jnp.zeros_like(line)
    for owner in range(8):
        lane = 120 * (owner % 4)
        line[0:1, 0:120] = total[320 + owner // 4 : 321 + owner // 4, lane : lane + 120]
        block = jnp.concatenate([total[40 * owner : 40 * owner + 40], line[...]], axis=0)
        out_ref[owner] = block.astype(jnp.bfloat16)


def spread_kernel(in_ref, *outs):
    for which, out in enumerate(outs):
        for owner in range(8):
            part = in_ref[owner, 0:40, 160 * which : 160 * which + 160]
            out[:, 160 * owner : 160 * owner + 160] = part.astype(jnp.float32)


def widen_kernel(in_ref, *outs):
    for which, out in enumerate(outs):
        out[...] = in_ref[which].astype(jnp.float32)


def whole(shape):
    return pl.BlockSpec(shape, lambda *_: (0,) * len(shape))


def seq_block(*lead, width):
    count = len(lead)
    return pl.BlockSpec((*lead, 32, width), lambda s, info: (*(0,) * count, s, 0))


def planes(
    inputs, cotangent, w_query, w_key, w_value, w_output, w_up, w_down,
    attn_gain, mlp_gain, query_scale, deal, lengths,
):
    f32, bf16 = jnp.float32, jnp.bfloat16
    z, y, c, x = (lax.axis_index(name) for name in ("z", "y", "core", "x"))
    plane = 4 * y + 2 * c + x
    width = 1280
    seqs = jnp.arange(16, dtype=jnp.int32)
    seq_lengths = jnp.sum(jnp.where(deal[None, :] == seqs[:, None], lengths[None, :], 0), axis=1)
    my_lengths = lax.dynamic_slice_in_dim(seq_lengths, 4 * z, 4, 0)
    info = jnp.concatenate([jnp.stack([z, plane]), my_lengths]).astype(jnp.int32)

    vec = jnp.concatenate([attn_gain, mlp_gain, query_scale]).astype(bf16)
    vec_block = jnp.zeros((1, 8, width), bf16).at[0, 0, :120].set(vec)
    in_four = inputs.reshape(4, 4, 8, width)
    sent = [jnp.concatenate([pick(in_four, (z + k) % 4), vec_block]) for k in range(4)]
    qkv = jnp.stack([w_query, w_key, w_value]).astype(bf16)
    *sent, qkv = lax.optimization_barrier((*sent, qkv))
    got = [sent[0]] + [ring_shift(sent[k], k) for k in (1, 2, 3)]
    x_rows = by_source([item[:4] for item in got], z, 1).reshape(128, width)
    vec_rows = by_source([item[4, 0] for item in got], z, 0)
    vec_rows = jnp.concatenate([vec_rows, jnp.zeros((4, width), bf16)])
    own = jnp.concatenate([x_rows, vec_rows])

    big = jnp.stack([w_output, w_up, w_down]).astype(bf16)
    big = lax.all_gather(big, "z", axis=0)

    qkv = qkv.reshape(3, 40, 8, 160).transpose(2, 1, 0, 3).reshape(8, 40, 480)
    qkv = lax.all_to_all(qkv, ("y", "core", "x"), split_axis=0, concat_axis=0, tiled=True)
    near = jnp.stack([own] + [plane_shift(own, step) for step in (1, 2, 3)])
    big, near, qkv = lax.optimization_barrier((big, near, qkv.reshape(320, 480)))
    w_qkv = lax.all_gather(qkv, "z", axis=0, tiled=True)
    far = core_swap(near)
    beside, across = plane_shift(big, 1), plane_shift(big, 2)
    relay_a, relay_b = beside[:2], across[2:]
    relay_a, relay_b = lax.optimization_barrier((relay_a, relay_b))
    across_a, across_b = plane_shift(relay_a, 2), plane_shift(relay_b, 1)

    vecs = jnp.stack([near[:, 128:132, :120], far[:, 128:132, :120]])
    vecs = vecs.astype(f32).reshape(2, 2, 2, 4, 120)
    vecs = jnp.where(c == 0, vecs, vecs[::-1])
    vecs = jnp.where(y == 0, vecs, vecs[:, ::-1])
    vecs = jnp.where(x == 0, vecs, vecs[:, :, ::-1])
    vecs = vecs.reshape(2, 2, 2, 4, 3, 40).transpose(4, 3, 1, 0, 2, 5).reshape(3, width)
    gain_one, gain_two = vecs[0:1], vecs[1:2]
    my_scale = lax.dynamic_slice_in_dim(vecs[2:3], 160 * plane, 160, 1)
    query_mult = LOG2E / math.sqrt(HD) * jax.nn.softplus(my_scale)
    query_mult, cotangent = lax.optimization_barrier((query_mult, cotangent))
    cot_rows = lax.all_to_all(cotangent.reshape(4, 4, 8, width), "z", split_axis=0, concat_axis=0, tiled=True)


    def limit(megabytes):
        return pltpu.CompilerParams(vmem_limit_bytes=megabytes * 1024 * 1024)

    pre, att_made = pl.pallas_call(
        attend_kernel,
        grid_spec=pltpu.PrefetchScalarGridSpec(
            num_scalar_prefetch=1,
            grid=(4,),
            in_specs=[
                seq_block(4, width=width), seq_block(4, width=width),
                whole((1, width)), whole((1, 160)), whole((width, 480)),
            ],
            out_specs=[seq_block(2, 4, width=480), seq_block(4, 2, width=160)],
        ),
        out_shape=[
            jax.ShapeDtypeStruct((2, 4, 128, 480), f32),
            jax.ShapeDtypeStruct((4, 2, 128, 160), bf16),
        ],
        compiler_params=limit(14),
        cost_estimate=pl.CostEstimate(flops=9_000_000_000, bytes_accessed=8_000_000, transcendentals=600_000),
        name="attend",
    )(info, near, far, gain_one, query_mult, w_qkv)

    near_rows = pair(big, beside, x, 2).reshape(4, 3, 80, width)
    att_made, near_rows, across_a, across_b, cot_rows = lax.optimization_barrier(
        (att_made, near_rows, across_a, across_b, cot_rows)
    )
    far_near_rows = core_swap(near_rows)
    atts = [att_made[0]] + [plane_shift(att_made[step], step) for step in (1, 2, 3)]
    atts = jnp.stack(atts)
    far_atts = core_swap(atts)
    across_a = pair(across[:2], across_a, x, 2).reshape(2, 3, 80, width)
    across_b = pair(across[2:], across_b, x, 2).reshape(2, 3, 80, width)
    far_across_a, far_across_b = core_swap(across_a), core_swap(across_b)
    cot_rows = cot_rows.transpose(1, 0, 2, 3).reshape(128, width)
    far_cot = core_swap(cot_rows)
    far_cot, far_atts, cot_rows = lax.optimization_barrier((far_cot, far_atts, cot_rows))
    datt_shape = jax.ShapeDtypeStruct((2, 128, 160), bf16)
    smem = pl.BlockSpec(memory_space=pltpu.SMEM)
    vmem = pl.BlockSpec(memory_space=pltpu.VMEM)
    hbm = pl.BlockSpec(memory_space=pltpu.HBM)
    out_rows, pack, grad_mid, *datts, gain_two_grad = pl.pallas_call(
        feed_kernel,
        in_specs=[smem] + [vmem] * 5 + [hbm] * 6,
        out_specs=[vmem] * 8,
        out_shape=[
            jax.ShapeDtypeStruct((4, 4, 8, width), bf16),
            jax.ShapeDtypeStruct((4, 128, width), bf16),
            jax.ShapeDtypeStruct((128, width), f32),
        ]
        + [datt_shape] * 4
        + [jax.ShapeDtypeStruct((1, width), f32)],
        scratch_shapes=[pltpu.VMEM((3, width, width), bf16), pltpu.SemaphoreType.DMA((3, 16))],
        compiler_params=limit(28),
        cost_estimate=pl.CostEstimate(flops=12_000_000_000, bytes_accessed=13_000_000, transcendentals=200_000),
        name="feed",
    )(info, x_rows, cot_rows, atts, far_atts, gain_two, near_rows, across_a, across_b, far_near_rows, far_across_a, far_across_b)

    back = [datts[0]] + [plane_shift(datts[step], step) for step in (1, 2, 3)]

    mine_a, away_a, mine_b, away_b = pl.pallas_call(
        grads_kernel,
        in_specs=[smem] + [vmem] * 6,
        out_specs=[vmem, hbm, vmem, hbm],
        out_shape=[jax.ShapeDtypeStruct((2, 3, 2, 40, width), bf16)] * 4,
        scratch_shapes=[pltpu.VMEM((3, 4, 2, 2, 40, width), bf16), pltpu.SemaphoreType.DMA((3, 8))],
        compiler_params=limit(22),
        cost_estimate=pl.CostEstimate(flops=6_000_000_000, bytes_accessed=8_000_000, transcendentals=0),
        name="grads",
    )(info, pack, core_swap(pack), atts, far_atts, cot_rows, far_cot)

    mine_a, away_a, mine_b, away_b, *back = lax.optimization_barrier((mine_a, away_a, mine_b, away_b, *back))
    away_a, away_b, grad_atts = lax.optimization_barrier((away_a, away_b, jnp.stack(back)))
    from_a, from_b = plane_shift(away_a, 1), plane_shift(away_b, 2)
    hid_near, hid_far, send = pl.pallas_call(
        attend_back_kernel,
        grid_spec=pltpu.PrefetchScalarGridSpec(
            num_scalar_prefetch=1,
            grid=(4,),
            in_specs=[
                seq_block(4, width=width), seq_block(4, width=width),
                whole((1, width)), whole((1, 160)), whole((width, 480)),
                seq_block(2, 4, width=480),
                *[pl.BlockSpec((4, 1, 32, 160), lambda s, info, core=core: (0, core, s, 0)) for core in range(2)],
                whole((1, width)),
            ],
            out_specs=[
                seq_block(4, width=width), seq_block(4, width=width),
                whole((4, 336, 480)),
            ],
            scratch_shapes=[
                pltpu.VMEM((width, 480), f32), pltpu.VMEM((1, width), f32),
                pltpu.VMEM((1, 160), f32), pltpu.VMEM((8, 1, 480), f32),
            ],
        ),
        out_shape=[
            jax.ShapeDtypeStruct((4, 128, width), bf16),
            jax.ShapeDtypeStruct((4, 128, width), bf16),
            jax.ShapeDtypeStruct((4, 336, 480), bf16),
        ],
        compiler_params=limit(22),
        cost_estimate=pl.CostEstimate(flops=15_000_000_000, bytes_accessed=12_000_000, transcendentals=600_000),
        name="attend_back",
    )(info, near, far, gain_one, query_mult, w_qkv, pre, grad_atts, core_swap(grad_atts), gain_two_grad)

    send, out_rows = lax.optimization_barrier((send, out_rows))
    sums = lax.psum_scatter(send, "z", scatter_dimension=0, tiled=True)
    out_sent = [pick(out_rows, (z + k) % 4) for k in range(4)]
    out_one, out_three = ring_shift(out_sent[1], 1), ring_shift(out_sent[3], 3)
    from_a, from_b, hid_far, out_one, out_three = lax.optimization_barrier(
        (from_a, from_b, hid_far, out_one, out_three)
    )
    swapped = core_swap(hid_far)
    hid = [sum_low(hid_near[i], swapped[i]) for i in range(4)]
    outputs = by_source([out_sent[0], out_one, ring_shift(out_sent[2], 2), out_three], z, 0).reshape(16, 8, width)
    keep_a, away_a, keep_b, away_b = pl.pallas_call(
        meet_kernel,
        in_specs=[smem] + [vmem] * 4,
        out_specs=[vmem] * 4,
        out_shape=[jax.ShapeDtypeStruct((2, 3, 40, width), bf16)] * 4,
        compiler_params=limit(18),
        cost_estimate=pl.CostEstimate(flops=3_000_000_000, bytes_accessed=8_000_000, transcendentals=0),
        name="meet",
    )(info, mine_a, from_a, mine_b, from_b)
    from_a, from_b = plane_shift(away_a, 2), plane_shift(away_b, 1)
    *hid, from_a, from_b, outputs = lax.optimization_barrier((*hid, from_a, from_b, outputs))
    kept = pl.pallas_call(
        join_kernel,
        in_specs=[vmem] * 4,
        out_specs=vmem,
        out_shape=jax.ShapeDtypeStruct((4, 3, 40, width), bf16),
        compiler_params=limit(12),
        cost_estimate=pl.CostEstimate(flops=2_000_000_000, bytes_accessed=4_000_000, transcendentals=0),
        name="join",
    )(keep_a, from_a, keep_b, from_b)
    moved = [plane_shift(hid[step], step) for step in (1, 2, 3)]
    moved[0], sums = lax.optimization_barrier((moved[0], sums))
    big_sums = lax.psum_scatter(kept, "z", scatter_dimension=0, tiled=True)[0]
    grad_home = pl.pallas_call(
        norm_kernel,
        in_specs=[smem] + [vmem] * 7,
        out_specs=[vmem] * 4,
        out_shape=[jax.ShapeDtypeStruct((4, 8, width), bf16)] * 4,
        scratch_shapes=[pltpu.VMEM((4, 4, 8, width), f32)],
        compiler_params=limit(10),
        cost_estimate=pl.CostEstimate(flops=2_000_000_000, bytes_accessed=2_500_000, transcendentals=128),
        name="norm",
    )(info, hid[0], *moved, x_rows, grad_mid, gain_one)
    sums = pl.pallas_call(
        fold_kernel,
        in_specs=[vmem],
        out_specs=vmem,
        out_shape=jax.ShapeDtypeStruct((8, 48, 480), bf16),
        scratch_shapes=[pltpu.VMEM((8, 480), f32)],
        compiler_params=limit(8),
        cost_estimate=pl.CostEstimate(flops=2_000_000_000, bytes_accessed=1_600_000, transcendentals=0),
        name="fold",
    )(sums)
    sums = lax.all_to_all(sums, ("y", "core", "x"), split_axis=0, concat_axis=0, tiled=True)
    rows_shape = [jax.ShapeDtypeStruct((40, width), f32)] * 3
    qkv_sums = pl.pallas_call(
        spread_kernel, in_specs=[vmem], out_specs=[vmem] * 3, out_shape=rows_shape, compiler_params=limit(6), name="spread"
    )(sums)
    big_sums = pl.pallas_call(
        widen_kernel, in_specs=[vmem], out_specs=[vmem] * 3, out_shape=rows_shape, compiler_params=limit(6), name="widen"
    )(big_sums)
    line_sums = jnp.sum(sums[:, 40, :120].astype(f32), axis=0).reshape(3, 40)
    scale_low = query_scale.astype(bf16).astype(f32)
    scale_sum = LOG2E / math.sqrt(HD) * jax.nn.sigmoid(scale_low) * line_sums[2]
    grad_home = [grad_home[0]] + [ring_shift(grad_home[k], k) for k in (1, 2, 3)]
    grad_home = by_source(grad_home, z, 0).reshape(16, 8, width)

    return (
        outputs, grad_home, qkv_sums[0], qkv_sums[1], qkv_sums[2],
        big_sums[0], big_sums[1], big_sums[2], line_sums[0], line_sums[1], scale_sum,
    )


def solution(mesh):
    names = ("dp", "ctx")
    body = per_device
    if dict(mesh.shape) == {"dp": 16, "ctx": 2}:
        mesh = Mesh(mesh.devices.reshape(4, 2, 2, 2), ("z", "y", "core", "x"))
        names = mesh.axis_names
        body = planes
    seq, mat, line = P(None, names, None), P(names, None), P(names)
    return jax.shard_map(
        body,
        mesh=mesh,
        in_specs=(seq,) * 2 + (mat,) * 6 + (line,) * 3 + (P(), P()),
        out_specs=(seq,) * 2 + (mat,) * 6 + (line,) * 3,
        check_vma=False,
    )
```

```python
import functools
import math

import jax
import jax.numpy as jnp
from jax import lax
from jax.experimental import pallas as pl
from jax.experimental.pallas import tpu as pltpu
from jax.sharding import Mesh, PartitionSpec as P

H = 16
HD = 80


def mult_trans(left, right):
    return lax.dot_general(
        left, right, (((1,), (1,)), ((), ())), preferred_element_type=jnp.float32
    )


def trans_mult(left, right):
    return lax.dot_general(
        left, right, (((0,), (0,)), ((), ())), preferred_element_type=jnp.float32
    )


def position_of(index, local_rows, piece_rows, groups):
    column = index // local_rows
    within = index % local_rows
    return (within // piece_rows * groups + column) * piece_rows + within % piece_rows


def norm_back(grad_hidden, normed, inverse, gain_value):
    grad_normed = grad_hidden * gain_value
    return inverse * (grad_normed - normed * jnp.mean(grad_normed * normed, axis=1, keepdims=True))


def per_device(
    inputs,
    cotangent,
    w_query,
    w_key,
    w_value,
    w_output,
    w_up,
    w_down,
    attn_gain,
    mlp_gain,
    query_scale,
    deal,
    lengths,
):
    groups = lax.axis_size("ctx")
    group_index = lax.axis_index("dp")
    ctx_index = lax.axis_index("ctx")
    head_count = H
    head_dim = HD
    piece_rows = inputs.shape[1]
    seq_numbers = jnp.arange(inputs.shape[0], dtype=jnp.int32)
    seq_lengths = jnp.sum(
        jnp.where(deal[None, :] == seq_numbers[:, None], lengths[None, :], 0), axis=1
    )
    local_in, local_cot = (
        lax.all_to_all(inputs, "dp", split_axis=0, concat_axis=1, tiled=True),
        lax.all_to_all(cotangent, "dp", split_axis=0, concat_axis=1, tiled=True),
    )
    seq_count, local_rows, model_width = local_in.shape
    padded = local_rows * groups
    token_count = seq_count * local_rows
    my_lengths = lax.dynamic_slice_in_dim(seq_lengths, group_index * seq_count, seq_count, 0)
    query_pos = position_of(
        ctx_index * local_rows + jnp.arange(local_rows, dtype=jnp.int32),
        local_rows,
        piece_rows,
        groups,
    )
    flat_in = local_in.reshape(token_count, model_width).astype(jnp.float32)
    flat_cot = local_cot.reshape(token_count, model_width)
    lowered = (
        w_query.astype(jnp.bfloat16),
        w_key.astype(jnp.bfloat16),
        w_value.astype(jnp.bfloat16),
        w_output.astype(jnp.bfloat16),
        w_up.astype(jnp.bfloat16),
        w_down.astype(jnp.bfloat16),
        attn_gain.astype(jnp.bfloat16),
        mlp_gain.astype(jnp.bfloat16),
        query_scale.astype(jnp.bfloat16),
    )
    gathered = (
        lax.all_gather(lowered[0], ("dp", "ctx"), axis=0, tiled=True),
        lax.all_gather(lowered[1], ("dp", "ctx"), axis=0, tiled=True),
        lax.all_gather(lowered[2], ("dp", "ctx"), axis=0, tiled=True),
        lax.all_gather(lowered[3], ("dp", "ctx"), axis=0, tiled=True),
        lax.all_gather(lowered[4], ("dp", "ctx"), axis=0, tiled=True),
        lax.all_gather(lowered[5], ("dp", "ctx"), axis=0, tiled=True),
        lax.all_gather(lowered[6], ("dp", "ctx"), axis=0, tiled=True),
        lax.all_gather(lowered[7], ("dp", "ctx"), axis=0, tiled=True),
        lax.all_gather(lowered[8], ("dp", "ctx"), axis=0, tiled=True),
    )
    (
        query_full,
        key_full,
        value_full,
        output_full,
        up_full,
        down_full,
        gain_one,
        gain_two,
        scale_raw,
    ) = gathered
    inv_one = lax.rsqrt(jnp.mean(flat_in * flat_in, axis=1, keepdims=True) + 1e-06)
    normed_one = flat_in * inv_one
    hidden_one = (normed_one * gain_one.astype(jnp.float32)).astype(jnp.bfloat16)
    scale_param = scale_raw.astype(jnp.float32)
    query_mult = 1.442695041 / math.sqrt(head_dim) * jax.nn.softplus(scale_param)
    query_pre = jnp.dot(hidden_one, query_full, preferred_element_type=jnp.float32)
    queries = (query_pre * query_mult).astype(jnp.bfloat16)
    keys_local = jnp.dot(hidden_one, key_full, preferred_element_type=jnp.float32).astype(
        jnp.bfloat16
    )
    values_local = jnp.dot(hidden_one, value_full, preferred_element_type=jnp.float32).astype(
        jnp.bfloat16
    )
    four_shape = (seq_count, local_rows, head_count, head_dim)
    query_four = queries.reshape(four_shape)
    keys_three = keys_local.reshape(seq_count, local_rows, model_width)
    values_three = values_local.reshape(seq_count, local_rows, model_width)

    def live_between(row_pos, key_pos):
        allowed = (key_pos[None, None, :] <= row_pos[None, :, None]) & (
            key_pos[None, None, :] < my_lengths[:, None, None]
        )
        return allowed[:, :, None, :]

    def live_mask(key_pos):
        return live_between(query_pos, key_pos)

    def attend_block(state_now, key_block, value_block, first_row):
        run_max, run_sum, run_acc = state_now
        block_len = key_block.shape[1]
        key_pos = position_of(
            first_row + jnp.arange(block_len, dtype=jnp.int32), local_rows, piece_rows, groups
        )
        key_four = key_block.reshape(seq_count, block_len, head_count, head_dim)
        value_four = value_block.reshape(seq_count, block_len, head_count, head_dim)
        scores = jnp.einsum(
            "srhd,skhd->srhk", query_four, key_four, preferred_element_type=jnp.float32
        )
        allowed = live_mask(key_pos)
        masked = jnp.where(allowed, scores, -1e30)
        new_max = jnp.maximum(run_max, jnp.max(masked, axis=3))
        weights_now = jnp.exp(jnp.where(allowed, masked - new_max[..., None], -1e30))
        factor = jnp.exp(run_max - new_max)
        new_sum = run_sum * factor + jnp.sum(weights_now, axis=3)
        added = jnp.einsum(
            "srhk,skhd->srhd",
            weights_now.astype(jnp.bfloat16),
            value_four,
            preferred_element_type=jnp.float32,
        )
        return (new_max, new_sum, run_acc * factor[..., None] + added)

    start_state = (
        jnp.full((seq_count, local_rows, head_count), -1e30, jnp.float32),
        jnp.zeros((seq_count, local_rows, head_count), jnp.float32),
        jnp.zeros(four_shape, jnp.float32),
    )
    key_piece = lax.all_gather(keys_three, "ctx", axis=1, tiled=True)
    value_piece = lax.all_gather(values_three, "ctx", axis=1, tiled=True)
    piece_len = key_piece.shape[1]
    fold_block_len = 512 if piece_len % 512 == 0 else piece_len

    def one_block(state_now, block_index):
        offset = block_index * fold_block_len
        key_block = lax.dynamic_slice_in_dim(key_piece, offset, fold_block_len, 1)
        value_block = lax.dynamic_slice_in_dim(value_piece, offset, fold_block_len, 1)
        return (attend_block(state_now, key_block, value_block, offset), None)

    result_state, unused = lax.scan(
        one_block, start_state, jnp.arange(piece_len // fold_block_len, dtype=jnp.int32)
    )
    run_max, run_sum, run_acc = result_state
    log_total = run_max + jnp.log(run_sum)
    attn_exact = run_acc / run_sum[..., None]
    attended = attn_exact.reshape(token_count, model_width).astype(jnp.bfloat16)
    middle = flat_in + jnp.dot(attended, output_full, preferred_element_type=jnp.float32)
    inv_two = lax.rsqrt(jnp.mean(middle * middle, axis=1, keepdims=True) + 1e-06)
    normed_two = middle * inv_two
    hidden_two = (normed_two * gain_two.astype(jnp.float32)).astype(jnp.bfloat16)
    up_pre = jnp.dot(hidden_two, up_full, preferred_element_type=jnp.float32)
    active = jax.nn.silu(up_pre).astype(jnp.bfloat16)
    result = (middle + jnp.dot(active, down_full, preferred_element_type=jnp.float32)).astype(
        jnp.bfloat16
    )
    back_weights = (
        lax.all_gather(lowered[0], ("dp", "ctx"), axis=0, tiled=True),
        lax.all_gather(lowered[1], ("dp", "ctx"), axis=0, tiled=True),
        lax.all_gather(lowered[2], ("dp", "ctx"), axis=0, tiled=True),
        lax.all_gather(lowered[3], ("dp", "ctx"), axis=0, tiled=True),
        lax.all_gather(lowered[4], ("dp", "ctx"), axis=0, tiled=True),
        lax.all_gather(lowered[5], ("dp", "ctx"), axis=0, tiled=True),
        lax.all_gather(lowered[6], ("dp", "ctx"), axis=0, tiled=True),
        lax.all_gather(lowered[7], ("dp", "ctx"), axis=0, tiled=True),
        lax.all_gather(lowered[8], ("dp", "ctx"), axis=0, tiled=True),
    )
    (
        query_back,
        key_back,
        value_back,
        output_back,
        up_back,
        down_back,
        gain_one_back,
        gain_two_back,
        scale_back,
    ) = back_weights
    cot_wide = flat_cot.astype(jnp.float32)
    grad_down = trans_mult(active, flat_cot)
    grad_active = mult_trans(flat_cot, down_back)
    sigma_up = jax.nn.sigmoid(up_pre)
    grad_up_pre = (grad_active * sigma_up * (1.0 + up_pre * (1.0 - sigma_up))).astype(jnp.bfloat16)
    grad_up = trans_mult(hidden_two, grad_up_pre)
    grad_hidden_two = mult_trans(grad_up_pre, up_back)
    grad_gain_two = jnp.sum(grad_hidden_two * normed_two, axis=0)
    grad_middle = cot_wide + norm_back(
        grad_hidden_two, normed_two, inv_two, gain_two_back.astype(jnp.float32)
    )
    grad_middle_low = grad_middle.astype(jnp.bfloat16)
    grad_output = trans_mult(attended, grad_middle_low)
    grad_attended = mult_trans(grad_middle_low, output_back).astype(jnp.bfloat16)
    grad_att_four = grad_attended.reshape(four_shape)
    delta_rows = jnp.sum(grad_att_four.astype(jnp.float32) * attn_exact, axis=3)
    key_all, value_all = (
        lax.all_gather(keys_three, "ctx", axis=1, tiled=True),
        lax.all_gather(values_three, "ctx", axis=1, tiled=True),
    )
    block_len = min(512, padded)

    def back_block(block_index, state_now):
        grad_query, grad_key_all, grad_value_all = state_now
        offset = block_index * block_len
        key_block = lax.dynamic_slice_in_dim(key_all, offset, block_len, 1).reshape(
            seq_count, block_len, head_count, head_dim
        )
        value_block = lax.dynamic_slice_in_dim(value_all, offset, block_len, 1).reshape(
            seq_count, block_len, head_count, head_dim
        )
        key_pos = position_of(
            offset + jnp.arange(block_len, dtype=jnp.int32), local_rows, piece_rows, groups
        )
        scores = jnp.einsum(
            "srhd,skhd->srhk", query_four, key_block, preferred_element_type=jnp.float32
        )
        probs = jnp.exp(jnp.where(live_mask(key_pos), scores - log_total[..., None], -1e30))
        grad_value_block = jnp.einsum(
            "srhk,srhd->skhd",
            probs.astype(jnp.bfloat16),
            grad_att_four,
            preferred_element_type=jnp.float32,
        )
        grad_probs = jnp.einsum(
            "srhd,skhd->srhk", grad_att_four, value_block, preferred_element_type=jnp.float32
        )
        grad_scores = (probs * (grad_probs - delta_rows[..., None])).astype(jnp.bfloat16)
        grad_query = grad_query + jnp.einsum(
            "srhk,skhd->srhd", grad_scores, key_block, preferred_element_type=jnp.float32
        )
        grad_key_block = jnp.einsum(
            "srhk,srhd->skhd", grad_scores, query_four, preferred_element_type=jnp.float32
        )
        grad_key_all = lax.dynamic_update_slice_in_dim(
            grad_key_all, grad_key_block.reshape(seq_count, block_len, model_width), offset, 1
        )
        grad_value_all = lax.dynamic_update_slice_in_dim(
            grad_value_all, grad_value_block.reshape(seq_count, block_len, model_width), offset, 1
        )
        return (grad_query, grad_key_all, grad_value_all)

    zero_all = jnp.zeros((seq_count, padded, model_width), jnp.float32)
    grad_query, grad_key_all, grad_value_all = lax.fori_loop(
        0, padded // block_len, back_block, (jnp.zeros(four_shape, jnp.float32), zero_all, zero_all)
    )
    grad_key_mine, grad_value_mine = (
        lax.psum_scatter(
            grad_key_all.astype(jnp.bfloat16), "ctx", scatter_dimension=1, tiled=True
        ).astype(jnp.float32),
        lax.psum_scatter(
            grad_value_all.astype(jnp.bfloat16), "ctx", scatter_dimension=1, tiled=True
        ).astype(jnp.float32),
    )
    grad_query_flat = grad_query.reshape(token_count, model_width)
    grad_query_pre = (grad_query_flat * query_mult).astype(jnp.bfloat16)
    grad_scale = (
        1.442695041
        / math.sqrt(head_dim)
        * jax.nn.sigmoid(scale_back.astype(jnp.float32))
        * jnp.sum(grad_query_flat * query_pre, axis=0)
    )
    grad_key_low = grad_key_mine.reshape(token_count, model_width).astype(jnp.bfloat16)
    grad_value_low = grad_value_mine.reshape(token_count, model_width).astype(jnp.bfloat16)
    grad_wq = trans_mult(hidden_one, grad_query_pre)
    grad_wk = trans_mult(hidden_one, grad_key_low)
    grad_wv = trans_mult(hidden_one, grad_value_low)
    grad_hidden_one = (
        mult_trans(grad_query_pre, query_back)
        + mult_trans(grad_key_low, key_back)
        + mult_trans(grad_value_low, value_back)
    )
    grad_gain_one = jnp.sum(grad_hidden_one * normed_one, axis=0)
    grad_in = grad_middle + norm_back(
        grad_hidden_one, normed_one, inv_one, gain_one_back.astype(jnp.float32)
    )
    matrix_stack = jnp.stack([grad_wq, grad_wk, grad_wv, grad_output, grad_up, grad_down], axis=0)
    vector_stack = jnp.stack([grad_gain_one, grad_gain_two, grad_scale], axis=0)
    matrix_sums, vector_sums = (
        lax.psum_scatter(matrix_stack, ("dp", "ctx"), scatter_dimension=1, tiled=True),
        lax.psum_scatter(vector_stack, ("dp", "ctx"), scatter_dimension=1, tiled=True),
    )
    out_local = result.reshape(seq_count, local_rows, model_width)
    grad_local = grad_in.astype(jnp.bfloat16).reshape(seq_count, local_rows, model_width)
    back_out, back_grad = (
        lax.all_to_all(out_local, "dp", split_axis=1, concat_axis=0, tiled=True),
        lax.all_to_all(grad_local, "dp", split_axis=1, concat_axis=0, tiled=True),
    )
    return (
        back_out,
        back_grad,
        matrix_sums[0],
        matrix_sums[1],
        matrix_sums[2],
        matrix_sums[3],
        matrix_sums[4],
        matrix_sums[5],
        vector_sums[0],
        vector_sums[1],
        vector_sums[2],
    )


LOG2E = 1.442695041
CODES = (0, 1, 4, 5)


def plane_shift(value, step):
    if step == 1:
        return lax.ppermute(value, "x", [(0, 1), (1, 0)])
    if step == 2:
        return lax.ppermute(value, "y", [(0, 1), (1, 0)])
    return lax.ppermute(value, ("y", "x"), [(0, 3), (1, 2), (2, 1), (3, 0)])


def core_swap(value):
    return lax.ppermute(value, "core", [(0, 1), (1, 0)])


def ring_shift(value, step):
    return lax.ppermute(value, "z", [(i, (i + step) % 4) for i in range(4)])


def pick(array, index):
    return lax.dynamic_index_in_dim(array, index, 0, keepdims=False)


def by_source(pieces, z_index, axis):
    pieces = [jnp.expand_dims(item, axis) for item in pieces]
    shape = [1] * pieces[0].ndim
    shape[axis] = 4
    hop = ((z_index - jnp.arange(4, dtype=jnp.int32)) % 4).reshape(shape)
    made = pieces[0]
    for k in (1, 2, 3):
        made = jnp.where(hop == k, pieces[k], made)
    return made


def pair(mine, other, index, axis):
    shape = [1] * (mine.ndim + 1)
    shape[axis] = 2
    slot = jnp.arange(2, dtype=jnp.int32).reshape(shape)
    return jnp.where(slot == index, jnp.expand_dims(mine, axis), jnp.expand_dims(other, axis))


def row_positions(shape, dim, plane_index):
    row = lax.broadcasted_iota(jnp.int32, shape, dim)
    chip = (row // 32) % 4
    code = (chip % 2) + 4 * (chip // 2) + 2 * (row // 128)
    return 64 * ((row % 32) // 8) + 8 * (plane_index ^ code) + row % 8


def live_pairs(info_ref, seq):
    shape = (256, 256)
    query_pos = row_positions(shape, 0, info_ref[1])
    key_pos = row_positions(shape, 1, info_ref[1])
    return (key_pos <= query_pos) & (key_pos < info_ref[2 + seq])


def block_rows(near_ref, far_ref):
    return jnp.concatenate([near_ref[...], far_ref[...]], axis=0).reshape(256, near_ref.shape[2])


def soft_probs(query, key, live):
    scores = mult_trans(query, key)
    scores = jnp.where(live, scores, -1e30)
    top = jnp.max(scores, axis=1, keepdims=True)
    weights = jnp.where(live, jnp.exp(scores - top), 0.0)
    return weights / jnp.sum(weights, axis=1, keepdims=True)


def attend_kernel(
    info_ref, near_ref, far_ref, gain_ref, mult_ref, w_ref, pre_ref, att_ref
):
    seq = pl.program_id(0)
    live = live_pairs(info_ref, seq)
    wide = block_rows(near_ref, far_ref).astype(jnp.float32)
    inverse = lax.rsqrt(jnp.mean(wide * wide, axis=1, keepdims=True) + 1e-06)
    hidden = (wide * inverse * gain_ref[...]).astype(jnp.bfloat16)
    pre = jnp.dot(hidden, w_ref[...], preferred_element_type=jnp.float32)
    pre_ref[...] = pre.reshape(2, 4, 32, 480)
    query = (pre[:, 0:160] * mult_ref[...]).astype(jnp.bfloat16)
    key = pre[:, 160:320].astype(jnp.bfloat16)
    value = pre[:, 320:480].astype(jnp.bfloat16)
    heads = []
    for head in range(2):
        part = slice(80 * head, 80 * head + 80)
        probs = soft_probs(query[:, part], key[:, part], live).astype(jnp.bfloat16)
        heads.append(jnp.dot(probs, value[:, part], preferred_element_type=jnp.float32))
    att = jnp.concatenate(heads, axis=1).astype(jnp.bfloat16).reshape(2, 4, 32, 160)
    for chip in range(4):
        for core in range(2):
            att_ref[chip, core] = att[core, chip]


def attend_back_kernel(
    info_ref, near_ref, far_ref, gain_ref, mult_ref, w_ref, pre_ref, grad_near, grad_far, gain_two_ref,
    hid_near, hid_far, send_ref, w_acc, gain_acc, scale_acc, lines,
):
    seq = pl.program_id(0)

    @pl.when(seq == 0)
    def _():
        w_acc[...] = jnp.zeros_like(w_acc)
        gain_acc[...] = jnp.zeros_like(gain_acc)
        scale_acc[...] = jnp.zeros_like(scale_acc)

    live = live_pairs(info_ref, seq)
    wide = block_rows(near_ref, far_ref).astype(jnp.float32)
    inverse = lax.rsqrt(jnp.mean(wide * wide, axis=1, keepdims=True) + 1e-06)
    normed = wide * inverse
    hidden = (normed * gain_ref[...]).astype(jnp.bfloat16)
    pre = pre_ref[...].reshape(256, 480)
    mult = mult_ref[...]
    query = (pre[:, 0:160] * mult).astype(jnp.bfloat16)
    key = pre[:, 160:320].astype(jnp.bfloat16)
    value = pre[:, 320:480].astype(jnp.bfloat16)
    grad_att = jnp.concatenate([grad_near[:, 0], grad_far[:, 0]], axis=0).reshape(256, 160)
    grad_q, grad_k, grad_v = [], [], []
    for head in range(2):
        part = slice(80 * head, 80 * head + 80)
        probs = soft_probs(query[:, part], key[:, part], live)
        grad_probs = mult_trans(grad_att[:, part], value[:, part])
        delta = jnp.sum(probs * grad_probs, axis=1, keepdims=True)
        grad_scores = (probs * (grad_probs - delta)).astype(jnp.bfloat16)
        grad_v.append(trans_mult(probs.astype(jnp.bfloat16), grad_att[:, part]))
        grad_q.append(jnp.dot(grad_scores, key[:, part], preferred_element_type=jnp.float32))
        grad_k.append(trans_mult(grad_scores, query[:, part]))
    grad_query = jnp.concatenate(grad_q, axis=1)
    scale_acc[...] += jnp.sum(grad_query * pre[:, 0:160], axis=0, keepdims=True)
    joined = jnp.concatenate([grad_query * mult] + grad_k + grad_v, axis=1).astype(jnp.bfloat16)
    w_acc[...] += trans_mult(hidden, joined)
    grad_hidden = mult_trans(joined, w_ref[...])
    gain_acc[...] += jnp.sum(grad_hidden * normed, axis=0, keepdims=True)
    low = grad_hidden.astype(jnp.bfloat16).reshape(2, 4, 32, 1280)
    hid_near[...] = low[0]
    hid_far[...] = low[1]

    @pl.when(seq == 3)
    def _():
        lines[...] = jnp.zeros_like(lines)
        for which, source in enumerate((gain_acc, gain_two_ref)):
            for owner in range(32):
                lane = 120 * (owner % 4) + 40 * which
                lines[owner // 4, :, lane : lane + 40] = source[:, 40 * owner : 40 * owner + 40]
        for part in range(4):
            lane = 120 * part + 80
            lines[info_ref[1], :, lane : lane + 40] = scale_acc[:, 40 * part : 40 * part + 40]
        blank = jnp.zeros((14, 480), jnp.float32)
        for target in range(4):
            rows = w_acc[320 * target : 320 * target + 320, :]
            block = jnp.concatenate([rows, lines[2 * target], lines[2 * target + 1], blank], axis=0)
            send_ref[target] = block.astype(jnp.bfloat16)


def feed_kernel(
    info_ref, x_ref, g_ref, atts, far_atts, gain_ref,
    near_rows, across_a, across_b, far_near_rows, far_across_a, far_across_b,
    out_ref, pack_ref, dmid_ref, datt_0, datt_1, datt_2, datt_3, gain_grad,
    weights, sems,
):
    y_index, core_index = info_ref[1] // 4, (info_ref[1] // 2) % 2
    copies = []
    for w in range(3):
        moved = []
        for core, own, others in (
            (core_index, near_rows, (across_a, across_b)),
            (1 - core_index, far_near_rows, (far_across_a, far_across_b)),
        ):
            moved.append((own.at[:, w], weights.at[w, :, y_index, core]))
            for half in range(2):
                moved.append((others[half].at[:, w], weights.at[w, pl.ds(2 * half, 2), 1 - y_index, core]))
        copies.append([pltpu.make_async_copy(*refs, sems.at[w, i]) for i, refs in enumerate(moved)])
    size = x_ref.shape[1]
    for group in copies:
        for copy in group:
            copy.start()
    datts = (datt_0, datt_1, datt_2, datt_3)

    for copy in copies[0]:
        copy.wait()
    heads = [(chip, core, info_ref[1] ^ (CODES[chip] + 2 * core)) for chip in range(4) for core in range(2)]
    middle = x_ref[...].astype(jnp.float32)
    for chip, core, source in heads:
        rows = weights[0, source // 2, source & 1].reshape(160, size)
        middle += jnp.dot((far_atts if core else atts)[chip, core], rows, preferred_element_type=jnp.float32)
    inverse = lax.rsqrt(jnp.mean(middle * middle, axis=1, keepdims=True) + 1e-06)
    normed = middle * inverse
    gain = gain_ref[...]
    hidden = (normed * gain).astype(jnp.bfloat16)
    pack_ref[1] = hidden
    for copy in copies[1]:
        copy.wait()
    up = jnp.dot(hidden, weights[1].reshape(size, size), preferred_element_type=jnp.float32)
    sigma = jax.nn.sigmoid(up)
    active = (up * sigma).astype(jnp.bfloat16)
    pack_ref[0] = active
    for copy in copies[2]:
        copy.wait()
    down = jnp.dot(active, weights[2].reshape(size, size), preferred_element_type=jnp.float32)
    result = middle + down
    for seq in range(4):
        for plane_z in range(4):
            row = 32 * seq + 8 * plane_z
            out_ref[plane_z, seq] = result[row : row + 8].astype(jnp.bfloat16)
    cot = g_ref[...]
    grad_act = mult_trans(cot, weights[2].reshape(size, size))
    grad_up = (grad_act * sigma * (1.0 + up * (1.0 - sigma))).astype(jnp.bfloat16)
    pack_ref[2] = grad_up
    grad_hidden = mult_trans(grad_up, weights[1].reshape(size, size))
    gain_grad[...] = jnp.sum(grad_hidden * normed, axis=0, keepdims=True)
    grad_mid = cot.astype(jnp.float32) + norm_back(grad_hidden, normed, inverse, gain)
    dmid_ref[...] = grad_mid
    low = grad_mid.astype(jnp.bfloat16)
    pack_ref[3] = low
    for chip, core, source in heads:
        rows = weights[0, source // 2, source & 1].reshape(160, size)
        datts[chip][core] = mult_trans(low, rows).astype(jnp.bfloat16)


def grads_kernel(
    info_ref, pack_ref, far_pack, atts, far_atts, cot_ref, far_cot, keep_a, away_a, keep_b, away_b, stage, sems
):
    y_index, core_index, x_index = info_ref[1] // 4, (info_ref[1] // 2) % 2, info_ref[1] % 2

    def leave(w):
        copies = []
        for half in range(2):
            for i in range(2):
                moves = ((stage.at[w, half, i, 1 - x_index], away_a), (stage.at[w, 2 + half, 1 - y_index, i], away_b))
                for j, (block, target) in enumerate(moves):
                    sem = sems.at[w, 4 * half + 2 * i + j]
                    copies.append(pltpu.make_async_copy(block, target.at[half, w, i], sem))
        return copies

    def keep():
        for half in range(2):
            for w in range(3):
                for i in range(2):
                    keep_a[half, w, i] = stage[w, half, i, x_index]
                    keep_b[half, w, i] = stage[w, 2 + half, y_index, i]

    def store(w, made):
        for i in range(16):
            stage[w, i // 4, (i // 2) % 2, i % 2] = made[40 * i : 40 * i + 40].astype(jnp.bfloat16)

    def both(near, far):
        return jnp.concatenate([near, far], axis=0)

    cots = both(cot_ref[...], far_cot[...])
    for core in range(2):

        @pl.when(core_index == core)
        def _():
            def own_columns(near, far):
                return both(*(
                    jnp.concatenate([ref[:, 160 * i + 80 * core : 160 * i + 80 * core + 80] for i in range(8)], axis=1)
                    for ref in (near, far)
                ))

            acts = own_columns(pack_ref.at[0], far_pack.at[0])
            store(2, trans_mult(acts, cots))
            for copy in leave(2):
                copy.start()
            acts = own_columns(pack_ref.at[1], far_pack.at[1])
            store(1, trans_mult(acts, both(pack_ref[2], far_pack[2])))
            for copy in leave(1):
                copy.start()
            grads = both(pack_ref[3], far_pack[3])
            pieces = []
            for chip in range(4):
                for source in range(2):
                    near, far = (far_atts, far_atts) if source else (atts, atts)
                    pieces.append(both(near[chip, source], far[chip, 1 - source])[:, 80 * core : 80 * core + 80])
            made = trans_mult(jnp.concatenate(pieces, axis=1), grads)
            for i in range(8):
                source = info_ref[1] ^ (CODES[i // 2] + 2 * (i % 2))
                for part in range(2):
                    row = 80 * i + 40 * part
                    stage[0, source // 2, source & 1, part] = made[row : row + 40].astype(jnp.bfloat16)
            for copy in leave(0):
                copy.start()

    keep()
    for w in range(3):
        for copy in leave(w):
            copy.wait()


def meet_kernel(far_side, info_ref, mine_a, from_a, mine_b, from_b, out_a, out_b):
    y_index, x_index = info_ref[1] // 4, info_ref[1] % 2
    if far_side:
        y_index, x_index = 1 - y_index, 1 - x_index
    for half in range(2):
        for w in range(3):
            out_a[half, w] = sum_low(mine_a[half, w, y_index], from_a[half, w, y_index])
            out_b[half, w] = sum_low(mine_b[half, w, x_index], from_b[half, w, x_index])


def join_kernel(keep_a, from_a, keep_b, from_b, out_ref):
    for half in range(2):
        for w in range(3):
            out_ref[half, w] = sum_low(keep_a[half, w], from_a[half, w])
            out_ref[2 + half, w] = sum_low(keep_b[half, w], from_b[half, w])


def sum_low(left, right):
    return (left.astype(jnp.float32) + right.astype(jnp.float32)).astype(jnp.bfloat16)


def norm_kernel(info_ref, hid_0, hid_1, hid_2, hid_3, x_ref, dmid_ref, gain_ref, out_0, out_1, out_2, out_3, rows):
    grad = hid_0[...].astype(jnp.float32)
    for item in (hid_1, hid_2, hid_3):
        grad += item[...].astype(jnp.float32)
    wide = x_ref[...].astype(jnp.float32)
    inverse = lax.rsqrt(jnp.mean(wide * wide, axis=1, keepdims=True) + 1e-06)
    grad = dmid_ref[...] + norm_back(grad, wide * inverse, inverse, gain_ref[...])
    for seq in range(4):
        for plane_z in range(4):
            row = 32 * seq + 8 * plane_z
            rows[plane_z, seq] = grad[row : row + 8]
    for hop, out in enumerate((out_0, out_1, out_2, out_3)):
        out[...] = rows[(info_ref[0] + hop) & 3].astype(jnp.bfloat16)


def fold_kernel(in_ref, out_ref, line):
    total = in_ref[0].astype(jnp.float32)
    line[...] = jnp.zeros_like(line)
    for owner in range(8):
        lane = 120 * (owner % 4)
        line[0:1, 0:120] = total[320 + owner // 4 : 321 + owner // 4, lane : lane + 120]
        block = jnp.concatenate([total[40 * owner : 40 * owner + 40], line[...]], axis=0)
        out_ref[owner] = block.astype(jnp.bfloat16)


def spread_kernel(in_ref, *outs):
    for which, out in enumerate(outs):
        for owner in range(8):
            part = in_ref[owner, 0:40, 160 * which : 160 * which + 160]
            out[:, 160 * owner : 160 * owner + 160] = part.astype(jnp.float32)


def widen_kernel(in_ref, *outs):
    for which, out in enumerate(outs):
        out[...] = in_ref[which].astype(jnp.float32)


def whole(shape):
    return pl.BlockSpec(shape, lambda *_: (0,) * len(shape))


def seq_block(*lead, width):
    count = len(lead)
    return pl.BlockSpec((*lead, 32, width), lambda s, info: (*(0,) * count, s, 0))


def planes(
    inputs, cotangent, w_query, w_key, w_value, w_output, w_up, w_down,
    attn_gain, mlp_gain, query_scale, deal, lengths,
):
    f32, bf16 = jnp.float32, jnp.bfloat16
    z, y, c, x = (lax.axis_index(name) for name in ("z", "y", "core", "x"))
    plane = 4 * y + 2 * c + x
    width = 1280
    seqs = jnp.arange(16, dtype=jnp.int32)
    seq_lengths = jnp.sum(jnp.where(deal[None, :] == seqs[:, None], lengths[None, :], 0), axis=1)
    my_lengths = lax.dynamic_slice_in_dim(seq_lengths, 4 * z, 4, 0)
    info = jnp.concatenate([jnp.stack([z, plane]), my_lengths]).astype(jnp.int32)

    vec = jnp.concatenate([attn_gain, mlp_gain, query_scale]).astype(bf16)
    vec_block = jnp.zeros((1, 8, width), bf16).at[0, 0, :120].set(vec)
    in_four = inputs.reshape(4, 4, 8, width)
    sent = [jnp.concatenate([pick(in_four, (z + k) % 4), vec_block]) for k in range(4)]
    qkv = jnp.stack([w_query, w_key, w_value]).astype(bf16)
    *sent, qkv = lax.optimization_barrier((*sent, qkv))
    got = [sent[0]] + [ring_shift(sent[k], k) for k in (1, 2, 3)]
    x_rows = by_source([item[:4] for item in got], z, 1).reshape(128, width)
    vec_rows = by_source([item[4, 0] for item in got], z, 0)
    vec_rows = jnp.concatenate([vec_rows, jnp.zeros((4, width), bf16)])
    own = jnp.concatenate([x_rows, vec_rows])

    big = jnp.stack([w_output, w_up, w_down]).astype(bf16)
    big = lax.all_gather(big, "z", axis=0)

    qkv = qkv.reshape(3, 40, 8, 160).transpose(2, 1, 0, 3).reshape(8, 40, 480)
    qkv = lax.all_to_all(qkv, ("y", "core", "x"), split_axis=0, concat_axis=0, tiled=True)
    near = jnp.stack([own] + [plane_shift(own, step) for step in (1, 2, 3)])
    big, near, cotangent, qkv = lax.optimization_barrier((big, near, cotangent, qkv.reshape(320, 480)))
    w_qkv = lax.all_gather(qkv, "z", axis=0, tiled=True)
    far = core_swap(near)
    beside, across = plane_shift(big, 1), plane_shift(big, 2)
    relay_a, relay_b = beside[:2], across[2:]
    cot_rows = lax.all_to_all(cotangent.reshape(4, 4, 8, width), "z", split_axis=0, concat_axis=0, tiled=True)
    relay_a, relay_b, cot_rows = lax.optimization_barrier((relay_a, relay_b, cot_rows))
    across_a, across_b = plane_shift(relay_a, 2), plane_shift(relay_b, 1)

    vecs = jnp.stack([near[:, 128:132, :120], far[:, 128:132, :120]])
    vecs = vecs.astype(f32).reshape(2, 2, 2, 4, 120)
    vecs = jnp.where(c == 0, vecs, vecs[::-1])
    vecs = jnp.where(y == 0, vecs, vecs[:, ::-1])
    vecs = jnp.where(x == 0, vecs, vecs[:, :, ::-1])
    vecs = vecs.reshape(2, 2, 2, 4, 3, 40).transpose(4, 3, 1, 0, 2, 5).reshape(3, width)
    gain_one, gain_two = vecs[0:1], vecs[1:2]
    my_scale = lax.dynamic_slice_in_dim(vecs[2:3], 160 * plane, 160, 1)
    query_mult = LOG2E / math.sqrt(HD) * jax.nn.softplus(my_scale)


    def limit(megabytes):
        return pltpu.CompilerParams(vmem_limit_bytes=megabytes * 1024 * 1024)

    pre, att_made = pl.pallas_call(
        attend_kernel,
        grid_spec=pltpu.PrefetchScalarGridSpec(
            num_scalar_prefetch=1,
            grid=(4,),
            in_specs=[
                seq_block(4, width=width), seq_block(4, width=width),
                whole((1, width)), whole((1, 160)), whole((width, 480)),
            ],
            out_specs=[seq_block(2, 4, width=480), seq_block(4, 2, width=160)],
        ),
        out_shape=[
            jax.ShapeDtypeStruct((2, 4, 128, 480), f32),
            jax.ShapeDtypeStruct((4, 2, 128, 160), bf16),
        ],
        compiler_params=limit(14),
        cost_estimate=pl.CostEstimate(flops=9_000_000_000, bytes_accessed=8_000_000, transcendentals=600_000),
        name="attend",
    )(info, near, far, gain_one, query_mult, w_qkv)

    near_rows = pair(big, beside, x, 2).reshape(4, 3, 80, width)
    att_made, near_rows, across_a, across_b = lax.optimization_barrier((att_made, near_rows, across_a, across_b))
    far_near_rows = core_swap(near_rows)
    atts = [att_made[0]] + [plane_shift(att_made[step], step) for step in (1, 2, 3)]
    atts = jnp.stack(atts)
    far_atts = core_swap(atts)
    across_a = pair(across[:2], across_a, x, 2).reshape(2, 3, 80, width)
    across_b = pair(across[2:], across_b, x, 2).reshape(2, 3, 80, width)
    far_across_a, far_across_b = core_swap(across_a), core_swap(across_b)
    cot_rows = cot_rows.transpose(1, 0, 2, 3).reshape(128, width)
    far_cot = core_swap(cot_rows)
    far_cot, far_atts, cot_rows = lax.optimization_barrier((far_cot, far_atts, cot_rows))
    datt_shape = jax.ShapeDtypeStruct((2, 128, 160), bf16)
    smem = pl.BlockSpec(memory_space=pltpu.SMEM)
    vmem = pl.BlockSpec(memory_space=pltpu.VMEM)
    hbm = pl.BlockSpec(memory_space=pltpu.HBM)
    out_rows, pack, grad_mid, *datts, gain_two_grad = pl.pallas_call(
        feed_kernel,
        in_specs=[smem] + [vmem] * 5 + [hbm] * 6,
        out_specs=[vmem] * 8,
        out_shape=[
            jax.ShapeDtypeStruct((4, 4, 8, width), bf16),
            jax.ShapeDtypeStruct((4, 128, width), bf16),
            jax.ShapeDtypeStruct((128, width), f32),
        ]
        + [datt_shape] * 4
        + [jax.ShapeDtypeStruct((1, width), f32)],
        scratch_shapes=[pltpu.VMEM((3, 4, 2, 2, 80, width), bf16), pltpu.SemaphoreType.DMA((3, 6))],
        compiler_params=limit(36),
        cost_estimate=pl.CostEstimate(flops=12_000_000_000, bytes_accessed=13_000_000, transcendentals=200_000),
        name="feed",
    )(info, x_rows, cot_rows, atts, far_atts, gain_two, near_rows, across_a, across_b, far_near_rows, far_across_a, far_across_b)

    back = [datts[0]] + [plane_shift(datts[step], step) for step in (1, 2, 3)]

    mine_a, away_a, mine_b, away_b = pl.pallas_call(
        grads_kernel,
        in_specs=[smem] + [vmem] * 6,
        out_specs=[vmem, hbm, vmem, hbm],
        out_shape=[jax.ShapeDtypeStruct((2, 3, 2, 40, width), bf16)] * 4,
        scratch_shapes=[pltpu.VMEM((3, 4, 2, 2, 40, width), bf16), pltpu.SemaphoreType.DMA((3, 8))],
        compiler_params=limit(22),
        cost_estimate=pl.CostEstimate(flops=6_000_000_000, bytes_accessed=8_000_000, transcendentals=0),
        name="grads",
    )(info, pack, core_swap(pack), atts, far_atts, cot_rows, far_cot)

    mine_a, away_a, mine_b, away_b, *back = lax.optimization_barrier((mine_a, away_a, mine_b, away_b, *back))
    away_a, away_b, grad_atts = lax.optimization_barrier((away_a, away_b, jnp.stack(back)))
    from_a, from_b = plane_shift(away_a, 1), plane_shift(away_b, 2)
    hid_near, hid_far, send = pl.pallas_call(
        attend_back_kernel,
        grid_spec=pltpu.PrefetchScalarGridSpec(
            num_scalar_prefetch=1,
            grid=(4,),
            in_specs=[
                seq_block(4, width=width), seq_block(4, width=width),
                whole((1, width)), whole((1, 160)), whole((width, 480)),
                seq_block(2, 4, width=480),
                *[pl.BlockSpec((4, 1, 32, 160), lambda s, info, core=core: (0, core, s, 0)) for core in range(2)],
                whole((1, width)),
            ],
            out_specs=[
                seq_block(4, width=width), seq_block(4, width=width),
                whole((4, 336, 480)),
            ],
            scratch_shapes=[
                pltpu.VMEM((width, 480), f32), pltpu.VMEM((1, width), f32),
                pltpu.VMEM((1, 160), f32), pltpu.VMEM((8, 1, 480), f32),
            ],
        ),
        out_shape=[
            jax.ShapeDtypeStruct((4, 128, width), bf16),
            jax.ShapeDtypeStruct((4, 128, width), bf16),
            jax.ShapeDtypeStruct((4, 336, 480), bf16),
        ],
        compiler_params=limit(22),
        cost_estimate=pl.CostEstimate(flops=15_000_000_000, bytes_accessed=12_000_000, transcendentals=600_000),
        name="attend_back",
    )(info, near, far, gain_one, query_mult, w_qkv, pre, grad_atts, core_swap(grad_atts), gain_two_grad)

    send, out_rows = lax.optimization_barrier((send, out_rows))
    sums = lax.psum_scatter(send, "z", scatter_dimension=0, tiled=True)
    out_sent = [pick(out_rows, (z + k) % 4) for k in range(4)]
    out_one, out_three = ring_shift(out_sent[1], 1), ring_shift(out_sent[3], 3)
    from_a, from_b, hid_far, out_one, out_three = lax.optimization_barrier(
        (from_a, from_b, hid_far, out_one, out_three)
    )
    swapped = core_swap(hid_far)
    hid = [sum_low(hid_near[i], swapped[i]) for i in range(4)]
    outputs = by_source([out_sent[0], out_one, ring_shift(out_sent[2], 2), out_three], z, 0).reshape(16, 8, width)
    def meet(far_side, *parts):
        return pl.pallas_call(
            functools.partial(meet_kernel, far_side),
            in_specs=[smem] + [vmem] * 4,
            out_specs=[vmem] * 2,
            out_shape=[jax.ShapeDtypeStruct((2, 3, 40, width), bf16)] * 2,
            compiler_params=limit(50),
            cost_estimate=pl.CostEstimate(flops=2_000_000_000, bytes_accessed=4_000_000, transcendentals=0),
            name="meet",
        )(info, *parts)

    parts = mine_a, from_a, mine_b, from_b
    away_a, away_b = meet(True, *parts)
    keep_a, keep_b = meet(False, *parts)
    from_a, from_b = plane_shift(away_a, 2), plane_shift(away_b, 1)
    *hid, from_a, from_b, outputs = lax.optimization_barrier((*hid, from_a, from_b, outputs))
    kept = pl.pallas_call(
        join_kernel,
        in_specs=[vmem] * 4,
        out_specs=vmem,
        out_shape=jax.ShapeDtypeStruct((4, 3, 40, width), bf16),
        compiler_params=limit(50),
        cost_estimate=pl.CostEstimate(flops=2_000_000_000, bytes_accessed=4_000_000, transcendentals=0),
        name="join",
    )(keep_a, from_a, keep_b, from_b)
    moved = [plane_shift(hid[step], step) for step in (1, 2, 3)]
    moved[0], sums = lax.optimization_barrier((moved[0], sums))
    big_sums = lax.psum_scatter(kept, "z", scatter_dimension=0, tiled=True)[0]
    grad_home = pl.pallas_call(
        norm_kernel,
        in_specs=[smem] + [vmem] * 7,
        out_specs=[vmem] * 4,
        out_shape=[jax.ShapeDtypeStruct((4, 8, width), bf16)] * 4,
        scratch_shapes=[pltpu.VMEM((4, 4, 8, width), f32)],
        compiler_params=limit(10),
        cost_estimate=pl.CostEstimate(flops=2_000_000_000, bytes_accessed=2_500_000, transcendentals=128),
        name="norm",
    )(info, hid[0], *moved, x_rows, grad_mid, gain_one)
    sums = pl.pallas_call(
        fold_kernel,
        in_specs=[vmem],
        out_specs=vmem,
        out_shape=jax.ShapeDtypeStruct((8, 48, 480), bf16),
        scratch_shapes=[pltpu.VMEM((8, 480), f32)],
        compiler_params=limit(8),
        cost_estimate=pl.CostEstimate(flops=2_000_000_000, bytes_accessed=1_600_000, transcendentals=0),
        name="fold",
    )(sums)
    sums = lax.all_to_all(sums, ("y", "core", "x"), split_axis=0, concat_axis=0, tiled=True)
    rows_shape = [jax.ShapeDtypeStruct((40, width), f32)] * 3
    qkv_sums = pl.pallas_call(
        spread_kernel, in_specs=[vmem], out_specs=[vmem] * 3, out_shape=rows_shape, compiler_params=limit(6), name="spread"
    )(sums)
    big_sums = pl.pallas_call(
        widen_kernel, in_specs=[vmem], out_specs=[vmem] * 3, out_shape=rows_shape, compiler_params=limit(6), name="widen"
    )(big_sums)
    line_sums = jnp.sum(sums[:, 40, :120].astype(f32), axis=0).reshape(3, 40)
    scale_low = query_scale.astype(bf16).astype(f32)
    scale_sum = LOG2E / math.sqrt(HD) * jax.nn.sigmoid(scale_low) * line_sums[2]
    grad_home = [grad_home[0]] + [ring_shift(grad_home[k], k) for k in (1, 2, 3)]
    grad_home = by_source(grad_home, z, 0).reshape(16, 8, width)

    return (
        outputs, grad_home, qkv_sums[0], qkv_sums[1], qkv_sums[2],
        big_sums[0], big_sums[1], big_sums[2], line_sums[0], line_sums[1], scale_sum,
    )


def solution(mesh):
    names = ("dp", "ctx")
    body = per_device
    if dict(mesh.shape) == {"dp": 16, "ctx": 2}:
        mesh = Mesh(mesh.devices.reshape(4, 2, 2, 2), ("z", "y", "core", "x"))
        names = mesh.axis_names
        body = planes
    seq, mat, line = P(None, names, None), P(names, None), P(names)
    return jax.shard_map(
        body,
        mesh=mesh,
        in_specs=(seq,) * 2 + (mat,) * 6 + (line,) * 3 + (P(), P()),
        out_specs=(seq,) * 2 + (mat,) * 6 + (line,) * 3,
        check_vma=False,
    )
```

```python
import functools
import math

import jax
import jax.numpy as jnp
from jax import lax
from jax.experimental import pallas as pl
from jax.experimental.pallas import tpu as pltpu
from jax.sharding import Mesh, PartitionSpec as P

H = 16
HD = 80


def mult_trans(left, right):
    return lax.dot_general(
        left, right, (((1,), (1,)), ((), ())), preferred_element_type=jnp.float32
    )


def trans_mult(left, right):
    return lax.dot_general(
        left, right, (((0,), (0,)), ((), ())), preferred_element_type=jnp.float32
    )


def position_of(index, local_rows, piece_rows, groups):
    column = index // local_rows
    within = index % local_rows
    return (within // piece_rows * groups + column) * piece_rows + within % piece_rows


def norm_back(grad_hidden, normed, inverse, gain_value):
    grad_normed = grad_hidden * gain_value
    return inverse * (grad_normed - normed * jnp.mean(grad_normed * normed, axis=1, keepdims=True))


def per_device(
    inputs,
    cotangent,
    w_query,
    w_key,
    w_value,
    w_output,
    w_up,
    w_down,
    attn_gain,
    mlp_gain,
    query_scale,
    deal,
    lengths,
):
    groups = lax.axis_size("ctx")
    group_index = lax.axis_index("dp")
    ctx_index = lax.axis_index("ctx")
    head_count = H
    head_dim = HD
    piece_rows = inputs.shape[1]
    seq_numbers = jnp.arange(inputs.shape[0], dtype=jnp.int32)
    seq_lengths = jnp.sum(
        jnp.where(deal[None, :] == seq_numbers[:, None], lengths[None, :], 0), axis=1
    )
    local_in, local_cot = (
        lax.all_to_all(inputs, "dp", split_axis=0, concat_axis=1, tiled=True),
        lax.all_to_all(cotangent, "dp", split_axis=0, concat_axis=1, tiled=True),
    )
    seq_count, local_rows, model_width = local_in.shape
    padded = local_rows * groups
    token_count = seq_count * local_rows
    my_lengths = lax.dynamic_slice_in_dim(seq_lengths, group_index * seq_count, seq_count, 0)
    query_pos = position_of(
        ctx_index * local_rows + jnp.arange(local_rows, dtype=jnp.int32),
        local_rows,
        piece_rows,
        groups,
    )
    flat_in = local_in.reshape(token_count, model_width).astype(jnp.float32)
    flat_cot = local_cot.reshape(token_count, model_width)
    lowered = (
        w_query.astype(jnp.bfloat16),
        w_key.astype(jnp.bfloat16),
        w_value.astype(jnp.bfloat16),
        w_output.astype(jnp.bfloat16),
        w_up.astype(jnp.bfloat16),
        w_down.astype(jnp.bfloat16),
        attn_gain.astype(jnp.bfloat16),
        mlp_gain.astype(jnp.bfloat16),
        query_scale.astype(jnp.bfloat16),
    )
    gathered = (
        lax.all_gather(lowered[0], ("dp", "ctx"), axis=0, tiled=True),
        lax.all_gather(lowered[1], ("dp", "ctx"), axis=0, tiled=True),
        lax.all_gather(lowered[2], ("dp", "ctx"), axis=0, tiled=True),
        lax.all_gather(lowered[3], ("dp", "ctx"), axis=0, tiled=True),
        lax.all_gather(lowered[4], ("dp", "ctx"), axis=0, tiled=True),
        lax.all_gather(lowered[5], ("dp", "ctx"), axis=0, tiled=True),
        lax.all_gather(lowered[6], ("dp", "ctx"), axis=0, tiled=True),
        lax.all_gather(lowered[7], ("dp", "ctx"), axis=0, tiled=True),
        lax.all_gather(lowered[8], ("dp", "ctx"), axis=0, tiled=True),
    )
    (
        query_full,
        key_full,
        value_full,
        output_full,
        up_full,
        down_full,
        gain_one,
        gain_two,
        scale_raw,
    ) = gathered
    inv_one = lax.rsqrt(jnp.mean(flat_in * flat_in, axis=1, keepdims=True) + 1e-06)
    normed_one = flat_in * inv_one
    hidden_one = (normed_one * gain_one.astype(jnp.float32)).astype(jnp.bfloat16)
    scale_param = scale_raw.astype(jnp.float32)
    query_mult = 1.442695041 / math.sqrt(head_dim) * jax.nn.softplus(scale_param)
    query_pre = jnp.dot(hidden_one, query_full, preferred_element_type=jnp.float32)
    queries = (query_pre * query_mult).astype(jnp.bfloat16)
    keys_local = jnp.dot(hidden_one, key_full, preferred_element_type=jnp.float32).astype(
        jnp.bfloat16
    )
    values_local = jnp.dot(hidden_one, value_full, preferred_element_type=jnp.float32).astype(
        jnp.bfloat16
    )
    four_shape = (seq_count, local_rows, head_count, head_dim)
    query_four = queries.reshape(four_shape)
    keys_three = keys_local.reshape(seq_count, local_rows, model_width)
    values_three = values_local.reshape(seq_count, local_rows, model_width)

    def live_between(row_pos, key_pos):
        allowed = (key_pos[None, None, :] <= row_pos[None, :, None]) & (
            key_pos[None, None, :] < my_lengths[:, None, None]
        )
        return allowed[:, :, None, :]

    def live_mask(key_pos):
        return live_between(query_pos, key_pos)

    def attend_block(state_now, key_block, value_block, first_row):
        run_max, run_sum, run_acc = state_now
        block_len = key_block.shape[1]
        key_pos = position_of(
            first_row + jnp.arange(block_len, dtype=jnp.int32), local_rows, piece_rows, groups
        )
        key_four = key_block.reshape(seq_count, block_len, head_count, head_dim)
        value_four = value_block.reshape(seq_count, block_len, head_count, head_dim)
        scores = jnp.einsum(
            "srhd,skhd->srhk", query_four, key_four, preferred_element_type=jnp.float32
        )
        allowed = live_mask(key_pos)
        masked = jnp.where(allowed, scores, -1e30)
        new_max = jnp.maximum(run_max, jnp.max(masked, axis=3))
        weights_now = jnp.exp(jnp.where(allowed, masked - new_max[..., None], -1e30))
        factor = jnp.exp(run_max - new_max)
        new_sum = run_sum * factor + jnp.sum(weights_now, axis=3)
        added = jnp.einsum(
            "srhk,skhd->srhd",
            weights_now.astype(jnp.bfloat16),
            value_four,
            preferred_element_type=jnp.float32,
        )
        return (new_max, new_sum, run_acc * factor[..., None] + added)

    start_state = (
        jnp.full((seq_count, local_rows, head_count), -1e30, jnp.float32),
        jnp.zeros((seq_count, local_rows, head_count), jnp.float32),
        jnp.zeros(four_shape, jnp.float32),
    )
    key_piece = lax.all_gather(keys_three, "ctx", axis=1, tiled=True)
    value_piece = lax.all_gather(values_three, "ctx", axis=1, tiled=True)
    piece_len = key_piece.shape[1]
    fold_block_len = 512 if piece_len % 512 == 0 else piece_len

    def one_block(state_now, block_index):
        offset = block_index * fold_block_len
        key_block = lax.dynamic_slice_in_dim(key_piece, offset, fold_block_len, 1)
        value_block = lax.dynamic_slice_in_dim(value_piece, offset, fold_block_len, 1)
        return (attend_block(state_now, key_block, value_block, offset), None)

    result_state, unused = lax.scan(
        one_block, start_state, jnp.arange(piece_len // fold_block_len, dtype=jnp.int32)
    )
    run_max, run_sum, run_acc = result_state
    log_total = run_max + jnp.log(run_sum)
    attn_exact = run_acc / run_sum[..., None]
    attended = attn_exact.reshape(token_count, model_width).astype(jnp.bfloat16)
    middle = flat_in + jnp.dot(attended, output_full, preferred_element_type=jnp.float32)
    inv_two = lax.rsqrt(jnp.mean(middle * middle, axis=1, keepdims=True) + 1e-06)
    normed_two = middle * inv_two
    hidden_two = (normed_two * gain_two.astype(jnp.float32)).astype(jnp.bfloat16)
    up_pre = jnp.dot(hidden_two, up_full, preferred_element_type=jnp.float32)
    active = jax.nn.silu(up_pre).astype(jnp.bfloat16)
    result = (middle + jnp.dot(active, down_full, preferred_element_type=jnp.float32)).astype(
        jnp.bfloat16
    )
    back_weights = (
        lax.all_gather(lowered[0], ("dp", "ctx"), axis=0, tiled=True),
        lax.all_gather(lowered[1], ("dp", "ctx"), axis=0, tiled=True),
        lax.all_gather(lowered[2], ("dp", "ctx"), axis=0, tiled=True),
        lax.all_gather(lowered[3], ("dp", "ctx"), axis=0, tiled=True),
        lax.all_gather(lowered[4], ("dp", "ctx"), axis=0, tiled=True),
        lax.all_gather(lowered[5], ("dp", "ctx"), axis=0, tiled=True),
        lax.all_gather(lowered[6], ("dp", "ctx"), axis=0, tiled=True),
        lax.all_gather(lowered[7], ("dp", "ctx"), axis=0, tiled=True),
        lax.all_gather(lowered[8], ("dp", "ctx"), axis=0, tiled=True),
    )
    (
        query_back,
        key_back,
        value_back,
        output_back,
        up_back,
        down_back,
        gain_one_back,
        gain_two_back,
        scale_back,
    ) = back_weights
    cot_wide = flat_cot.astype(jnp.float32)
    grad_down = trans_mult(active, flat_cot)
    grad_active = mult_trans(flat_cot, down_back)
    sigma_up = jax.nn.sigmoid(up_pre)
    grad_up_pre = (grad_active * sigma_up * (1.0 + up_pre * (1.0 - sigma_up))).astype(jnp.bfloat16)
    grad_up = trans_mult(hidden_two, grad_up_pre)
    grad_hidden_two = mult_trans(grad_up_pre, up_back)
    grad_gain_two = jnp.sum(grad_hidden_two * normed_two, axis=0)
    grad_middle = cot_wide + norm_back(
        grad_hidden_two, normed_two, inv_two, gain_two_back.astype(jnp.float32)
    )
    grad_middle_low = grad_middle.astype(jnp.bfloat16)
    grad_output = trans_mult(attended, grad_middle_low)
    grad_attended = mult_trans(grad_middle_low, output_back).astype(jnp.bfloat16)
    grad_att_four = grad_attended.reshape(four_shape)
    delta_rows = jnp.sum(grad_att_four.astype(jnp.float32) * attn_exact, axis=3)
    key_all, value_all = (
        lax.all_gather(keys_three, "ctx", axis=1, tiled=True),
        lax.all_gather(values_three, "ctx", axis=1, tiled=True),
    )
    block_len = min(512, padded)

    def back_block(block_index, state_now):
        grad_query, grad_key_all, grad_value_all = state_now
        offset = block_index * block_len
        key_block = lax.dynamic_slice_in_dim(key_all, offset, block_len, 1).reshape(
            seq_count, block_len, head_count, head_dim
        )
        value_block = lax.dynamic_slice_in_dim(value_all, offset, block_len, 1).reshape(
            seq_count, block_len, head_count, head_dim
        )
        key_pos = position_of(
            offset + jnp.arange(block_len, dtype=jnp.int32), local_rows, piece_rows, groups
        )
        scores = jnp.einsum(
            "srhd,skhd->srhk", query_four, key_block, preferred_element_type=jnp.float32
        )
        probs = jnp.exp(jnp.where(live_mask(key_pos), scores - log_total[..., None], -1e30))
        grad_value_block = jnp.einsum(
            "srhk,srhd->skhd",
            probs.astype(jnp.bfloat16),
            grad_att_four,
            preferred_element_type=jnp.float32,
        )
        grad_probs = jnp.einsum(
            "srhd,skhd->srhk", grad_att_four, value_block, preferred_element_type=jnp.float32
        )
        grad_scores = (probs * (grad_probs - delta_rows[..., None])).astype(jnp.bfloat16)
        grad_query = grad_query + jnp.einsum(
            "srhk,skhd->srhd", grad_scores, key_block, preferred_element_type=jnp.float32
        )
        grad_key_block = jnp.einsum(
            "srhk,srhd->skhd", grad_scores, query_four, preferred_element_type=jnp.float32
        )
        grad_key_all = lax.dynamic_update_slice_in_dim(
            grad_key_all, grad_key_block.reshape(seq_count, block_len, model_width), offset, 1
        )
        grad_value_all = lax.dynamic_update_slice_in_dim(
            grad_value_all, grad_value_block.reshape(seq_count, block_len, model_width), offset, 1
        )
        return (grad_query, grad_key_all, grad_value_all)

    zero_all = jnp.zeros((seq_count, padded, model_width), jnp.float32)
    grad_query, grad_key_all, grad_value_all = lax.fori_loop(
        0, padded // block_len, back_block, (jnp.zeros(four_shape, jnp.float32), zero_all, zero_all)
    )
    grad_key_mine, grad_value_mine = (
        lax.psum_scatter(
            grad_key_all.astype(jnp.bfloat16), "ctx", scatter_dimension=1, tiled=True
        ).astype(jnp.float32),
        lax.psum_scatter(
            grad_value_all.astype(jnp.bfloat16), "ctx", scatter_dimension=1, tiled=True
        ).astype(jnp.float32),
    )
    grad_query_flat = grad_query.reshape(token_count, model_width)
    grad_query_pre = (grad_query_flat * query_mult).astype(jnp.bfloat16)
    grad_scale = (
        1.442695041
        / math.sqrt(head_dim)
        * jax.nn.sigmoid(scale_back.astype(jnp.float32))
        * jnp.sum(grad_query_flat * query_pre, axis=0)
    )
    grad_key_low = grad_key_mine.reshape(token_count, model_width).astype(jnp.bfloat16)
    grad_value_low = grad_value_mine.reshape(token_count, model_width).astype(jnp.bfloat16)
    grad_wq = trans_mult(hidden_one, grad_query_pre)
    grad_wk = trans_mult(hidden_one, grad_key_low)
    grad_wv = trans_mult(hidden_one, grad_value_low)
    grad_hidden_one = (
        mult_trans(grad_query_pre, query_back)
        + mult_trans(grad_key_low, key_back)
        + mult_trans(grad_value_low, value_back)
    )
    grad_gain_one = jnp.sum(grad_hidden_one * normed_one, axis=0)
    grad_in = grad_middle + norm_back(
        grad_hidden_one, normed_one, inv_one, gain_one_back.astype(jnp.float32)
    )
    matrix_stack = jnp.stack([grad_wq, grad_wk, grad_wv, grad_output, grad_up, grad_down], axis=0)
    vector_stack = jnp.stack([grad_gain_one, grad_gain_two, grad_scale], axis=0)
    matrix_sums, vector_sums = (
        lax.psum_scatter(matrix_stack, ("dp", "ctx"), scatter_dimension=1, tiled=True),
        lax.psum_scatter(vector_stack, ("dp", "ctx"), scatter_dimension=1, tiled=True),
    )
    out_local = result.reshape(seq_count, local_rows, model_width)
    grad_local = grad_in.astype(jnp.bfloat16).reshape(seq_count, local_rows, model_width)
    back_out, back_grad = (
        lax.all_to_all(out_local, "dp", split_axis=1, concat_axis=0, tiled=True),
        lax.all_to_all(grad_local, "dp", split_axis=1, concat_axis=0, tiled=True),
    )
    return (
        back_out,
        back_grad,
        matrix_sums[0],
        matrix_sums[1],
        matrix_sums[2],
        matrix_sums[3],
        matrix_sums[4],
        matrix_sums[5],
        vector_sums[0],
        vector_sums[1],
        vector_sums[2],
    )


LOG2E = 1.442695041
CODES = (0, 1, 4, 5)


def plane_shift(value, step):
    if step == 1:
        return lax.ppermute(value, "x", [(0, 1), (1, 0)])
    if step == 2:
        return lax.ppermute(value, "y", [(0, 1), (1, 0)])
    return lax.ppermute(value, ("y", "x"), [(0, 3), (1, 2), (2, 1), (3, 0)])


def core_swap(value):
    return lax.ppermute(value, "core", [(0, 1), (1, 0)])


def ring_shift(value, step):
    return lax.ppermute(value, "z", [(i, (i + step) % 4) for i in range(4)])


def pick(array, index):
    return lax.dynamic_index_in_dim(array, index, 0, keepdims=False)


def by_source(pieces, z_index, axis):
    pieces = [jnp.expand_dims(item, axis) for item in pieces]
    shape = [1] * pieces[0].ndim
    shape[axis] = 4
    hop = ((z_index - jnp.arange(4, dtype=jnp.int32)) % 4).reshape(shape)
    made = pieces[0]
    for k in (1, 2, 3):
        made = jnp.where(hop == k, pieces[k], made)
    return made


def pair(mine, other, index, axis):
    shape = [1] * (mine.ndim + 1)
    shape[axis] = 2
    slot = jnp.arange(2, dtype=jnp.int32).reshape(shape)
    return jnp.where(slot == index, jnp.expand_dims(mine, axis), jnp.expand_dims(other, axis))


def row_positions(shape, dim, plane_index):
    row = lax.broadcasted_iota(jnp.int32, shape, dim)
    chip = (row // 32) % 4
    code = (chip % 2) + 4 * (chip // 2) + 2 * (row // 128)
    return 64 * ((row % 32) // 8) + 8 * (plane_index ^ code) + row % 8


def live_pairs(info_ref, seq):
    shape = (256, 256)
    query_pos = row_positions(shape, 0, info_ref[1])
    key_pos = row_positions(shape, 1, info_ref[1])
    return (key_pos <= query_pos) & (key_pos < info_ref[2 + seq])


def block_rows(near_ref, far_ref):
    return jnp.concatenate([near_ref[...], far_ref[...]], axis=0).reshape(256, near_ref.shape[2])


def soft_probs(query, key, live):
    scores = mult_trans(query, key)
    scores = jnp.where(live, scores, -1e30)
    top = jnp.max(scores, axis=1, keepdims=True)
    weights = jnp.where(live, jnp.exp(scores - top), 0.0)
    return weights / jnp.sum(weights, axis=1, keepdims=True)


def attend_kernel(
    info_ref, near_ref, far_ref, gain_ref, mult_ref, w_ref, pre_ref, att_ref
):
    seq = pl.program_id(0)
    live = live_pairs(info_ref, seq)
    wide = block_rows(near_ref, far_ref).astype(jnp.float32)
    inverse = lax.rsqrt(jnp.mean(wide * wide, axis=1, keepdims=True) + 1e-06)
    hidden = (wide * inverse * gain_ref[...]).astype(jnp.bfloat16)
    pre = jnp.dot(hidden, w_ref[...], preferred_element_type=jnp.float32)
    pre_ref[...] = pre.reshape(2, 4, 32, 480)
    query = (pre[:, 0:160] * mult_ref[...]).astype(jnp.bfloat16)
    key = pre[:, 160:320].astype(jnp.bfloat16)
    value = pre[:, 320:480].astype(jnp.bfloat16)
    heads = []
    for head in range(2):
        part = slice(80 * head, 80 * head + 80)
        probs = soft_probs(query[:, part], key[:, part], live).astype(jnp.bfloat16)
        heads.append(jnp.dot(probs, value[:, part], preferred_element_type=jnp.float32))
    att = jnp.concatenate(heads, axis=1).astype(jnp.bfloat16).reshape(2, 4, 32, 160)
    for chip in range(4):
        for core in range(2):
            att_ref[chip, core] = att[core, chip]


def attend_back_kernel(
    info_ref, near_ref, far_ref, gain_ref, mult_ref, w_ref, pre_ref, grad_near, grad_far, gain_two_ref,
    hid_near, hid_far, send_ref, w_acc, gain_acc, scale_acc, lines,
):
    seq = pl.program_id(0)

    @pl.when(seq == 0)
    def _():
        w_acc[...] = jnp.zeros_like(w_acc)
        gain_acc[...] = jnp.zeros_like(gain_acc)
        scale_acc[...] = jnp.zeros_like(scale_acc)

    live = live_pairs(info_ref, seq)
    wide = block_rows(near_ref, far_ref).astype(jnp.float32)
    inverse = lax.rsqrt(jnp.mean(wide * wide, axis=1, keepdims=True) + 1e-06)
    normed = wide * inverse
    hidden = (normed * gain_ref[...]).astype(jnp.bfloat16)
    pre = pre_ref[...].reshape(256, 480)
    mult = mult_ref[...]
    query = (pre[:, 0:160] * mult).astype(jnp.bfloat16)
    key = pre[:, 160:320].astype(jnp.bfloat16)
    value = pre[:, 320:480].astype(jnp.bfloat16)
    grad_att = jnp.concatenate([grad_near[:, 0], grad_far[:, 0]], axis=0).reshape(256, 160)
    grad_q, grad_k, grad_v = [], [], []
    for head in range(2):
        part = slice(80 * head, 80 * head + 80)
        probs = soft_probs(query[:, part], key[:, part], live)
        grad_probs = mult_trans(grad_att[:, part], value[:, part])
        delta = jnp.sum(probs * grad_probs, axis=1, keepdims=True)
        grad_scores = (probs * (grad_probs - delta)).astype(jnp.bfloat16)
        grad_v.append(trans_mult(probs.astype(jnp.bfloat16), grad_att[:, part]))
        grad_q.append(jnp.dot(grad_scores, key[:, part], preferred_element_type=jnp.float32))
        grad_k.append(trans_mult(grad_scores, query[:, part]))
    grad_query = jnp.concatenate(grad_q, axis=1)
    scale_acc[...] += jnp.sum(grad_query * pre[:, 0:160], axis=0, keepdims=True)
    joined = jnp.concatenate([grad_query * mult] + grad_k + grad_v, axis=1).astype(jnp.bfloat16)
    w_acc[...] += trans_mult(hidden, joined)
    grad_hidden = mult_trans(joined, w_ref[...])
    gain_acc[...] += jnp.sum(grad_hidden * normed, axis=0, keepdims=True)
    low = grad_hidden.astype(jnp.bfloat16).reshape(2, 4, 32, 1280)
    hid_near[...] = low[0]
    hid_far[...] = low[1]

    @pl.when(seq == 3)
    def _():
        lines[...] = jnp.zeros_like(lines)
        for which, source in enumerate((gain_acc, gain_two_ref)):
            for owner in range(32):
                lane = 120 * (owner % 4) + 40 * which
                lines[owner // 4, :, lane : lane + 40] = source[:, 40 * owner : 40 * owner + 40]
        for part in range(4):
            lane = 120 * part + 80
            lines[info_ref[1], :, lane : lane + 40] = scale_acc[:, 40 * part : 40 * part + 40]
        blank = jnp.zeros((14, 480), jnp.float32)
        for target in range(4):
            rows = w_acc[320 * target : 320 * target + 320, :]
            block = jnp.concatenate([rows, lines[2 * target], lines[2 * target + 1], blank], axis=0)
            send_ref[target] = block.astype(jnp.bfloat16)


def feed_kernel(
    info_ref, x_ref, g_ref, atts, far_atts, gain_ref,
    near_rows, across_a, across_b, far_near_rows, far_across_a, far_across_b,
    out_ref, pack_ref, dmid_ref, datt_0, datt_1, datt_2, datt_3, gain_grad,
    weights, sems,
):
    y_index, core_index = info_ref[1] // 4, (info_ref[1] // 2) % 2
    copies = []
    for w in range(3):
        moved = []
        for core, own, others in (
            (core_index, near_rows, (across_a, across_b)),
            (1 - core_index, far_near_rows, (far_across_a, far_across_b)),
        ):
            moved.append((own.at[:, w], weights.at[w, :, y_index, core]))
            for half in range(2):
                moved.append((others[half].at[:, w], weights.at[w, pl.ds(2 * half, 2), 1 - y_index, core]))
        copies.append([pltpu.make_async_copy(*refs, sems.at[w, i]) for i, refs in enumerate(moved)])
    size = x_ref.shape[1]
    for group in copies:
        for copy in group:
            copy.start()
    datts = (datt_0, datt_1, datt_2, datt_3)

    for copy in copies[0]:
        copy.wait()
    heads = [(chip, core, info_ref[1] ^ (CODES[chip] + 2 * core)) for chip in range(4) for core in range(2)]
    middle = x_ref[...].astype(jnp.float32)
    for chip, core, source in heads:
        rows = weights[0, source // 2, source & 1].reshape(160, size)
        middle += jnp.dot((far_atts if core else atts)[chip, core], rows, preferred_element_type=jnp.float32)
    inverse = lax.rsqrt(jnp.mean(middle * middle, axis=1, keepdims=True) + 1e-06)
    normed = middle * inverse
    gain = gain_ref[...]
    hidden = (normed * gain).astype(jnp.bfloat16)
    pack_ref[1] = hidden
    for copy in copies[1]:
        copy.wait()
    up = jnp.dot(hidden, weights[1].reshape(size, size), preferred_element_type=jnp.float32)
    sigma = jax.nn.sigmoid(up)
    active = (up * sigma).astype(jnp.bfloat16)
    pack_ref[0] = active
    for copy in copies[2]:
        copy.wait()
    down = jnp.dot(active, weights[2].reshape(size, size), preferred_element_type=jnp.float32)
    result = middle + down
    for seq in range(4):
        for plane_z in range(4):
            row = 32 * seq + 8 * plane_z
            out_ref[plane_z, seq] = result[row : row + 8].astype(jnp.bfloat16)
    cot = g_ref[...]
    grad_act = mult_trans(cot, weights[2].reshape(size, size))
    grad_up = (grad_act * sigma * (1.0 + up * (1.0 - sigma))).astype(jnp.bfloat16)
    pack_ref[2] = grad_up
    grad_hidden = mult_trans(grad_up, weights[1].reshape(size, size))
    gain_grad[...] = jnp.sum(grad_hidden * normed, axis=0, keepdims=True)
    grad_mid = cot.astype(jnp.float32) + norm_back(grad_hidden, normed, inverse, gain)
    dmid_ref[...] = grad_mid
    low = grad_mid.astype(jnp.bfloat16)
    pack_ref[3] = low
    for chip, core, source in heads:
        rows = weights[0, source // 2, source & 1].reshape(160, size)
        datts[chip][core] = mult_trans(low, rows).astype(jnp.bfloat16)


def grads_kernel(
    info_ref, pack_ref, far_pack, atts, far_atts, cot_ref, far_cot, keep_a, away_a, keep_b, away_b, stage, sems
):
    y_index, core_index, x_index = info_ref[1] // 4, (info_ref[1] // 2) % 2, info_ref[1] % 2

    def leave(w):
        copies = []
        for half in range(2):
            for i in range(2):
                moves = ((stage.at[w, half, i, 1 - x_index], away_a), (stage.at[w, 2 + half, 1 - y_index, i], away_b))
                for j, (block, target) in enumerate(moves):
                    sem = sems.at[w, 4 * half + 2 * i + j]
                    copies.append(pltpu.make_async_copy(block, target.at[half, w, i], sem))
        return copies

    def keep():
        for half in range(2):
            for w in range(3):
                for i in range(2):
                    keep_a[half, w, i] = stage[w, half, i, x_index]
                    keep_b[half, w, i] = stage[w, 2 + half, y_index, i]

    def store(w, made):
        for i in range(16):
            stage[w, i // 4, (i // 2) % 2, i % 2] = made[40 * i : 40 * i + 40].astype(jnp.bfloat16)

    def both(near, far):
        return jnp.concatenate([near, far], axis=0)

    cots = both(cot_ref[...], far_cot[...])
    for core in range(2):

        @pl.when(core_index == core)
        def _():
            def own_columns(near, far):
                return both(*(
                    jnp.concatenate([ref[:, 160 * i + 80 * core : 160 * i + 80 * core + 80] for i in range(8)], axis=1)
                    for ref in (near, far)
                ))

            acts = own_columns(pack_ref.at[0], far_pack.at[0])
            store(2, trans_mult(acts, cots))
            for copy in leave(2):
                copy.start()
            acts = own_columns(pack_ref.at[1], far_pack.at[1])
            store(1, trans_mult(acts, both(pack_ref[2], far_pack[2])))
            for copy in leave(1):
                copy.start()
            grads = both(pack_ref[3], far_pack[3])
            pieces = []
            for chip in range(4):
                for source in range(2):
                    near, far = (far_atts, far_atts) if source else (atts, atts)
                    pieces.append(both(near[chip, source], far[chip, 1 - source])[:, 80 * core : 80 * core + 80])
            made = trans_mult(jnp.concatenate(pieces, axis=1), grads)
            for i in range(8):
                source = info_ref[1] ^ (CODES[i // 2] + 2 * (i % 2))
                for part in range(2):
                    row = 80 * i + 40 * part
                    stage[0, source // 2, source & 1, part] = made[row : row + 40].astype(jnp.bfloat16)
            for copy in leave(0):
                copy.start()

    keep()
    for w in range(3):
        for copy in leave(w):
            copy.wait()


def meet_kernel(far_side, info_ref, mine_a, from_a, mine_b, from_b, out_a, out_b):
    y_index, x_index = info_ref[1] // 4, info_ref[1] % 2
    if far_side:
        y_index, x_index = 1 - y_index, 1 - x_index
    for half in range(2):
        for w in range(3):
            out_a[half, w] = sum_low(mine_a[half, w, y_index], from_a[half, w, y_index])
            out_b[half, w] = sum_low(mine_b[half, w, x_index], from_b[half, w, x_index])


def join_kernel(keep_a, from_a, keep_b, from_b, out_ref):
    for half in range(2):
        for w in range(3):
            out_ref[half, w] = sum_low(keep_a[half, w], from_a[half, w])
            out_ref[2 + half, w] = sum_low(keep_b[half, w], from_b[half, w])


def sum_low(left, right):
    return (left.astype(jnp.float32) + right.astype(jnp.float32)).astype(jnp.bfloat16)


def norm_kernel(info_ref, hid_0, hid_1, hid_2, hid_3, x_ref, dmid_ref, gain_ref, out_0, out_1, out_2, out_3, rows):
    grad = hid_0[...].astype(jnp.float32)
    for item in (hid_1, hid_2, hid_3):
        grad += item[...].astype(jnp.float32)
    wide = x_ref[...].astype(jnp.float32)
    inverse = lax.rsqrt(jnp.mean(wide * wide, axis=1, keepdims=True) + 1e-06)
    grad = dmid_ref[...] + norm_back(grad, wide * inverse, inverse, gain_ref[...])
    for seq in range(4):
        for plane_z in range(4):
            row = 32 * seq + 8 * plane_z
            rows[plane_z, seq] = grad[row : row + 8]
    for hop, out in enumerate((out_0, out_1, out_2, out_3)):
        out[...] = rows[(info_ref[0] + hop) & 3].astype(jnp.bfloat16)


def fold_kernel(in_ref, out_ref, line):
    total = in_ref[0].astype(jnp.float32)
    line[...] = jnp.zeros_like(line)
    for owner in range(8):
        lane = 120 * (owner % 4)
        line[0:1, 0:120] = total[320 + owner // 4 : 321 + owner // 4, lane : lane + 120]
        block = jnp.concatenate([total[40 * owner : 40 * owner + 40], line[...]], axis=0)
        out_ref[owner] = block.astype(jnp.bfloat16)


def spread_kernel(in_ref, *outs):
    for which, out in enumerate(outs):
        for owner in range(8):
            part = in_ref[owner, 0:40, 160 * which : 160 * which + 160]
            out[:, 160 * owner : 160 * owner + 160] = part.astype(jnp.float32)


def widen_kernel(in_ref, *outs):
    for which, out in enumerate(outs):
        out[...] = in_ref[which].astype(jnp.float32)


def whole(shape):
    return pl.BlockSpec(shape, lambda *_: (0,) * len(shape))


def seq_block(*lead, width):
    count = len(lead)
    return pl.BlockSpec((*lead, 32, width), lambda s, info: (*(0,) * count, s, 0))


def planes(
    inputs, cotangent, w_query, w_key, w_value, w_output, w_up, w_down,
    attn_gain, mlp_gain, query_scale, deal, lengths,
):
    f32, bf16 = jnp.float32, jnp.bfloat16
    z, y, c, x = (lax.axis_index(name) for name in ("z", "y", "core", "x"))
    plane = 4 * y + 2 * c + x
    width = 1280
    seqs = jnp.arange(16, dtype=jnp.int32)
    seq_lengths = jnp.sum(jnp.where(deal[None, :] == seqs[:, None], lengths[None, :], 0), axis=1)
    my_lengths = lax.dynamic_slice_in_dim(seq_lengths, 4 * z, 4, 0)
    info = jnp.concatenate([jnp.stack([z, plane]), my_lengths]).astype(jnp.int32)

    vec = jnp.concatenate([attn_gain, mlp_gain, query_scale]).astype(bf16)
    vec_block = jnp.zeros((1, 8, width), bf16).at[0, 0, :120].set(vec)
    in_four = inputs.reshape(4, 4, 8, width)
    sent = [jnp.concatenate([pick(in_four, (z + k) % 4), vec_block]) for k in range(4)]
    qkv = jnp.stack([w_query, w_key, w_value]).astype(bf16)
    *sent, qkv = lax.optimization_barrier((*sent, qkv))
    got = [sent[0]] + [ring_shift(sent[k], k) for k in (1, 2, 3)]
    x_rows = by_source([item[:4] for item in got], z, 1).reshape(128, width)
    vec_rows = by_source([item[4, 0] for item in got], z, 0)
    vec_rows = jnp.concatenate([vec_rows, jnp.zeros((4, width), bf16)])
    own = jnp.concatenate([x_rows, vec_rows])

    big = jnp.stack([w_output, w_up, w_down]).astype(bf16)
    big = lax.all_gather(big, "z", axis=0)

    qkv = qkv.reshape(3, 40, 8, 160).transpose(2, 1, 0, 3).reshape(8, 40, 480)
    qkv = lax.all_to_all(qkv, ("y", "core", "x"), split_axis=0, concat_axis=0, tiled=True)
    near = jnp.stack([own] + [plane_shift(own, step) for step in (1, 2, 3)])
    big, near, cotangent, qkv = lax.optimization_barrier((big, near, cotangent, qkv.reshape(320, 480)))
    w_qkv = lax.all_gather(qkv, "z", axis=0, tiled=True)
    far = core_swap(near)
    beside, across = plane_shift(big, 1), plane_shift(big, 2)
    relay_a, relay_b = beside[:2], across[2:]
    cot_rows = lax.all_to_all(cotangent.reshape(4, 4, 8, width), "z", split_axis=0, concat_axis=0, tiled=True)
    relay_a, relay_b, cot_rows = lax.optimization_barrier((relay_a, relay_b, cot_rows))
    across_a, across_b = plane_shift(relay_a, 2), plane_shift(relay_b, 1)

    vecs = jnp.stack([near[:, 128:132, :120], far[:, 128:132, :120]])
    vecs = vecs.astype(f32).reshape(2, 2, 2, 4, 120)
    vecs = jnp.where(c == 0, vecs, vecs[::-1])
    vecs = jnp.where(y == 0, vecs, vecs[:, ::-1])
    vecs = jnp.where(x == 0, vecs, vecs[:, :, ::-1])
    vecs = vecs.reshape(2, 2, 2, 4, 3, 40).transpose(4, 3, 1, 0, 2, 5).reshape(3, width)
    gain_one, gain_two = vecs[0:1], vecs[1:2]
    my_scale = lax.dynamic_slice_in_dim(vecs[2:3], 160 * plane, 160, 1)
    query_mult = LOG2E / math.sqrt(HD) * jax.nn.softplus(my_scale)


    def limit(megabytes):
        return pltpu.CompilerParams(vmem_limit_bytes=megabytes * 1024 * 1024)

    pre, att_made = pl.pallas_call(
        attend_kernel,
        grid_spec=pltpu.PrefetchScalarGridSpec(
            num_scalar_prefetch=1,
            grid=(4,),
            in_specs=[
                seq_block(4, width=width), seq_block(4, width=width),
                whole((1, width)), whole((1, 160)), whole((width, 480)),
            ],
            out_specs=[seq_block(2, 4, width=480), seq_block(4, 2, width=160)],
        ),
        out_shape=[
            jax.ShapeDtypeStruct((2, 4, 128, 480), f32),
            jax.ShapeDtypeStruct((4, 2, 128, 160), bf16),
        ],
        compiler_params=limit(14),
        cost_estimate=pl.CostEstimate(flops=9_000_000_000, bytes_accessed=8_000_000, transcendentals=600_000),
        name="attend",
    )(info, near, far, gain_one, query_mult, w_qkv)

    near_rows = pair(big, beside, x, 2).reshape(4, 3, 80, width)
    att_made, far_near_rows, across_a, across_b = lax.optimization_barrier(
        (att_made, core_swap(near_rows), across_a, across_b)
    )
    atts = [att_made[0]] + [plane_shift(att_made[step], step) for step in (1, 2, 3)]
    atts = jnp.stack(atts)
    far_atts = core_swap(atts)
    across_a = pair(across[:2], across_a, x, 2).reshape(2, 3, 80, width)
    across_b = pair(across[2:], across_b, x, 2).reshape(2, 3, 80, width)
    far_across_a, far_across_b = core_swap(across_a), core_swap(across_b)
    cot_rows = cot_rows.transpose(1, 0, 2, 3).reshape(128, width)
    far_cot = core_swap(cot_rows)
    far_cot, far_atts, cot_rows = lax.optimization_barrier((far_cot, far_atts, cot_rows))
    datt_shape = jax.ShapeDtypeStruct((2, 128, 160), bf16)
    smem = pl.BlockSpec(memory_space=pltpu.SMEM)
    vmem = pl.BlockSpec(memory_space=pltpu.VMEM)
    hbm = pl.BlockSpec(memory_space=pltpu.HBM)
    out_rows, pack, grad_mid, *datts, gain_two_grad = pl.pallas_call(
        feed_kernel,
        in_specs=[smem] + [vmem] * 5 + [hbm] * 6,
        out_specs=[vmem] * 8,
        out_shape=[
            jax.ShapeDtypeStruct((4, 4, 8, width), bf16),
            jax.ShapeDtypeStruct((4, 128, width), bf16),
            jax.ShapeDtypeStruct((128, width), f32),
        ]
        + [datt_shape] * 4
        + [jax.ShapeDtypeStruct((1, width), f32)],
        scratch_shapes=[pltpu.VMEM((3, 4, 2, 2, 80, width), bf16), pltpu.SemaphoreType.DMA((3, 6))],
        compiler_params=limit(36),
        cost_estimate=pl.CostEstimate(flops=12_000_000_000, bytes_accessed=13_000_000, transcendentals=200_000),
        name="feed",
    )(info, x_rows, cot_rows, atts, far_atts, gain_two, near_rows, across_a, across_b, far_near_rows, far_across_a, far_across_b)

    back = [datts[0]] + [plane_shift(datts[step], step) for step in (1, 2, 3)]

    mine_a, away_a, mine_b, away_b = pl.pallas_call(
        grads_kernel,
        in_specs=[smem] + [vmem] * 6,
        out_specs=[vmem, hbm, vmem, hbm],
        out_shape=[jax.ShapeDtypeStruct((2, 3, 2, 40, width), bf16)] * 4,
        scratch_shapes=[pltpu.VMEM((3, 4, 2, 2, 40, width), bf16), pltpu.SemaphoreType.DMA((3, 8))],
        compiler_params=limit(22),
        cost_estimate=pl.CostEstimate(flops=6_000_000_000, bytes_accessed=8_000_000, transcendentals=0),
        name="grads",
    )(info, pack, core_swap(pack), atts, far_atts, cot_rows, far_cot)

    mine_a, away_a, mine_b, away_b, *back = lax.optimization_barrier((mine_a, away_a, mine_b, away_b, *back))
    away_a, away_b, grad_atts = lax.optimization_barrier((away_a, away_b, jnp.stack(back)))
    from_a, from_b = plane_shift(away_a, 1), plane_shift(away_b, 2)
    hid_near, hid_far, send = pl.pallas_call(
        attend_back_kernel,
        grid_spec=pltpu.PrefetchScalarGridSpec(
            num_scalar_prefetch=1,
            grid=(4,),
            in_specs=[
                seq_block(4, width=width), seq_block(4, width=width),
                whole((1, width)), whole((1, 160)), whole((width, 480)),
                seq_block(2, 4, width=480),
                *[pl.BlockSpec((4, 1, 32, 160), lambda s, info, core=core: (0, core, s, 0)) for core in range(2)],
                whole((1, width)),
            ],
            out_specs=[
                seq_block(4, width=width), seq_block(4, width=width),
                whole((4, 336, 480)),
            ],
            scratch_shapes=[
                pltpu.VMEM((width, 480), f32), pltpu.VMEM((1, width), f32),
                pltpu.VMEM((1, 160), f32), pltpu.VMEM((8, 1, 480), f32),
            ],
        ),
        out_shape=[
            jax.ShapeDtypeStruct((4, 128, width), bf16),
            jax.ShapeDtypeStruct((4, 128, width), bf16),
            jax.ShapeDtypeStruct((4, 336, 480), bf16),
        ],
        compiler_params=limit(22),
        cost_estimate=pl.CostEstimate(flops=15_000_000_000, bytes_accessed=12_000_000, transcendentals=600_000),
        name="attend_back",
    )(info, near, far, gain_one, query_mult, w_qkv, pre, grad_atts, core_swap(grad_atts), gain_two_grad)

    send, out_rows = lax.optimization_barrier((send, out_rows))
    sums = lax.psum_scatter(send, "z", scatter_dimension=0, tiled=True)
    out_sent = [pick(out_rows, (z + k) % 4) for k in range(4)]
    out_one, out_three = ring_shift(out_sent[1], 1), ring_shift(out_sent[3], 3)
    from_a, from_b, hid_far, out_one, out_three = lax.optimization_barrier(
        (from_a, from_b, hid_far, out_one, out_three)
    )
    swapped = core_swap(hid_far)
    hid = [sum_low(hid_near[i], swapped[i]) for i in range(4)]
    def meet(far_side, *parts):
        return pl.pallas_call(
            functools.partial(meet_kernel, far_side),
            in_specs=[smem] + [vmem] * 4,
            out_specs=[vmem] * 2,
            out_shape=[jax.ShapeDtypeStruct((2, 3, 40, width), bf16)] * 2,
            compiler_params=limit(50),
            cost_estimate=pl.CostEstimate(flops=2_000_000_000, bytes_accessed=4_000_000, transcendentals=0),
            name="meet",
        )(info, *parts)

    parts = mine_a, from_a, mine_b, from_b
    away_a, away_b = meet(True, *parts)
    keep_a, keep_b = meet(False, *parts)
    from_a, from_b = plane_shift(away_a, 2), plane_shift(away_b, 1)
    *hid, from_a, from_b, out_sent[2] = lax.optimization_barrier((*hid, from_a, from_b, out_sent[2]))
    out_two = ring_shift(out_sent[2], 2)
    kept = pl.pallas_call(
        join_kernel,
        in_specs=[vmem] * 4,
        out_specs=vmem,
        out_shape=jax.ShapeDtypeStruct((4, 3, 40, width), bf16),
        compiler_params=limit(50),
        cost_estimate=pl.CostEstimate(flops=2_000_000_000, bytes_accessed=4_000_000, transcendentals=0),
        name="join",
    )(keep_a, from_a, keep_b, from_b)
    moved = [plane_shift(hid[step], step) for step in (1, 2, 3)]
    moved[0], sums, out_two = lax.optimization_barrier((moved[0], sums, out_two))
    outputs = by_source([out_sent[0], out_one, out_two, out_three], z, 0).reshape(16, 8, width)
    big_sums = lax.psum_scatter(kept, "z", scatter_dimension=0, tiled=True)[0]
    grad_home = pl.pallas_call(
        norm_kernel,
        in_specs=[smem] + [vmem] * 7,
        out_specs=[vmem] * 4,
        out_shape=[jax.ShapeDtypeStruct((4, 8, width), bf16)] * 4,
        scratch_shapes=[pltpu.VMEM((4, 4, 8, width), f32)],
        compiler_params=limit(10),
        cost_estimate=pl.CostEstimate(flops=2_000_000_000, bytes_accessed=2_500_000, transcendentals=128),
        name="norm",
    )(info, hid[0], *moved, x_rows, grad_mid, gain_one)
    sums = pl.pallas_call(
        fold_kernel,
        in_specs=[vmem],
        out_specs=vmem,
        out_shape=jax.ShapeDtypeStruct((8, 48, 480), bf16),
        scratch_shapes=[pltpu.VMEM((8, 480), f32)],
        compiler_params=limit(8),
        cost_estimate=pl.CostEstimate(flops=2_000_000_000, bytes_accessed=1_600_000, transcendentals=0),
        name="fold",
    )(sums)
    sums = lax.all_to_all(sums, ("y", "core", "x"), split_axis=0, concat_axis=0, tiled=True)
    rows_shape = [jax.ShapeDtypeStruct((40, width), f32)] * 3
    qkv_sums = pl.pallas_call(
        spread_kernel, in_specs=[vmem], out_specs=[vmem] * 3, out_shape=rows_shape, compiler_params=limit(6), name="spread"
    )(sums)
    big_sums = pl.pallas_call(
        widen_kernel, in_specs=[vmem], out_specs=[vmem] * 3, out_shape=rows_shape, compiler_params=limit(6), name="widen"
    )(big_sums)
    line_sums = jnp.sum(sums[:, 40, :120].astype(f32), axis=0).reshape(3, 40)
    scale_low = query_scale.astype(bf16).astype(f32)
    scale_sum = LOG2E / math.sqrt(HD) * jax.nn.sigmoid(scale_low) * line_sums[2]
    grad_home = [grad_home[0]] + [ring_shift(grad_home[k], k) for k in (1, 2, 3)]
    grad_home[2], *qkv_sums, scale_sum = lax.optimization_barrier((grad_home[2], *qkv_sums, scale_sum))
    grad_home = by_source(grad_home, z, 0).reshape(16, 8, width)

    return (
        outputs, grad_home, qkv_sums[0], qkv_sums[1], qkv_sums[2],
        big_sums[0], big_sums[1], big_sums[2], line_sums[0], line_sums[1], scale_sum,
    )


def solution(mesh):
    names = ("dp", "ctx")
    body = per_device
    if dict(mesh.shape) == {"dp": 16, "ctx": 2}:
        mesh = Mesh(mesh.devices.reshape(4, 2, 2, 2), ("z", "y", "core", "x"))
        names = mesh.axis_names
        body = planes
    seq, mat, line = P(None, names, None), P(names, None), P(names)
    return jax.shard_map(
        body,
        mesh=mesh,
        in_specs=(seq,) * 2 + (mat,) * 6 + (line,) * 3 + (P(), P()),
        out_specs=(seq,) * 2 + (mat,) * 6 + (line,) * 3,
        check_vma=False,
    )
```

```python
import functools
import math

import jax
import jax.numpy as jnp
from jax import lax
from jax.experimental import pallas as pl
from jax.experimental.pallas import tpu as pltpu
from jax.sharding import Mesh, PartitionSpec as P

H = 16
HD = 80


def mult_trans(left, right):
    return lax.dot_general(
        left, right, (((1,), (1,)), ((), ())), preferred_element_type=jnp.float32
    )


def trans_mult(left, right):
    return lax.dot_general(
        left, right, (((0,), (0,)), ((), ())), preferred_element_type=jnp.float32
    )


def position_of(index, local_rows, piece_rows, groups):
    column = index // local_rows
    within = index % local_rows
    return (within // piece_rows * groups + column) * piece_rows + within % piece_rows


def norm_back(grad_hidden, normed, inverse, gain_value):
    grad_normed = grad_hidden * gain_value
    return inverse * (grad_normed - normed * jnp.mean(grad_normed * normed, axis=1, keepdims=True))


def per_device(
    inputs,
    cotangent,
    w_query,
    w_key,
    w_value,
    w_output,
    w_up,
    w_down,
    attn_gain,
    mlp_gain,
    query_scale,
    deal,
    lengths,
):
    groups = lax.axis_size("ctx")
    group_index = lax.axis_index("dp")
    ctx_index = lax.axis_index("ctx")
    head_count = H
    head_dim = HD
    piece_rows = inputs.shape[1]
    seq_numbers = jnp.arange(inputs.shape[0], dtype=jnp.int32)
    seq_lengths = jnp.sum(
        jnp.where(deal[None, :] == seq_numbers[:, None], lengths[None, :], 0), axis=1
    )
    local_in, local_cot = (
        lax.all_to_all(inputs, "dp", split_axis=0, concat_axis=1, tiled=True),
        lax.all_to_all(cotangent, "dp", split_axis=0, concat_axis=1, tiled=True),
    )
    seq_count, local_rows, model_width = local_in.shape
    padded = local_rows * groups
    token_count = seq_count * local_rows
    my_lengths = lax.dynamic_slice_in_dim(seq_lengths, group_index * seq_count, seq_count, 0)
    query_pos = position_of(
        ctx_index * local_rows + jnp.arange(local_rows, dtype=jnp.int32),
        local_rows,
        piece_rows,
        groups,
    )
    flat_in = local_in.reshape(token_count, model_width).astype(jnp.float32)
    flat_cot = local_cot.reshape(token_count, model_width)
    lowered = (
        w_query.astype(jnp.bfloat16),
        w_key.astype(jnp.bfloat16),
        w_value.astype(jnp.bfloat16),
        w_output.astype(jnp.bfloat16),
        w_up.astype(jnp.bfloat16),
        w_down.astype(jnp.bfloat16),
        attn_gain.astype(jnp.bfloat16),
        mlp_gain.astype(jnp.bfloat16),
        query_scale.astype(jnp.bfloat16),
    )
    gathered = (
        lax.all_gather(lowered[0], ("dp", "ctx"), axis=0, tiled=True),
        lax.all_gather(lowered[1], ("dp", "ctx"), axis=0, tiled=True),
        lax.all_gather(lowered[2], ("dp", "ctx"), axis=0, tiled=True),
        lax.all_gather(lowered[3], ("dp", "ctx"), axis=0, tiled=True),
        lax.all_gather(lowered[4], ("dp", "ctx"), axis=0, tiled=True),
        lax.all_gather(lowered[5], ("dp", "ctx"), axis=0, tiled=True),
        lax.all_gather(lowered[6], ("dp", "ctx"), axis=0, tiled=True),
        lax.all_gather(lowered[7], ("dp", "ctx"), axis=0, tiled=True),
        lax.all_gather(lowered[8], ("dp", "ctx"), axis=0, tiled=True),
    )
    (
        query_full,
        key_full,
        value_full,
        output_full,
        up_full,
        down_full,
        gain_one,
        gain_two,
        scale_raw,
    ) = gathered
    inv_one = lax.rsqrt(jnp.mean(flat_in * flat_in, axis=1, keepdims=True) + 1e-06)
    normed_one = flat_in * inv_one
    hidden_one = (normed_one * gain_one.astype(jnp.float32)).astype(jnp.bfloat16)
    scale_param = scale_raw.astype(jnp.float32)
    query_mult = 1.442695041 / math.sqrt(head_dim) * jax.nn.softplus(scale_param)
    query_pre = jnp.dot(hidden_one, query_full, preferred_element_type=jnp.float32)
    queries = (query_pre * query_mult).astype(jnp.bfloat16)
    keys_local = jnp.dot(hidden_one, key_full, preferred_element_type=jnp.float32).astype(
        jnp.bfloat16
    )
    values_local = jnp.dot(hidden_one, value_full, preferred_element_type=jnp.float32).astype(
        jnp.bfloat16
    )
    four_shape = (seq_count, local_rows, head_count, head_dim)
    query_four = queries.reshape(four_shape)
    keys_three = keys_local.reshape(seq_count, local_rows, model_width)
    values_three = values_local.reshape(seq_count, local_rows, model_width)

    def live_between(row_pos, key_pos):
        allowed = (key_pos[None, None, :] <= row_pos[None, :, None]) & (
            key_pos[None, None, :] < my_lengths[:, None, None]
        )
        return allowed[:, :, None, :]

    def live_mask(key_pos):
        return live_between(query_pos, key_pos)

    def attend_block(state_now, key_block, value_block, first_row):
        run_max, run_sum, run_acc = state_now
        block_len = key_block.shape[1]
        key_pos = position_of(
            first_row + jnp.arange(block_len, dtype=jnp.int32), local_rows, piece_rows, groups
        )
        key_four = key_block.reshape(seq_count, block_len, head_count, head_dim)
        value_four = value_block.reshape(seq_count, block_len, head_count, head_dim)
        scores = jnp.einsum(
            "srhd,skhd->srhk", query_four, key_four, preferred_element_type=jnp.float32
        )
        allowed = live_mask(key_pos)
        masked = jnp.where(allowed, scores, -1e30)
        new_max = jnp.maximum(run_max, jnp.max(masked, axis=3))
        weights_now = jnp.exp(jnp.where(allowed, masked - new_max[..., None], -1e30))
        factor = jnp.exp(run_max - new_max)
        new_sum = run_sum * factor + jnp.sum(weights_now, axis=3)
        added = jnp.einsum(
            "srhk,skhd->srhd",
            weights_now.astype(jnp.bfloat16),
            value_four,
            preferred_element_type=jnp.float32,
        )
        return (new_max, new_sum, run_acc * factor[..., None] + added)

    start_state = (
        jnp.full((seq_count, local_rows, head_count), -1e30, jnp.float32),
        jnp.zeros((seq_count, local_rows, head_count), jnp.float32),
        jnp.zeros(four_shape, jnp.float32),
    )
    key_piece = lax.all_gather(keys_three, "ctx", axis=1, tiled=True)
    value_piece = lax.all_gather(values_three, "ctx", axis=1, tiled=True)
    piece_len = key_piece.shape[1]
    fold_block_len = 512 if piece_len % 512 == 0 else piece_len

    def one_block(state_now, block_index):
        offset = block_index * fold_block_len
        key_block = lax.dynamic_slice_in_dim(key_piece, offset, fold_block_len, 1)
        value_block = lax.dynamic_slice_in_dim(value_piece, offset, fold_block_len, 1)
        return (attend_block(state_now, key_block, value_block, offset), None)

    result_state, unused = lax.scan(
        one_block, start_state, jnp.arange(piece_len // fold_block_len, dtype=jnp.int32)
    )
    run_max, run_sum, run_acc = result_state
    log_total = run_max + jnp.log(run_sum)
    attn_exact = run_acc / run_sum[..., None]
    attended = attn_exact.reshape(token_count, model_width).astype(jnp.bfloat16)
    middle = flat_in + jnp.dot(attended, output_full, preferred_element_type=jnp.float32)
    inv_two = lax.rsqrt(jnp.mean(middle * middle, axis=1, keepdims=True) + 1e-06)
    normed_two = middle * inv_two
    hidden_two = (normed_two * gain_two.astype(jnp.float32)).astype(jnp.bfloat16)
    up_pre = jnp.dot(hidden_two, up_full, preferred_element_type=jnp.float32)
    active = jax.nn.silu(up_pre).astype(jnp.bfloat16)
    result = (middle + jnp.dot(active, down_full, preferred_element_type=jnp.float32)).astype(
        jnp.bfloat16
    )
    back_weights = (
        lax.all_gather(lowered[0], ("dp", "ctx"), axis=0, tiled=True),
        lax.all_gather(lowered[1], ("dp", "ctx"), axis=0, tiled=True),
        lax.all_gather(lowered[2], ("dp", "ctx"), axis=0, tiled=True),
        lax.all_gather(lowered[3], ("dp", "ctx"), axis=0, tiled=True),
        lax.all_gather(lowered[4], ("dp", "ctx"), axis=0, tiled=True),
        lax.all_gather(lowered[5], ("dp", "ctx"), axis=0, tiled=True),
        lax.all_gather(lowered[6], ("dp", "ctx"), axis=0, tiled=True),
        lax.all_gather(lowered[7], ("dp", "ctx"), axis=0, tiled=True),
        lax.all_gather(lowered[8], ("dp", "ctx"), axis=0, tiled=True),
    )
    (
        query_back,
        key_back,
        value_back,
        output_back,
        up_back,
        down_back,
        gain_one_back,
        gain_two_back,
        scale_back,
    ) = back_weights
    cot_wide = flat_cot.astype(jnp.float32)
    grad_down = trans_mult(active, flat_cot)
    grad_active = mult_trans(flat_cot, down_back)
    sigma_up = jax.nn.sigmoid(up_pre)
    grad_up_pre = (grad_active * sigma_up * (1.0 + up_pre * (1.0 - sigma_up))).astype(jnp.bfloat16)
    grad_up = trans_mult(hidden_two, grad_up_pre)
    grad_hidden_two = mult_trans(grad_up_pre, up_back)
    grad_gain_two = jnp.sum(grad_hidden_two * normed_two, axis=0)
    grad_middle = cot_wide + norm_back(
        grad_hidden_two, normed_two, inv_two, gain_two_back.astype(jnp.float32)
    )
    grad_middle_low = grad_middle.astype(jnp.bfloat16)
    grad_output = trans_mult(attended, grad_middle_low)
    grad_attended = mult_trans(grad_middle_low, output_back).astype(jnp.bfloat16)
    grad_att_four = grad_attended.reshape(four_shape)
    delta_rows = jnp.sum(grad_att_four.astype(jnp.float32) * attn_exact, axis=3)
    key_all, value_all = (
        lax.all_gather(keys_three, "ctx", axis=1, tiled=True),
        lax.all_gather(values_three, "ctx", axis=1, tiled=True),
    )
    block_len = min(512, padded)

    def back_block(block_index, state_now):
        grad_query, grad_key_all, grad_value_all = state_now
        offset = block_index * block_len
        key_block = lax.dynamic_slice_in_dim(key_all, offset, block_len, 1).reshape(
            seq_count, block_len, head_count, head_dim
        )
        value_block = lax.dynamic_slice_in_dim(value_all, offset, block_len, 1).reshape(
            seq_count, block_len, head_count, head_dim
        )
        key_pos = position_of(
            offset + jnp.arange(block_len, dtype=jnp.int32), local_rows, piece_rows, groups
        )
        scores = jnp.einsum(
            "srhd,skhd->srhk", query_four, key_block, preferred_element_type=jnp.float32
        )
        probs = jnp.exp(jnp.where(live_mask(key_pos), scores - log_total[..., None], -1e30))
        grad_value_block = jnp.einsum(
            "srhk,srhd->skhd",
            probs.astype(jnp.bfloat16),
            grad_att_four,
            preferred_element_type=jnp.float32,
        )
        grad_probs = jnp.einsum(
            "srhd,skhd->srhk", grad_att_four, value_block, preferred_element_type=jnp.float32
        )
        grad_scores = (probs * (grad_probs - delta_rows[..., None])).astype(jnp.bfloat16)
        grad_query = grad_query + jnp.einsum(
            "srhk,skhd->srhd", grad_scores, key_block, preferred_element_type=jnp.float32
        )
        grad_key_block = jnp.einsum(
            "srhk,srhd->skhd", grad_scores, query_four, preferred_element_type=jnp.float32
        )
        grad_key_all = lax.dynamic_update_slice_in_dim(
            grad_key_all, grad_key_block.reshape(seq_count, block_len, model_width), offset, 1
        )
        grad_value_all = lax.dynamic_update_slice_in_dim(
            grad_value_all, grad_value_block.reshape(seq_count, block_len, model_width), offset, 1
        )
        return (grad_query, grad_key_all, grad_value_all)

    zero_all = jnp.zeros((seq_count, padded, model_width), jnp.float32)
    grad_query, grad_key_all, grad_value_all = lax.fori_loop(
        0, padded // block_len, back_block, (jnp.zeros(four_shape, jnp.float32), zero_all, zero_all)
    )
    grad_key_mine, grad_value_mine = (
        lax.psum_scatter(
            grad_key_all.astype(jnp.bfloat16), "ctx", scatter_dimension=1, tiled=True
        ).astype(jnp.float32),
        lax.psum_scatter(
            grad_value_all.astype(jnp.bfloat16), "ctx", scatter_dimension=1, tiled=True
        ).astype(jnp.float32),
    )
    grad_query_flat = grad_query.reshape(token_count, model_width)
    grad_query_pre = (grad_query_flat * query_mult).astype(jnp.bfloat16)
    grad_scale = (
        1.442695041
        / math.sqrt(head_dim)
        * jax.nn.sigmoid(scale_back.astype(jnp.float32))
        * jnp.sum(grad_query_flat * query_pre, axis=0)
    )
    grad_key_low = grad_key_mine.reshape(token_count, model_width).astype(jnp.bfloat16)
    grad_value_low = grad_value_mine.reshape(token_count, model_width).astype(jnp.bfloat16)
    grad_wq = trans_mult(hidden_one, grad_query_pre)
    grad_wk = trans_mult(hidden_one, grad_key_low)
    grad_wv = trans_mult(hidden_one, grad_value_low)
    grad_hidden_one = (
        mult_trans(grad_query_pre, query_back)
        + mult_trans(grad_key_low, key_back)
        + mult_trans(grad_value_low, value_back)
    )
    grad_gain_one = jnp.sum(grad_hidden_one * normed_one, axis=0)
    grad_in = grad_middle + norm_back(
        grad_hidden_one, normed_one, inv_one, gain_one_back.astype(jnp.float32)
    )
    matrix_stack = jnp.stack([grad_wq, grad_wk, grad_wv, grad_output, grad_up, grad_down], axis=0)
    vector_stack = jnp.stack([grad_gain_one, grad_gain_two, grad_scale], axis=0)
    matrix_sums, vector_sums = (
        lax.psum_scatter(matrix_stack, ("dp", "ctx"), scatter_dimension=1, tiled=True),
        lax.psum_scatter(vector_stack, ("dp", "ctx"), scatter_dimension=1, tiled=True),
    )
    out_local = result.reshape(seq_count, local_rows, model_width)
    grad_local = grad_in.astype(jnp.bfloat16).reshape(seq_count, local_rows, model_width)
    back_out, back_grad = (
        lax.all_to_all(out_local, "dp", split_axis=1, concat_axis=0, tiled=True),
        lax.all_to_all(grad_local, "dp", split_axis=1, concat_axis=0, tiled=True),
    )
    return (
        back_out,
        back_grad,
        matrix_sums[0],
        matrix_sums[1],
        matrix_sums[2],
        matrix_sums[3],
        matrix_sums[4],
        matrix_sums[5],
        vector_sums[0],
        vector_sums[1],
        vector_sums[2],
    )


LOG2E = 1.442695041
CODES = (0, 1, 4, 5)


def plane_shift(value, step):
    if step == 1:
        return lax.ppermute(value, "x", [(0, 1), (1, 0)])
    if step == 2:
        return lax.ppermute(value, "y", [(0, 1), (1, 0)])
    return lax.ppermute(value, ("y", "x"), [(0, 3), (1, 2), (2, 1), (3, 0)])


def core_swap(value):
    return lax.ppermute(value, "core", [(0, 1), (1, 0)])


def ring_shift(value, step):
    return lax.ppermute(value, "z", [(i, (i + step) % 4) for i in range(4)])


def pick(array, index):
    return lax.dynamic_index_in_dim(array, index, 0, keepdims=False)


def by_source(pieces, z_index, axis):
    pieces = [jnp.expand_dims(item, axis) for item in pieces]
    shape = [1] * pieces[0].ndim
    shape[axis] = 4
    hop = ((z_index - jnp.arange(4, dtype=jnp.int32)) % 4).reshape(shape)
    made = pieces[0]
    for k in (1, 2, 3):
        made = jnp.where(hop == k, pieces[k], made)
    return made


def pair(mine, other, index, axis):
    shape = [1] * (mine.ndim + 1)
    shape[axis] = 2
    slot = jnp.arange(2, dtype=jnp.int32).reshape(shape)
    return jnp.where(slot == index, jnp.expand_dims(mine, axis), jnp.expand_dims(other, axis))


def row_positions(shape, dim, plane_index):
    row = lax.broadcasted_iota(jnp.int32, shape, dim)
    chip = (row // 32) % 4
    code = (chip % 2) + 4 * (chip // 2) + 2 * (row // 128)
    return 64 * ((row % 32) // 8) + 8 * (plane_index ^ code) + row % 8


def live_pairs(info_ref, seq):
    shape = (256, 256)
    query_pos = row_positions(shape, 0, info_ref[1])
    key_pos = row_positions(shape, 1, info_ref[1])
    return (key_pos <= query_pos) & (key_pos < info_ref[2 + seq])


def block_rows(near_ref, far_ref):
    return jnp.concatenate([near_ref[...], far_ref[...]], axis=0).reshape(256, near_ref.shape[2])


def soft_probs(query, key, live):
    scores = mult_trans(query, key)
    scores = jnp.where(live, scores, -1e30)
    top = jnp.max(scores, axis=1, keepdims=True)
    weights = jnp.where(live, jnp.exp(scores - top), 0.0)
    return weights / jnp.sum(weights, axis=1, keepdims=True)


def attend_kernel(
    info_ref, near_ref, far_ref, gain_ref, mult_ref, w_ref, pre_ref, att_ref
):
    seq = pl.program_id(0)
    live = live_pairs(info_ref, seq)
    wide = block_rows(near_ref, far_ref).astype(jnp.float32)
    inverse = lax.rsqrt(jnp.mean(wide * wide, axis=1, keepdims=True) + 1e-06)
    hidden = (wide * inverse * gain_ref[...]).astype(jnp.bfloat16)
    pre = jnp.dot(hidden, w_ref[...], preferred_element_type=jnp.float32)
    pre_ref[...] = pre.reshape(2, 4, 32, 480)
    query = (pre[:, 0:160] * mult_ref[...]).astype(jnp.bfloat16)
    key = pre[:, 160:320].astype(jnp.bfloat16)
    value = pre[:, 320:480].astype(jnp.bfloat16)
    heads = []
    for head in range(2):
        part = slice(80 * head, 80 * head + 80)
        probs = soft_probs(query[:, part], key[:, part], live).astype(jnp.bfloat16)
        heads.append(jnp.dot(probs, value[:, part], preferred_element_type=jnp.float32))
    att = jnp.concatenate(heads, axis=1).astype(jnp.bfloat16).reshape(2, 4, 32, 160)
    for chip in range(4):
        for core in range(2):
            att_ref[chip, core] = att[core, chip]


def attend_back_kernel(
    info_ref, near_ref, far_ref, gain_ref, mult_ref, w_ref, pre_ref, grad_near, grad_far, gain_two_ref,
    hid_near, hid_far, send_ref, w_acc, gain_acc, scale_acc, lines,
):
    seq = pl.program_id(0)

    @pl.when(seq == 0)
    def _():
        w_acc[...] = jnp.zeros_like(w_acc)
        gain_acc[...] = jnp.zeros_like(gain_acc)
        scale_acc[...] = jnp.zeros_like(scale_acc)

    live = live_pairs(info_ref, seq)
    wide = block_rows(near_ref, far_ref).astype(jnp.float32)
    inverse = lax.rsqrt(jnp.mean(wide * wide, axis=1, keepdims=True) + 1e-06)
    normed = wide * inverse
    hidden = (normed * gain_ref[...]).astype(jnp.bfloat16)
    pre = pre_ref[...].reshape(256, 480)
    mult = mult_ref[...]
    query = (pre[:, 0:160] * mult).astype(jnp.bfloat16)
    key = pre[:, 160:320].astype(jnp.bfloat16)
    value = pre[:, 320:480].astype(jnp.bfloat16)
    grad_att = jnp.concatenate([grad_near[:, 0], grad_far[:, 0]], axis=0).reshape(256, 160)
    grad_q, grad_k, grad_v = [], [], []
    for head in range(2):
        part = slice(80 * head, 80 * head + 80)
        probs = soft_probs(query[:, part], key[:, part], live)
        grad_probs = mult_trans(grad_att[:, part], value[:, part])
        delta = jnp.sum(probs * grad_probs, axis=1, keepdims=True)
        grad_scores = (probs * (grad_probs - delta)).astype(jnp.bfloat16)
        grad_v.append(trans_mult(probs.astype(jnp.bfloat16), grad_att[:, part]))
        grad_q.append(jnp.dot(grad_scores, key[:, part], preferred_element_type=jnp.float32))
        grad_k.append(trans_mult(grad_scores, query[:, part]))
    grad_query = jnp.concatenate(grad_q, axis=1)
    scale_acc[...] += jnp.sum(grad_query * pre[:, 0:160], axis=0, keepdims=True)
    joined = jnp.concatenate([grad_query * mult] + grad_k + grad_v, axis=1).astype(jnp.bfloat16)
    w_acc[...] += trans_mult(hidden, joined)
    grad_hidden = mult_trans(joined, w_ref[...])
    gain_acc[...] += jnp.sum(grad_hidden * normed, axis=0, keepdims=True)
    low = grad_hidden.astype(jnp.bfloat16).reshape(2, 4, 32, 1280)
    hid_near[...] = low[0]
    hid_far[...] = low[1]

    @pl.when(seq == 3)
    def _():
        lines[...] = jnp.zeros_like(lines)
        for which, source in enumerate((gain_acc, gain_two_ref)):
            for owner in range(32):
                lane = 120 * (owner % 4) + 40 * which
                lines[owner // 4, :, lane : lane + 40] = source[:, 40 * owner : 40 * owner + 40]
        for part in range(4):
            lane = 120 * part + 80
            lines[info_ref[1], :, lane : lane + 40] = scale_acc[:, 40 * part : 40 * part + 40]
        blank = jnp.zeros((14, 480), jnp.float32)
        for target in range(4):
            rows = w_acc[320 * target : 320 * target + 320, :]
            block = jnp.concatenate([rows, lines[2 * target], lines[2 * target + 1], blank], axis=0)
            send_ref[target] = block.astype(jnp.bfloat16)


def feed_kernel(
    info_ref, x_ref, g_ref, atts, far_atts, gain_ref,
    near_rows, across_a, across_b, far_near_rows, far_across_a, far_across_b,
    out_ref, pack_ref, dmid_ref, datt_0, datt_1, datt_2, datt_3, gain_grad,
    weights, sems,
):
    y_index, core_index = info_ref[1] // 4, (info_ref[1] // 2) % 2
    copies = []
    for w in range(3):
        moved = []
        for core, own, others in (
            (core_index, near_rows, (across_a, across_b)),
            (1 - core_index, far_near_rows, (far_across_a, far_across_b)),
        ):
            moved.append((own.at[:, w], weights.at[w, :, y_index, core]))
            for half in range(2):
                moved.append((others[half].at[:, w], weights.at[w, pl.ds(2 * half, 2), 1 - y_index, core]))
        copies.append([pltpu.make_async_copy(*refs, sems.at[w, i]) for i, refs in enumerate(moved)])
    size = x_ref.shape[1]
    for group in copies:
        for copy in group:
            copy.start()
    datts = (datt_0, datt_1, datt_2, datt_3)

    for copy in copies[0]:
        copy.wait()
    heads = [(chip, core, info_ref[1] ^ (CODES[chip] + 2 * core)) for chip in range(4) for core in range(2)]
    middle = x_ref[...].astype(jnp.float32)
    for chip, core, source in heads:
        rows = weights[0, source // 2, source & 1].reshape(160, size)
        middle += jnp.dot((far_atts if core else atts)[chip, core], rows, preferred_element_type=jnp.float32)
    inverse = lax.rsqrt(jnp.mean(middle * middle, axis=1, keepdims=True) + 1e-06)
    normed = middle * inverse
    gain = gain_ref[...]
    hidden = (normed * gain).astype(jnp.bfloat16)
    pack_ref[1] = hidden
    for copy in copies[1]:
        copy.wait()
    up = jnp.dot(hidden, weights[1].reshape(size, size), preferred_element_type=jnp.float32)
    sigma = jax.nn.sigmoid(up)
    active = (up * sigma).astype(jnp.bfloat16)
    pack_ref[0] = active
    for copy in copies[2]:
        copy.wait()
    down = jnp.dot(active, weights[2].reshape(size, size), preferred_element_type=jnp.float32)
    result = middle + down
    for seq in range(4):
        for plane_z in range(4):
            row = 32 * seq + 8 * plane_z
            out_ref[plane_z, seq] = result[row : row + 8].astype(jnp.bfloat16)
    cot = g_ref[...]
    grad_act = mult_trans(cot, weights[2].reshape(size, size))
    grad_up = (grad_act * sigma * (1.0 + up * (1.0 - sigma))).astype(jnp.bfloat16)
    pack_ref[2] = grad_up
    grad_hidden = mult_trans(grad_up, weights[1].reshape(size, size))
    gain_grad[...] = jnp.sum(grad_hidden * normed, axis=0, keepdims=True)
    grad_mid = cot.astype(jnp.float32) + norm_back(grad_hidden, normed, inverse, gain)
    dmid_ref[...] = grad_mid
    low = grad_mid.astype(jnp.bfloat16)
    pack_ref[3] = low
    for chip, core, source in heads:
        rows = weights[0, source // 2, source & 1].reshape(160, size)
        datts[chip][core] = mult_trans(low, rows).astype(jnp.bfloat16)


def grads_kernel(
    info_ref, pack_ref, far_pack, atts, far_atts, cot_ref, far_cot, keep_a, away_a, keep_b, away_b, stage, sems
):
    y_index, core_index, x_index = info_ref[1] // 4, (info_ref[1] // 2) % 2, info_ref[1] % 2

    def leave(w):
        copies = []
        for half in range(2):
            for i in range(2):
                moves = ((stage.at[w, half, i, 1 - x_index], away_a), (stage.at[w, 2 + half, 1 - y_index, i], away_b))
                for j, (block, target) in enumerate(moves):
                    sem = sems.at[w, 4 * half + 2 * i + j]
                    copies.append(pltpu.make_async_copy(block, target.at[half, w, i], sem))
        return copies

    def keep():
        for half in range(2):
            for w in range(3):
                for i in range(2):
                    keep_a[half, w, i] = stage[w, half, i, x_index]
                    keep_b[half, w, i] = stage[w, 2 + half, y_index, i]

    def store(w, made):
        for i in range(16):
            stage[w, i // 4, (i // 2) % 2, i % 2] = made[40 * i : 40 * i + 40].astype(jnp.bfloat16)

    def both(near, far):
        return jnp.concatenate([near, far], axis=0)

    cots = both(cot_ref[...], far_cot[...])
    for core in range(2):

        @pl.when(core_index == core)
        def _():
            def own_columns(near, far):
                return both(*(
                    jnp.concatenate([ref[:, 160 * i + 80 * core : 160 * i + 80 * core + 80] for i in range(8)], axis=1)
                    for ref in (near, far)
                ))

            acts = own_columns(pack_ref.at[0], far_pack.at[0])
            store(2, trans_mult(acts, cots))
            for copy in leave(2):
                copy.start()
            acts = own_columns(pack_ref.at[1], far_pack.at[1])
            store(1, trans_mult(acts, both(pack_ref[2], far_pack[2])))
            for copy in leave(1):
                copy.start()
            grads = both(pack_ref[3], far_pack[3])
            pieces = []
            for chip in range(4):
                for source in range(2):
                    near, far = (far_atts, far_atts) if source else (atts, atts)
                    pieces.append(both(near[chip, source], far[chip, 1 - source])[:, 80 * core : 80 * core + 80])
            made = trans_mult(jnp.concatenate(pieces, axis=1), grads)
            for i in range(8):
                source = info_ref[1] ^ (CODES[i // 2] + 2 * (i % 2))
                for part in range(2):
                    row = 80 * i + 40 * part
                    stage[0, source // 2, source & 1, part] = made[row : row + 40].astype(jnp.bfloat16)
            for copy in leave(0):
                copy.start()

    keep()
    for w in range(3):
        for copy in leave(w):
            copy.wait()


def meet_kernel(far_side, info_ref, mine_a, from_a, mine_b, from_b, out_a, out_b):
    y_index, x_index = info_ref[1] // 4, info_ref[1] % 2
    if far_side:
        y_index, x_index = 1 - y_index, 1 - x_index
    for half in range(2):
        for w in range(3):
            out_a[half, w] = sum_low(mine_a[half, w, y_index], from_a[half, w, y_index])
            out_b[half, w] = sum_low(mine_b[half, w, x_index], from_b[half, w, x_index])


def join_kernel(keep_a, from_a, keep_b, from_b, out_ref):
    for half in range(2):
        for w in range(3):
            out_ref[half, w] = sum_low(keep_a[half, w], from_a[half, w])
            out_ref[2 + half, w] = sum_low(keep_b[half, w], from_b[half, w])


def sum_low(left, right):
    return (left.astype(jnp.float32) + right.astype(jnp.float32)).astype(jnp.bfloat16)


def norm_kernel(info_ref, hid_0, hid_1, hid_2, hid_3, x_ref, dmid_ref, gain_ref, out_0, out_1, out_2, out_3, rows):
    grad = hid_0[...].astype(jnp.float32)
    for item in (hid_1, hid_2, hid_3):
        grad += item[...].astype(jnp.float32)
    wide = x_ref[...].astype(jnp.float32)
    inverse = lax.rsqrt(jnp.mean(wide * wide, axis=1, keepdims=True) + 1e-06)
    grad = dmid_ref[...] + norm_back(grad, wide * inverse, inverse, gain_ref[...])
    for seq in range(4):
        for plane_z in range(4):
            row = 32 * seq + 8 * plane_z
            rows[plane_z, seq] = grad[row : row + 8]
    for hop, out in enumerate((out_0, out_1, out_2, out_3)):
        out[...] = rows[(info_ref[0] + hop) & 3].astype(jnp.bfloat16)


def fold_kernel(in_ref, out_ref, line):
    total = in_ref[0].astype(jnp.float32)
    line[...] = jnp.zeros_like(line)
    for owner in range(8):
        lane = 120 * (owner % 4)
        line[0:1, 0:120] = total[320 + owner // 4 : 321 + owner // 4, lane : lane + 120]
        block = jnp.concatenate([total[40 * owner : 40 * owner + 40], line[...]], axis=0)
        out_ref[owner] = block.astype(jnp.bfloat16)


def spread_kernel(in_ref, *outs):
    for which, out in enumerate(outs):
        for owner in range(8):
            part = in_ref[owner, 0:40, 160 * which : 160 * which + 160]
            out[:, 160 * owner : 160 * owner + 160] = part.astype(jnp.float32)


def widen_kernel(in_ref, *outs):
    for which, out in enumerate(outs):
        out[...] = in_ref[which].astype(jnp.float32)


def whole(shape):
    return pl.BlockSpec(shape, lambda *_: (0,) * len(shape))


def seq_block(*lead, width):
    count = len(lead)
    return pl.BlockSpec((*lead, 32, width), lambda s, info: (*(0,) * count, s, 0))


def planes(
    inputs, cotangent, w_query, w_key, w_value, w_output, w_up, w_down,
    attn_gain, mlp_gain, query_scale, deal, lengths,
):
    f32, bf16 = jnp.float32, jnp.bfloat16
    z, y, c, x = (lax.axis_index(name) for name in ("z", "y", "core", "x"))
    plane = 4 * y + 2 * c + x
    width = 1280
    seqs = jnp.arange(16, dtype=jnp.int32)
    seq_lengths = jnp.sum(jnp.where(deal[None, :] == seqs[:, None], lengths[None, :], 0), axis=1)
    my_lengths = lax.dynamic_slice_in_dim(seq_lengths, 4 * z, 4, 0)
    info = jnp.concatenate([jnp.stack([z, plane]), my_lengths]).astype(jnp.int32)

    vec = jnp.concatenate([attn_gain, mlp_gain, query_scale]).astype(bf16)
    vec_block = jnp.zeros((1, 8, width), bf16).at[0, 0, :120].set(vec)
    in_four = inputs.reshape(4, 4, 8, width)
    sent = [jnp.concatenate([pick(in_four, (z + k) % 4), vec_block]) for k in range(4)]
    qkv = jnp.stack([w_query, w_key, w_value]).astype(bf16)
    *sent, qkv = lax.optimization_barrier((*sent, qkv))
    got = [sent[0]] + [ring_shift(sent[k], k) for k in (1, 2, 3)]
    x_rows = by_source([item[:4] for item in got], z, 1).reshape(128, width)
    vec_rows = by_source([item[4, 0] for item in got], z, 0)
    vec_rows = jnp.concatenate([vec_rows, jnp.zeros((4, width), bf16)])
    own = jnp.concatenate([x_rows, vec_rows])

    big = jnp.stack([w_output, w_up, w_down]).astype(bf16)
    big = lax.all_gather(big, "z", axis=0)

    qkv = qkv.reshape(3, 40, 8, 160).transpose(2, 1, 0, 3).reshape(8, 40, 480)
    qkv = lax.all_to_all(qkv, ("y", "core", "x"), split_axis=0, concat_axis=0, tiled=True)
    own, qkv = lax.optimization_barrier((own, qkv))
    near = jnp.stack([own] + [plane_shift(own, step) for step in (1, 2, 3)])
    big, near, cotangent, qkv = lax.optimization_barrier((big, near, cotangent, qkv.reshape(320, 480)))
    w_qkv = lax.all_gather(qkv, "z", axis=0, tiled=True)
    far = core_swap(near)
    beside, across = plane_shift(big, 1), plane_shift(big, 2)
    relay_a, relay_b = beside[:2], across[2:]
    cot_rows = lax.all_to_all(cotangent.reshape(4, 4, 8, width), "z", split_axis=0, concat_axis=0, tiled=True)
    relay_a, relay_b, cot_rows = lax.optimization_barrier((relay_a, relay_b, cot_rows))
    across_a, across_b = plane_shift(relay_a, 2), plane_shift(relay_b, 1)

    vecs = jnp.stack([near[:, 128:132, :120], far[:, 128:132, :120]])
    vecs = vecs.astype(f32).reshape(2, 2, 2, 4, 120)
    vecs = jnp.where(c == 0, vecs, vecs[::-1])
    vecs = jnp.where(y == 0, vecs, vecs[:, ::-1])
    vecs = jnp.where(x == 0, vecs, vecs[:, :, ::-1])
    vecs = vecs.reshape(2, 2, 2, 4, 3, 40).transpose(4, 3, 1, 0, 2, 5).reshape(3, width)
    gain_one, gain_two = vecs[0:1], vecs[1:2]
    my_scale = lax.dynamic_slice_in_dim(vecs[2:3], 160 * plane, 160, 1)
    query_mult = LOG2E / math.sqrt(HD) * jax.nn.softplus(my_scale)


    def limit(megabytes):
        return pltpu.CompilerParams(vmem_limit_bytes=megabytes * 1024 * 1024)

    pre, att_made = pl.pallas_call(
        attend_kernel,
        grid_spec=pltpu.PrefetchScalarGridSpec(
            num_scalar_prefetch=1,
            grid=(4,),
            in_specs=[
                seq_block(4, width=width), seq_block(4, width=width),
                whole((1, width)), whole((1, 160)), whole((width, 480)),
            ],
            out_specs=[seq_block(2, 4, width=480), seq_block(4, 2, width=160)],
        ),
        out_shape=[
            jax.ShapeDtypeStruct((2, 4, 128, 480), f32),
            jax.ShapeDtypeStruct((4, 2, 128, 160), bf16),
        ],
        compiler_params=limit(14),
        cost_estimate=pl.CostEstimate(flops=9_000_000_000, bytes_accessed=8_000_000, transcendentals=600_000),
        name="attend",
    )(info, near, far, gain_one, query_mult, w_qkv)

    near_rows = pair(big, beside, x, 2).reshape(4, 3, 80, width)
    att_made, far_near_rows, across_a, across_b = lax.optimization_barrier(
        (att_made, core_swap(near_rows), across_a, across_b)
    )
    atts = [att_made[0]] + [plane_shift(att_made[step], step) for step in (1, 2, 3)]
    atts = jnp.stack(atts)
    far_atts = core_swap(atts)
    across_a = pair(across[:2], across_a, x, 2).reshape(2, 3, 80, width)
    across_b = pair(across[2:], across_b, x, 2).reshape(2, 3, 80, width)
    far_across_a, far_across_b = core_swap(across_a), core_swap(across_b)
    cot_rows = cot_rows.transpose(1, 0, 2, 3).reshape(128, width)
    far_cot = core_swap(cot_rows)
    far_cot, far_atts, cot_rows = lax.optimization_barrier((far_cot, far_atts, cot_rows))
    datt_shape = jax.ShapeDtypeStruct((2, 128, 160), bf16)
    smem = pl.BlockSpec(memory_space=pltpu.SMEM)
    vmem = pl.BlockSpec(memory_space=pltpu.VMEM)
    hbm = pl.BlockSpec(memory_space=pltpu.HBM)
    out_rows, pack, grad_mid, *datts, gain_two_grad = pl.pallas_call(
        feed_kernel,
        in_specs=[smem] + [vmem] * 5 + [hbm] * 6,
        out_specs=[vmem] * 8,
        out_shape=[
            jax.ShapeDtypeStruct((4, 4, 8, width), bf16),
            jax.ShapeDtypeStruct((4, 128, width), bf16),
            jax.ShapeDtypeStruct((128, width), f32),
        ]
        + [datt_shape] * 4
        + [jax.ShapeDtypeStruct((1, width), f32)],
        scratch_shapes=[pltpu.VMEM((3, 4, 2, 2, 80, width), bf16), pltpu.SemaphoreType.DMA((3, 6))],
        compiler_params=limit(36),
        cost_estimate=pl.CostEstimate(flops=12_000_000_000, bytes_accessed=13_000_000, transcendentals=200_000),
        name="feed",
    )(info, x_rows, cot_rows, atts, far_atts, gain_two, near_rows, across_a, across_b, far_near_rows, far_across_a, far_across_b)

    back = [datts[0]] + [plane_shift(datts[step], step) for step in (1, 2, 3)]

    mine_a, away_a, mine_b, away_b = pl.pallas_call(
        grads_kernel,
        in_specs=[smem] + [vmem] * 6,
        out_specs=[vmem, hbm, vmem, hbm],
        out_shape=[jax.ShapeDtypeStruct((2, 3, 2, 40, width), bf16)] * 4,
        scratch_shapes=[pltpu.VMEM((3, 4, 2, 2, 40, width), bf16), pltpu.SemaphoreType.DMA((3, 8))],
        compiler_params=limit(22),
        cost_estimate=pl.CostEstimate(flops=6_000_000_000, bytes_accessed=8_000_000, transcendentals=0),
        name="grads",
    )(info, pack, core_swap(pack), atts, far_atts, cot_rows, far_cot)

    mine_a, away_a, mine_b, away_b, *back = lax.optimization_barrier((mine_a, away_a, mine_b, away_b, *back))
    away_a, away_b, grad_atts = lax.optimization_barrier((away_a, away_b, jnp.stack(back)))
    from_a, from_b = plane_shift(away_a, 1), plane_shift(away_b, 2)
    hid_near, hid_far, send = pl.pallas_call(
        attend_back_kernel,
        grid_spec=pltpu.PrefetchScalarGridSpec(
            num_scalar_prefetch=1,
            grid=(4,),
            in_specs=[
                seq_block(4, width=width), seq_block(4, width=width),
                whole((1, width)), whole((1, 160)), whole((width, 480)),
                seq_block(2, 4, width=480),
                *[pl.BlockSpec((4, 1, 32, 160), lambda s, info, core=core: (0, core, s, 0)) for core in range(2)],
                whole((1, width)),
            ],
            out_specs=[
                seq_block(4, width=width), seq_block(4, width=width),
                whole((4, 336, 480)),
            ],
            scratch_shapes=[
                pltpu.VMEM((width, 480), f32), pltpu.VMEM((1, width), f32),
                pltpu.VMEM((1, 160), f32), pltpu.VMEM((8, 1, 480), f32),
            ],
        ),
        out_shape=[
            jax.ShapeDtypeStruct((4, 128, width), bf16),
            jax.ShapeDtypeStruct((4, 128, width), bf16),
            jax.ShapeDtypeStruct((4, 336, 480), bf16),
        ],
        compiler_params=limit(22),
        cost_estimate=pl.CostEstimate(flops=15_000_000_000, bytes_accessed=12_000_000, transcendentals=600_000),
        name="attend_back",
    )(info, near, far, gain_one, query_mult, w_qkv, pre, grad_atts, core_swap(grad_atts), gain_two_grad)

    send, out_rows = lax.optimization_barrier((send, out_rows))
    sums = lax.psum_scatter(send, "z", scatter_dimension=0, tiled=True)
    out_sent = [pick(out_rows, (z + k) % 4) for k in range(4)]
    out_one, out_three = ring_shift(out_sent[1], 1), ring_shift(out_sent[3], 3)
    from_a, from_b, hid_far, out_one, out_three = lax.optimization_barrier(
        (from_a, from_b, hid_far, out_one, out_three)
    )
    swapped = core_swap(hid_far)
    hid = [sum_low(hid_near[i], swapped[i]) for i in range(4)]
    def meet(far_side, *parts):
        return pl.pallas_call(
            functools.partial(meet_kernel, far_side),
            in_specs=[smem] + [vmem] * 4,
            out_specs=[vmem] * 2,
            out_shape=[jax.ShapeDtypeStruct((2, 3, 40, width), bf16)] * 2,
            compiler_params=limit(50),
            cost_estimate=pl.CostEstimate(flops=2_000_000_000, bytes_accessed=4_000_000, transcendentals=0),
            name="meet",
        )(info, *parts)

    parts = mine_a, from_a, mine_b, from_b
    away_a, away_b = meet(True, *parts)
    keep_a, keep_b = meet(False, *parts)
    from_a, from_b = plane_shift(away_a, 2), plane_shift(away_b, 1)
    *hid, from_a, from_b, out_sent[2] = lax.optimization_barrier((*hid, from_a, from_b, out_sent[2]))
    out_two = ring_shift(out_sent[2], 2)
    kept = pl.pallas_call(
        join_kernel,
        in_specs=[vmem] * 4,
        out_specs=vmem,
        out_shape=jax.ShapeDtypeStruct((4, 3, 40, width), bf16),
        compiler_params=limit(50),
        cost_estimate=pl.CostEstimate(flops=2_000_000_000, bytes_accessed=4_000_000, transcendentals=0),
        name="join",
    )(keep_a, from_a, keep_b, from_b)
    moved = [plane_shift(hid[step], step) for step in (1, 2, 3)]
    moved[0], sums, out_two = lax.optimization_barrier((moved[0], sums, out_two))
    outputs = by_source([out_sent[0], out_one, out_two, out_three], z, 0).reshape(16, 8, width)
    big_sums = lax.psum_scatter(kept, "z", scatter_dimension=0, tiled=True)[0]
    grad_home = pl.pallas_call(
        norm_kernel,
        in_specs=[smem] + [vmem] * 7,
        out_specs=[vmem] * 4,
        out_shape=[jax.ShapeDtypeStruct((4, 8, width), bf16)] * 4,
        scratch_shapes=[pltpu.VMEM((4, 4, 8, width), f32)],
        compiler_params=limit(10),
        cost_estimate=pl.CostEstimate(flops=2_000_000_000, bytes_accessed=2_500_000, transcendentals=128),
        name="norm",
    )(info, hid[0], *moved, x_rows, grad_mid, gain_one)
    sums = pl.pallas_call(
        fold_kernel,
        in_specs=[vmem],
        out_specs=vmem,
        out_shape=jax.ShapeDtypeStruct((8, 48, 480), bf16),
        scratch_shapes=[pltpu.VMEM((8, 480), f32)],
        compiler_params=limit(8),
        cost_estimate=pl.CostEstimate(flops=2_000_000_000, bytes_accessed=1_600_000, transcendentals=0),
        name="fold",
    )(sums)
    sums = lax.all_to_all(sums, ("y", "core", "x"), split_axis=0, concat_axis=0, tiled=True)
    rows_shape = [jax.ShapeDtypeStruct((40, width), f32)] * 3
    qkv_sums = pl.pallas_call(
        spread_kernel, in_specs=[vmem], out_specs=[vmem] * 3, out_shape=rows_shape, compiler_params=limit(6), name="spread"
    )(sums)
    big_sums = pl.pallas_call(
        widen_kernel, in_specs=[vmem], out_specs=[vmem] * 3, out_shape=rows_shape, compiler_params=limit(6), name="widen"
    )(big_sums)
    line_sums = jnp.sum(sums[:, 40, :120].astype(f32), axis=0).reshape(3, 40)
    scale_low = query_scale.astype(bf16).astype(f32)
    scale_sum = LOG2E / math.sqrt(HD) * jax.nn.sigmoid(scale_low) * line_sums[2]
    grad_home = [grad_home[0]] + [ring_shift(grad_home[k], k) for k in (1, 2, 3)]
    grad_home[2], *qkv_sums, scale_sum = lax.optimization_barrier((grad_home[2], *qkv_sums, scale_sum))
    grad_home = by_source(grad_home, z, 0).reshape(16, 8, width)

    return (
        outputs, grad_home, qkv_sums[0], qkv_sums[1], qkv_sums[2],
        big_sums[0], big_sums[1], big_sums[2], line_sums[0], line_sums[1], scale_sum,
    )


def solution(mesh):
    names = ("dp", "ctx")
    body = per_device
    if dict(mesh.shape) == {"dp": 16, "ctx": 2}:
        mesh = Mesh(mesh.devices.reshape(4, 2, 2, 2), ("z", "y", "core", "x"))
        names = mesh.axis_names
        body = planes
    seq, mat, line = P(None, names, None), P(names, None), P(names)
    return jax.shard_map(
        body,
        mesh=mesh,
        in_specs=(seq,) * 2 + (mat,) * 6 + (line,) * 3 + (P(), P()),
        out_specs=(seq,) * 2 + (mat,) * 6 + (line,) * 3,
        check_vma=False,
    )
```
